32 devices in a mesh: ctx: 8 (over z, x), tp: 4 (over y, core).
Axes of the slice: x: 2, y: 2, z: 4, core: 2. Of those that a mesh axis runs over, the one named last changes fastest.
Arguments:
- block_input: bfloat16 [6144, 2048], P('ctx'), may hold values from -6 to 6
- cotangent: bfloat16 [6144, 2048], P('ctx'), may hold values from -6 to 6
- ln1_gain: float32 [2048], replicated, may hold values from 0.1 to 1.9
- ln1_bias: float32 [2048], replicated, may hold values from -1.5 to 1.5
- w_qkv: bfloat16 [3, 2048, 2048], P(None, None, 'tp'), may hold values from -0.125 to 0.125
- qv_bias: float32 [2, 2048], P(None, 'tp'), may hold values from -1.5 to 1.5
- w_out: bfloat16 [2048, 2048], P('tp'), may hold values from -0.5 to 0.5
- out_bias: float32 [2048], replicated, may hold values from -1.5 to 1.5
- ln2_gain: float32 [2048], replicated, may hold values from 0.1 to 1.9
- ln2_bias: float32 [2048], replicated, may hold values from -1.5 to 1.5
- w_fc1: bfloat16 [2048, 8192], P(None, 'tp'), may hold values from -0.125 to 0.125
- fc1_bias: float32 [8192], P('tp'), may hold values from -1.5 to 1.5
- w_fc2: bfloat16 [8192, 2048], P('tp'), may hold values from -0.09375 to 0.09375
- fc2_bias: float32 [2048], replicated, may hold values from -1.5 to 1.5
- exit_layer: int32 [6144], P('ctx'), may hold values from 0 to 24
- layer_index: int32 [1], replicated, may hold values from 8 to 13
- lengths: int32 [4], replicated, may hold values from 1 to 4, as said below
- stretch_map: int32 [8], replicated, may hold values from 0 to 7, as said below
Outputs:
- activations: bfloat16 [6144, 2048], P('ctx')
- input_grad: bfloat16 [6144, 2048], P('ctx')
- ln1_gain_grad: float32 [2048], replicated
- ln1_bias_grad: float32 [2048], replicated
- w_qkv_grad: float32 [3, 2048, 2048], P(None, 'ctx', 'tp')
- qv_bias_grad: float32 [2, 2048], P(None, 'tp')
- w_out_grad: float32 [2048, 2048], P('tp', 'ctx')
- out_bias_grad: float32 [2048], replicated
- ln2_gain_grad: float32 [2048], replicated
- ln2_bias_grad: float32 [2048], replicated
- w_fc1_grad: float32 [2048, 8192], P('ctx', 'tp')
- fc1_bias_grad: float32 [8192], P('tp')
- w_fc2_grad: float32 [8192, 2048], P('tp', 'ctx')
- fc2_bias_grad: float32 [2048], replicated
The draws below stay inside these ranges and needn't reach their ends.
Inputs may be any that keep to these rules, and one draw needn't show every extreme that they name: `lengths`: they add up to 8, and the longest is 4. `stretch_map`: each number once.
All inputs are finite; a program needn't handle non-finite values.
Results may differ from the reference program's by a relative error of at most 0.014.
Values may be sent and summed in bfloat16 or wider, within the bound.
A program may use at most 256 MiB of HBM per device.

```python
import jax
import jax.numpy as jnp
from jax import lax

D = 2048
HEADS = 32
HEAD = 64
FF = 8192
LAYERS = 24
TOK_DEV = 768
PREFIX = 256
TOKENS = 6144
N_CTX = 8


def stretch_plan(key):
    group_count = N_CTX // 8
    subkeys = jax.random.split(key, 5)
    first_len = jax.random.randint(subkeys[0], (group_count,), 1, 5)
    forced = jax.random.randint(subkeys[1], (), 0, group_count)
    first_len = jnp.where(jnp.arange(group_count) == forced, 4, first_len)
    second_len = jax.random.randint(subkeys[2], (group_count,), 1, jnp.minimum(5, 7 - first_len))
    third_low = jnp.maximum(1, 4 - first_len - second_len)
    third_high = jnp.minimum(4, 7 - first_len - second_len)
    third_len = jax.random.randint(subkeys[3], (group_count,), third_low, third_high + 1)
    fourth_len = 8 - first_len - second_len - third_len
    lengths = jnp.stack([first_len, second_len, third_len, fourth_len], axis=1).reshape(-1).astype(jnp.int32)
    starts = jnp.cumsum(lengths) - lengths
    head_start = starts[4 * forced]
    placing = jax.random.permutation(subkeys[4], N_CTX).astype(jnp.int32)
    for target_slot, offset_in in ((N_CTX // 2, 0), (0, 1), (N_CTX // 2 + 1, 2), (N_CTX - 1, 3)):
        wanted = (head_start + offset_in).astype(jnp.int32)
        location = jnp.argmax(placing == wanted)
        displaced = placing[target_slot]
        placing = placing.at[location].set(displaced).at[target_slot].set(wanted)
    return (lengths, placing.astype(jnp.int32))


def draw_lengths(key, part):
    return stretch_plan(key)[0]


def draw_stretch_map(key, part):
    return stretch_plan(key)[1]


def draw_exit_layer(key, part):
    key = jax.random.fold_in(key, 7)
    subkeys = jax.random.split(key, 4)
    base_level = jax.random.randint(subkeys[0], (N_CTX, 1), 0, 17)
    jitter = jax.random.randint(subkeys[1], (N_CTX, TOK_DEV), 0, 12)
    levels = jnp.minimum(base_level + jitter, LAYERS).reshape(-1)
    total_rows = N_CTX * TOK_DEV
    top_slot = jax.random.randint(subkeys[2], (), 0, total_rows)
    zero_slot = (top_slot + 1 + jax.random.randint(subkeys[3], (), 0, total_rows - 1)) % total_rows
    return levels.at[top_slot].set(LAYERS).at[zero_slot].set(0).astype(jnp.int32)


def block_levels(stream_key, dims, cuts, least, top_value):
    level, own = 1.0, jax.random.fold_in(stream_key, 6)
    for dim, blocks in cuts:
        heights = jnp.exp(jax.random.uniform(jax.random.fold_in(own, dim), (blocks,), jnp.float32, least / len(cuts), top_value / len(cuts)))
        level = level * jnp.repeat(heights, dims[dim] // blocks).reshape([-1 if axis == dim else 1 for axis in range(len(dims))])
    return level


def normal_values(own_key, dims, width, reach, cuts=(), kind=jnp.bfloat16):
    entries = width * jax.random.normal(own_key, dims, jnp.float32)
    if cuts:
        entries = entries * block_levels(own_key, dims, cuts, -0.22, 0.18)
    return jnp.clip(entries, -reach, reach).astype(kind)


def setup_inputs(seed: int = 0) -> dict:
    splits = jax.random.split(jax.random.key(seed), 19)
    block_input = normal_values(splits[0], (TOKENS, D), 1.0, 6.0, ((0, 8),))
    cotangent = normal_values(splits[1], (TOKENS, D), 1.0, 6.0, ((0, 8),))
    ln1_gain = jnp.clip(1.0 + 0.18 * jax.random.normal(splits[2], (D,), jnp.float32), 0.1, 1.9)
    ln1_bias = normal_values(splits[3], (D,), 0.3, 1.5, (), jnp.float32)
    w_qkv = normal_values(splits[4], (3, D, D), D ** -0.5, 0.125, ((2, 4),))
    qv_bias = normal_values(splits[5], (2, D), 0.3, 1.5, ((1, 4),), jnp.float32)
    w_out = normal_values(splits[6], (D, D), (D // 16) ** -0.5, 0.5, ((0, 4),))
    out_bias = normal_values(splits[7], (D,), 0.3, 1.5, (), jnp.float32)
    ln2_gain = jnp.clip(1.0 + 0.18 * jax.random.normal(splits[8], (D,), jnp.float32), 0.1, 1.9)
    ln2_bias = normal_values(splits[9], (D,), 0.3, 1.5, (), jnp.float32)
    w_fc1 = normal_values(splits[10], (D, FF), D ** -0.5, 0.125, ((1, 4),))
    fc1_bias = normal_values(splits[11], (FF,), 0.3, 1.5, ((0, 4),), jnp.float32)
    w_fc2 = normal_values(splits[12], (FF, D), (FF // 2) ** -0.5, 0.09375, ((0, 4),))
    fc2_bias = normal_values(splits[13], (D,), 0.3, 1.5, (), jnp.float32)
    exit_layer = draw_exit_layer(jax.random.fold_in(splits[18], 71), 0)
    layer_index = jax.random.randint(splits[15], (1,), 8, 14).astype(jnp.int32)
    lengths = draw_lengths(jax.random.fold_in(splits[18], 71), 0)
    stretch_map = draw_stretch_map(jax.random.fold_in(splits[18], 71), 0)
    return {"block_input": block_input, "cotangent": cotangent, "ln1_gain": ln1_gain, "ln1_bias": ln1_bias, "w_qkv": w_qkv, "qv_bias": qv_bias, "w_out": w_out, "out_bias": out_bias, "ln2_gain": ln2_gain, "ln2_bias": ln2_bias, "w_fc1": w_fc1, "fc1_bias": fc1_bias, "w_fc2": w_fc2, "fc2_bias": fc2_bias, "exit_layer": exit_layer, "layer_index": layer_index, "lengths": lengths, "stretch_map": stretch_map}


@jax.custom_vjp
def low(v):
    return lax.optimization_barrier(v.astype(jnp.bfloat16)).astype(jnp.float32)

@jax.custom_vjp
def low_back(v):
    return v

def low_keep(v):
    return (low(v), None)

def low_pass(kept, grad):
    return (grad,)

def back_keep(v):
    return (v, None)

def back_low(kept, grad):
    return (low(grad),)
low.defvjp(low_keep, low_pass)
low_back.defvjp(back_keep, back_low)
HIGHEST = lax.Precision.HIGHEST
NEGATIVE = -1e+30
EPSILON = 1e-05

def layer_norm(values_in, gain_row, shift_row):
    centred = values_in - lax.optimization_barrier(jnp.mean(values_in, axis=1, keepdims=True))
    spread = lax.optimization_barrier(jnp.mean(centred * centred, axis=1, keepdims=True))
    return centred * lax.rsqrt(spread + EPSILON) * gain_row + shift_row

def plan(lengths, stretch_map):
    seq_total = lengths.shape[0]
    starts = (jnp.cumsum(lengths) - lengths).astype(jnp.int32)
    inside = (stretch_map[:, None] >= starts[None, :]).astype(jnp.int32)
    seq_of = (lax.optimization_barrier(jnp.sum(inside, axis=1)) - 1).astype(jnp.int32)
    chosen = jnp.arange(seq_total, dtype=jnp.int32)[None, :] == seq_of[:, None]
    first_stretch = lax.optimization_barrier(jnp.sum(jnp.where(chosen, starts[None, :], 0), axis=1)).astype(jnp.int32)
    block_part = (stretch_map - first_stretch).astype(jnp.int32)
    devices = jnp.arange(stretch_map.shape[0], dtype=jnp.int32)
    block_owner = lax.optimization_barrier(jnp.sum(jnp.where(stretch_map[None, :] == first_stretch[:, None], devices[None, :], 0), axis=1)).astype(jnp.int32)
    seq_owner = lax.optimization_barrier(jnp.sum(jnp.where(stretch_map[None, :] == starts[:, None], devices[None, :], 0), axis=1)).astype(jnp.int32)
    return (seq_of, block_part, block_owner, seq_owner)

def block_attention(query_rows, key_rows, value_rows, prefix_keys, prefix_values, has_prefix):
    row_count = query_rows.shape[0]
    score_scale = HEAD ** (-0.5)
    near_scores = jnp.einsum('ihd,jhd->hij', query_rows, key_rows, precision=HIGHEST)
    far_scores = jnp.einsum('ihd,jhd->hij', query_rows, prefix_keys, precision=HIGHEST)
    scores = low_back(jnp.concatenate([near_scores, far_scores], axis=2) * score_scale)
    position = jnp.arange(row_count, dtype=jnp.int32)
    causal = position[:, None] >= position[None, :]
    prefix_reach = jnp.broadcast_to(has_prefix, (row_count, PREFIX))
    visible = jnp.concatenate([causal, prefix_reach], axis=1)
    probs = low(jax.nn.softmax(jnp.where(visible[None], scores, NEGATIVE), axis=-1))
    value_all = jnp.concatenate([value_rows, prefix_values], axis=0)
    return jnp.einsum('hij,jhd->ihd', probs, value_all, precision=HIGHEST)

def block_forward(inputs, ln1_gain, ln1_bias, w_qkv, qv_bias, w_out, out_bias, ln2_gain, ln2_bias, w_fc1, fc1_bias, w_fc2, fc2_bias, active, block_part, block_owner):
    block_count = block_part.shape[0]
    row_count = inputs.shape[0] // block_count
    h_low = low(layer_norm(inputs, ln1_gain, ln1_bias))
    query = low(low_back(jnp.dot(h_low, w_qkv[0], precision=HIGHEST) + qv_bias[0]))
    key_all = low(low_back(jnp.dot(h_low, w_qkv[1], precision=HIGHEST)))
    value = low(low_back(jnp.dot(h_low, w_qkv[2], precision=HIGHEST) + qv_bias[1]))
    split_shape = (block_count, row_count, HEADS, HEAD)
    query_blocks = query.reshape(split_shape)
    key_blocks = key_all.reshape(split_shape)
    value_blocks = value.reshape(split_shape)
    prefix_keys = key_blocks[block_owner, :PREFIX]
    prefix_values = value_blocks[block_owner, :PREFIX]
    attend = jax.checkpoint(block_attention)
    attended = lax.map(lambda entry_tuple: attend(*entry_tuple), (query_blocks, key_blocks, value_blocks, prefix_keys, prefix_values, block_part > 0))
    attended = low(low_back(attended.reshape(block_count * row_count, HEADS * HEAD)))
    branch = low_back(jnp.dot(attended, w_out, precision=HIGHEST) + out_bias)
    middle = inputs + active * branch
    h2_low = low(layer_norm(middle, ln2_gain, ln2_bias))
    hidden_pre = low_back(jnp.dot(h2_low, w_fc1, precision=HIGHEST) + fc1_bias)
    hidden_low = low(jax.nn.gelu(hidden_pre))
    ffn_branch = low_back(jnp.dot(hidden_low, w_fc2, precision=HIGHEST) + fc2_bias)
    return middle + active * ffn_branch

def reference(block_input, cotangent, ln1_gain, ln1_bias, w_qkv, qv_bias, w_out, out_bias, ln2_gain, ln2_bias, w_fc1, fc1_bias, w_fc2, fc2_bias, exit_layer, layer_index, lengths, stretch_map):
    seq_of, block_part, block_owner, seq_owner = plan(lengths, stretch_map)
    token_total = block_input.shape[0]
    row_count = token_total // N_CTX
    index_all = jnp.arange(token_total, dtype=jnp.int32)
    first_part = block_part[index_all // row_count] == 0
    active = ((exit_layer > layer_index[0]) | first_part & (index_all % row_count < PREFIX)).astype(jnp.float32)[:, None]
    weights = tuple((weight.astype(jnp.float32) for weight in (ln1_gain, ln1_bias, w_qkv, qv_bias, w_out, out_bias, ln2_gain, ln2_bias, w_fc1, fc1_bias, w_fc2, fc2_bias)))

    def run(inputs, *params):
        return block_forward(inputs, *params, active, block_part, block_owner)
    result, pullback = jax.vjp(run, block_input.astype(jnp.float32), *weights)
    grads = pullback(cotangent.astype(jnp.float32))
    return (result.astype(jnp.bfloat16), grads[0].astype(jnp.bfloat16), grads[1], grads[2], grads[3], grads[4], grads[5], grads[6], grads[7], grads[8], grads[9], grads[10], grads[11], grads[12])
```

```python
import jax
import jax.numpy as jnp
from jax import lax
from jax.sharding import PartitionSpec as P

HEAD = 64
PREFIX = 256


NEGATIVE = -1e30
EPSILON = 1e-05


def layer_norm(values_in, gain_row, shift_row):
    centred = values_in - jnp.mean(values_in, axis=1, keepdims=True)
    spread = jnp.mean(centred * centred, axis=1, keepdims=True)
    return centred * lax.rsqrt(spread + EPSILON) * gain_row + shift_row


def product(left, right):
    return jnp.dot(left, right, preferred_element_type=jnp.float32)


def inner_rows(left, right):
    return lax.dot_general(
        left, right, (((0,), (0,)), ((), ())), preferred_element_type=jnp.float32
    )


def outer_cols(left, right):
    return lax.dot_general(
        left, right, (((1,), (1,)), ((), ())), preferred_element_type=jnp.float32
    )


def plan(lengths, stretch_map):
    seq_total = lengths.shape[0]
    starts = jnp.cumsum(lengths) - lengths
    inside = (stretch_map[:, None] >= starts[None, :]).astype(jnp.int32)
    seq_of = jnp.sum(inside, axis=1) - 1
    chosen = jnp.arange(seq_total, dtype=jnp.int32)[None, :] == seq_of[:, None]
    first_stretch = jnp.sum(jnp.where(chosen, starts[None, :], 0), axis=1)
    block_part = stretch_map - first_stretch
    devices = jnp.arange(stretch_map.shape[0], dtype=jnp.int32)
    block_owner = jnp.sum(
        jnp.where(stretch_map[None, :] == first_stretch[:, None], devices[None, :], 0), axis=1
    )
    seq_owner = jnp.sum(
        jnp.where(stretch_map[None, :] == starts[:, None], devices[None, :], 0), axis=1
    )
    return (seq_of, block_part, block_owner, seq_owner)


def body(
    block_input,
    cotangent,
    ln1_gain,
    ln1_bias,
    w_qkv,
    qv_bias,
    w_out,
    out_bias,
    ln2_gain,
    ln2_bias,
    w_fc1,
    fc1_bias,
    w_fc2,
    fc2_bias,
    exit_layer,
    layer_index,
    lengths,
    stretch_map,
):
    row_count = block_input.shape[0]
    head_cols = w_qkv.shape[2]
    head_count = head_cols // HEAD
    score_scale = HEAD ** (-0.5)
    device = lax.axis_index("ctx")
    seq_of, block_part, block_owner, seq_owner = plan(lengths, stretch_map)
    my_part = block_part[device]
    my_owner = block_owner[device]
    has_prefix = my_part > 0
    position = jnp.arange(row_count, dtype=jnp.int32)
    active = ((exit_layer > layer_index[0]) | (my_part == 0) & (position < PREFIX)).astype(
        jnp.float32
    )[:, None]
    causal = position[:, None] >= position[None, :]
    visible = jnp.concatenate([causal, jnp.broadcast_to(has_prefix, (row_count, PREFIX))], axis=1)[
        None
    ]
    input_wide = block_input.astype(jnp.float32)

    def attention_scores(query_heads, key_heads):
        raw_scores = (
            jnp.einsum("ihd,jhd->hij", query_heads, key_heads, preferred_element_type=jnp.float32)
            * score_scale
        )
        return jnp.where(visible, raw_scores, NEGATIVE)

    tp_index = lax.axis_index("tp")
    tp_size = lax.axis_size("tp")
    own_rows = row_count // tp_size
    slice_rows = PREFIX // tp_size

    def mine(array):
        return lax.dynamic_slice_in_dim(array, tp_index * own_rows, own_rows, 0)

    def sum_rows(partial):
        low = partial.astype(jnp.bfloat16)
        return lax.psum_scatter(low, "tp", scatter_dimension=0, tiled=True).astype(jnp.float32)

    def all_rows(own):
        return lax.all_gather(own, "tp", axis=0, tiled=True)

    def sum_blocks(partial, dim):
        low = partial.astype(jnp.bfloat16)
        return lax.psum_scatter(low, "ctx", scatter_dimension=dim, tiled=True).astype(jnp.float32)

    start = lax.dynamic_slice_in_dim(block_input, tp_index * slice_rows, slice_rows, 0)
    starts_all = lax.all_gather(start, "ctx", axis=0, tiled=True)
    picked = lax.dynamic_slice_in_dim(starts_all, my_owner * slice_rows, slice_rows, 0)
    prefix_input = lax.all_gather(picked, "tp", axis=0, tiled=True)
    h_low = layer_norm(input_wide, ln1_gain, ln1_bias).astype(jnp.bfloat16)
    h_prefix = layer_norm(prefix_input.astype(jnp.float32), ln1_gain, ln1_bias).astype(jnp.bfloat16)
    query_low = (product(h_low, w_qkv[0]) + qv_bias[0]).astype(jnp.bfloat16)
    key_low = product(h_low, w_qkv[1]).astype(jnp.bfloat16)
    value_low = (product(h_low, w_qkv[2]) + qv_bias[1]).astype(jnp.bfloat16)
    key_prefix = product(h_prefix, w_qkv[1]).astype(jnp.bfloat16)
    value_prefix = (product(h_prefix, w_qkv[2]) + qv_bias[1]).astype(jnp.bfloat16)
    query_heads = query_low.reshape(row_count, head_count, HEAD)
    key_heads = jnp.concatenate([key_low, key_prefix], axis=0).reshape(-1, head_count, HEAD)
    value_heads = jnp.concatenate([value_low, value_prefix], axis=0).reshape(-1, head_count, HEAD)
    masked = attention_scores(query_heads, key_heads)
    peak = jnp.max(masked, axis=2, keepdims=True)
    log_total = peak + jnp.log(jnp.sum(jnp.exp(masked - peak), axis=2, keepdims=True))
    probs_low = jnp.exp(masked - log_total).astype(jnp.bfloat16)
    attended = jnp.einsum(
        "hij,jhd->ihd", probs_low, value_heads, preferred_element_type=jnp.float32
    )
    attended = attended.astype(jnp.bfloat16).reshape(row_count, head_cols)
    own_active = mine(active)
    own_input = mine(block_input).astype(jnp.float32)
    own_cotangent = mine(cotangent).astype(jnp.float32)
    branch = sum_rows(product(attended, w_out)) + out_bias
    middle = own_input + own_active * branch
    h2_low = all_rows(layer_norm(middle, ln2_gain, ln2_bias).astype(jnp.bfloat16))
    upstream = cotangent.astype(jnp.float32)
    grad_ffn = (active * upstream).astype(jnp.bfloat16)
    d_fc2_bias = jnp.sum(mine(grad_ffn).astype(jnp.float32), axis=0)
    hidden_pre = product(h2_low, w_fc1) + fc1_bias
    hidden_low = jax.nn.gelu(hidden_pre).astype(jnp.bfloat16)
    d_hidden = outer_cols(grad_ffn, w_fc2)
    gelu_back = jax.vjp(jax.nn.gelu, hidden_pre)[1]
    d_pre_low = gelu_back(d_hidden)[0].astype(jnp.bfloat16)
    d_h2 = sum_rows(outer_cols(d_pre_low, w_fc1))
    fc2_grad = sum_blocks(inner_rows(hidden_low, grad_ffn), 1)
    fc1_grad = sum_blocks(inner_rows(h2_low, d_pre_low), 0)
    d_fc1_bias = jnp.sum(d_pre_low.astype(jnp.float32), axis=0)
    ffn_branch = sum_rows(product(hidden_low, w_fc2)) + fc2_bias
    output_rows = all_rows((middle + own_active * ffn_branch).astype(jnp.bfloat16))
    norm2_back = jax.vjp(layer_norm, middle, ln2_gain, ln2_bias)[1]
    d_middle_part, d_ln2_gain, d_ln2_bias = norm2_back(d_h2)
    d_middle = own_cotangent + d_middle_part
    own_grad_attn = (own_active * d_middle).astype(jnp.bfloat16)
    d_out_bias = jnp.sum(own_grad_attn.astype(jnp.float32), axis=0)
    grad_attn = all_rows(own_grad_attn)
    d_attended = (
        outer_cols(grad_attn, w_out).astype(jnp.bfloat16).reshape(row_count, head_count, HEAD)
    )
    out_grad = sum_blocks(inner_rows(attended, grad_attn), 1)
    masked = attention_scores(query_heads, key_heads)
    probs = jnp.exp(masked - log_total)
    probs_low = probs.astype(jnp.bfloat16)
    d_value_heads = jnp.einsum(
        "hij,ihd->jhd", probs_low, d_attended, preferred_element_type=jnp.float32
    )
    d_probs = jnp.einsum(
        "ihd,jhd->hij", d_attended, value_heads, preferred_element_type=jnp.float32
    )
    row_inner = jnp.sum(probs * d_probs, axis=2, keepdims=True)
    d_scores = (probs * (d_probs - row_inner)).astype(jnp.bfloat16)
    d_query = (
        jnp.einsum("hij,jhd->ihd", d_scores, key_heads, preferred_element_type=jnp.float32)
        * score_scale
    )
    d_query = d_query.astype(jnp.bfloat16).reshape(row_count, head_cols)
    d_key_heads = (
        jnp.einsum("hij,ihd->jhd", d_scores, query_heads, preferred_element_type=jnp.float32)
        * score_scale
    )
    d_key_rows = d_key_heads.reshape(-1, head_cols)
    d_value_rows = d_value_heads.reshape(-1, head_cols)
    prefix_term = jnp.concatenate([d_key_rows[row_count:], d_value_rows[row_count:]], axis=1)
    owner_of_row = jnp.arange(PREFIX * lax.axis_size("ctx"), dtype=jnp.int32) // PREFIX
    wanted = ((owner_of_row == my_owner) & has_prefix)[:, None]
    returned = lax.psum_scatter(
        jnp.where(
            wanted,
            jnp.tile(prefix_term.astype(jnp.bfloat16), (lax.axis_size("ctx"), 1)),
            jnp.bfloat16(0.0),
        ),
        "ctx",
        scatter_dimension=0,
        tiled=True,
    ).astype(jnp.float32)
    d_key = jnp.concatenate(
        [d_key_rows[:PREFIX] + returned[:, :head_cols], d_key_rows[PREFIX:row_count]], axis=0
    ).astype(jnp.bfloat16)
    d_value = jnp.concatenate(
        [d_value_rows[:PREFIX] + returned[:, head_cols:], d_value_rows[PREFIX:row_count]], axis=0
    ).astype(jnp.bfloat16)
    d_h = sum_rows(
        outer_cols(d_query, w_qkv[0]) + outer_cols(d_key, w_qkv[1]) + outer_cols(d_value, w_qkv[2])
    )
    d_qkv = jnp.stack(
        [inner_rows(h_low, d_query), inner_rows(h_low, d_key), inner_rows(h_low, d_value)]
    )
    qkv_grad = sum_blocks(d_qkv, 1)
    d_qv_bias = jnp.stack(
        [jnp.sum(d_query.astype(jnp.float32), axis=0), jnp.sum(d_value.astype(jnp.float32), axis=0)]
    )
    norm1_back = jax.vjp(layer_norm, own_input, ln1_gain, ln1_bias)[1]
    d_input_part, d_ln1_gain, d_ln1_bias = norm1_back(d_h)
    input_grad = all_rows((d_middle + d_input_part).astype(jnp.bfloat16))
    shared = lax.psum(
        jnp.stack([d_ln1_gain, d_ln1_bias, d_out_bias, d_ln2_gain, d_ln2_bias, d_fc2_bias]),
        ("ctx", "tp"),
    )
    gain1_grad, bias1_grad, out_bias_grad, gain2_grad, bias2_grad, fc2_bias_grad = shared
    qv_grad, fc1_bias_grad = lax.psum((d_qv_bias, d_fc1_bias), "ctx")
    return (
        output_rows,
        input_grad,
        gain1_grad,
        bias1_grad,
        qkv_grad,
        qv_grad,
        out_grad,
        out_bias_grad,
        gain2_grad,
        bias2_grad,
        fc1_grad,
        fc1_bias_grad,
        fc2_grad,
        fc2_bias_grad,
    )


def solution(mesh):
    in_specs = (
        P("ctx", None),
        P("ctx", None),
        P(),
        P(),
        P(None, None, "tp"),
        P(None, "tp"),
        P("tp", None),
        P(),
        P(),
        P(),
        P(None, "tp"),
        P("tp"),
        P("tp", None),
        P(),
        P("ctx"),
        P(),
        P(),
        P(),
    )
    out_specs = (
        P("ctx", None),
        P("ctx", None),
        P(),
        P(),
        P(None, "ctx", "tp"),
        P(None, "tp"),
        P("tp", "ctx"),
        P(),
        P(),
        P(),
        P("ctx", "tp"),
        P("tp"),
        P("tp", "ctx"),
        P(),
    )
    return jax.shard_map(body, mesh=mesh, in_specs=in_specs, out_specs=out_specs, check_vma=False)
```

```python
import functools

import jax
import jax.numpy as jnp
from jax import lax
from jax.experimental import pallas as pl
from jax.experimental.pallas import tpu as pltpu
from jax.sharding import PartitionSpec as P

HEAD = 64
PREFIX = 256
COLS = 512
RING = 16
SKEW = 2
STAGES = 4
MESH = pl.DeviceIdType.MESH


NEGATIVE = -1e30
EPSILON = 1e-05


def layer_norm(values_in, gain_row, shift_row):
    centred = values_in - jnp.mean(values_in, axis=1, keepdims=True)
    spread = jnp.mean(centred * centred, axis=1, keepdims=True)
    return centred * lax.rsqrt(spread + EPSILON) * gain_row + shift_row


def product(left, right):
    return jnp.dot(left, right, preferred_element_type=jnp.float32)


def inner_rows(left, right):
    return lax.dot_general(
        left, right, (((0,), (0,)), ((), ())), preferred_element_type=jnp.float32
    )


def outer_cols(left, right):
    return lax.dot_general(
        left, right, (((1,), (1,)), ((), ())), preferred_element_type=jnp.float32
    )


def plan(lengths, stretch_map):
    seq_total = lengths.shape[0]
    starts = jnp.cumsum(lengths) - lengths
    inside = (stretch_map[:, None] >= starts[None, :]).astype(jnp.int32)
    seq_of = jnp.sum(inside, axis=1) - 1
    chosen = jnp.arange(seq_total, dtype=jnp.int32)[None, :] == seq_of[:, None]
    first_stretch = jnp.sum(jnp.where(chosen, starts[None, :], 0), axis=1)
    block_part = stretch_map - first_stretch
    devices = jnp.arange(stretch_map.shape[0], dtype=jnp.int32)
    block_owner = jnp.sum(
        jnp.where(stretch_map[None, :] == first_stretch[:, None], devices[None, :], 0), axis=1
    )
    seq_owner = jnp.sum(
        jnp.where(stretch_map[None, :] == starts[:, None], devices[None, :], 0), axis=1
    )
    return (seq_of, block_part, block_owner, seq_owner)


def reduce_kernel(lines, groups, ops, *refs):
    operands=refs[:ops]; out=refs[ops]
    (xs,xr,zb,stage,s_xs,s_xr,s_zr,s_zs,s_out)=refs[ops+1:]
    ctx=lax.axis_index("ctx"); tp=lax.axis_index("tp")
    z=ctx//2; side=ctx%2
    partner=(z*2+1-side,tp); left=(ctx-2,tp); right=(ctx+2,tp)
    barrier=pltpu.get_barrier_semaphore()
    pl.semaphore_signal(barrier,inc=1,device_id=partner,device_id_type=MESH)
    @pl.when(z>0)
    def _(): pl.semaphore_signal(barrier,inc=1,device_id=left,device_id_type=MESH)
    @pl.when(z<lines-1)
    def _(): pl.semaphore_signal(barrier,inc=1,device_id=right,device_id_type=MESH)
    pl.semaphore_wait(barrier,1+jnp.where(z>0,1,0)+jnp.where(z<lines-1,1,0))
    rows=xr.shape[2]
    steps=sum(g[2] for g in groups)*lines
    def owner_of(k):
        o=k
        return o
    def part(xt,y,depth,j,block):
        lhs=xt[pl.ds(pl.multiple_of(block*rows,rows),rows),:depth]
        rhs=y[:depth,pl.ds(pl.multiple_of(j*COLS,COLS),COLS)]
        return jnp.dot(lhs,rhs,preferred_element_type=jnp.float32)
    def xcopy(slot,job,o):
        return pltpu.make_async_remote_copy(src_ref=xs.at[slot],dst_ref=xr.at[job,o],send_sem=s_xs.at[slot],recv_sem=s_xr.at[job,o],device_id=partner,device_id_type=MESH)
    def send(g,i,job0,wait):
        xi,yi,count,depth=g
        j=i//lines; o=owner_of(i%lines); job=job0+j
        slot=lax.rem(job0*lines+i,RING)
        if wait:
            xcopy(slot,job,o).wait_send()
        xs[slot]=part(operands[xi],operands[yi],depth,j,o*2+1-side).astype(jnp.bfloat16)
        xcopy(slot,job,o).start()
    flat=[]
    job0=0
    for g in groups:
        for i in range(g[2]*lines): flat.append((g,i,job0))
        job0+=g[2]
    def run_group_sends(lo,hi,wait):
        k=0;jb=0
        for g in groups:
            n=g[2]*lines
            a=max(lo,k)-k; b=min(hi,k+n)-k
            if b>a:
                def body(i,_,g=g,jb=jb): send(g,i,jb,wait); return 0
                lax.fori_loop(a,b,body,0)
            k+=n; jb+=g[2]
    run_group_sends(0,min(RING,steps),False)
    def zl(job,o):
        return pltpu.make_async_remote_copy(src_ref=xr.at[job,o],dst_ref=zb.at[job,o],send_sem=s_zs.at[job,o],recv_sem=s_zr.at[job,o],device_id=right,device_id_type=MESH)
    def zr(job,o,dst):
        return pltpu.make_async_remote_copy(src_ref=xr.at[job,o],dst_ref=zb.at[job,dst],send_sem=s_zs.at[job,o],recv_sem=s_zr.at[job,dst],device_id=left,device_id_type=MESH)
    def recv(g,i,job0):
        xi,yi,count,depth=g
        j=i//lines; o=owner_of(i%lines); job=job0+j
        xcopy(0,job,o).wait_recv()
        val=part(operands[xi],operands[yi],depth,j,o*2+side)+xr[job,o].astype(jnp.float32)
        @pl.when(z!=o)
        def _(): xr[job,o]=val.astype(jnp.bfloat16)
        @pl.when(z==o)
        def _():
            slot=lax.rem(job,STAGES)
            @pl.when(job>=STAGES)
            def _(): pltpu.make_async_copy(stage.at[slot],out.at[job-STAGES],s_out.at[slot]).wait()
            stage[slot]=val
    def flow(t):
        f=t-SKEW*z
        job=f//lines; o=lax.rem(f,lines)
        @pl.when((f>=0)&(f<steps)&(z<o))
        def _():
            @pl.when(z>0)
            def _():
                zl(job,o).wait_recv()
                xr[job,o]=(xr[job,o].astype(jnp.float32)+zb[job,o].astype(jnp.float32)).astype(jnp.bfloat16)
            zl(job,o).start()
        f2=t-SKEW*(lines-1-z)
        job2=f2//lines; o2=lax.rem(f2,lines)
        @pl.when((f2>=0)&(f2<steps)&(z>o2))
        def _():
            @pl.when(z<lines-1)
            def _():
                zr(job2,o2,o2).wait_recv()
                xr[job2,o2]=(xr[job2,o2].astype(jnp.float32)+zb[job2,o2].astype(jnp.float32)).astype(jnp.bfloat16)
            zr(job2,o2,jnp.where(z-1==o2,lines,o2)).start()
        f3=t-SKEW*(lines-1)
        job3=f3//lines; o3=lax.rem(f3,lines)
        @pl.when((f3>=0)&(f3<steps)&(o3==z))
        def _():
            slot=lax.rem(job3,STAGES)
            @pl.when(z>0)
            def _():
                zl(job3,z).wait_recv()
                stage[slot]+=zb[job3,z].astype(jnp.float32)
            @pl.when(z<lines-1)
            def _():
                zr(job3,z,lines).wait_recv()
                stage[slot]+=zb[job3,lines].astype(jnp.float32)
            pltpu.make_async_copy(stage.at[slot],out.at[job3],s_out.at[slot]).start()
    k=0; jb=0
    pend=RING
    bounds=set([0,steps])
    acc=0
    for g in groups:
        acc+=g[2]*lines; bounds.add(acc)
        if acc-RING>0: bounds.add(acc-RING)
    bounds=sorted(b for b in bounds if b<=steps)
    def find(f):
        k=0;jb=0
        for g in groups:
            n=g[2]*lines
            if f<k+n: return g,k,jb
            k+=n; jb+=g[2]
        return None
    for lo,hi in zip(bounds[:-1],bounds[1:]):
        rg=find(lo); sg=find(lo+RING)
        def body(f,_,rg=rg,sg=sg):
            recv(rg[0],f-rg[1],rg[2])
            flow(f)
            if sg is not None: send(sg[0],f+RING-sg[1],sg[2],True)
            return 0
        lax.fori_loop(lo,hi,body,0)
    def tail(t,_):
        flow(t); return 0
    lax.fori_loop(steps,steps+SKEW*(lines-1),tail,0)
    def drain_x(s,_):
        xcopy(s,0,0).wait_send(); return 0
    lax.fori_loop(0,min(RING,steps),drain_x,0)
    jobs=steps//lines
    def drain_z(f,_):
        job=f//lines; o=f%lines
        @pl.when(o!=z)
        def _(): zl(job,o).wait_send()
        return 0
    lax.fori_loop(0,steps,drain_z,0)
    for d in range(max(0,jobs-STAGES),jobs):
        pltpu.make_async_copy(stage.at[d%STAGES],out.at[d],s_out.at[d%STAGES]).wait()

def reduce_grads(mesh,groups,operands,cid):
    n_ctx=mesh.shape["ctx"]; lines=n_ctx//2
    jobs=sum(g[2] for g in groups); rows=2048//n_ctx
    return pl.pallas_call(functools.partial(reduce_kernel,lines,groups,len(operands)),
        out_shape=jax.ShapeDtypeStruct((jobs,rows,COLS),jnp.float32),
        in_specs=[pl.BlockSpec(memory_space=pltpu.VMEM)]*len(operands), out_specs=pl.BlockSpec(memory_space=pl.ANY),
        scratch_shapes=[pltpu.VMEM((RING,rows,COLS),jnp.bfloat16),pltpu.VMEM((jobs,lines,rows,COLS),jnp.bfloat16),
            pltpu.VMEM((jobs,lines+1,rows,COLS),jnp.bfloat16),pltpu.VMEM((STAGES,rows,COLS),jnp.float32),
            pltpu.SemaphoreType.DMA((RING,)),pltpu.SemaphoreType.DMA((jobs,lines)),pltpu.SemaphoreType.DMA((jobs,lines+1)),pltpu.SemaphoreType.DMA((jobs,lines)),pltpu.SemaphoreType.DMA((STAGES,))],
        compiler_params=pltpu.CompilerParams(collective_id=cid,has_side_effects=True,vmem_limit_bytes=63*2**20))(*operands)


def body(
    mesh,
    block_input,
    cotangent,
    ln1_gain,
    ln1_bias,
    w_qkv,
    qv_bias,
    w_out,
    out_bias,
    ln2_gain,
    ln2_bias,
    w_fc1,
    fc1_bias,
    w_fc2,
    fc2_bias,
    exit_layer,
    layer_index,
    lengths,
    stretch_map,
):
    row_count = block_input.shape[0]
    head_cols = w_qkv.shape[2]
    head_count = head_cols // HEAD
    score_scale = HEAD ** (-0.5)
    device = lax.axis_index("ctx")
    seq_of, block_part, block_owner, seq_owner = plan(lengths, stretch_map)
    my_part = block_part[device]
    my_owner = block_owner[device]
    has_prefix = my_part > 0
    position = jnp.arange(row_count, dtype=jnp.int32)
    active = ((exit_layer > layer_index[0]) | (my_part == 0) & (position < PREFIX)).astype(
        jnp.float32
    )[:, None]
    causal = position[:, None] >= position[None, :]
    visible = jnp.concatenate([causal, jnp.broadcast_to(has_prefix, (row_count, PREFIX))], axis=1)[
        None
    ]
    input_wide = block_input.astype(jnp.float32)

    def attention_scores(query_heads, key_heads):
        raw_scores = (
            jnp.einsum("ihd,jhd->hij", query_heads, key_heads, preferred_element_type=jnp.float32)
            * score_scale
        )
        return jnp.where(visible, raw_scores, NEGATIVE)

    tp_index = lax.axis_index("tp")
    tp_size = lax.axis_size("tp")
    own_rows = row_count // tp_size
    slice_rows = PREFIX // tp_size

    def mine(array):
        return lax.dynamic_slice_in_dim(array, tp_index * own_rows, own_rows, 0)

    def sum_rows(partial):
        low = partial.astype(jnp.bfloat16)
        return lax.psum_scatter(low, "tp", scatter_dimension=0, tiled=True).astype(jnp.float32)

    def all_rows(own):
        return lax.all_gather(own, "tp", axis=0, tiled=True)

    def sum_blocks(partial, dim):
        low = partial.astype(jnp.bfloat16)
        return lax.psum_scatter(low, "ctx", scatter_dimension=dim, tiled=True).astype(jnp.float32)

    start = lax.dynamic_slice_in_dim(block_input, tp_index * slice_rows, slice_rows, 0)
    starts_all = lax.all_gather(start, "ctx", axis=0, tiled=True)
    picked = lax.dynamic_slice_in_dim(starts_all, my_owner * slice_rows, slice_rows, 0)
    prefix_input = lax.all_gather(picked, "tp", axis=0, tiled=True)
    h_low = layer_norm(input_wide, ln1_gain, ln1_bias).astype(jnp.bfloat16)
    h_prefix = layer_norm(prefix_input.astype(jnp.float32), ln1_gain, ln1_bias).astype(jnp.bfloat16)
    query_low = (product(h_low, w_qkv[0]) + qv_bias[0]).astype(jnp.bfloat16)
    key_low = product(h_low, w_qkv[1]).astype(jnp.bfloat16)
    value_low = (product(h_low, w_qkv[2]) + qv_bias[1]).astype(jnp.bfloat16)
    key_prefix = product(h_prefix, w_qkv[1]).astype(jnp.bfloat16)
    value_prefix = (product(h_prefix, w_qkv[2]) + qv_bias[1]).astype(jnp.bfloat16)
    query_heads = query_low.reshape(row_count, head_count, HEAD)
    key_heads = jnp.concatenate([key_low, key_prefix], axis=0).reshape(-1, head_count, HEAD)
    value_heads = jnp.concatenate([value_low, value_prefix], axis=0).reshape(-1, head_count, HEAD)
    masked = attention_scores(query_heads, key_heads)
    peak = jnp.max(masked, axis=2, keepdims=True)
    log_total = peak + jnp.log(jnp.sum(jnp.exp(masked - peak), axis=2, keepdims=True))
    probs_low = jnp.exp(masked - log_total).astype(jnp.bfloat16)
    attended = jnp.einsum(
        "hij,jhd->ihd", probs_low, value_heads, preferred_element_type=jnp.float32
    )
    attended = attended.astype(jnp.bfloat16).reshape(row_count, head_cols)
    own_active = mine(active)
    own_input = mine(block_input).astype(jnp.float32)
    own_cotangent = mine(cotangent).astype(jnp.float32)
    branch = sum_rows(product(attended, w_out)) + out_bias
    middle = own_input + own_active * branch
    h2_low = all_rows(layer_norm(middle, ln2_gain, ln2_bias).astype(jnp.bfloat16))
    upstream = cotangent.astype(jnp.float32)
    grad_ffn = (active * upstream).astype(jnp.bfloat16)
    d_fc2_bias = jnp.sum(mine(grad_ffn).astype(jnp.float32), axis=0)
    hidden_pre = product(h2_low, w_fc1) + fc1_bias
    hidden_low = jax.nn.gelu(hidden_pre).astype(jnp.bfloat16)
    d_hidden = outer_cols(grad_ffn, w_fc2)
    gelu_back = jax.vjp(jax.nn.gelu, hidden_pre)[1]
    d_pre_low = gelu_back(d_hidden)[0].astype(jnp.bfloat16)
    d_h2 = sum_rows(outer_cols(d_pre_low, w_fc1))
    d_fc1_bias = jnp.sum(d_pre_low.astype(jnp.float32), axis=0)
    ffn_branch = sum_rows(product(hidden_low, w_fc2)) + fc2_bias
    output_rows = all_rows((middle + own_active * ffn_branch).astype(jnp.bfloat16))
    norm2_back = jax.vjp(layer_norm, middle, ln2_gain, ln2_bias)[1]
    d_middle_part, d_ln2_gain, d_ln2_bias = norm2_back(d_h2)
    d_middle = own_cotangent + d_middle_part
    own_grad_attn = (own_active * d_middle).astype(jnp.bfloat16)
    d_out_bias = jnp.sum(own_grad_attn.astype(jnp.float32), axis=0)
    grad_attn = all_rows(own_grad_attn)
    d_attended = (
        outer_cols(grad_attn, w_out).astype(jnp.bfloat16).reshape(row_count, head_count, HEAD)
    )
    masked = attention_scores(query_heads, key_heads)
    probs = jnp.exp(masked - log_total)
    probs_low = probs.astype(jnp.bfloat16)
    d_value_heads = jnp.einsum(
        "hij,ihd->jhd", probs_low, d_attended, preferred_element_type=jnp.float32
    )
    d_probs = jnp.einsum(
        "ihd,jhd->hij", d_attended, value_heads, preferred_element_type=jnp.float32
    )
    row_inner = jnp.sum(probs * d_probs, axis=2, keepdims=True)
    d_scores = (probs * (d_probs - row_inner)).astype(jnp.bfloat16)
    d_query = (
        jnp.einsum("hij,jhd->ihd", d_scores, key_heads, preferred_element_type=jnp.float32)
        * score_scale
    )
    d_query = d_query.astype(jnp.bfloat16).reshape(row_count, head_cols)
    d_key_heads = (
        jnp.einsum("hij,ihd->jhd", d_scores, query_heads, preferred_element_type=jnp.float32)
        * score_scale
    )
    d_key_rows = d_key_heads.reshape(-1, head_cols)
    d_value_rows = d_value_heads.reshape(-1, head_cols)
    prefix_term = jnp.concatenate([d_key_rows[row_count:], d_value_rows[row_count:]], axis=1)
    owner_of_row = jnp.arange(PREFIX * lax.axis_size("ctx"), dtype=jnp.int32) // PREFIX
    wanted = ((owner_of_row == my_owner) & has_prefix)[:, None]
    returned = lax.psum_scatter(
        jnp.where(
            wanted,
            jnp.tile(prefix_term.astype(jnp.bfloat16), (lax.axis_size("ctx"), 1)),
            jnp.bfloat16(0.0),
        ),
        "ctx",
        scatter_dimension=0,
        tiled=True,
    ).astype(jnp.float32)
    d_key = jnp.concatenate(
        [d_key_rows[:PREFIX] + returned[:, :head_cols], d_key_rows[PREFIX:row_count]], axis=0
    ).astype(jnp.bfloat16)
    d_value = jnp.concatenate(
        [d_value_rows[:PREFIX] + returned[:, head_cols:], d_value_rows[PREFIX:row_count]], axis=0
    ).astype(jnp.bfloat16)
    d_h = sum_rows(
        outer_cols(d_query, w_qkv[0]) + outer_cols(d_key, w_qkv[1]) + outer_cols(d_value, w_qkv[2])
    )
    groups = ((0, 1, 4, row_count), (2, 3, 4, row_count), (4, 5, 1, row_count), (6, 7, 3, row_count))
    grads = reduce_grads(
        mesh,
        groups,
        (
            grad_ffn.T,
            hidden_low,
            h2_low.T,
            d_pre_low,
            grad_attn.T,
            attended,
            h_low.T,
            jnp.concatenate([d_query, d_key, d_value], axis=1),
        ),
        0,
    )
    fc2_grad = grads[0:4].transpose(0, 2, 1).reshape(4 * COLS, -1)
    fc1_grad = grads[4:8].transpose(1, 0, 2).reshape(-1, 4 * COLS)
    out_grad = grads[8].T
    qkv_grad = grads[9:12]
    d_qv_bias = jnp.stack(
        [jnp.sum(d_query.astype(jnp.float32), axis=0), jnp.sum(d_value.astype(jnp.float32), axis=0)]
    )
    norm1_back = jax.vjp(layer_norm, own_input, ln1_gain, ln1_bias)[1]
    d_input_part, d_ln1_gain, d_ln1_bias = norm1_back(d_h)
    input_grad = all_rows((d_middle + d_input_part).astype(jnp.bfloat16))
    shared = lax.psum(
        jnp.stack([d_ln1_gain, d_ln1_bias, d_out_bias, d_ln2_gain, d_ln2_bias, d_fc2_bias]),
        ("ctx", "tp"),
    )
    gain1_grad, bias1_grad, out_bias_grad, gain2_grad, bias2_grad, fc2_bias_grad = shared
    qv_grad, fc1_bias_grad = lax.psum((d_qv_bias, d_fc1_bias), "ctx")
    return (
        output_rows,
        input_grad,
        gain1_grad,
        bias1_grad,
        qkv_grad,
        qv_grad,
        out_grad,
        out_bias_grad,
        gain2_grad,
        bias2_grad,
        fc1_grad,
        fc1_bias_grad,
        fc2_grad,
        fc2_bias_grad,
    )


def solution(mesh):
    in_specs = (
        P("ctx", None),
        P("ctx", None),
        P(),
        P(),
        P(None, None, "tp"),
        P(None, "tp"),
        P("tp", None),
        P(),
        P(),
        P(),
        P(None, "tp"),
        P("tp"),
        P("tp", None),
        P(),
        P("ctx"),
        P(),
        P(),
        P(),
    )
    out_specs = (
        P("ctx", None),
        P("ctx", None),
        P(),
        P(),
        P(None, "ctx", "tp"),
        P(None, "tp"),
        P("tp", "ctx"),
        P(),
        P(),
        P(),
        P("ctx", "tp"),
        P("tp"),
        P("tp", "ctx"),
        P(),
    )
    return jax.shard_map(functools.partial(body, mesh), mesh=mesh, in_specs=in_specs, out_specs=out_specs, check_vma=False)
```

```python
import functools

import jax
import jax.numpy as jnp
from jax import lax
from jax.experimental import pallas as pl
from jax.experimental.pallas import tpu as pltpu
from jax.sharding import PartitionSpec as P

HEAD = 64
PREFIX = 256
COLS = 512
MESH = pl.DeviceIdType.MESH
NEGATIVE = -1e30
EPSILON = 1e-05
AHEAD = 8
SKEW = 2
STAGES = 4
DEPTH = 3


class Ring:
    def __init__(self, lines, groups, refs, out, final=None):
        self.lines, self.groups, self.out, self.final = lines, groups, out, final
        (self.xs, self.xr, self.zb, self.stage, self.s_xs, self.s_xr, self.s_zs, self.s_zr, self.s_out,
         self.c_x, self.c_left, self.c_right) = refs
        self.jobs = sum(count for count, _ in groups)
        self.steps = self.jobs * lines
        self.slots = self.xr.shape[0]
        self.lag = SKEW * (lines - 1) + 2
        ctx, tp = lax.axis_index("ctx"), lax.axis_index("tp")
        self.z, self.side = ctx // 2, lax.rem(ctx, 2)
        self.partner = (self.z * 2 + 1 - self.side, tp)
        self.left, self.right = (ctx - 2, tp), (ctx + 2, tp)

    @staticmethod
    def scratch(lines, rows):
        slots = AHEAD + SKEW * (lines - 1) + 4
        chunk = (rows, COLS)
        return [
            pltpu.VMEM((AHEAD, *chunk), jnp.bfloat16),
            pltpu.VMEM((slots, *chunk), jnp.bfloat16),
            pltpu.VMEM((DEPTH, lines + 1, *chunk), jnp.bfloat16),
            pltpu.VMEM((STAGES, *chunk), jnp.float32),
            pltpu.SemaphoreType.DMA((AHEAD,)),
            pltpu.SemaphoreType.DMA((slots,)),
            pltpu.SemaphoreType.DMA((slots,)),
            pltpu.SemaphoreType.DMA((DEPTH, lines + 1)),
            pltpu.SemaphoreType.DMA((STAGES,)),
            pltpu.SemaphoreType.REGULAR,
            pltpu.SemaphoreType.REGULAR,
            pltpu.SemaphoreType.REGULAR,
        ]

    def peers(self):
        return [(None, self.partner), (self.z > 0, self.left), (self.z < self.lines - 1, self.right)]

    def x_copy(self, f):
        slot, to = lax.rem(f, AHEAD), lax.rem(f, self.slots)
        return pltpu.make_async_remote_copy(
            src_ref=self.xs.at[slot], dst_ref=self.xr.at[to], send_sem=self.s_xs.at[slot],
            recv_sem=self.s_xr.at[to], device_id=self.partner, device_id_type=MESH)

    def z_copy(self, f, to, device):
        slot, level = lax.rem(f, self.slots), lax.rem(f // self.lines, DEPTH)
        return pltpu.make_async_remote_copy(
            src_ref=self.xr.at[slot], dst_ref=self.zb.at[level, to], send_sem=self.s_zs.at[slot],
            recv_sem=self.s_zr.at[level, to], device_id=device, device_id_type=MESH)

    def out_copy(self, job):
        slot = lax.rem(job, STAGES)
        return pltpu.make_async_copy(self.stage.at[slot], self.out.at[job], self.s_out.at[slot])

    def send(self, f, part, job0, fresh):
        if not fresh:
            self.x_copy(f).wait_send()

            @pl.when(f >= self.slots)
            def _():
                pl.semaphore_wait(self.c_x, 1)

        owner = lax.rem(f, self.lines)
        self.xs[lax.rem(f, AHEAD)] = part(f // self.lines - job0, owner * 2 + 1 - self.side).astype(jnp.bfloat16)
        self.x_copy(f).start()

    def receive(self, f, part, job0):
        job, owner, slot = f // self.lines, lax.rem(f, self.lines), lax.rem(f, self.slots)
        self.x_copy(f).wait_recv()
        total = part(job - job0, owner * 2 + self.side) + self.xr[slot].astype(jnp.float32)

        @pl.when(owner != self.z)
        def _():
            self.xr[slot] = total.astype(jnp.bfloat16)

        @pl.when(owner == self.z)
        def _():
            @pl.when(job >= STAGES)
            def _():
                self.out_copy(job - STAGES).wait()
            self.stage[lax.rem(job, STAGES)] = total

    def add(self, f, index):
        job = f // self.lines
        slot, level = lax.rem(f, self.slots), lax.rem(job, DEPTH)

        @pl.when(lax.rem(f, self.lines) == self.z)
        def _():
            self.stage[lax.rem(job, STAGES)] += self.zb[level, index].astype(jnp.float32)

        @pl.when(lax.rem(f, self.lines) != self.z)
        def _():
            self.xr[slot] = (self.xr[slot].astype(jnp.float32) + self.zb[level, index].astype(jnp.float32)).astype(jnp.bfloat16)

    def flow(self, t):
        lines, z = self.lines, self.z
        f = t - SKEW * z
        owner = lax.rem(f + lines * SKEW * lines, lines)

        @pl.when((f >= 0) & (f < self.steps) & (owner >= z))
        def _():
            @pl.when(z > 0)
            def _():
                self.z_copy(f, owner, self.left).wait_recv()
                self.add(f, owner)
                pl.semaphore_signal(self.c_right, inc=1, device_id=self.left, device_id_type=MESH)

            @pl.when(owner > z)
            def _():
                @pl.when(f >= DEPTH * lines)
                def _():
                    pl.semaphore_wait(self.c_right, 1)
                self.z_copy(f, owner, self.right).start()

        g = t - SKEW * (lines - 1 - z)
        owner2 = lax.rem(g + lines * SKEW * lines, lines)

        @pl.when((g >= 0) & (g < self.steps) & (owner2 <= z))
        def _():
            @pl.when(z < lines - 1)
            def _():
                index = jnp.where(owner2 == z, lines, owner2)
                self.z_copy(g, index, self.right).wait_recv()
                self.add(g, index)
                pl.semaphore_signal(self.c_left, inc=1, device_id=self.right, device_id_type=MESH)

            @pl.when(owner2 < z)
            def _():
                @pl.when(g >= DEPTH * lines)
                def _():
                    pl.semaphore_wait(self.c_left, 1)
                self.z_copy(g, jnp.where(owner2 == z - 1, lines, owner2), self.left).start()

        h = t - SKEW * (lines - 1)

        @pl.when((h >= 0) & (h < self.steps) & (lax.rem(h + lines * SKEW * lines, lines) == z))
        def _():
            self.out_copy(h // lines).start()
            if self.final is not None:
                first, count, target, size = self.final
                job = h // lines

                @pl.when((job >= first) & (job < first + count))
                def _():
                    target[pl.ds(pl.multiple_of((job - first) * size, size), size)] = self.stage[lax.rem(job, STAGES)]

        d = t - self.lag

        @pl.when((d >= 0) & (d < self.steps))
        def _():
            @pl.when(lax.rem(d + lines * (SKEW * lines + 2), lines) != z)
            def _():
                self.z_copy(d, 0, self.left).wait_send()
            pl.semaphore_signal(self.c_x, inc=1, device_id=self.partner, device_id_type=MESH)

    def find(self, f):
        job = 0
        for count, part in self.groups:
            if f < (job + count) * self.lines:
                return part, job
            job += count
        return None

    def pieces(self, lo, hi):
        cuts, job = {lo, hi}, 0
        for count, _ in self.groups:
            job += count
            cuts |= {job * self.lines, job * self.lines - AHEAD}
        cuts = sorted(c for c in cuts if lo <= c <= hi)
        return zip(cuts[:-1], cuts[1:])

    def start(self):
        for lo, hi in self.pieces(0, AHEAD):
            part, job0 = self.find(lo)
            lax.fori_loop(lo, hi, lambda f, _, part=part, job0=job0: (self.send(f, part, job0, True), 0)[1], 0)

    def run(self, lo, hi):
        for a, b in self.pieces(lo, min(hi, self.steps)):
            here, ahead = self.find(a), self.find(a + AHEAD)

            def body(f, _, here=here, ahead=ahead):
                self.receive(f, *here)
                self.flow(f)
                if ahead is not None:
                    self.send(f + AHEAD, *ahead, False)
                return 0

            lax.fori_loop(a, b, body, 0)
        if hi > self.steps:
            lax.fori_loop(max(lo, self.steps), hi, lambda t, _: (self.flow(t), 0)[1], 0)

    def run_some(self, lo, count):
        here = self.find(0)

        def body(f, _):
            self.receive(f, *here)
            self.flow(f)

            @pl.when(f + AHEAD < self.steps)
            def _():
                self.send(f + AHEAD, *here, False)
            return 0

        lax.fori_loop(lo, lo + count, body, 0)

    def finish(self, lo):
        lines, z = self.lines, self.z
        self.run(lo, self.steps + self.lag)
        lax.fori_loop(self.steps - AHEAD, self.steps, lambda f, _: (self.x_copy(f).wait_send(), 0)[1], 0)
        for job in range(self.jobs - STAGES, self.jobs):
            self.out_copy(job).wait()
        pl.semaphore_wait(self.c_x, self.slots)

        @pl.when(z < lines - 1)
        def _():
            pl.semaphore_wait(self.c_right, DEPTH * (lines - 1 - z))

        @pl.when(z > 0)
        def _():
            pl.semaphore_wait(self.c_left, DEPTH * z)


def meet(peers):
    barrier = pltpu.get_barrier_semaphore()
    count = 0
    for there, device in peers:
        if there is None:
            pl.semaphore_signal(barrier, inc=1, device_id=device, device_id_type=MESH)
            count += 1
        else:
            @pl.when(there)
            def _():
                pl.semaphore_signal(barrier, inc=1, device_id=device, device_id_type=MESH)
            count += jnp.where(there, 1, 0)
    pl.semaphore_wait(barrier, count)
class Quad:
    def __init__(self, refs, rows, extra=0):
        (self.tmp, self.cs, self.cr, self.ys, self.yr, self.acc, self.s_c, self.r_c, self.s_y, self.r_y,
         self.s_g, self.r_g) = refs
        ctx, tp = lax.axis_index("ctx"), lax.axis_index("tp")
        self.y, self.core, self.tp = tp // 2, lax.rem(tp, 2), tp
        self.across = (ctx, self.y * 2 + 1 - self.core)
        self.over = (ctx, (1 - self.y) * 2 + self.core)
        self.head, self.rest = PREFIX // 4, (rows - PREFIX) // 4
        self.tiles = self.cs.shape[1]

    @staticmethod
    def scratch(rows, width):
        tiles = width // COLS
        return [
            pltpu.VMEM((2, rows, COLS), jnp.float32),
            pltpu.VMEM((2, tiles, rows, COLS), jnp.bfloat16),
            pltpu.VMEM((2, tiles, rows, COLS), jnp.bfloat16),
            pltpu.VMEM((tiles, rows, COLS), jnp.bfloat16),
            pltpu.VMEM((tiles, rows, COLS), jnp.bfloat16),
            pltpu.VMEM((rows, width), jnp.float32),
            pltpu.SemaphoreType.DMA((2, tiles)),
            pltpu.SemaphoreType.DMA((2, tiles)),
            pltpu.SemaphoreType.DMA((tiles,)),
            pltpu.SemaphoreType.DMA((tiles,)),
            pltpu.SemaphoreType.DMA((3, 2)),
            pltpu.SemaphoreType.DMA((3, 2)),
        ]

    def peers(self):
        return [(None, self.across), (None, self.over)]

    def spans(self, quarter):
        return [
            pl.ds(pl.multiple_of(quarter * self.head, 16), self.head),
            pl.ds(pl.multiple_of(PREFIX + quarter * self.rest, 16), self.rest),
        ]

    def rows_of(self, ref, quarter):
        return jnp.concatenate([ref[span] for span in self.spans(quarter)], axis=0)

    def half_of(self, ref, half):
        return jnp.concatenate([self.rows_of(ref, half * 2), self.rows_of(ref, half * 2 + 1)], axis=0)

    def c_copy(self, k, n):
        return pltpu.make_async_remote_copy(
            src_ref=self.cs.at[k, n], dst_ref=self.cr.at[k, n], send_sem=self.s_c.at[k, n],
            recv_sem=self.r_c.at[k, n], device_id=self.across, device_id_type=MESH)

    def y_copy(self, n):
        return pltpu.make_async_remote_copy(
            src_ref=self.ys.at[n], dst_ref=self.yr.at[n], send_sem=self.s_y.at[n],
            recv_sem=self.r_y.at[n], device_id=self.over, device_id_type=MESH)

    def columns(self, n):
        return pl.ds(pl.multiple_of(n * COLS, COLS), COLS)

    def split(self, value, k, n):
        rows = self.acc.shape[0]
        self.tmp[0] = value[:rows]
        self.tmp[1] = value[rows:]
        self.cs[k, n] = self.tmp[1 - self.core].astype(jnp.bfloat16)
        self.c_copy(k, n).start()
        self.acc[:, self.columns(n)] = self.tmp[self.core]

    def relay(self, n):
        self.c_copy(0, n).wait_recv()
        self.ys[n] = (self.acc[:, self.columns(n)] + self.cr[0, n].astype(jnp.float32)).astype(jnp.bfloat16)
        self.y_copy(n).start()

    def scatter_send(self, chunk):
        def far(n, _):
            self.split(chunk(1 - self.y, n), 0, n)

            @pl.when(n > 0)
            def _():
                self.relay(n - 1)
            return 0

        lax.fori_loop(0, self.tiles, far, 0)
        self.relay(self.tiles - 1)

        def near(n, _):
            self.split(chunk(self.y, n), 1, n)
            return 0

        lax.fori_loop(0, self.tiles, near, 0)

    def scatter_add(self, n):
        self.c_copy(1, n).wait_recv()
        self.y_copy(n).wait_recv()
        self.acc[:, self.columns(n)] += self.cr[1, n].astype(jnp.float32) + self.yr[n].astype(jnp.float32)

    def scatter_done(self):
        for n in range(self.tiles):
            self.c_copy(0, n).wait_send()
            self.c_copy(1, n).wait_send()
            self.y_copy(n).wait_send()

    def g_copy(self, full, k, s, quarter, device):
        span = self.spans(quarter)[s]
        return pltpu.make_async_remote_copy(
            src_ref=full.at[span], dst_ref=full.at[span], send_sem=self.s_g.at[k, s],
            recv_sem=self.r_g.at[k, s], device_id=device, device_id_type=MESH)

    def gather_send(self, full):
        for s in range(2):
            self.g_copy(full, 0, s, self.tp, self.over).start()
        for s in range(2):
            self.g_copy(full, 1, s, self.tp, self.across).start()

    def gather_near(self, full):
        for s in range(2):
            self.g_copy(full, 1, s, self.y * 2 + 1 - self.core, self.across).wait_recv()

    def gather_pass(self, full):
        other = (1 - self.y) * 2 + self.core
        for s in range(2):
            self.g_copy(full, 0, s, other, self.over).wait_recv()
            self.g_copy(full, 2, s, other, self.across).start()

    def gather_far(self, full):
        for s in range(2):
            self.g_copy(full, 2, s, (1 - self.y) * 2 + 1 - self.core, self.across).wait_recv()

    def gather_done(self, full):
        other = (1 - self.y) * 2 + self.core
        for s in range(2):
            self.g_copy(full, 0, s, self.tp, self.over).wait_send()
            self.g_copy(full, 1, s, self.tp, self.across).wait_send()
            self.g_copy(full, 2, s, other, self.across).wait_send()


def nt(left, right):
    return lax.dot_general(left, right, (((1,), (1,)), ((), ())), preferred_element_type=jnp.float32)


def normed(values_in):
    centred = values_in - jnp.mean(values_in, axis=1, keepdims=True)
    scale = lax.rsqrt(jnp.mean(centred * centred, axis=1, keepdims=True) + EPSILON)
    return centred * scale, scale


def branch_kernel(att, w_out, x_ref, act_ref, bias, gain, shift, mid_ref, full, *scratch):
    quad = Quad(scratch, att.shape[0])
    meet(quad.peers())
    quad.scatter_send(lambda half, n: jnp.dot(quad.half_of(att, half), w_out[:, quad.columns(n)], preferred_element_type=jnp.float32))
    lax.fori_loop(0, quad.tiles, lambda n, _: (quad.scatter_add(n), 0)[1], 0)
    start = 0
    for span in quad.spans(quad.tp):
        size = span.size
        middle = x_ref[span].astype(jnp.float32) + act_ref[span] * (quad.acc[start:start + size] + bias[...])
        mid_ref[start:start + size] = middle
        full[span] = (normed(middle)[0] * gain[...] + shift[...]).astype(jnp.bfloat16)
        start += size
    quad.gather_send(full)
    quad.gather_near(full)
    quad.gather_pass(full)
    quad.gather_far(full)
    quad.gather_done(full)
    quad.scatter_done()


def branch_call(att, w_out, x, act, bias, gain, shift):
    rows, width = x.shape
    own = rows // 4
    vm = pl.BlockSpec(memory_space=pltpu.VMEM)
    return pl.pallas_call(
        branch_kernel,
        out_shape=(jax.ShapeDtypeStruct((own, width), jnp.float32), jax.ShapeDtypeStruct((rows, width), jnp.bfloat16)),
        in_specs=[vm] * 7,
        out_specs=[vm] * 2,
        scratch_shapes=Quad.scratch(own, width),
        compiler_params=pltpu.CompilerParams(collective_id=1, has_side_effects=True, vmem_limit_bytes=50 * 2**20),
    )(att, w_out, x, act, bias[None], gain[None], shift[None])
def tn(left, right):
    return lax.dot_general(left, right, (((0,), (0,)), ((), ())), preferred_element_type=jnp.float32)


def nn(left, right):
    return jnp.dot(left, right, preferred_element_type=jnp.float32)


def lane_mask(rows, head):
    lane = lax.broadcasted_iota(jnp.int32, (rows, 2 * HEAD), 1)
    return (lane < HEAD) if head == 0 else (lane >= HEAD)


def scores_of(keys, query, bias):
    scores = nt(keys, query)
    count = scores.shape[0]
    row = lax.broadcasted_iota(jnp.int32, (PREFIX, PREFIX), 0)
    col = lax.broadcasted_iota(jnp.int32, (PREFIX, PREFIX), 1)
    parts = [scores[:PREFIX] + bias]
    if count > 2 * PREFIX:
        parts.append(scores[PREFIX : count - PREFIX])
    parts.append(jnp.where(row <= col, scores[count - PREFIX :], NEGATIVE))
    return jnp.concatenate(parts, axis=0)


def attend_kernel(bias_ref, q_ref, k_ref, v_ref, o_ref, l_ref):
    rows, pairs = q_ref.shape[0], q_ref.shape[1] // (2 * HEAD)
    bias = bias_ref[0, 0]

    def pair(p, _):
        lanes = pl.ds(pl.multiple_of(p * 2 * HEAD, 2 * HEAD), 2 * HEAD)
        value_t = v_ref[:, lanes].T
        for r in range(rows // PREFIX):
            count, own = (r + 2) * PREFIX, slice(r * PREFIX, (r + 1) * PREFIX)
            query, keys = q_ref[own, lanes], k_ref[:count, lanes]
            outs = []
            for e in range(2):
                masked = jnp.where(lane_mask(PREFIX, e), query, jnp.zeros_like(query))
                scores = scores_of(keys, masked, bias)
                peak = jnp.max(scores, axis=0, keepdims=True)
                raised = jnp.exp(scores - peak)
                total = jnp.sum(raised, axis=0, keepdims=True)
                probs = (raised * (1.0 / total)).astype(jnp.bfloat16)
                l_ref[p, e : e + 1, own] = peak + jnp.log(total)
                outs.append(nn(value_t[e * HEAD : (e + 1) * HEAD, :count], probs))
            o_ref[own, lanes] = jnp.concatenate(outs, axis=0).astype(jnp.bfloat16).T
        return 0

    lax.fori_loop(0, pairs, pair, 0)


def attend(bias, q, k, v):
    rows, cols = q.shape
    vm = pl.BlockSpec(memory_space=pltpu.VMEM)
    return pl.pallas_call(
        attend_kernel,
        out_shape=(
            jax.ShapeDtypeStruct((rows, cols), jnp.bfloat16),
            jax.ShapeDtypeStruct((cols // (2 * HEAD), 2, rows), jnp.float32),
        ),
        in_specs=[pl.BlockSpec(memory_space=pltpu.SMEM)] + [vm] * 3,
        out_specs=[vm] * 2,
        compiler_params=pltpu.CompilerParams(vmem_limit_bytes=40 * 2**20),
    )(bias, q, k, v)


def attend_back(p, bias, q_ref, k_ref, v_ref, l_ref, g_ref, d_ref, d_key, d_value):
    rows, width = q_ref.shape
    blocks = rows // PREFIX
    base = pl.multiple_of(p * 2 * HEAD, 2 * HEAD)
    lanes = pl.ds(base, 2 * HEAD)
    sums = jnp.zeros((1, 2 * HEAD), jnp.float32)
    for r in reversed(range(blocks)):
        count, own = (r + 2) * PREFIX, slice(r * PREFIX, (r + 1) * PREFIX)
        query, grad, keys, values = q_ref[own, lanes], g_ref[own, lanes], k_ref[:count, lanes], v_ref[:count, lanes]
        d_queries, d_keys, d_values = [], None, None
        for e in range(2):
            mask = lane_mask(PREFIX, e)
            query_e = jnp.where(mask, query, jnp.zeros_like(query))
            grad_e = jnp.where(mask, grad, jnp.zeros_like(grad))
            probs = jnp.exp(scores_of(keys, query_e, bias) - l_ref[p, e : e + 1, own])
            d_probs = nt(values, grad_e)
            inner = jnp.sum(probs * d_probs, axis=0, keepdims=True)
            d_scores = (probs * (d_probs - inner)).astype(jnp.bfloat16)
            keys_e, values_e = nn(d_scores, query_e), nn(probs.astype(jnp.bfloat16), grad_e)
            d_keys = keys_e if d_keys is None else d_keys + keys_e
            d_values = values_e if d_values is None else d_values + values_e
            d_queries.append(tn(d_scores, keys))
        d_query = jnp.where(lane_mask(PREFIX, 0), d_queries[0], d_queries[1]) * HEAD ** (-0.5)
        sums += jnp.sum(d_query, axis=0, keepdims=True)
        d_ref[(r + 1) * PREFIX : (r + 2) * PREFIX, lanes] = d_query.astype(jnp.bfloat16)
        if r == blocks - 1:
            d_key[:count], d_value[:count] = d_keys, d_values
        else:
            d_key[:count] += d_keys
            d_value[:count] += d_values
    d_ref[:PREFIX, lanes] = jnp.zeros((PREFIX, 2 * HEAD), jnp.bfloat16)
    d_ref[:, pl.ds(pl.multiple_of(base + width, 2 * HEAD), 2 * HEAD)] = d_key[...].astype(jnp.bfloat16)
    d_ref[:, pl.ds(pl.multiple_of(base + 2 * width, 2 * HEAD), 2 * HEAD)] = d_value[...].astype(jnp.bfloat16)
    return sums, jnp.sum(d_value[...], axis=0, keepdims=True)


def own_block(quad, i, size):
    first = quad.head // size
    start = jnp.where(i < first, quad.tp * quad.head + i * size, PREFIX + quad.tp * quad.rest + (i - first) * size)
    return pl.ds(pl.multiple_of(start, size), size), pl.ds(pl.multiple_of(i * size, size), size)


def norm_back(grad, source, gain):
    unit, scale = normed(source)
    scaled = grad * gain
    mean = jnp.mean(scaled, axis=1, keepdims=True)
    slope = jnp.mean(scaled * unit, axis=1, keepdims=True)
    return scale * (scaled - mean - unit * slope), grad * unit


def column_sum(values_in):
    return jnp.sum(values_in, axis=0, keepdims=True)


def product_part(left, right, index, turned, rows):
    def part(j, block):
        k = index(j)
        cols = pl.ds(pl.multiple_of(k[1] * COLS, COLS), COLS)
        span = pl.ds(pl.multiple_of(block * rows, rows), rows)
        if turned:
            return nn(left(k[0])[span, :], right(k[0])[:, cols])
        return tn(left(k[0])[:, span], right(k[0])[:, cols])

    return part


def middle_kernel(lines, turned, *refs):
    (g_hbm, h2_hbm, hid_hbm, dpre_hbm, w1_hbm, w2_hbm, mid_hbm, cot_hbm, act, gain, ffn_bias, w_out, bias, q, k, v, lse, vec_in,
     grads, dmid_hbm, ga_hbm, d_all, out_hbm, vec, *scratch) = refs
    ring_refs, scratch = scratch[:12], scratch[12:]
    quad_refs, scratch = scratch[:12], scratch[12:]
    x_all, y_all, weights, mid, cot, full, d_att, d_key, d_value, loads, stores = scratch
    rows = act.shape[0]
    quad = Quad(quad_refs, rows)
    tiles = y_all.shape[2] // COLS
    block_rows = ring_refs[0].shape[1]
    part = product_part(lambda m: x_all.at[m], lambda m: y_all.at[m], lambda j: (j // tiles, lax.rem(j, tiles)), turned, block_rows)
    ring = Ring(lines, [(2 * tiles, part)], ring_refs, grads)

    def load(n, source, target):
        return pltpu.make_async_copy(source, target, loads.at[n])

    spans = quad.spans(quad.tp)
    copies = [
        load(0, hid_hbm, y_all.at[0]),
        load(1, g_hbm, x_all.at[0]),
        load(2, dpre_hbm, y_all.at[1]),
        load(3, w1_hbm, weights),
        load(4, h2_hbm, x_all.at[1]),
        load(5, mid_hbm, mid),
        load(6, cot_hbm.at[spans[0]], cot.at[: quad.head]),
        load(7, cot_hbm.at[spans[1]], cot.at[quad.head :]),
    ]
    for copy in copies:
        copy.start()
    meet(ring.peers() + quad.peers())
    copies[0].wait()
    copies[1].wait()
    ring.start()
    copies[2].wait()
    copies[3].wait()
    d_pre, hidden = y_all.at[1], y_all.at[0]
    quad.scatter_send(lambda half, n: nt(quad.half_of(d_pre, half), weights[quad.columns(n), :]))
    second = load(3, w2_hbm, weights)
    second.start()
    for copy in copies[4:]:
        copy.wait()
    ring.run(0, 2)
    lax.fori_loop(0, quad.tiles, lambda n, _: (quad.scatter_add(n), 0)[1], 0)
    vec[...] = vec_in[...]
    size = 32

    def back_rows(i, _):
        whole, own = own_block(quad, i, size)
        grad = quad.acc[own]
        change, gain_terms = norm_back(grad, mid[own], gain[...])
        d_middle = cot[own].astype(jnp.float32) + change
        quad.acc[own] = d_middle
        low = (act[whole] * d_middle).astype(jnp.bfloat16)
        full[whole] = low
        vec[2:3] += column_sum(low.astype(jnp.float32))
        vec[3:4] += column_sum(gain_terms)
        vec[4:5] += column_sum(grad)
        return 0

    count = (quad.head + quad.rest) // size
    lax.fori_loop(0, count, back_rows, 0)
    quad.gather_send(full)
    keep = pltpu.make_async_copy(quad.acc, dmid_hbm, stores.at[0])
    keep.start()
    ring.run(2, 5)
    quad.gather_near(full)
    quad.gather_pass(full)
    quad.gather_far(full)
    ga_copy = pltpu.make_async_copy(full, ga_hbm, stores.at[1])
    ga_copy.start()

    def attended_rows(i, _):
        span = pl.ds(pl.multiple_of(i * PREFIX, PREFIX), PREFIX)
        d_att[span] = nt(full[span], w_out[...]).astype(jnp.bfloat16)
        return 0

    lax.fori_loop(0, rows // PREFIX, attended_rows, 0)
    pairs = q.shape[1] // (2 * HEAD)
    width = q.shape[1]

    def pair(p, _):
        sums, value_sums = attend_back(p, bias[0, 0], q, k, v, lse, d_att, d_all, d_key, d_value)
        base = pl.multiple_of(p * 2 * HEAD, 2 * HEAD)
        vec[7:8, pl.ds(base, 2 * HEAD)] = sums
        vec[7:8, pl.ds(pl.multiple_of(base + width, 2 * HEAD), 2 * HEAD)] = value_sums
        ring.run_some(5 + 2 * p, 2)
        return 0

    lax.fori_loop(0, pairs, pair, 0)
    now = 5 + 2 * pairs
    quad.gather_done(full)
    quad.scatter_done()
    keep.wait()
    ga_copy.wait()
    second.wait()
    quad.scatter_send(lambda half, n: nn(quad.half_of(hidden, half), weights[:, quad.columns(n)]))
    ring.run(now, now + 3)
    lax.fori_loop(0, quad.tiles, lambda n, _: (quad.scatter_add(n), 0)[1], 0)

    def out_rows(i, _):
        whole, own = own_block(quad, i, size)
        full[whole] = (mid[own] + act[whole] * (quad.acc[own] + ffn_bias[...])).astype(jnp.bfloat16)
        return 0

    lax.fori_loop(0, count, out_rows, 0)
    quad.gather_send(full)
    ring.run(now + 3, now + 7)
    quad.gather_near(full)
    quad.gather_pass(full)
    quad.gather_far(full)
    out_copy = pltpu.make_async_copy(full, out_hbm, stores.at[2])
    out_copy.start()
    ring.finish(now + 7)
    quad.gather_done(full)
    quad.scatter_done()
    out_copy.wait()


def middle_call(n_ctx, turned, g, h2, hid, dpre, w1, w2, mid, cot, act, gain, ffn_bias, w_out, bias, q, k, v, lse, vec):
    lines, rows, width = n_ctx // 2, cot.shape[0], cot.shape[1]
    block_rows, own, cols = width // n_ctx, rows // 4, q.shape[1]
    hidden = hid.shape[1]
    vm, hbm, sm = (pl.BlockSpec(memory_space=s) for s in (pltpu.VMEM, pl.ANY, pltpu.SMEM))
    bf, f4 = jnp.bfloat16, jnp.float32
    return pl.pallas_call(
        functools.partial(middle_kernel, lines, turned),
        out_shape=(
            jax.ShapeDtypeStruct((2 * hidden // COLS, block_rows, COLS), f4),
            jax.ShapeDtypeStruct((own, width), f4),
            jax.ShapeDtypeStruct((rows, width), bf),
            jax.ShapeDtypeStruct((rows + PREFIX, 3 * cols), bf),
            jax.ShapeDtypeStruct((rows, width), bf),
            jax.ShapeDtypeStruct(vec.shape, f4),
        ),
        in_specs=[hbm] * 8 + [vm] * 4 + [sm] + [vm] * 5,
        out_specs=[hbm, hbm, hbm, vm, hbm, vm],
        scratch_shapes=Ring.scratch(lines, block_rows)
        + Quad.scratch(own, width)
        + [
            pltpu.VMEM((2, *g.shape), bf),
            pltpu.VMEM((2, rows, hidden), bf),
            pltpu.VMEM(w1.shape, bf),
            pltpu.VMEM((own, width), f4),
            pltpu.VMEM((own, width), bf),
            pltpu.VMEM((rows, width), bf),
            pltpu.VMEM((rows, cols), bf),
            pltpu.VMEM((rows + PREFIX, 2 * HEAD), f4),
            pltpu.VMEM((rows + PREFIX, 2 * HEAD), f4),
            pltpu.SemaphoreType.DMA((8,)),
            pltpu.SemaphoreType.DMA((3,)),
        ],
        compiler_params=pltpu.CompilerParams(collective_id=2, has_side_effects=True, vmem_limit_bytes=63 * 2**20),
    )(g, h2, hid, dpre, w1, w2, mid, cot, act, gain[None], ffn_bias[None], w_out, bias, q, k, v, lse, vec)


class Wide(Quad):
    def rows_of(self, ref, quarter):
        own = [pl.ds(pl.multiple_of(span.start + PREFIX, 16), span.size) for span in self.spans(quarter)]
        return jnp.concatenate([ref[span] for span in [self.spans(quarter)[0]] + own], axis=0)


def last_kernel(lines, turned, *refs):
    (d_all, w_qkv, h_all, x_hbm, dmid_hbm, att, ga, gain, weight, vec_in, grads, out, vec, *scratch) = refs
    ring_refs, scratch = scratch[:12], scratch[12:]
    quad_refs, scratch = scratch[:12], scratch[12:]
    x, dmid, fresh, back, v_send, v_recv, loads, s_v, r_v = scratch
    rows, width = out.shape
    quad = Wide(quad_refs, rows)
    block_rows = ring_refs[0].shape[1]
    extra = PREFIX * COLS * (width // COLS) // 4 // (block_rows * COLS)

    def prefix_part(j, block):
        return fresh[pl.ds(pl.multiple_of(j * block_rows, block_rows), block_rows)] * weight[block]

    out_part = product_part(lambda m: ga, lambda m: att, lambda j: (0, j), turned, block_rows)
    head_part = product_part(lambda m: h_all, lambda m: d_all, lambda j: (0, j), turned, block_rows)
    tail_part = product_part(lambda m: h_all, lambda m: d_all, lambda j: (0, j + 1), turned, block_rows)
    cols = att.shape[1] // COLS
    ring = Ring(
        lines, [(cols, out_part), (cols, head_part), (extra, prefix_part), (2 * cols, tail_part)], ring_refs, grads,
        (2 * cols, extra, back, block_rows),
    )
    spans = quad.spans(quad.tp)
    copies = [
        pltpu.make_async_copy(dmid_hbm, dmid, loads.at[0]),
        pltpu.make_async_copy(x_hbm.at[spans[0]], x.at[: quad.head], loads.at[1]),
        pltpu.make_async_copy(x_hbm.at[spans[1]], x.at[quad.head :], loads.at[2]),
    ]
    for copy in copies:
        copy.start()
    ctx, tp = lax.axis_index("ctx"), lax.axis_index("tp")
    swaps, bit = [], 1
    while bit < 2 * lines:
        swaps.append((ctx + bit - 2 * bit * lax.rem(ctx // bit, 2), tp))
        bit *= 2
    swaps += [quad.across, quad.over]
    meet(ring.peers() + quad.peers() + [(None, device) for device in swaps[2:-2]])
    ring.start()
    depth = w_qkv.shape[2]

    def chunk(half, n):
        left = quad.half_of(d_all, half)
        terms = [nt(left[:, m * depth : (m + 1) * depth], w_qkv[m, quad.columns(n), :]) for m in range(3)]
        return terms[0] + terms[1] + terms[2]

    quad.scatter_send(chunk)
    lax.fori_loop(0, quad.tiles, lambda n, _: (quad.scatter_add(n), 0)[1], 0)
    for n in range(quad.tiles):
        fresh[n * quad.head : (n + 1) * quad.head] = quad.acc[: quad.head, n * COLS : (n + 1) * COLS]
    ready = (2 * cols + extra) * lines + SKEW * (lines - 1)
    ring.run(0, ready)
    for copy in copies:
        copy.wait()
    for n in range(quad.tiles):
        quad.acc[quad.head : 2 * quad.head, n * COLS : (n + 1) * COLS] += back[n * quad.head : (n + 1) * quad.head]
    vec[...] = vec_in[...]
    size = 32

    def back_rows(i, _):
        whole, own = own_block(quad, i, size)
        grad = quad.acc[pl.ds(pl.multiple_of(quad.head + i * size, size), size)]
        change, gain_terms = norm_back(grad, x[own].astype(jnp.float32), gain[...])
        out[whole] = (dmid[own] + change).astype(jnp.bfloat16)
        vec[0:1] += column_sum(gain_terms)
        vec[1:2] += column_sum(grad)
        return 0

    lax.fori_loop(0, (quad.head + quad.rest) // size, back_rows, 0)
    quad.gather_send(out)
    middle = max(ready, ring.steps)
    ring.run(ready, middle)
    quad.gather_near(out)
    quad.gather_pass(out)
    ring.finish(middle)
    quad.gather_far(out)
    for n, device in enumerate(swaps):
        v_send[n] = vec[...]
        swap = pltpu.make_async_remote_copy(
            src_ref=v_send.at[n], dst_ref=v_recv.at[n], send_sem=s_v.at[n], recv_sem=r_v.at[n],
            device_id=device, device_id_type=MESH)
        swap.start()
        swap.wait()
        if n < len(swaps) - 2:
            vec[...] += v_recv[n]
        else:
            vec[:6] += v_recv[n, :6]
    quad.gather_done(out)
    quad.scatter_done()


def last_call(n_ctx, turned, d_all, w_qkv, h_all, x, dmid, att, ga, gain, weight, vec):
    lines, (rows, width) = n_ctx // 2, x.shape
    block_rows, own = width // n_ctx, rows // 4
    extra = PREFIX * width // 4 // (block_rows * COLS)
    cols = att.shape[1] // COLS
    vm, hbm, sm = (pl.BlockSpec(memory_space=s) for s in (pltpu.VMEM, pl.ANY, pltpu.SMEM))
    bf, f4 = jnp.bfloat16, jnp.float32
    rounds = n_ctx.bit_length() + 1
    return pl.pallas_call(
        functools.partial(last_kernel, lines, turned),
        out_shape=(
            jax.ShapeDtypeStruct((4 * cols + extra, block_rows, COLS), f4),
            jax.ShapeDtypeStruct((rows, width), bf),
            jax.ShapeDtypeStruct(vec.shape, f4),
        ),
        in_specs=[vm] * 3 + [hbm] * 2 + [vm] * 3 + [sm] + [vm],
        out_specs=[hbm, vm, vm],
        scratch_shapes=Ring.scratch(lines, block_rows)
        + Quad.scratch(own + PREFIX // 4, width)
        + [
            pltpu.VMEM((own, width), bf),
            pltpu.VMEM((own, width), f4),
            pltpu.VMEM((PREFIX * width // 4 // COLS, COLS), f4),
            pltpu.VMEM((PREFIX * width // 4 // COLS, COLS), f4),
            pltpu.VMEM((rounds, *vec.shape), f4),
            pltpu.VMEM((rounds, *vec.shape), f4),
            pltpu.SemaphoreType.DMA((3,)),
            pltpu.SemaphoreType.DMA((rounds,)),
            pltpu.SemaphoreType.DMA((rounds,)),
        ],
        compiler_params=pltpu.CompilerParams(collective_id=3, has_side_effects=True, vmem_limit_bytes=63 * 2**20),
    )(d_all, w_qkv, h_all, x, dmid, att, ga, gain[None], weight, vec)
def layer_norm(values_in, gain_row, shift_row):
    centred = values_in - jnp.mean(values_in, axis=1, keepdims=True)
    spread = jnp.mean(centred * centred, axis=1, keepdims=True)
    return centred * lax.rsqrt(spread + EPSILON) * gain_row + shift_row


def outer_cols(left, right):
    return nt(left, right)


def plan(lengths, stretch_map):
    seq_total = lengths.shape[0]
    starts = jnp.cumsum(lengths) - lengths
    inside = (stretch_map[:, None] >= starts[None, :]).astype(jnp.int32)
    seq_of = jnp.sum(inside, axis=1) - 1
    chosen = jnp.arange(seq_total, dtype=jnp.int32)[None, :] == seq_of[:, None]
    first_stretch = jnp.sum(jnp.where(chosen, starts[None, :], 0), axis=1)
    block_part = stretch_map - first_stretch
    devices = jnp.arange(stretch_map.shape[0], dtype=jnp.int32)
    block_owner = jnp.sum(
        jnp.where(stretch_map[None, :] == first_stretch[:, None], devices[None, :], 0), axis=1
    )
    return block_part, block_owner


def body(
    mesh,
    block_input,
    cotangent,
    ln1_gain,
    ln1_bias,
    w_qkv,
    qv_bias,
    w_out,
    out_bias,
    ln2_gain,
    ln2_bias,
    w_fc1,
    fc1_bias,
    w_fc2,
    fc2_bias,
    exit_layer,
    layer_index,
    lengths,
    stretch_map,
):
    n_ctx = mesh.shape["ctx"]
    row_count, width = block_input.shape
    block_rows = width // n_ctx
    turned = block_rows % 128 != 0

    def tokens_last(array):
        return array.T if turned else array

    device = lax.axis_index("ctx")
    block_part, block_owner = plan(lengths, stretch_map)
    my_part = block_part[device]
    my_owner = block_owner[device]
    has_prefix = my_part > 0
    position = jnp.arange(row_count, dtype=jnp.int32)
    active = ((exit_layer > layer_index[0]) | (my_part == 0) & (position < PREFIX)).astype(
        jnp.float32
    )[:, None]
    bias = jnp.where(has_prefix, 0.0, NEGATIVE).reshape(1, 1)
    weight = ((jnp.arange(n_ctx, dtype=jnp.int32) == my_owner) & has_prefix).astype(jnp.float32)

    slice_rows = PREFIX // lax.axis_size("tp")
    start = lax.dynamic_slice_in_dim(block_input, lax.axis_index("tp") * slice_rows, slice_rows, 0)
    starts_all = lax.all_gather(start, "ctx", axis=0, tiled=True)
    picked = lax.dynamic_slice_in_dim(starts_all, my_owner * slice_rows, slice_rows, 0)
    prefix_input = lax.all_gather(picked, "tp", axis=0, tiled=True)
    h_low = layer_norm(block_input.astype(jnp.float32), ln1_gain, ln1_bias).astype(jnp.bfloat16)
    h_prefix = layer_norm(prefix_input.astype(jnp.float32), ln1_gain, ln1_bias).astype(jnp.bfloat16)
    query = (nn(h_low, w_qkv[0]) + qv_bias[0]).astype(jnp.bfloat16) * jnp.bfloat16(HEAD**-0.5)
    key = jnp.concatenate(
        [nn(h_prefix, w_qkv[1]).astype(jnp.bfloat16), nn(h_low, w_qkv[1]).astype(jnp.bfloat16)], axis=0
    )
    value = jnp.concatenate(
        [
            (nn(h_prefix, w_qkv[2]) + qv_bias[1]).astype(jnp.bfloat16),
            (nn(h_low, w_qkv[2]) + qv_bias[1]).astype(jnp.bfloat16),
        ],
        axis=0,
    )
    h_all = jnp.concatenate([h_prefix, h_low], axis=0)
    attended, log_total = attend(bias, query, key, value)
    middle, h2_low = branch_call(attended, w_out, block_input, active, out_bias, ln2_gain, ln2_bias)
    grad_ffn = (active * cotangent.astype(jnp.float32)).astype(jnp.bfloat16)
    hidden_pre = nn(h2_low, w_fc1) + fc1_bias
    hidden_low = jax.nn.gelu(hidden_pre).astype(jnp.bfloat16)
    d_hidden = nt(grad_ffn, w_fc2)
    d_pre_low = jax.vjp(jax.nn.gelu, hidden_pre)[1](d_hidden)[0].astype(jnp.bfloat16)
    d_fc2_bias = jnp.sum(grad_ffn.astype(jnp.float32), axis=0) / lax.axis_size("tp")
    d_fc1_bias = jnp.sum(d_pre_low.astype(jnp.float32), axis=0)
    zero = jnp.zeros((width,), jnp.float32)
    vectors = jnp.stack([zero, zero, zero, zero, zero, d_fc2_bias, d_fc1_bias, zero])
    ffn_grads, d_middle, grad_attn, d_all, output_rows, vectors = middle_call(
        n_ctx, turned, tokens_last(grad_ffn), tokens_last(h2_low), hidden_low, d_pre_low, w_fc1, w_fc2,
        middle, cotangent, active, ln2_gain, fc2_bias, w_out, bias, query, key, value, log_total, vectors,
    )
    head_grads, input_grad, vectors = last_call(
        n_ctx, turned, d_all, w_qkv, tokens_last(h_all), block_input, d_middle, attended,
        tokens_last(grad_attn), ln1_gain, weight, vectors,
    )
    tiles = hidden_low.shape[1] // COLS
    fc2_grad = ffn_grads[:tiles].transpose(0, 2, 1).reshape(tiles * COLS, block_rows)
    fc1_grad = ffn_grads[tiles:].transpose(1, 0, 2).reshape(block_rows, tiles * COLS)
    out_grad = head_grads[0].T
    qkv_grad = jnp.stack([head_grads[1], head_grads[-2], head_grads[-1]])
    qv_grad = vectors[7, : 2 * query.shape[1]].reshape(2, -1)
    return (
        output_rows,
        input_grad,
        vectors[0],
        vectors[1],
        qkv_grad,
        qv_grad,
        out_grad,
        vectors[2],
        vectors[3],
        vectors[4],
        fc1_grad,
        vectors[6],
        fc2_grad,
        vectors[5],
    )


def solution(mesh):
    in_specs = (
        P("ctx", None),
        P("ctx", None),
        P(),
        P(),
        P(None, None, "tp"),
        P(None, "tp"),
        P("tp", None),
        P(),
        P(),
        P(),
        P(None, "tp"),
        P("tp"),
        P("tp", None),
        P(),
        P("ctx"),
        P(),
        P(),
        P(),
    )
    out_specs = (
        P("ctx", None),
        P("ctx", None),
        P(),
        P(),
        P(None, "ctx", "tp"),
        P(None, "tp"),
        P("tp", "ctx"),
        P(),
        P(),
        P(),
        P("ctx", "tp"),
        P("tp"),
        P("tp", "ctx"),
        P(),
    )
    return jax.shard_map(functools.partial(body, mesh), mesh=mesh, in_specs=in_specs, out_specs=out_specs, check_vma=False)
```

```python
import functools

import jax
import jax.numpy as jnp
from jax import lax
from jax.experimental import pallas as pl
from jax.experimental.pallas import tpu as pltpu
from jax.sharding import PartitionSpec as P

HEAD = 64
PREFIX = 256
COLS = 512
MESH = pl.DeviceIdType.MESH
NEGATIVE = -1e30
EPSILON = 1e-05
AHEAD = 8
SKEW = 2
STAGES = 4
DEPTH = 3


class Ring:
    def __init__(self, lines, groups, refs, out, final=None):
        self.lines, self.groups, self.out, self.final = lines, groups, out, final
        (self.xs, self.xr, self.zb, self.stage, self.s_xs, self.s_xr, self.s_zs, self.s_zr, self.s_out,
         self.c_x, self.c_left, self.c_right) = refs
        self.jobs = sum(count for count, _ in groups)
        self.steps = self.jobs * lines
        self.slots = self.xr.shape[0]
        self.lag = SKEW * (lines - 1) + 2
        ctx, tp = lax.axis_index("ctx"), lax.axis_index("tp")
        self.z, self.side = ctx // 2, lax.rem(ctx, 2)
        self.partner = (self.z * 2 + 1 - self.side, tp)
        self.left, self.right = (ctx - 2, tp), (ctx + 2, tp)

    @staticmethod
    def scratch(lines, rows):
        slots = AHEAD + SKEW * (lines - 1) + 4
        chunk = (rows, COLS)
        return [
            pltpu.VMEM((AHEAD, *chunk), jnp.bfloat16),
            pltpu.VMEM((slots, *chunk), jnp.bfloat16),
            pltpu.VMEM((DEPTH, lines + 1, *chunk), jnp.bfloat16),
            pltpu.VMEM((STAGES, *chunk), jnp.float32),
            pltpu.SemaphoreType.DMA((AHEAD,)),
            pltpu.SemaphoreType.DMA((slots,)),
            pltpu.SemaphoreType.DMA((slots,)),
            pltpu.SemaphoreType.DMA((DEPTH, lines + 1)),
            pltpu.SemaphoreType.DMA((STAGES,)),
            pltpu.SemaphoreType.REGULAR,
            pltpu.SemaphoreType.REGULAR,
            pltpu.SemaphoreType.REGULAR,
        ]

    def peers(self):
        return [(None, self.partner), (self.z > 0, self.left), (self.z < self.lines - 1, self.right)]

    def x_copy(self, f):
        slot, to = lax.rem(f, AHEAD), lax.rem(f, self.slots)
        return pltpu.make_async_remote_copy(
            src_ref=self.xs.at[slot], dst_ref=self.xr.at[to], send_sem=self.s_xs.at[slot],
            recv_sem=self.s_xr.at[to], device_id=self.partner, device_id_type=MESH)

    def z_copy(self, f, to, device):
        slot, level = lax.rem(f, self.slots), lax.rem(f // self.lines, DEPTH)
        return pltpu.make_async_remote_copy(
            src_ref=self.xr.at[slot], dst_ref=self.zb.at[level, to], send_sem=self.s_zs.at[slot],
            recv_sem=self.s_zr.at[level, to], device_id=device, device_id_type=MESH)

    def out_copy(self, job):
        slot = lax.rem(job, STAGES)
        return pltpu.make_async_copy(self.stage.at[slot], self.out.at[job], self.s_out.at[slot])

    def send(self, f, part, job0, fresh):
        if not fresh:
            self.x_copy(f).wait_send()

            @pl.when(f >= self.slots)
            def _():
                pl.semaphore_wait(self.c_x, 1)

        owner = lax.rem(f, self.lines)
        self.xs[lax.rem(f, AHEAD)] = part(f // self.lines - job0, owner * 2 + 1 - self.side).astype(jnp.bfloat16)
        self.x_copy(f).start()

    def receive(self, f, part, job0):
        job, owner, slot = f // self.lines, lax.rem(f, self.lines), lax.rem(f, self.slots)
        self.x_copy(f).wait_recv()
        total = part(job - job0, owner * 2 + self.side) + self.xr[slot].astype(jnp.float32)

        @pl.when(owner != self.z)
        def _():
            self.xr[slot] = total.astype(jnp.bfloat16)

        @pl.when(owner == self.z)
        def _():
            @pl.when(job >= STAGES)
            def _():
                self.out_copy(job - STAGES).wait()
            self.stage[lax.rem(job, STAGES)] = total

    def add(self, f, index):
        job = f // self.lines
        slot, level = lax.rem(f, self.slots), lax.rem(job, DEPTH)

        @pl.when(lax.rem(f, self.lines) == self.z)
        def _():
            self.stage[lax.rem(job, STAGES)] += self.zb[level, index].astype(jnp.float32)

        @pl.when(lax.rem(f, self.lines) != self.z)
        def _():
            self.xr[slot] = (self.xr[slot].astype(jnp.float32) + self.zb[level, index].astype(jnp.float32)).astype(jnp.bfloat16)

    def flow(self, t):
        lines, z = self.lines, self.z
        f = t - SKEW * z
        owner = lax.rem(f + lines * SKEW * lines, lines)

        @pl.when((f >= 0) & (f < self.steps) & (owner >= z))
        def _():
            @pl.when(z > 0)
            def _():
                self.z_copy(f, owner, self.left).wait_recv()
                self.add(f, owner)
                pl.semaphore_signal(self.c_right, inc=1, device_id=self.left, device_id_type=MESH)

            @pl.when(owner > z)
            def _():
                @pl.when(f >= DEPTH * lines)
                def _():
                    pl.semaphore_wait(self.c_right, 1)
                self.z_copy(f, owner, self.right).start()

        g = t - SKEW * (lines - 1 - z)
        owner2 = lax.rem(g + lines * SKEW * lines, lines)

        @pl.when((g >= 0) & (g < self.steps) & (owner2 <= z))
        def _():
            @pl.when(z < lines - 1)
            def _():
                index = jnp.where(owner2 == z, lines, owner2)
                self.z_copy(g, index, self.right).wait_recv()
                self.add(g, index)
                pl.semaphore_signal(self.c_left, inc=1, device_id=self.right, device_id_type=MESH)

            @pl.when(owner2 < z)
            def _():
                @pl.when(g >= DEPTH * lines)
                def _():
                    pl.semaphore_wait(self.c_left, 1)
                self.z_copy(g, jnp.where(owner2 == z - 1, lines, owner2), self.left).start()

        h = t - SKEW * (lines - 1)

        @pl.when((h >= 0) & (h < self.steps) & (lax.rem(h + lines * SKEW * lines, lines) == z))
        def _():
            self.out_copy(h // lines).start()
            if self.final is not None:
                first, count, target, size = self.final
                job = h // lines

                @pl.when((job >= first) & (job < first + count))
                def _():
                    target[pl.ds(pl.multiple_of((job - first) * size, size), size)] = self.stage[lax.rem(job, STAGES)]

        d = t - self.lag

        @pl.when((d >= 0) & (d < self.steps))
        def _():
            @pl.when(lax.rem(d + lines * (SKEW * lines + 2), lines) != z)
            def _():
                self.z_copy(d, 0, self.left).wait_send()
            pl.semaphore_signal(self.c_x, inc=1, device_id=self.partner, device_id_type=MESH)

    def find(self, f):
        job = 0
        for count, part in self.groups:
            if f < (job + count) * self.lines:
                return part, job
            job += count
        return None

    def pieces(self, lo, hi):
        cuts, job = {lo, hi}, 0
        for count, _ in self.groups:
            job += count
            cuts |= {job * self.lines, job * self.lines - AHEAD}
        cuts = sorted(c for c in cuts if lo <= c <= hi)
        return zip(cuts[:-1], cuts[1:])

    def start(self):
        for lo, hi in self.pieces(0, AHEAD):
            part, job0 = self.find(lo)
            lax.fori_loop(lo, hi, lambda f, _, part=part, job0=job0: (self.send(f, part, job0, True), 0)[1], 0)

    def run(self, lo, hi):
        for a, b in self.pieces(lo, min(hi, self.steps)):
            here, ahead = self.find(a), self.find(a + AHEAD)

            def body(f, _, here=here, ahead=ahead):
                self.receive(f, *here)
                self.flow(f)
                if ahead is not None:
                    self.send(f + AHEAD, *ahead, False)
                return 0

            lax.fori_loop(a, b, body, 0)
        if hi > self.steps:
            lax.fori_loop(max(lo, self.steps), hi, lambda t, _: (self.flow(t), 0)[1], 0)

    def run_some(self, lo, count):
        here = self.find(0)

        def body(f, _):
            self.receive(f, *here)
            self.flow(f)

            @pl.when(f + AHEAD < self.steps)
            def _():
                self.send(f + AHEAD, *here, False)
            return 0

        lax.fori_loop(lo, lo + count, body, 0)

    def finish(self, lo):
        lines, z = self.lines, self.z
        self.run(lo, self.steps + self.lag)
        lax.fori_loop(self.steps - AHEAD, self.steps, lambda f, _: (self.x_copy(f).wait_send(), 0)[1], 0)
        for job in range(self.jobs - STAGES, self.jobs):
            self.out_copy(job).wait()
        pl.semaphore_wait(self.c_x, min(self.slots, self.steps))

        @pl.when(z < lines - 1)
        def _():
            pl.semaphore_wait(self.c_right, DEPTH * (lines - 1 - z))

        @pl.when(z > 0)
        def _():
            pl.semaphore_wait(self.c_left, DEPTH * z)


def meet(peers):
    barrier = pltpu.get_barrier_semaphore()
    count = 0
    for there, device in peers:
        if there is None:
            pl.semaphore_signal(barrier, inc=1, device_id=device, device_id_type=MESH)
            count += 1
        else:
            @pl.when(there)
            def _():
                pl.semaphore_signal(barrier, inc=1, device_id=device, device_id_type=MESH)
            count += jnp.where(there, 1, 0)
    pl.semaphore_wait(barrier, count)
class Quad:
    def __init__(self, refs, rows, height):
        (self.tmp, self.cs, self.cr, self.ys, self.yr, self.acc, self.s_c, self.r_c, self.s_y, self.r_y,
         self.s_g, self.r_g) = refs
        ctx, tp = lax.axis_index("ctx"), lax.axis_index("tp")
        self.y, self.core, self.tp = tp // 2, lax.rem(tp, 2), tp
        self.across = (ctx, self.y * 2 + 1 - self.core)
        self.over = (ctx, (1 - self.y) * 2 + self.core)
        self.head, self.rest = PREFIX // 4, (rows - PREFIX) // 4
        self.tiles = self.cs.shape[1]
        self.height = height

    @staticmethod
    def scratch(rows, width):
        tiles = width // COLS
        return [
            pltpu.VMEM((2, rows, COLS), jnp.float32),
            pltpu.VMEM((2, tiles, rows, COLS), jnp.bfloat16),
            pltpu.VMEM((2, tiles, rows, COLS), jnp.bfloat16),
            pltpu.VMEM((tiles, rows, COLS), jnp.bfloat16),
            pltpu.VMEM((tiles, rows, COLS), jnp.bfloat16),
            pltpu.VMEM((rows, width), jnp.float32),
            pltpu.SemaphoreType.DMA((2, tiles)),
            pltpu.SemaphoreType.DMA((2, tiles)),
            pltpu.SemaphoreType.DMA((tiles,)),
            pltpu.SemaphoreType.DMA((tiles,)),
            pltpu.SemaphoreType.DMA((2, 3, 2)),
            pltpu.SemaphoreType.DMA((2, 3, 2)),
        ]

    def peers(self):
        return [(None, self.across), (None, self.over)]

    def spans(self, quarter):
        return [
            pl.ds(pl.multiple_of(quarter * self.head, 16), self.head),
            pl.ds(pl.multiple_of(PREFIX + quarter * self.rest, 16), self.rest),
        ]

    def rows_of(self, ref, quarter):
        return jnp.concatenate([ref[span] for span in self.spans(quarter)], axis=0)

    def half_of(self, ref, half):
        return jnp.concatenate([self.rows_of(ref, half * 2), self.rows_of(ref, half * 2 + 1)], axis=0)

    def c_copy(self, k, n):
        return pltpu.make_async_remote_copy(
            src_ref=self.cs.at[k, n, : self.height], dst_ref=self.cr.at[k, n, : self.height], send_sem=self.s_c.at[k, n],
            recv_sem=self.r_c.at[k, n], device_id=self.across, device_id_type=MESH)

    def y_copy(self, n):
        return pltpu.make_async_remote_copy(
            src_ref=self.ys.at[n, : self.height], dst_ref=self.yr.at[n, : self.height], send_sem=self.s_y.at[n],
            recv_sem=self.r_y.at[n], device_id=self.over, device_id_type=MESH)

    def columns(self, n):
        return pl.ds(pl.multiple_of(n * COLS, COLS), COLS)

    def split(self, value, k, n):
        rows = self.height
        self.tmp[0, :rows] = value[:rows]
        self.tmp[1, :rows] = value[rows:]
        self.cs[k, n, :rows] = self.tmp[1 - self.core, :rows].astype(jnp.bfloat16)
        self.c_copy(k, n).start()
        self.acc[:rows, self.columns(n)] = self.tmp[self.core, :rows]

    def relay(self, n):
        self.c_copy(0, n).wait_recv()
        rows = self.height
        total = self.acc[:rows, self.columns(n)] + self.cr[0, n, :rows].astype(jnp.float32)
        self.ys[n, :rows] = total.astype(jnp.bfloat16)
        self.y_copy(n).start()

    def scatter_send(self, chunk):
        def far(n, _):
            self.split(chunk(1 - self.y, n), 0, n)

            @pl.when(n > 0)
            def _():
                self.relay(n - 1)
            return 0

        lax.fori_loop(0, self.tiles, far, 0)
        self.relay(self.tiles - 1)

        def near(n, _):
            self.split(chunk(self.y, n), 1, n)
            return 0

        lax.fori_loop(0, self.tiles, near, 0)

    def scatter_add(self, n):
        self.c_copy(1, n).wait_recv()
        self.y_copy(n).wait_recv()
        rows = self.height
        came = self.cr[1, n, :rows].astype(jnp.float32) + self.yr[n, :rows].astype(jnp.float32)
        self.acc[:rows, self.columns(n)] += came

    def scatter_done(self):
        for n in range(self.tiles):
            self.c_copy(0, n).wait_send()
            self.c_copy(1, n).wait_send()
            self.y_copy(n).wait_send()

    def g_copy(self, full, k, s, quarter, device, turn):
        span = self.spans(quarter)[s]
        return pltpu.make_async_remote_copy(
            src_ref=full.at[span], dst_ref=full.at[span], send_sem=self.s_g.at[turn, k, s],
            recv_sem=self.r_g.at[turn, k, s], device_id=device, device_id_type=MESH)

    def gather_send(self, full, turn=0):
        for s in range(2):
            self.g_copy(full, 0, s, self.tp, self.over, turn).start()
        for s in range(2):
            self.g_copy(full, 1, s, self.tp, self.across, turn).start()

    def gather_near(self, full, turn=0):
        for s in range(2):
            self.g_copy(full, 1, s, self.y * 2 + 1 - self.core, self.across, turn).wait_recv()

    def gather_pass(self, full, turn=0):
        other = (1 - self.y) * 2 + self.core
        for s in range(2):
            self.g_copy(full, 0, s, other, self.over, turn).wait_recv()
            self.g_copy(full, 2, s, other, self.across, turn).start()

    def gather_far(self, full, turn=0):
        for s in range(2):
            self.g_copy(full, 2, s, (1 - self.y) * 2 + 1 - self.core, self.across, turn).wait_recv()

    def gather_done(self, full, turn=0):
        other = (1 - self.y) * 2 + self.core
        for s in range(2):
            self.g_copy(full, 0, s, self.tp, self.over, turn).wait_send()
            self.g_copy(full, 1, s, self.tp, self.across, turn).wait_send()
            self.g_copy(full, 2, s, other, self.across, turn).wait_send()


def nt(left, right):
    return lax.dot_general(left, right, (((1,), (1,)), ((), ())), preferred_element_type=jnp.float32)


def normed(values_in):
    centred = values_in - jnp.mean(values_in, axis=1, keepdims=True)
    scale = lax.rsqrt(jnp.mean(centred * centred, axis=1, keepdims=True) + EPSILON)
    return centred * scale, scale


def branch_kernel(att, w_out, x_ref, act_ref, bias, gain, shift, mid_ref, full, *scratch):
    quad = Quad(scratch, att.shape[0], mid_ref.shape[0])
    meet(quad.peers())
    quad.scatter_send(lambda half, n: jnp.dot(quad.half_of(att, half), w_out[:, quad.columns(n)], preferred_element_type=jnp.float32))
    lax.fori_loop(0, quad.tiles, lambda n, _: (quad.scatter_add(n), 0)[1], 0)
    start = 0
    for span in quad.spans(quad.tp):
        size = span.size
        middle = x_ref[span].astype(jnp.float32) + act_ref[span] * (quad.acc[start:start + size] + bias[...])
        mid_ref[start:start + size] = middle
        full[span] = (normed(middle)[0] * gain[...] + shift[...]).astype(jnp.bfloat16)
        start += size
    quad.gather_send(full)
    quad.gather_near(full)
    quad.gather_pass(full)
    quad.gather_far(full)
    quad.gather_done(full)
    quad.scatter_done()


def branch_call(att, w_out, x, act, bias, gain, shift):
    rows, width = x.shape
    own = rows // 4
    vm = pl.BlockSpec(memory_space=pltpu.VMEM)
    return pl.pallas_call(
        branch_kernel,
        out_shape=(jax.ShapeDtypeStruct((own, width), jnp.float32), jax.ShapeDtypeStruct((rows, width), jnp.bfloat16)),
        in_specs=[vm] * 7,
        out_specs=[vm] * 2,
        scratch_shapes=Quad.scratch(own, width),
        compiler_params=pltpu.CompilerParams(collective_id=1, has_side_effects=True, vmem_limit_bytes=50 * 2**20),
    )(att, w_out, x, act, bias[None], gain[None], shift[None])
def tn(left, right):
    return lax.dot_general(left, right, (((0,), (0,)), ((), ())), preferred_element_type=jnp.float32)


def nn(left, right):
    return jnp.dot(left, right, preferred_element_type=jnp.float32)


def lane_mask(rows, head):
    lane = lax.broadcasted_iota(jnp.int32, (rows, 2 * HEAD), 1)
    return (lane < HEAD) if head == 0 else (lane >= HEAD)


def scores_of(keys, query, bias):
    scores = nt(keys, query)
    count = scores.shape[0]
    row = lax.broadcasted_iota(jnp.int32, (PREFIX, PREFIX), 0)
    col = lax.broadcasted_iota(jnp.int32, (PREFIX, PREFIX), 1)
    parts = [scores[:PREFIX] + bias]
    if count > 2 * PREFIX:
        parts.append(scores[PREFIX : count - PREFIX])
    parts.append(jnp.where(row <= col, scores[count - PREFIX :], NEGATIVE))
    return jnp.concatenate(parts, axis=0)


def attend_kernel(bias_ref, q_ref, k_ref, v_ref, o_ref, l_ref):
    rows, pairs = q_ref.shape[0], q_ref.shape[1] // (2 * HEAD)
    bias = bias_ref[0, 0]

    def pair(p, _):
        lanes = pl.ds(pl.multiple_of(p * 2 * HEAD, 2 * HEAD), 2 * HEAD)
        value_t = v_ref[:, lanes].T
        for r in range(rows // PREFIX):
            count, own = (r + 2) * PREFIX, slice(r * PREFIX, (r + 1) * PREFIX)
            query, keys = q_ref[own, lanes], k_ref[:count, lanes]
            outs = []
            for e in range(2):
                masked = jnp.where(lane_mask(PREFIX, e), query, jnp.zeros_like(query))
                scores = scores_of(keys, masked, bias)
                peak = jnp.max(scores, axis=0, keepdims=True)
                raised = jnp.exp(scores - peak)
                total = jnp.sum(raised, axis=0, keepdims=True)
                probs = (raised * (1.0 / total)).astype(jnp.bfloat16)
                l_ref[p, e : e + 1, own] = peak + jnp.log(total)
                outs.append(nn(value_t[e * HEAD : (e + 1) * HEAD, :count], probs))
            o_ref[own, lanes] = jnp.concatenate(outs, axis=0).astype(jnp.bfloat16).T
        return 0

    lax.fori_loop(0, pairs, pair, 0)


def attend(bias, q, k, v):
    rows, cols = q.shape
    vm = pl.BlockSpec(memory_space=pltpu.VMEM)
    return pl.pallas_call(
        attend_kernel,
        out_shape=(
            jax.ShapeDtypeStruct((rows, cols), jnp.bfloat16),
            jax.ShapeDtypeStruct((cols // (2 * HEAD), 2, rows), jnp.float32),
        ),
        in_specs=[pl.BlockSpec(memory_space=pltpu.SMEM)] + [vm] * 3,
        out_specs=[vm] * 2,
        compiler_params=pltpu.CompilerParams(vmem_limit_bytes=40 * 2**20),
    )(bias, q, k, v)


def attend_back(p, bias, q_ref, k_ref, v_ref, l_ref, g_ref, d_ref, d_key, d_value):
    rows, width = q_ref.shape
    blocks = rows // PREFIX
    base = pl.multiple_of(p * 2 * HEAD, 2 * HEAD)
    lanes = pl.ds(base, 2 * HEAD)
    sums = jnp.zeros((1, 2 * HEAD), jnp.float32)
    for r in reversed(range(blocks)):
        count, own = (r + 2) * PREFIX, slice(r * PREFIX, (r + 1) * PREFIX)
        query, grad, keys, values = q_ref[own, lanes], g_ref[own, lanes], k_ref[:count, lanes], v_ref[:count, lanes]
        d_queries, d_keys, d_values = [], None, None
        for e in range(2):
            mask = lane_mask(PREFIX, e)
            query_e = jnp.where(mask, query, jnp.zeros_like(query))
            grad_e = jnp.where(mask, grad, jnp.zeros_like(grad))
            probs = jnp.exp(scores_of(keys, query_e, bias) - l_ref[p, e : e + 1, own])
            d_probs = nt(values, grad_e)
            inner = jnp.sum(probs * d_probs, axis=0, keepdims=True)
            d_scores = (probs * (d_probs - inner)).astype(jnp.bfloat16)
            keys_e, values_e = nn(d_scores, query_e), nn(probs.astype(jnp.bfloat16), grad_e)
            d_keys = keys_e if d_keys is None else d_keys + keys_e
            d_values = values_e if d_values is None else d_values + values_e
            d_queries.append(tn(d_scores, keys))
        d_query = jnp.where(lane_mask(PREFIX, 0), d_queries[0], d_queries[1]) * HEAD ** (-0.5)
        sums += jnp.sum(d_query, axis=0, keepdims=True)
        d_ref[(r + 1) * PREFIX : (r + 2) * PREFIX, lanes] = d_query.astype(jnp.bfloat16)
        if r == blocks - 1:
            d_key[:count], d_value[:count] = d_keys, d_values
        else:
            d_key[:count] += d_keys
            d_value[:count] += d_values
    d_ref[:PREFIX, lanes] = jnp.zeros((PREFIX, 2 * HEAD), jnp.bfloat16)
    d_ref[:, pl.ds(pl.multiple_of(base + width, 2 * HEAD), 2 * HEAD)] = d_key[...].astype(jnp.bfloat16)
    d_ref[:, pl.ds(pl.multiple_of(base + 2 * width, 2 * HEAD), 2 * HEAD)] = d_value[...].astype(jnp.bfloat16)
    return sums, jnp.sum(d_value[...], axis=0, keepdims=True)


def own_block(quad, i, size):
    first = quad.head // size
    start = jnp.where(i < first, quad.tp * quad.head + i * size, PREFIX + quad.tp * quad.rest + (i - first) * size)
    return pl.ds(pl.multiple_of(start, size), size), pl.ds(pl.multiple_of(i * size, size), size)


def norm_back(grad, source, gain):
    unit, scale = normed(source)
    scaled = grad * gain
    mean = jnp.mean(scaled, axis=1, keepdims=True)
    slope = jnp.mean(scaled * unit, axis=1, keepdims=True)
    return scale * (scaled - mean - unit * slope), grad * unit


def column_sum(values_in):
    return jnp.sum(values_in, axis=0, keepdims=True)


def product_part(left, right, index, turned, rows):
    def part(j, block):
        k = index(j)
        cols = pl.ds(pl.multiple_of(k[1] * COLS, COLS), COLS)
        span = pl.ds(pl.multiple_of(block * rows, rows), rows)
        if turned:
            return nn(left(k[0])[span, :], right(k[0])[:, cols])
        return tn(left(k[0])[:, span], right(k[0])[:, cols])

    return part


class Wide(Quad):
    def rows_of(self, ref, quarter):
        own = [pl.ds(pl.multiple_of(span.start + PREFIX, 16), span.size) for span in self.spans(quarter)]
        return jnp.concatenate([ref[span] for span in [self.spans(quarter)[0]] + own], axis=0)


def middle_kernel(lines, turned, *refs):
    (g_hbm, h2_hbm, hid_hbm, dpre_hbm, w1_hbm, w_qkv_hbm, mid_hbm, cot_hbm, act, gain, w_out, bias, weight, q, k, v, lse, vec_in,
     grads, dmid_hbm, ga_hbm, d_all, dh_hbm, vec, *scratch) = refs
    ring_refs, scratch = scratch[:12], scratch[12:]
    quad_refs, scratch = scratch[:12], scratch[12:]
    x_all, y_all, weights, mid, cot, full, d_att, d_key, d_value, fresh, back, loads, stores = scratch
    rows, width = full.shape
    quad, wide = Quad(quad_refs, rows, rows // 4), Wide(quad_refs, rows, (rows + PREFIX) // 4)
    tiles = y_all.shape[2] // COLS
    block_rows = ring_refs[0].shape[1]
    extra = fresh.shape[0] // block_rows

    def prefix_part(j, block):
        return fresh[pl.ds(pl.multiple_of(j * block_rows, block_rows), block_rows)] * weight[block]

    part = product_part(lambda m: x_all.at[m], lambda m: y_all.at[m], lambda j: (j // tiles, lax.rem(j, tiles)), turned, block_rows)
    ring = Ring(lines, [(2 * tiles, part), (extra, prefix_part)], ring_refs, grads, (2 * tiles, extra, back, block_rows))

    def load(n, source, target):
        return pltpu.make_async_copy(source, target, loads.at[n])

    spans = quad.spans(quad.tp)
    copies = [
        load(0, hid_hbm, y_all.at[0]),
        load(1, g_hbm, x_all.at[0]),
        load(2, dpre_hbm, y_all.at[1]),
        load(3, w1_hbm, weights),
        load(4, h2_hbm, x_all.at[1]),
        load(5, mid_hbm, mid),
        load(6, cot_hbm.at[spans[0]], cot.at[: quad.head]),
        load(7, cot_hbm.at[spans[1]], cot.at[quad.head :]),
    ]
    for copy in copies:
        copy.start()
    meet(ring.peers() + quad.peers())
    copies[0].wait()
    copies[1].wait()
    ring.start()
    copies[2].wait()
    copies[3].wait()
    d_pre = y_all.at[1]
    quad.scatter_send(lambda half, n: nt(quad.half_of(d_pre, half), weights[quad.columns(n), :]))
    depth = q.shape[1]
    heads = [load(8 + m, w_qkv_hbm.at[m], weights.at[:, m * depth : (m + 1) * depth]) for m in range(3)]
    for copy in heads:
        copy.start()
    for copy in copies[4:]:
        copy.wait()
    ring.run(0, 2)
    lax.fori_loop(0, quad.tiles, lambda n, _: (quad.scatter_add(n), 0)[1], 0)
    vec[...] = vec_in[...]
    size = 32
    own_rows = quad.height

    def back_rows(i, _):
        whole, own = own_block(quad, i, size)
        grad = quad.acc[own]
        change, gain_terms = norm_back(grad, mid[own], gain[...])
        d_middle = cot[own].astype(jnp.float32) + change
        quad.acc[own] = d_middle
        low = (act[whole] * d_middle).astype(jnp.bfloat16)
        full[whole] = low
        vec[2:3] += column_sum(low.astype(jnp.float32))
        vec[3:4] += column_sum(gain_terms)
        vec[4:5] += column_sum(grad)
        return 0

    lax.fori_loop(0, own_rows // size, back_rows, 0)
    quad.gather_send(full)
    keep = pltpu.make_async_copy(quad.acc.at[:own_rows], dmid_hbm, stores.at[0])
    keep.start()
    ring.run(2, 5)
    quad.gather_near(full)
    quad.gather_pass(full)
    quad.gather_far(full)
    ga_copy = pltpu.make_async_copy(full, ga_hbm, stores.at[1])
    ga_copy.start()

    def attended_rows(i, _):
        span = pl.ds(pl.multiple_of(i * PREFIX, PREFIX), PREFIX)
        d_att[span] = nt(full[span], w_out[...]).astype(jnp.bfloat16)
        return 0

    lax.fori_loop(0, rows // PREFIX, attended_rows, 0)
    pairs = q.shape[1] // (2 * HEAD)

    def pair(p, _):
        sums, value_sums = attend_back(p, bias[0, 0], q, k, v, lse, d_att, d_all, d_key, d_value)
        base = pl.multiple_of(p * 2 * HEAD, 2 * HEAD)
        vec[7:8, pl.ds(base, 2 * HEAD)] = sums
        vec[7:8, pl.ds(pl.multiple_of(base + depth, 2 * HEAD), 2 * HEAD)] = value_sums
        ring.run_some(5 + 2 * p, 2)
        return 0

    lax.fori_loop(0, pairs, pair, 0)
    now = 5 + 2 * pairs
    quad.gather_done(full)
    quad.scatter_done()
    keep.wait()
    for copy in heads:
        copy.wait()
    wide.scatter_send(lambda half, n: nt(wide.half_of(d_all, half), weights[wide.columns(n), : 3 * depth]))
    ring.run(now, now + 4)
    lax.fori_loop(0, wide.tiles, lambda n, _: (wide.scatter_add(n), 0)[1], 0)
    for n in range(wide.tiles):
        fresh[n * wide.head : (n + 1) * wide.head] = wide.acc[: wide.head, n * COLS : (n + 1) * COLS]
    ready = (2 * tiles + extra) * lines + SKEW * (lines - 1)
    ring.run(now + 4, ready)
    for n in range(wide.tiles):
        wide.acc[wide.head : 2 * wide.head, n * COLS : (n + 1) * COLS] += back[n * wide.head : (n + 1) * wide.head]
    dh_copy = pltpu.make_async_copy(wide.acc.at[pl.ds(wide.head, own_rows)], dh_hbm, stores.at[2])
    dh_copy.start()
    ring.finish(ready)
    wide.scatter_done()
    ga_copy.wait()
    dh_copy.wait()


def middle_call(n_ctx, turned, g, h2, hid, dpre, w1, w_qkv, mid, cot, act, gain, w_out, bias, weight, q, k, v, lse, vec):
    lines, rows, width = n_ctx // 2, cot.shape[0], cot.shape[1]
    block_rows, own, cols = width // n_ctx, rows // 4, q.shape[1]
    hidden = hid.shape[1]
    returned = PREFIX * width // 4 // COLS
    vm, hbm, sm = (pl.BlockSpec(memory_space=s) for s in (pltpu.VMEM, pl.ANY, pltpu.SMEM))
    bf, f4 = jnp.bfloat16, jnp.float32
    return pl.pallas_call(
        functools.partial(middle_kernel, lines, turned),
        out_shape=(
            jax.ShapeDtypeStruct((2 * hidden // COLS + returned // block_rows, block_rows, COLS), f4),
            jax.ShapeDtypeStruct((own, width), f4),
            jax.ShapeDtypeStruct((rows, width), bf),
            jax.ShapeDtypeStruct((rows + PREFIX, 3 * cols), bf),
            jax.ShapeDtypeStruct((own, width), f4),
            jax.ShapeDtypeStruct(vec.shape, f4),
        ),
        in_specs=[hbm] * 8 + [vm] * 3 + [sm] * 2 + [vm] * 5,
        out_specs=[hbm, hbm, hbm, vm, hbm, vm],
        scratch_shapes=Ring.scratch(lines, block_rows)
        + Quad.scratch(own + PREFIX // 4, width)
        + [
            pltpu.VMEM((2, *g.shape), bf),
            pltpu.VMEM((2, rows, hidden), bf),
            pltpu.VMEM(w1.shape, bf),
            pltpu.VMEM((own, width), f4),
            pltpu.VMEM((own, width), bf),
            pltpu.VMEM((rows, width), bf),
            pltpu.VMEM((rows, cols), bf),
            pltpu.VMEM((rows + PREFIX, 2 * HEAD), f4),
            pltpu.VMEM((rows + PREFIX, 2 * HEAD), f4),
            pltpu.VMEM((returned, COLS), f4),
            pltpu.VMEM((returned, COLS), f4),
            pltpu.SemaphoreType.DMA((11,)),
            pltpu.SemaphoreType.DMA((3,)),
        ],
        compiler_params=pltpu.CompilerParams(collective_id=2, has_side_effects=True, vmem_limit_bytes=63 * 2**20),
    )(g, h2, hid, dpre, w1, w_qkv, mid, cot, act, gain[None], w_out, bias, weight, q, k, v, lse, vec)


def last_kernel(lines, turned, *refs):
    (d_all, h_all, att, ga, hid, w2, gain, ffn_bias, act, x_hbm, dmid_hbm, dh_hbm, mid_hbm, vec_in,
     grads, out, result, vec, *scratch) = refs
    ring_refs, scratch = scratch[:12], scratch[12:]
    quad_refs, scratch = scratch[:12], scratch[12:]
    x, dmid, d_h, mid, v_send, v_recv, loads, s_v, r_v = scratch
    rows, width = out.shape
    quad = Quad(quad_refs, rows, rows // 4)
    block_rows = ring_refs[0].shape[1]
    out_part = product_part(lambda m: ga, lambda m: att, lambda j: (0, j), turned, block_rows)
    head_part = product_part(lambda m: h_all, lambda m: d_all, lambda j: (0, j), turned, block_rows)
    cols = att.shape[1] // COLS
    ring = Ring(lines, [(cols, out_part), (3 * cols, head_part)], ring_refs, grads)
    spans = quad.spans(quad.tp)
    copies = [
        pltpu.make_async_copy(dh_hbm, d_h, loads.at[0]),
        pltpu.make_async_copy(x_hbm.at[spans[0]], x.at[: quad.head], loads.at[1]),
        pltpu.make_async_copy(x_hbm.at[spans[1]], x.at[quad.head :], loads.at[2]),
        pltpu.make_async_copy(dmid_hbm, dmid, loads.at[3]),
        pltpu.make_async_copy(mid_hbm, mid, loads.at[4]),
    ]
    for copy in copies:
        copy.start()
    ctx, tp = lax.axis_index("ctx"), lax.axis_index("tp")
    swaps, bit = [quad.across, quad.over], 1
    while bit < 2 * lines:
        swaps.append((ctx + bit - 2 * bit * lax.rem(ctx // bit, 2), tp))
        bit *= 2
    meet(ring.peers() + quad.peers() + [(None, device) for device in swaps[4:]])

    def swap(n):
        return pltpu.make_async_remote_copy(
            src_ref=v_send.at[n], dst_ref=v_recv.at[n], send_sem=s_v.at[n], recv_sem=r_v.at[n],
            device_id=swaps[n], device_id_type=MESH)

    def swap_start(n):
        v_send[n] = vec[...]
        swap(n).start()

    def swap_end(n):
        swap(n).wait()
        if n < 2:
            vec[:6] += v_recv[n, :6]
        else:
            vec[...] += v_recv[n]

    ring.start()
    for copy in copies:
        copy.wait()
    vec[...] = vec_in[...]
    size = 32

    def back_rows(i, _):
        whole, own = own_block(quad, i, size)
        grad = d_h[own]
        change, gain_terms = norm_back(grad, x[own].astype(jnp.float32), gain[...])
        out[whole] = (dmid[own] + change).astype(jnp.bfloat16)
        vec[0:1] += column_sum(gain_terms)
        vec[1:2] += column_sum(grad)
        return 0

    lax.fori_loop(0, quad.height // size, back_rows, 0)
    quad.gather_send(out)
    swap_start(0)
    quad.scatter_send(lambda half, n: nn(quad.half_of(hid, half), w2[:, quad.columns(n)]))
    swap_end(0)
    swap_start(1)
    ring.run(0, 4)
    swap_end(1)
    quad.gather_near(out)
    quad.gather_pass(out)
    ring.run(4, 8)
    swap_start(2)
    lax.fori_loop(0, quad.tiles, lambda n, _: (quad.scatter_add(n), 0)[1], 0)

    def out_rows(i, _):
        whole, own = own_block(quad, i, size)
        result[whole] = (mid[own] + act[whole] * (quad.acc[own] + ffn_bias[...])).astype(jnp.bfloat16)
        return 0

    lax.fori_loop(0, quad.height // size, out_rows, 0)
    quad.gather_send(result, 1)
    quad.gather_far(out)
    ring.run(8, ring.steps)
    quad.gather_near(result, 1)
    quad.gather_pass(result, 1)
    swap_end(2)
    swap_start(3)
    ring.run(ring.steps, ring.steps + SKEW)
    for n in range(3, len(swaps)):
        swap_end(n)
        if n + 1 < len(swaps):
            swap_start(n + 1)
    ring.finish(ring.steps + SKEW)
    quad.gather_far(result, 1)
    quad.gather_done(out)
    quad.gather_done(result, 1)
    quad.scatter_done()


def last_call(n_ctx, turned, d_all, h_all, att, ga, hid, w2, gain, ffn_bias, act, x, dmid, dh, mid, vec):
    lines, (rows, width) = n_ctx // 2, x.shape
    block_rows, own = width // n_ctx, rows // 4
    cols = att.shape[1] // COLS
    vm, hbm = (pl.BlockSpec(memory_space=s) for s in (pltpu.VMEM, pl.ANY))
    bf, f4 = jnp.bfloat16, jnp.float32
    rounds = n_ctx.bit_length() + 1
    return pl.pallas_call(
        functools.partial(last_kernel, lines, turned),
        out_shape=(
            jax.ShapeDtypeStruct((4 * cols, block_rows, COLS), f4),
            jax.ShapeDtypeStruct((rows, width), bf),
            jax.ShapeDtypeStruct((rows, width), bf),
            jax.ShapeDtypeStruct(vec.shape, f4),
        ),
        in_specs=[vm] * 9 + [hbm] * 4 + [vm],
        out_specs=[hbm, vm, vm, vm],
        scratch_shapes=Ring.scratch(lines, block_rows)
        + Quad.scratch(own, width)
        + [
            pltpu.VMEM((own, width), bf),
            pltpu.VMEM((own, width), f4),
            pltpu.VMEM((own, width), f4),
            pltpu.VMEM((own, width), f4),
            pltpu.VMEM((rounds, *vec.shape), f4),
            pltpu.VMEM((rounds, *vec.shape), f4),
            pltpu.SemaphoreType.DMA((5,)),
            pltpu.SemaphoreType.DMA((rounds,)),
            pltpu.SemaphoreType.DMA((rounds,)),
        ],
        compiler_params=pltpu.CompilerParams(collective_id=3, has_side_effects=True, vmem_limit_bytes=63 * 2**20),
    )(d_all, h_all, att, ga, hid, w2, gain[None], ffn_bias[None], act, x, dmid, dh, mid, vec)


def find_block(lengths, placed, block):
    mine, start, first = placed[block], 0, 0
    for s in range(lengths.shape[0]):
        first = jnp.where(start <= mine, start, first)
        start = start + lengths[s]
    owner = 0
    for e in range(placed.shape[0]):
        owner = owner + jnp.where(placed[e] == first, e, 0)
    return mine - first, jnp.minimum(owner, placed.shape[0] - 1)


def first_kernel(lines, *refs):
    (lengths, placed, layer, exits, x_hbm, w_hbm, gain, shift, qv_bias,
     q, k, v, h_all, act, bias, weight, *scratch) = refs
    x, w, line, x_send, x_recv, prefix, loads, s_l, s_r, r_z, s_x, r_x, s_g, r_g = scratch
    rows, width = x.shape
    part = prefix.shape[0] // 4
    ctx, tp = lax.axis_index("ctx"), lax.axis_index("tp")
    z, side, y, core = ctx // 2, lax.rem(ctx, 2), tp // 2, lax.rem(tp, 2)
    left, right, partner = (ctx - 2, tp), (ctx + 2, tp), (z * 2 + 1 - side, tp)
    across, over = (ctx, y * 2 + 1 - core), (ctx, (1 - y) * 2 + core)
    own = pl.ds(pl.multiple_of(tp * part, 16), part)
    copies = [
        pltpu.make_async_copy(x_hbm.at[own], line.at[z], loads.at[0]),
        pltpu.make_async_copy(x_hbm, x, loads.at[1]),
        pltpu.make_async_copy(w_hbm, w, loads.at[2]),
    ]
    for copy in copies:
        copy.start()
    meet([(None, partner), (z > 0, left), (z < lines - 1, right), (None, across), (None, over)])

    def hop(o, device, sems):
        return pltpu.make_async_remote_copy(
            src_ref=line.at[o], dst_ref=line.at[o], send_sem=sems.at[o], recv_sem=r_z.at[o],
            device_id=device, device_id_type=MESH)

    def pass_on(o, there, device, sems):
        @pl.when(there)
        def _():
            hop(o, device, sems).start()

    copies[0].wait()
    pass_on(z, z < lines - 1, right, s_r)
    pass_on(z, z > 0, left, s_l)

    def hops(d):
        @pl.when(z - d >= 0)
        def _():
            hop(z - d, left, s_l).wait_recv()
            pass_on(z - d, z < lines - 1, right, s_r)

        @pl.when(z + d < lines)
        def _():
            hop(z + d, right, s_r).wait_recv()
            pass_on(z + d, z > 0, left, s_l)

    my_part, my_owner = find_block(lengths, placed, ctx)
    _, partner_owner = find_block(lengths, placed, z * 2 + 1 - side)
    bias[0, 0] = jnp.where(my_part > 0, 0.0, NEGATIVE)
    for e in range(weight.shape[0]):
        weight[e] = jnp.where((my_owner == e) & (my_part > 0), 1.0, 0.0)
    row = lax.broadcasted_iota(jnp.int32, exits.shape, 0)
    first_rows = jnp.where(my_part == 0, PREFIX, 0)
    act[...] = jnp.where((exits[...] > layer[0]) | (row < first_rows), 1.0, 0.0)
    size = 64

    def norm_rows(source, start, to):
        def some(i, _):
            span = pl.ds(pl.multiple_of(start + i * size, size), size)
            values = source[span].astype(jnp.float32)
            target = pl.ds(pl.multiple_of(to + i * size, size), size)
            h_all[target] = (normed(values)[0] * gain[...] + shift[...]).astype(jnp.bfloat16)
            return 0

        lax.fori_loop(0, PREFIX // size, some, 0)

    def keys_of(span, rows_in):
        k[span] = nn(rows_in, w[1]).astype(jnp.bfloat16)
        v[span] = (nn(rows_in, w[2]) + qv_bias[1:2]).astype(jnp.bfloat16)

    for r in range(rows // PREFIX):
        norm_rows(x_wait(copies, r, x), r * PREFIX, (r + 1) * PREFIX)
        if r == 0:
            copies[2].wait()
        span = slice((r + 1) * PREFIX, (r + 2) * PREFIX)
        rows_in = h_all[span]
        low = (nn(rows_in, w[0]) + qv_bias[0:1]).astype(jnp.bfloat16)
        q[r * PREFIX : (r + 1) * PREFIX] = low * jnp.bfloat16(HEAD**-0.5)
        keys_of(span, rows_in)
        if r + 1 < lines:
            hops(r + 1)
    for d in range(rows // PREFIX + 1, lines):
        hops(d)
    x_send[...] = line[partner_owner // 2]
    trade = pltpu.make_async_remote_copy(
        src_ref=x_send, dst_ref=x_recv, send_sem=s_x, recv_sem=r_x, device_id=partner, device_id_type=MESH)
    trade.start()
    near = line[my_owner // 2]
    trade.wait_recv()
    prefix[own] = jnp.where(lax.rem(my_owner, 2) == side, near, x_recv[...])

    def give(n, quarter, device):
        span = pl.ds(pl.multiple_of(quarter * part, 16), part)
        return pltpu.make_async_remote_copy(
            src_ref=prefix.at[span], dst_ref=prefix.at[span], send_sem=s_g.at[n], recv_sem=r_g.at[n],
            device_id=device, device_id_type=MESH)

    far = (1 - y) * 2 + core
    give(0, tp, over).start()
    give(1, tp, across).start()
    give(0, far, over).wait_recv()
    give(2, far, across).start()
    give(1, y * 2 + 1 - core, across).wait_recv()
    give(2, (1 - y) * 2 + 1 - core, across).wait_recv()
    norm_rows(prefix, 0, 0)
    keys_of(slice(0, PREFIX), h_all[:PREFIX])
    trade.wait_send()
    give(0, tp, over).wait_send()
    give(1, tp, across).wait_send()
    give(2, far, across).wait_send()
    for o in range(lines):
        @pl.when((z < lines - 1) & (z >= o))
        def _():
            hop(o, right, s_r).wait_send()

        @pl.when((z > 0) & (z <= o))
        def _():
            hop(o, left, s_l).wait_send()


def x_wait(copies, r, x):
    if r == 0:
        copies[1].wait()
    return x


def first_call(n_ctx, lengths, placed, layer, exits, x, w_qkv, gain, shift, qv_bias):
    lines, (rows, width) = n_ctx // 2, x.shape
    cols = w_qkv.shape[2]
    vm, hbm, sm = (pl.BlockSpec(memory_space=s) for s in (pltpu.VMEM, pl.ANY, pltpu.SMEM))
    bf, f4 = jnp.bfloat16, jnp.float32
    return pl.pallas_call(
        functools.partial(first_kernel, lines),
        out_shape=(
            jax.ShapeDtypeStruct((rows, cols), bf),
            jax.ShapeDtypeStruct((rows + PREFIX, cols), bf),
            jax.ShapeDtypeStruct((rows + PREFIX, cols), bf),
            jax.ShapeDtypeStruct((rows + PREFIX, width), bf),
            jax.ShapeDtypeStruct((rows, 1), f4),
            jax.ShapeDtypeStruct((1, 1), f4),
            jax.ShapeDtypeStruct((n_ctx,), f4),
        ),
        in_specs=[sm] * 3 + [vm] + [hbm] * 2 + [vm] * 3,
        out_specs=[vm] * 5 + [sm] * 2,
        scratch_shapes=[
            pltpu.VMEM((rows, width), bf),
            pltpu.VMEM(w_qkv.shape, bf),
            pltpu.VMEM((lines, PREFIX // 4, width), bf),
            pltpu.VMEM((PREFIX // 4, width), bf),
            pltpu.VMEM((PREFIX // 4, width), bf),
            pltpu.VMEM((PREFIX, width), bf),
            pltpu.SemaphoreType.DMA((3,)),
            pltpu.SemaphoreType.DMA((lines,)),
            pltpu.SemaphoreType.DMA((lines,)),
            pltpu.SemaphoreType.DMA((lines,)),
            pltpu.SemaphoreType.DMA,
            pltpu.SemaphoreType.DMA,
            pltpu.SemaphoreType.DMA((3,)),
            pltpu.SemaphoreType.DMA((3,)),
        ],
        compiler_params=pltpu.CompilerParams(collective_id=4, has_side_effects=True, vmem_limit_bytes=50 * 2**20),
    )(lengths, placed, layer, exits[:, None], x, w_qkv, gain[None], shift[None], qv_bias)


def body(
    mesh,
    block_input,
    cotangent,
    ln1_gain,
    ln1_bias,
    w_qkv,
    qv_bias,
    w_out,
    out_bias,
    ln2_gain,
    ln2_bias,
    w_fc1,
    fc1_bias,
    w_fc2,
    fc2_bias,
    exit_layer,
    layer_index,
    lengths,
    stretch_map,
):
    n_ctx = mesh.shape["ctx"]
    row_count, width = block_input.shape
    block_rows = width // n_ctx
    turned = block_rows % 128 != 0

    def tokens_last(array):
        return array.T if turned else array

    query, key, value, h_all, active, bias, weight = first_call(
        n_ctx, lengths, stretch_map, layer_index, exit_layer, block_input, w_qkv, ln1_gain, ln1_bias, qv_bias
    )
    attended, log_total = attend(bias, query, key, value)
    middle, h2_low = branch_call(attended, w_out, block_input, active, out_bias, ln2_gain, ln2_bias)
    grad_ffn = (active * cotangent.astype(jnp.float32)).astype(jnp.bfloat16)
    hidden_pre = nn(h2_low, w_fc1) + fc1_bias
    hidden_low = jax.nn.gelu(hidden_pre).astype(jnp.bfloat16)
    d_hidden = nt(grad_ffn, w_fc2)
    d_pre_low = jax.vjp(jax.nn.gelu, hidden_pre)[1](d_hidden)[0].astype(jnp.bfloat16)
    d_fc2_bias = jnp.sum(grad_ffn.astype(jnp.float32), axis=0) / lax.axis_size("tp")
    d_fc1_bias = jnp.sum(d_pre_low.astype(jnp.float32), axis=0)
    zero = jnp.zeros((width,), jnp.float32)
    vectors = jnp.stack([zero, zero, zero, zero, zero, d_fc2_bias, d_fc1_bias, zero])
    ffn_grads, d_middle, grad_attn, d_all, d_h, vectors = middle_call(
        n_ctx, turned, tokens_last(grad_ffn), tokens_last(h2_low), hidden_low, d_pre_low, w_fc1, w_qkv,
        middle, cotangent, active, ln2_gain, w_out, bias, weight, query, key, value, log_total, vectors,
    )
    head_grads, input_grad, output_rows, vectors = last_call(
        n_ctx, turned, d_all, tokens_last(h_all), attended, tokens_last(grad_attn), hidden_low, w_fc2,
        ln1_gain, fc2_bias, active, block_input, d_middle, d_h, middle, vectors,
    )
    tiles = hidden_low.shape[1] // COLS
    fc2_grad = ffn_grads[:tiles].transpose(0, 2, 1).reshape(tiles * COLS, block_rows)
    fc1_grad = ffn_grads[tiles : 2 * tiles].transpose(1, 0, 2).reshape(block_rows, tiles * COLS)
    out_grad = head_grads[0].T
    qkv_grad = head_grads[1:4]
    qv_grad = vectors[7, : 2 * query.shape[1]].reshape(2, -1)
    return (
        output_rows,
        input_grad,
        vectors[0],
        vectors[1],
        qkv_grad,
        qv_grad,
        out_grad,
        vectors[2],
        vectors[3],
        vectors[4],
        fc1_grad,
        vectors[6],
        fc2_grad,
        vectors[5],
    )


def solution(mesh):
    in_specs = (
        P("ctx", None),
        P("ctx", None),
        P(),
        P(),
        P(None, None, "tp"),
        P(None, "tp"),
        P("tp", None),
        P(),
        P(),
        P(),
        P(None, "tp"),
        P("tp"),
        P("tp", None),
        P(),
        P("ctx"),
        P(),
        P(),
        P(),
    )
    out_specs = (
        P("ctx", None),
        P("ctx", None),
        P(),
        P(),
        P(None, "ctx", "tp"),
        P(None, "tp"),
        P("tp", "ctx"),
        P(),
        P(),
        P(),
        P("ctx", "tp"),
        P("tp"),
        P("tp", "ctx"),
        P(),
    )
    return jax.shard_map(functools.partial(body, mesh), mesh=mesh, in_specs=in_specs, out_specs=out_specs, check_vma=False)
```

```python
import functools

import jax
import jax.numpy as jnp
from jax import lax
from jax.experimental import pallas as pl
from jax.experimental.pallas import tpu as pltpu
from jax.sharding import PartitionSpec as P

HEAD = 64
PREFIX = 256
COLS = 512
MESH = pl.DeviceIdType.MESH
NEGATIVE = -1e30
EPSILON = 1e-05
AHEAD = 8
SKEW = 2
STAGES = 2
DEPTH = 2


class Ring:
    def __init__(self, lines, groups, refs, outs, later=(), prefix=None):
        self.lines, self.groups, self.outs, self.later, self.prefix = lines, groups, outs, later, prefix
        (self.xs, self.xr, self.zb, self.stage, self.turned, self.kept, self.swap, self.s_xs, self.s_xr, self.s_zs,
         self.s_zr, self.s_out, self.s_swap, self.c_x, self.c_left, self.c_right) = refs
        self.jobs = sum(group[0] for group in groups)
        marks, job = [], 0
        for group in groups:
            marks += [job + n for n in range(group[0]) if group[2]]
            job += group[0]
        self.fetched = (marks[0], marks[-1]) if marks else (self.jobs, self.jobs)
        self.steps = self.jobs * lines
        self.slots = self.xr.shape[0]
        self.lag = SKEW * (lines - 1) + 2
        ctx, tp = lax.axis_index("ctx"), lax.axis_index("tp")
        self.z, self.side = ctx // 2, lax.rem(ctx, 2)
        self.partner = (self.z * 2 + 1 - self.side, tp)
        self.left, self.right = (ctx - 2, tp), (ctx + 2, tp)

    @staticmethod
    def scratch(lines, rows):
        slots = AHEAD + SKEW * (lines - 1) + 4
        chunk = (rows, COLS)
        return [
            pltpu.VMEM((AHEAD, *chunk), jnp.bfloat16),
            pltpu.VMEM((slots, *chunk), jnp.bfloat16),
            pltpu.VMEM((DEPTH, lines + 1, *chunk), jnp.bfloat16),
            pltpu.VMEM((STAGES, *chunk), jnp.float32),
            pltpu.VMEM((STAGES, COLS, rows), jnp.float32),
            pltpu.VMEM(chunk, jnp.bfloat16),
            pltpu.VMEM((4, *chunk), jnp.bfloat16),
            pltpu.SemaphoreType.DMA((AHEAD,)),
            pltpu.SemaphoreType.DMA((slots,)),
            pltpu.SemaphoreType.DMA((slots,)),
            pltpu.SemaphoreType.DMA((DEPTH, lines + 1)),
            pltpu.SemaphoreType.DMA((STAGES,)),
            pltpu.SemaphoreType.DMA((4,)),
            pltpu.SemaphoreType.REGULAR,
            pltpu.SemaphoreType.REGULAR,
            pltpu.SemaphoreType.REGULAR,
        ]

    def sends(self, f):
        job = f // self.lines
        found = (job < self.fetched[0]) | (job > self.fetched[1]) | (lax.rem(f, self.lines) == 0)
        for pair in self.later:
            found = found & (job != pair[0]) & (job != pair[1])
        return found

    def peers(self):
        return [(None, self.partner), (self.z > 0, self.left), (self.z < self.lines - 1, self.right)]

    def x_copy(self, f):
        slot, to = lax.rem(f, AHEAD), lax.rem(f, self.slots)
        return pltpu.make_async_remote_copy(
            src_ref=self.xs.at[slot], dst_ref=self.xr.at[to], send_sem=self.s_xs.at[slot],
            recv_sem=self.s_xr.at[to], device_id=self.partner, device_id_type=MESH)

    def z_copy(self, f, to, device):
        slot, level = lax.rem(f, self.slots), lax.rem(f // self.lines, DEPTH)
        return pltpu.make_async_remote_copy(
            src_ref=self.xr.at[slot], dst_ref=self.zb.at[level, to], send_sem=self.s_zs.at[slot],
            recv_sem=self.s_zr.at[level, to], device_id=device, device_id_type=MESH)

    def out_copies(self, job, act):
        slot = lax.rem(job, STAGES)
        for there, turn, place in self.outs(job):
            @pl.when(there)
            def _():
                source = self.turned if turn else self.stage
                act(pltpu.make_async_copy(source.at[slot], place, self.s_out.at[slot]))

    def out_start(self, job):
        slot = lax.rem(job, STAGES)
        for there, turn, _ in self.outs(job):
            if turn:
                @pl.when(there)
                def _():
                    self.turned[slot] = self.stage[slot].T
        self.out_copies(job, lambda copy: copy.start())

    def out_wait(self, job):
        self.out_copies(job, lambda copy: copy.wait())

    def swap_copy(self, n):
        return pltpu.make_async_remote_copy(
            src_ref=self.swap.at[2 * n], dst_ref=self.swap.at[2 * n + 1], send_sem=self.s_swap.at[2 * n],
            recv_sem=self.s_swap.at[2 * n + 1], device_id=self.partner, device_id_type=MESH)

    def send(self, f, group, job0, fresh):
        _, part, is_prefix = group
        if not fresh:
            @pl.when(self.sends(f - AHEAD))
            def _():
                self.x_copy(f).wait_send()

            @pl.when(f >= self.slots)
            def _():
                pl.semaphore_wait(self.c_x, 1)

        @pl.when(self.sends(f))
        def _():
            owner = lax.rem(f, self.lines)
            value = part(f // self.lines - job0, None if is_prefix else owner * 2 + 1 - self.side)
            self.xs[lax.rem(f, AHEAD)] = value.astype(jnp.bfloat16)
            self.x_copy(f).start()

    def receive(self, f, group, job0):
        _, part, is_prefix = group
        job, owner, slot = f // self.lines, lax.rem(f, self.lines), lax.rem(f, self.slots)
        came = self.sends(f)

        @pl.when(came)
        def _():
            self.x_copy(f).wait_recv()
            if is_prefix:
                self.kept[...] = self.xr[slot]

        block = owner * 2 + self.side
        if is_prefix:
            mine, theirs = self.prefix[0][block], self.prefix[1][block]
            total = part(job - job0, None) * mine + self.kept[...].astype(jnp.float32) * theirs
        else:
            @pl.when(jnp.logical_not(came))
            def _():
                self.xr[slot] = jnp.zeros(self.xr.shape[1:], jnp.bfloat16)

            for pair in self.later:
                block = jnp.where(job == pair[0], owner * 2 + 1 - self.side, block)
            total = part(job - job0, block) + self.xr[slot].astype(jnp.float32)

        @pl.when(owner != self.z)
        def _():
            self.xr[slot] = total.astype(jnp.bfloat16)

        @pl.when(owner == self.z)
        def _():
            @pl.when(job >= STAGES)
            def _():
                self.out_wait(job - STAGES)
            self.stage[lax.rem(job, STAGES)] = total

    def add(self, f, index):
        job = f // self.lines
        slot, level = lax.rem(f, self.slots), lax.rem(job, DEPTH)

        @pl.when(lax.rem(f, self.lines) == self.z)
        def _():
            self.stage[lax.rem(job, STAGES)] += self.zb[level, index].astype(jnp.float32)

        @pl.when(lax.rem(f, self.lines) != self.z)
        def _():
            self.xr[slot] = (self.xr[slot].astype(jnp.float32) + self.zb[level, index].astype(jnp.float32)).astype(jnp.bfloat16)

    def flow(self, t):
        lines, z = self.lines, self.z
        f = t - SKEW * z
        owner = lax.rem(f + lines * SKEW * lines, lines)

        @pl.when((f >= 0) & (f < self.steps) & (owner >= z))
        def _():
            @pl.when(z > 0)
            def _():
                self.z_copy(f, owner, self.left).wait_recv()
                self.add(f, owner)
                pl.semaphore_signal(self.c_right, inc=1, device_id=self.left, device_id_type=MESH)

            @pl.when(owner > z)
            def _():
                @pl.when(f >= DEPTH * lines)
                def _():
                    pl.semaphore_wait(self.c_right, 1)
                self.z_copy(f, owner, self.right).start()

        g = t - SKEW * (lines - 1 - z)
        owner2 = lax.rem(g + lines * SKEW * lines, lines)

        @pl.when((g >= 0) & (g < self.steps) & (owner2 <= z))
        def _():
            @pl.when(z < lines - 1)
            def _():
                index = jnp.where(owner2 == z, lines, owner2)
                self.z_copy(g, index, self.right).wait_recv()
                self.add(g, index)
                pl.semaphore_signal(self.c_left, inc=1, device_id=self.right, device_id_type=MESH)

            @pl.when(owner2 < z)
            def _():
                @pl.when(g >= DEPTH * lines)
                def _():
                    pl.semaphore_wait(self.c_left, 1)
                self.z_copy(g, jnp.where(owner2 == z - 1, lines, owner2), self.left).start()

        h = t - SKEW * (lines - 1)

        @pl.when((h >= 0) & (h < self.steps) & (lax.rem(h + lines * SKEW * lines, lines) == z))
        def _():
            job = h // lines
            stage = lax.rem(job, STAGES)
            for n, pair in enumerate(self.later):
                @pl.when(job == pair[0])
                def _():
                    self.swap[2 * n] = self.stage[stage].astype(jnp.bfloat16)
                    self.swap_copy(n).start()

                @pl.when(job == pair[1])
                def _():
                    self.swap_copy(n).wait()
                    self.stage[stage] += self.swap[2 * n + 1].astype(jnp.float32)
            if self.prefix is not None:
                target, rows = self.prefix[2], self.stage.shape[1]

                @pl.when((job >= self.fetched[0]) & (job <= self.fetched[1]))
                def _():
                    span = pl.ds(pl.multiple_of((job - self.fetched[0]) * rows, rows), rows)
                    target[span] = self.stage[stage]
            self.out_start(job)

        d = t - self.lag

        @pl.when((d >= 0) & (d < self.steps))
        def _():
            @pl.when(lax.rem(d + lines * (SKEW * lines + 2), lines) != z)
            def _():
                self.z_copy(d, 0, self.left).wait_send()
            pl.semaphore_signal(self.c_x, inc=1, device_id=self.partner, device_id_type=MESH)

    def find(self, f):
        job = 0
        for group in self.groups:
            if f < (job + group[0]) * self.lines:
                return group, job
            job += group[0]
        return None

    def pieces(self, lo, hi):
        cuts, job = {lo, hi}, 0
        for group in self.groups:
            job += group[0]
            cuts |= {job * self.lines, job * self.lines - AHEAD}
        cuts = sorted(c for c in cuts if lo <= c <= hi)
        return zip(cuts[:-1], cuts[1:])

    def start(self):
        for lo, hi in self.pieces(0, AHEAD):
            here = self.find(lo)
            lax.fori_loop(lo, hi, lambda f, _, here=here: (self.send(f, *here, True), 0)[1], 0)

    def run(self, lo, hi):
        for a, b in self.pieces(lo, min(hi, self.steps)):
            here, ahead = self.find(a), self.find(a + AHEAD)

            def body(f, _, here=here, ahead=ahead):
                self.receive(f, *here)
                self.flow(f)
                if ahead is not None:
                    self.send(f + AHEAD, *ahead, False)
                return 0

            lax.fori_loop(a, b, body, 0)
        if hi > self.steps:
            lax.fori_loop(max(lo, self.steps), hi, lambda t, _: (self.flow(t), 0)[1], 0)

    def run_some(self, lo, count):
        here = self.find(0)

        def body(f, _):
            self.receive(f, *here)
            self.flow(f)

            @pl.when(f + AHEAD < self.steps)
            def _():
                self.send(f + AHEAD, *here, False)
            return 0

        lax.fori_loop(lo, lo + count, body, 0)

    def finish(self, lo):
        lines, z = self.lines, self.z
        self.run(lo, self.steps + self.lag)

        def drain(f, _):
            @pl.when(self.sends(f))
            def _():
                self.x_copy(f).wait_send()
            return 0

        lax.fori_loop(self.steps - AHEAD, self.steps, drain, 0)
        for job in range(self.jobs - STAGES, self.jobs):
            self.out_wait(job)
        pl.semaphore_wait(self.c_x, min(self.slots, self.steps))

        @pl.when(z < lines - 1)
        def _():
            pl.semaphore_wait(self.c_right, DEPTH * (lines - 1 - z))

        @pl.when(z > 0)
        def _():
            pl.semaphore_wait(self.c_left, DEPTH * z)


def meet(peers):
    barrier = pltpu.get_barrier_semaphore()
    count = 0
    for there, device in peers:
        if there is None:
            pl.semaphore_signal(barrier, inc=1, device_id=device, device_id_type=MESH)
            count += 1
        else:
            @pl.when(there)
            def _():
                pl.semaphore_signal(barrier, inc=1, device_id=device, device_id_type=MESH)
            count += jnp.where(there, 1, 0)
    pl.semaphore_wait(barrier, count)
class Quad:
    def __init__(self, refs, rows, height):
        (self.tmp, self.cs, self.cr, self.ys, self.yr, self.acc, self.s_c, self.r_c, self.s_y, self.r_y,
         self.s_g, self.r_g) = refs
        ctx, tp = lax.axis_index("ctx"), lax.axis_index("tp")
        self.y, self.core, self.tp = tp // 2, lax.rem(tp, 2), tp
        self.across = (ctx, self.y * 2 + 1 - self.core)
        self.over = (ctx, (1 - self.y) * 2 + self.core)
        self.head, self.rest = PREFIX // 4, (rows - PREFIX) // 4
        self.tiles = self.cs.shape[1]
        self.height = height

    @staticmethod
    def scratch(rows, width):
        tiles = width // COLS
        return [
            pltpu.VMEM((2, rows, COLS), jnp.float32),
            pltpu.VMEM((2, tiles, rows, COLS), jnp.bfloat16),
            pltpu.VMEM((2, tiles, rows, COLS), jnp.bfloat16),
            pltpu.VMEM((tiles, rows, COLS), jnp.bfloat16),
            pltpu.VMEM((tiles, rows, COLS), jnp.bfloat16),
            pltpu.VMEM((rows, width), jnp.float32),
            pltpu.SemaphoreType.DMA((2, tiles)),
            pltpu.SemaphoreType.DMA((2, tiles)),
            pltpu.SemaphoreType.DMA((tiles,)),
            pltpu.SemaphoreType.DMA((tiles,)),
            pltpu.SemaphoreType.DMA((2, 3, 2)),
            pltpu.SemaphoreType.DMA((2, 3, 2)),
        ]

    def peers(self):
        return [(None, self.across), (None, self.over)]

    def spans(self, quarter):
        return [
            pl.ds(pl.multiple_of(quarter * self.head, 16), self.head),
            pl.ds(pl.multiple_of(PREFIX + quarter * self.rest, 16), self.rest),
        ]

    def rows_of(self, ref, quarter):
        return jnp.concatenate([ref[span] for span in self.spans(quarter)], axis=0)

    def half_of(self, ref, half):
        return jnp.concatenate([self.rows_of(ref, half * 2), self.rows_of(ref, half * 2 + 1)], axis=0)

    def c_copy(self, k, n):
        return pltpu.make_async_remote_copy(
            src_ref=self.cs.at[k, n, : self.height], dst_ref=self.cr.at[k, n, : self.height], send_sem=self.s_c.at[k, n],
            recv_sem=self.r_c.at[k, n], device_id=self.across, device_id_type=MESH)

    def y_copy(self, n):
        return pltpu.make_async_remote_copy(
            src_ref=self.ys.at[n, : self.height], dst_ref=self.yr.at[n, : self.height], send_sem=self.s_y.at[n],
            recv_sem=self.r_y.at[n], device_id=self.over, device_id_type=MESH)

    def columns(self, n):
        return pl.ds(pl.multiple_of(n * COLS, COLS), COLS)

    def split(self, value, k, n):
        rows = self.height
        self.tmp[0, :rows] = value[:rows]
        self.tmp[1, :rows] = value[rows:]
        self.cs[k, n, :rows] = self.tmp[1 - self.core, :rows].astype(jnp.bfloat16)
        self.c_copy(k, n).start()
        self.acc[:rows, self.columns(n)] = self.tmp[self.core, :rows]

    def relay(self, n):
        self.c_copy(0, n).wait_recv()
        rows = self.height
        total = self.acc[:rows, self.columns(n)] + self.cr[0, n, :rows].astype(jnp.float32)
        self.ys[n, :rows] = total.astype(jnp.bfloat16)
        self.y_copy(n).start()

    def scatter_send(self, chunk):
        def far(n, _):
            self.split(chunk(1 - self.y, n), 0, n)

            @pl.when(n > 0)
            def _():
                self.relay(n - 1)
            return 0

        lax.fori_loop(0, self.tiles, far, 0)
        self.relay(self.tiles - 1)

        def near(n, _):
            self.split(chunk(self.y, n), 1, n)
            return 0

        lax.fori_loop(0, self.tiles, near, 0)

    def scatter_add(self, n):
        self.c_copy(1, n).wait_recv()
        self.y_copy(n).wait_recv()
        rows = self.height
        came = self.cr[1, n, :rows].astype(jnp.float32) + self.yr[n, :rows].astype(jnp.float32)
        self.acc[:rows, self.columns(n)] += came

    def scatter_done(self):
        for n in range(self.tiles):
            self.c_copy(0, n).wait_send()
            self.c_copy(1, n).wait_send()
            self.y_copy(n).wait_send()

    def g_copy(self, full, k, s, quarter, device, turn):
        span = self.spans(quarter)[s]
        return pltpu.make_async_remote_copy(
            src_ref=full.at[span], dst_ref=full.at[span], send_sem=self.s_g.at[turn, k, s],
            recv_sem=self.r_g.at[turn, k, s], device_id=device, device_id_type=MESH)

    def gather_send(self, full, turn=0):
        for s in range(2):
            self.g_copy(full, 0, s, self.tp, self.over, turn).start()
        for s in range(2):
            self.g_copy(full, 1, s, self.tp, self.across, turn).start()

    def gather_near(self, full, turn=0):
        for s in range(2):
            self.g_copy(full, 1, s, self.y * 2 + 1 - self.core, self.across, turn).wait_recv()

    def gather_pass(self, full, turn=0):
        other = (1 - self.y) * 2 + self.core
        for s in range(2):
            self.g_copy(full, 0, s, other, self.over, turn).wait_recv()
            self.g_copy(full, 2, s, other, self.across, turn).start()

    def gather_far(self, full, turn=0):
        for s in range(2):
            self.g_copy(full, 2, s, (1 - self.y) * 2 + 1 - self.core, self.across, turn).wait_recv()

    def gather_done(self, full, turn=0):
        other = (1 - self.y) * 2 + self.core
        for s in range(2):
            self.g_copy(full, 0, s, self.tp, self.over, turn).wait_send()
            self.g_copy(full, 1, s, self.tp, self.across, turn).wait_send()
            self.g_copy(full, 2, s, other, self.across, turn).wait_send()


def nt(left, right):
    return lax.dot_general(left, right, (((1,), (1,)), ((), ())), preferred_element_type=jnp.float32)


def normed(values_in):
    centred = values_in - jnp.mean(values_in, axis=1, keepdims=True)
    scale = lax.rsqrt(jnp.mean(centred * centred, axis=1, keepdims=True) + EPSILON)
    return centred * scale, scale


def branch_kernel(att, w_out, x_ref, act_ref, bias, gain, shift, mid_ref, full, *scratch):
    quad = Quad(scratch, att.shape[0], mid_ref.shape[0])
    meet(quad.peers())
    quad.scatter_send(lambda half, n: jnp.dot(quad.half_of(att, half), w_out[:, quad.columns(n)], preferred_element_type=jnp.float32))
    lax.fori_loop(0, quad.tiles, lambda n, _: (quad.scatter_add(n), 0)[1], 0)
    start = 0
    for span in quad.spans(quad.tp):
        size = span.size
        middle = x_ref[span].astype(jnp.float32) + act_ref[span] * (quad.acc[start:start + size] + bias[...])
        mid_ref[start:start + size] = middle
        full[span] = (normed(middle)[0] * gain[...] + shift[...]).astype(jnp.bfloat16)
        start += size
    quad.gather_send(full)
    quad.gather_near(full)
    quad.gather_pass(full)
    quad.gather_far(full)
    quad.gather_done(full)
    quad.scatter_done()


def branch_call(att, w_out, x, act, bias, gain, shift):
    rows, width = x.shape
    own = rows // 4
    vm = pl.BlockSpec(memory_space=pltpu.VMEM)
    return pl.pallas_call(
        branch_kernel,
        out_shape=(jax.ShapeDtypeStruct((own, width), jnp.float32), jax.ShapeDtypeStruct((rows, width), jnp.bfloat16)),
        in_specs=[vm] * 7,
        out_specs=[vm] * 2,
        scratch_shapes=Quad.scratch(own, width),
        compiler_params=pltpu.CompilerParams(collective_id=1, has_side_effects=True, vmem_limit_bytes=50 * 2**20),
    )(att, w_out, x, act, bias[None], gain[None], shift[None])
def tn(left, right):
    return lax.dot_general(left, right, (((0,), (0,)), ((), ())), preferred_element_type=jnp.float32)


def nn(left, right):
    return jnp.dot(left, right, preferred_element_type=jnp.float32)


def lane_mask(rows, head):
    lane = lax.broadcasted_iota(jnp.int32, (rows, 2 * HEAD), 1)
    return (lane < HEAD) if head == 0 else (lane >= HEAD)


def scores_of(keys, query, bias):
    scores = nt(keys, query)
    count = scores.shape[0]
    row = lax.broadcasted_iota(jnp.int32, (PREFIX, PREFIX), 0)
    col = lax.broadcasted_iota(jnp.int32, (PREFIX, PREFIX), 1)
    parts = [scores[:PREFIX] + bias]
    if count > 2 * PREFIX:
        parts.append(scores[PREFIX : count - PREFIX])
    parts.append(jnp.where(row <= col, scores[count - PREFIX :], NEGATIVE))
    return jnp.concatenate(parts, axis=0)


def attend_kernel(bias_ref, q_ref, k_ref, v_ref, o_ref, l_ref):
    rows, pairs = q_ref.shape[0], q_ref.shape[1] // (2 * HEAD)
    bias = bias_ref[0, 0]

    def pair(p, _):
        lanes = pl.ds(pl.multiple_of(p * 2 * HEAD, 2 * HEAD), 2 * HEAD)
        value_t = v_ref[:, lanes].T
        for r in range(rows // PREFIX):
            count, own = (r + 2) * PREFIX, slice(r * PREFIX, (r + 1) * PREFIX)
            query, keys = q_ref[own, lanes], k_ref[:count, lanes]
            outs = []
            for e in range(2):
                masked = jnp.where(lane_mask(PREFIX, e), query, jnp.zeros_like(query))
                scores = scores_of(keys, masked, bias)
                peak = jnp.max(scores, axis=0, keepdims=True)
                raised = jnp.exp(scores - peak)
                total = jnp.sum(raised, axis=0, keepdims=True)
                probs = (raised * (1.0 / total)).astype(jnp.bfloat16)
                l_ref[p, e : e + 1, own] = peak + jnp.log(total)
                outs.append(nn(value_t[e * HEAD : (e + 1) * HEAD, :count], probs))
            o_ref[own, lanes] = jnp.concatenate(outs, axis=0).astype(jnp.bfloat16).T
        return 0

    lax.fori_loop(0, pairs, pair, 0)


def attend(bias, q, k, v):
    rows, cols = q.shape
    vm = pl.BlockSpec(memory_space=pltpu.VMEM)
    return pl.pallas_call(
        attend_kernel,
        out_shape=(
            jax.ShapeDtypeStruct((rows, cols), jnp.bfloat16),
            jax.ShapeDtypeStruct((cols // (2 * HEAD), 2, rows), jnp.float32),
        ),
        in_specs=[pl.BlockSpec(memory_space=pltpu.SMEM)] + [vm] * 3,
        out_specs=[vm] * 2,
        compiler_params=pltpu.CompilerParams(vmem_limit_bytes=40 * 2**20),
    )(bias, q, k, v)


def attend_back(p, bias, q_ref, k_ref, v_ref, l_ref, g_ref, d_ref, room):
    rows, width = q_ref.shape
    blocks = rows // PREFIX
    base = pl.multiple_of(p * 2 * HEAD, 2 * HEAD)
    lanes = pl.ds(base, 2 * HEAD)
    sums = jnp.zeros((1, 2 * HEAD), jnp.float32)
    for r in reversed(range(blocks)):
        count, own = (r + 2) * PREFIX, slice(r * PREFIX, (r + 1) * PREFIX)
        query, grad, keys, values = q_ref[own, lanes], g_ref[own, lanes], k_ref[:count, lanes], v_ref[:count, lanes]
        d_queries, d_keys, d_values = [], None, None
        for e in range(2):
            mask = lane_mask(PREFIX, e)
            query_e = jnp.where(mask, query, jnp.zeros_like(query))
            grad_e = jnp.where(mask, grad, jnp.zeros_like(grad))
            probs = jnp.exp(scores_of(keys, query_e, bias) - l_ref[p, e : e + 1, own])
            d_probs = nt(values, grad_e)
            inner = jnp.sum(probs * d_probs, axis=0, keepdims=True)
            d_scores = (probs * (d_probs - inner)).astype(jnp.bfloat16)
            keys_e, values_e = nn(d_scores, query_e), nn(probs.astype(jnp.bfloat16), grad_e)
            d_keys = keys_e if d_keys is None else d_keys + keys_e
            d_values = values_e if d_values is None else d_values + values_e
            d_queries.append(tn(d_scores, keys))
        d_query = jnp.where(lane_mask(PREFIX, 0), d_queries[0], d_queries[1]) * HEAD ** (-0.5)
        sums += jnp.sum(d_query, axis=0, keepdims=True)
        d_ref[(r + 1) * PREFIX : (r + 2) * PREFIX, lanes] = d_query.astype(jnp.bfloat16)
        for n in range(r + 2):
            for at, sums_of in ((n, d_keys), (blocks + 1 + n, d_values)):
                place, term = slice(at * 2 * HEAD, (at + 1) * 2 * HEAD), sums_of[n * PREFIX : (n + 1) * PREFIX]
                if r == blocks - 1:
                    room[:PREFIX, place] = term
                else:
                    room[:PREFIX, place] += term
    d_ref[:PREFIX, lanes] = jnp.zeros((PREFIX, 2 * HEAD), jnp.bfloat16)
    value_sums = jnp.zeros((1, 2 * HEAD), jnp.float32)
    for n in range(blocks + 1):
        span = slice(n * PREFIX, (n + 1) * PREFIX)
        for m, at in ((1, n), (2, blocks + 1 + n)):
            total = room[:PREFIX, at * 2 * HEAD : (at + 1) * 2 * HEAD]
            d_ref[span, pl.ds(pl.multiple_of(base + m * width, 2 * HEAD), 2 * HEAD)] = total.astype(jnp.bfloat16)
            if m == 2:
                value_sums += column_sum(total)
    return sums, value_sums


def own_block(quad, i, size):
    first = quad.head // size
    start = jnp.where(i < first, quad.tp * quad.head + i * size, PREFIX + quad.tp * quad.rest + (i - first) * size)
    return pl.ds(pl.multiple_of(start, size), size), pl.ds(pl.multiple_of(i * size, size), size)


def norm_back(grad, source, gain):
    unit, scale = normed(source)
    scaled = grad * gain
    mean = jnp.mean(scaled, axis=1, keepdims=True)
    slope = jnp.mean(scaled * unit, axis=1, keepdims=True)
    return scale * (scaled - mean - unit * slope), grad * unit


def column_sum(values_in):
    return jnp.sum(values_in, axis=0, keepdims=True)


def product_part(left, right, tile, turned, rows):
    def part(j, block):
        cols = pl.ds(pl.multiple_of(tile(j) * COLS, COLS), COLS)
        span = pl.ds(pl.multiple_of(block * rows, rows), rows)
        if turned:
            return nn(left[span, :], right[:, cols])
        return tn(left[:, span], right[:, cols])

    return part


def pick(table, j):
    found = table[0]
    for n, entry in enumerate(table[1:]):
        found = jnp.where(j == n + 1, entry, found)
    return found


class Wide(Quad):
    def rows_of(self, ref, quarter):
        own = [pl.ds(pl.multiple_of(span.start + PREFIX, 16), span.size) for span in self.spans(quarter)]
        return jnp.concatenate([ref[span] for span in [self.spans(quarter)[0]] + own], axis=0)


def back_kernel(lines, turned, *refs):
    (g_hbm, h2_hbm, hid_hbm, dpre_hbm, w1_hbm, w_qkv_hbm, w2_hbm, wo_hbm, h_hbm, att_hbm, mid_hbm, cot_hbm, x_hbm,
     act, gain1, gain2, ffn_bias, bias, weight, theirs, q, k, v, lse, vec_in,
     fc2_out, fc1_out, out_grad, qkv_grad, in_hbm, act_hbm, dmid_hbm, dh_hbm, vec, *scratch) = refs
    ring_refs, scratch = scratch[:16], scratch[16:]
    quad_refs, scratch = scratch[:12], scratch[12:]
    (x0, x1, y0, y1, weights, mid, own_in, full, d_att, d_all, fresh, back, v_send, v_recv, loads, stores, s_v, r_v,
     c_over) = scratch
    rows, width = full.shape
    quad, wide = Quad(quad_refs, rows, rows // 4), Wide(quad_refs, rows, (rows + PREFIX) // 4)
    own_rows, depth = quad.height, q.shape[1]
    tiles, cols = y0.shape[1] // COLS, depth // COLS
    block_rows = ring_refs[0].shape[1]
    extra = fresh.shape[0] // block_rows
    order2 = [tiles - 1, *range(tiles - 1), tiles - 1]
    order1 = [*range(tiles - 2), tiles - 1, tiles - 2, tiles - 1]
    half = tiles + 1
    later = ((0, tiles), (half + tiles - 2, half + tiles))
    base = 2 * half + extra
    g_part = x0.at[:, :rows] if turned else x0.at[:rows]
    columns = lambda n: pl.ds(pl.multiple_of(n * COLS, COLS), COLS)

    def prefix_part(j, block):
        return fresh[pl.ds(pl.multiple_of(j * block_rows, block_rows), block_rows)]

    def outs(job):
        local = job - half
        head = jnp.maximum(job - base - cols, 0)
        place2, place1 = columns(pick(order2, job)), columns(pick(order1, local))
        is2 = (job < half) & (job != later[0][0])
        is1 = (job >= half) & (job < 2 * half) & (job != later[1][0])
        is_out = (job >= base) & (job < base + cols)
        out_span = columns(jnp.clip(job - base, 0, cols - 1))
        return [
            (is2, True, fc2_out.at[place2]),
            (is1, False, fc1_out.at[:, place1]),
            (is_out, True, out_grad.at[out_span]),
            (job >= base + cols, False, qkv_grad.at[head // cols, :, columns(lax.rem(head, cols))]),
        ]

    groups = [
        (half, product_part(g_part, y0, lambda j: pick(order2, j), turned, block_rows), False),
        (half, product_part(x1, y1, lambda j: pick(order1, j), turned, block_rows), False),
        (extra, prefix_part, True),
        (cols, product_part(x1 if turned else full, d_att, lambda j: j, turned, block_rows), False),
        (3 * cols, product_part(x0, d_all, lambda j: j, turned, block_rows), False),
    ]
    ring = Ring(lines, groups, ring_refs, outs, later, (weight, theirs, back))

    def load(n, source, target):
        return pltpu.make_async_copy(source, target, loads.at[n])

    def store(n, source, target):
        return pltpu.make_async_copy(source, target, stores.at[n])

    def begin(*copies):
        for copy in copies:
            copy.start()

    def end(*copies):
        for copy in copies:
            copy.wait()

    spans = quad.spans(quad.tp)
    first = [load(0, hid_hbm, y0), load(1, g_hbm, g_part)]
    second = [load(2, dpre_hbm, y1), load(3, w1_hbm, weights)]
    third = [
        load(4, h2_hbm, x1),
        load(5, mid_hbm, mid),
        load(6, cot_hbm.at[spans[0]], own_in.at[: quad.head]),
        load(7, cot_hbm.at[spans[1]], own_in.at[quad.head :]),
    ]
    begin(*first, *second, *third)
    ctx, tp = lax.axis_index("ctx"), lax.axis_index("tp")
    swaps, bit = [quad.across, quad.over], 1
    while bit < 2 * lines:
        swaps.append((ctx + bit - 2 * bit * lax.rem(ctx // bit, 2), tp))
        bit *= 2
    meet(ring.peers() + quad.peers() + [(None, device) for device in swaps[4:]])

    def swap(n):
        return pltpu.make_async_remote_copy(
            src_ref=v_send.at[n], dst_ref=v_recv.at[n], send_sem=s_v.at[n], recv_sem=r_v.at[n],
            device_id=swaps[n], device_id_type=MESH)

    def swap_start(n):
        v_send[n] = vec[...]
        swap(n).start()

    def swap_end(n):
        swap(n).wait()
        if n < 2:
            vec[:6] += v_recv[n, :6]
        else:
            vec[...] += v_recv[n]

    def add_all(group):
        lax.fori_loop(0, group.tiles, lambda n, _: (group.scatter_add(n), 0)[1], 0)

    end(*first)
    ring.start()
    end(*second)
    quad.scatter_send(lambda part, n: nt(quad.half_of(y1, part), weights[quad.columns(n), :]))
    wo_copy = load(3, wo_hbm, weights.at[:depth])
    wo_copy.start()
    end(*third)
    ring.run(0, 2)
    add_all(quad)
    vec[...] = vec_in[...]
    size = 32

    def middle_rows(i, _):
        whole, own = own_block(quad, i, size)
        grad = quad.acc[own]
        change, gain_terms = norm_back(grad, mid[own], gain2[...])
        d_middle = own_in[own].astype(jnp.float32) + change
        quad.acc[own] = d_middle
        low = (act[whole] * d_middle).astype(jnp.bfloat16)
        full[whole] = low
        vec[2:3] += column_sum(low.astype(jnp.float32))
        vec[3:4] += column_sum(gain_terms)
        vec[4:5] += column_sum(grad)
        return 0

    lax.fori_loop(0, own_rows // size, middle_rows, 0)
    quad.gather_send(full)
    keep = store(0, quad.acc.at[:own_rows], dmid_hbm)
    x_copies = [load(6, x_hbm.at[spans[0]], own_in.at[: quad.head]), load(7, x_hbm.at[spans[1]], own_in.at[quad.head :])]
    begin(keep, *x_copies)
    ring.run(2, 4)
    quad.gather_near(full)
    quad.gather_pass(full)
    quad.gather_far(full)
    wo_copy.wait()

    def attended_rows(i, _):
        span = pl.ds(pl.multiple_of(i * PREFIX, PREFIX), PREFIX)
        d_att[span] = nt(full[span], weights[:depth, :]).astype(jnp.bfloat16)
        return 0

    lax.fori_loop(0, rows // PREFIX, attended_rows, 0)
    heads = [load(8 + m, w_qkv_hbm.at[m], weights.at[:, m * depth : (m + 1) * depth]) for m in range(3)]
    begin(*heads)
    keep.wait()
    pairs = depth // (2 * HEAD)

    def pair(p, _):
        sums, value_sums = attend_back(p, bias[0, 0], q, k, v, lse, d_att, d_all, quad.acc)
        start = pl.multiple_of(p * 2 * HEAD, 2 * HEAD)
        vec[7:8, pl.ds(start, 2 * HEAD)] = sums
        vec[7:8, pl.ds(pl.multiple_of(start + depth, 2 * HEAD), 2 * HEAD)] = value_sums
        ring.run_some(4 + 2 * p, 2)
        return 0

    lax.fori_loop(0, pairs, pair, 0)
    now = 4 + 2 * pairs
    att_copy = load(2, att_hbm, d_att)
    att_copy.start()
    quad.gather_done(full)
    quad.scatter_done()
    end(*heads)
    wide.scatter_send(lambda part, n: nt(wide.half_of(d_all, part), weights[wide.columns(n), : 3 * depth]))
    w2_copy = load(3, w2_hbm, weights)
    w2_copy.start()
    ring.run(now, now + 4)
    add_all(wide)
    pl.semaphore_signal(c_over, inc=1, device_id=quad.over, device_id_type=MESH)
    for n in range(wide.tiles):
        fresh[n * wide.head : (n + 1) * wide.head] = wide.acc[: wide.head, n * COLS : (n + 1) * COLS]
    dh_copy = store(1, wide.acc.at[pl.ds(wide.head, own_rows)], dh_hbm)
    dh_copy.start()
    free0, free1 = half * lines, 2 * half * lines
    ring.run(now + 4, free0)
    h_copy = load(1, h_hbm, x0)
    h_copy.start()
    att_copy.wait()
    ring.run(free0, free1 - AHEAD)
    h_copy.wait()
    ring.run(free1 - AHEAD, free1)
    if turned:

        def flip(n, _):
            x1[columns(n), :] = full[:, columns(n)].T
            return 0

        lax.fori_loop(0, width // COLS, flip, 0)
    wide.scatter_done()
    end(dh_copy, w2_copy)
    pl.semaphore_wait(c_over, 1)
    quad.scatter_send(lambda part, n: nn(quad.half_of(y0, part), weights[:, quad.columns(n)]))
    ring.run(free1, free1 + lines)
    add_all(quad)

    def out_rows(i, _):
        whole, own = own_block(quad, i, size)
        y1[whole] = (mid[own] + act[whole] * (quad.acc[own] + ffn_bias[...])).astype(jnp.bfloat16)
        return 0

    lax.fori_loop(0, own_rows // size, out_rows, 0)
    quad.gather_send(y1)
    again = [load(4, dh_hbm, quad.acc.at[:own_rows]), load(5, dmid_hbm, mid)]
    begin(*again)
    ready = base * lines + SKEW * (lines - 1)
    ring.run(free1 + lines, ready)
    quad.gather_near(y1)
    quad.gather_pass(y1)
    quad.gather_far(y1)
    act_copy = store(0, y1, act_hbm)
    act_copy.start()
    end(*again, *x_copies)
    for n in range(quad.tiles):
        quad.acc[: quad.head, n * COLS : (n + 1) * COLS] += back[n * quad.head : (n + 1) * quad.head]

    def input_rows(i, _):
        whole, own = own_block(quad, i, size)
        grad = quad.acc[own]
        change, gain_terms = norm_back(grad, own_in[own].astype(jnp.float32), gain1[...])
        y0[whole] = (mid[own] + change).astype(jnp.bfloat16)
        vec[0:1] += column_sum(gain_terms)
        vec[1:2] += column_sum(grad)
        return 0

    lax.fori_loop(0, own_rows // size, input_rows, 0)
    quad.gather_send(y0, 1)
    swap_start(0)
    late = max(ready, ring.steps - lines)
    ring.run(ready, late)
    swap_end(0)
    swap_start(1)
    ring.run(late, ring.steps)
    quad.gather_near(y0, 1)
    quad.gather_pass(y0, 1)
    swap_end(1)
    swap_start(2)
    ring.run(ring.steps, ring.steps + SKEW)
    quad.gather_far(y0, 1)
    in_copy = store(1, y0, in_hbm)
    in_copy.start()
    for n in range(2, len(swaps)):
        swap_end(n)
        if n + 1 < len(swaps):
            swap_start(n + 1)
    ring.finish(ring.steps + SKEW)
    quad.gather_done(y1)
    quad.gather_done(y0, 1)
    quad.scatter_done()
    end(act_copy, in_copy)


def back_call(n_ctx, turned, g, h2, hid, dpre, w1, w_qkv, w2, w_out, h_all, att, mid, cot, x, act, gain1, gain2, ffn_bias,
              bias, weight, theirs, q, k, v, lse, vec):
    lines, rows, width = n_ctx // 2, cot.shape[0], cot.shape[1]
    block_rows, own, cols = width // n_ctx, rows // 4, q.shape[1]
    hidden = hid.shape[1]
    returned = PREFIX * width // 4 // COLS
    rounds = n_ctx.bit_length() + 1
    vm, hbm, sm = (pl.BlockSpec(memory_space=s) for s in (pltpu.VMEM, pl.ANY, pltpu.SMEM))
    bf, f4 = jnp.bfloat16, jnp.float32
    shape = jax.ShapeDtypeStruct
    return pl.pallas_call(
        functools.partial(back_kernel, lines, turned),
        out_shape=(
            shape((hidden, block_rows), f4),
            shape((block_rows, hidden), f4),
            shape((cols, block_rows), f4),
            shape((3, block_rows, cols), f4),
            shape((rows, width), bf),
            shape((rows, width), bf),
            shape((own, width), f4),
            shape((own, width), f4),
            shape(vec.shape, f4),
        ),
        in_specs=[hbm] * 13 + [vm] * 4 + [sm] * 3 + [vm] * 5,
        out_specs=[hbm] * 8 + [vm],
        scratch_shapes=Ring.scratch(lines, block_rows)
        + Quad.scratch(own + PREFIX // 4, width)
        + [
            pltpu.VMEM(h_all.shape, bf),
            pltpu.VMEM(h2.shape, bf),
            pltpu.VMEM((rows, hidden), bf),
            pltpu.VMEM((rows, hidden), bf),
            pltpu.VMEM(w1.shape, bf),
            pltpu.VMEM((own, width), f4),
            pltpu.VMEM((own, width), bf),
            pltpu.VMEM((rows, width), bf),
            pltpu.VMEM((rows, cols), bf),
            pltpu.VMEM((rows + PREFIX, 3 * cols), bf),
            pltpu.VMEM((returned, COLS), f4),
            pltpu.VMEM((returned, COLS), f4),
            pltpu.VMEM((rounds, *vec.shape), f4),
            pltpu.VMEM((rounds, *vec.shape), f4),
            pltpu.SemaphoreType.DMA((11,)),
            pltpu.SemaphoreType.DMA((2,)),
            pltpu.SemaphoreType.DMA((rounds,)),
            pltpu.SemaphoreType.DMA((rounds,)),
            pltpu.SemaphoreType.REGULAR,
        ],
        compiler_params=pltpu.CompilerParams(collective_id=2, has_side_effects=True, vmem_limit_bytes=63 * 2**20),
    )(g, h2, hid, dpre, w1, w_qkv, w2, w_out, h_all, att, mid, cot, x, act, gain1[None], gain2[None], ffn_bias[None],
      bias, weight, theirs, q, k, v, lse, vec)


def find_block(lengths, placed, block):
    mine, start, first = placed[block], 0, 0
    for s in range(lengths.shape[0]):
        first = jnp.where(start <= mine, start, first)
        start = start + lengths[s]
    owner = 0
    for e in range(placed.shape[0]):
        owner = owner + jnp.where(placed[e] == first, e, 0)
    return mine - first, jnp.minimum(owner, placed.shape[0] - 1)


def first_kernel(lines, *refs):
    (lengths, placed, layer, exits, x_hbm, w_hbm, gain, shift, qv_bias,
     q, k, v, h_all, act, bias, weight, theirs, *scratch) = refs
    x, w, line, x_send, x_recv, prefix, loads, s_l, s_r, r_z, s_x, r_x, s_g, r_g = scratch
    rows, width = x.shape
    part = prefix.shape[0] // 4
    ctx, tp = lax.axis_index("ctx"), lax.axis_index("tp")
    z, side, y, core = ctx // 2, lax.rem(ctx, 2), tp // 2, lax.rem(tp, 2)
    left, right, partner = (ctx - 2, tp), (ctx + 2, tp), (z * 2 + 1 - side, tp)
    across, over = (ctx, y * 2 + 1 - core), (ctx, (1 - y) * 2 + core)
    own = pl.ds(pl.multiple_of(tp * part, 16), part)
    copies = [
        pltpu.make_async_copy(x_hbm.at[own], line.at[z], loads.at[0]),
        pltpu.make_async_copy(x_hbm, x, loads.at[1]),
        pltpu.make_async_copy(w_hbm, w, loads.at[2]),
    ]
    for copy in copies:
        copy.start()
    meet([(None, partner), (z > 0, left), (z < lines - 1, right), (None, across), (None, over)])

    def hop(o, device, sems):
        return pltpu.make_async_remote_copy(
            src_ref=line.at[o], dst_ref=line.at[o], send_sem=sems.at[o], recv_sem=r_z.at[o],
            device_id=device, device_id_type=MESH)

    def pass_on(o, there, device, sems):
        @pl.when(there)
        def _():
            hop(o, device, sems).start()

    copies[0].wait()
    pass_on(z, z < lines - 1, right, s_r)
    pass_on(z, z > 0, left, s_l)

    def hops(d):
        @pl.when(z - d >= 0)
        def _():
            hop(z - d, left, s_l).wait_recv()
            pass_on(z - d, z < lines - 1, right, s_r)

        @pl.when(z + d < lines)
        def _():
            hop(z + d, right, s_r).wait_recv()
            pass_on(z + d, z > 0, left, s_l)

    my_part, my_owner = find_block(lengths, placed, ctx)
    partner_part, partner_owner = find_block(lengths, placed, z * 2 + 1 - side)
    bias[0, 0] = jnp.where(my_part > 0, 0.0, NEGATIVE)
    for e in range(weight.shape[0]):
        weight[e] = jnp.where((my_owner == e) & (my_part > 0), 1.0, 0.0)
        theirs[e] = jnp.where((partner_owner == e) & (partner_part > 0), 1.0, 0.0)
    row = lax.broadcasted_iota(jnp.int32, exits.shape, 0)
    first_rows = jnp.where(my_part == 0, PREFIX, 0)
    act[...] = jnp.where((exits[...] > layer[0]) | (row < first_rows), 1.0, 0.0)
    size = 64

    def norm_rows(source, start, to):
        def some(i, _):
            span = pl.ds(pl.multiple_of(start + i * size, size), size)
            values = source[span].astype(jnp.float32)
            target = pl.ds(pl.multiple_of(to + i * size, size), size)
            h_all[target] = (normed(values)[0] * gain[...] + shift[...]).astype(jnp.bfloat16)
            return 0

        lax.fori_loop(0, PREFIX // size, some, 0)

    def keys_of(span, rows_in):
        k[span] = nn(rows_in, w[1]).astype(jnp.bfloat16)
        v[span] = (nn(rows_in, w[2]) + qv_bias[1:2]).astype(jnp.bfloat16)

    for r in range(rows // PREFIX):
        norm_rows(x_wait(copies, r, x), r * PREFIX, (r + 1) * PREFIX)
        if r == 0:
            copies[2].wait()
        span = slice((r + 1) * PREFIX, (r + 2) * PREFIX)
        rows_in = h_all[span]
        low = (nn(rows_in, w[0]) + qv_bias[0:1]).astype(jnp.bfloat16)
        q[r * PREFIX : (r + 1) * PREFIX] = low * jnp.bfloat16(HEAD**-0.5)
        keys_of(span, rows_in)
        if r + 1 < lines:
            hops(r + 1)
    for d in range(rows // PREFIX + 1, lines):
        hops(d)
    x_send[...] = line[partner_owner // 2]
    trade = pltpu.make_async_remote_copy(
        src_ref=x_send, dst_ref=x_recv, send_sem=s_x, recv_sem=r_x, device_id=partner, device_id_type=MESH)
    trade.start()
    near = line[my_owner // 2]
    trade.wait_recv()
    prefix[own] = jnp.where(lax.rem(my_owner, 2) == side, near, x_recv[...])

    def give(n, quarter, device):
        span = pl.ds(pl.multiple_of(quarter * part, 16), part)
        return pltpu.make_async_remote_copy(
            src_ref=prefix.at[span], dst_ref=prefix.at[span], send_sem=s_g.at[n], recv_sem=r_g.at[n],
            device_id=device, device_id_type=MESH)

    far = (1 - y) * 2 + core
    give(0, tp, over).start()
    give(1, tp, across).start()
    give(0, far, over).wait_recv()
    give(2, far, across).start()
    give(1, y * 2 + 1 - core, across).wait_recv()
    give(2, (1 - y) * 2 + 1 - core, across).wait_recv()
    norm_rows(prefix, 0, 0)
    keys_of(slice(0, PREFIX), h_all[:PREFIX])
    trade.wait_send()
    give(0, tp, over).wait_send()
    give(1, tp, across).wait_send()
    give(2, far, across).wait_send()
    for o in range(lines):
        @pl.when((z < lines - 1) & (z >= o))
        def _():
            hop(o, right, s_r).wait_send()

        @pl.when((z > 0) & (z <= o))
        def _():
            hop(o, left, s_l).wait_send()


def x_wait(copies, r, x):
    if r == 0:
        copies[1].wait()
    return x


def first_call(n_ctx, lengths, placed, layer, exits, x, w_qkv, gain, shift, qv_bias):
    lines, (rows, width) = n_ctx // 2, x.shape
    cols = w_qkv.shape[2]
    vm, hbm, sm = (pl.BlockSpec(memory_space=s) for s in (pltpu.VMEM, pl.ANY, pltpu.SMEM))
    bf, f4 = jnp.bfloat16, jnp.float32
    return pl.pallas_call(
        functools.partial(first_kernel, lines),
        out_shape=(
            jax.ShapeDtypeStruct((rows, cols), bf),
            jax.ShapeDtypeStruct((rows + PREFIX, cols), bf),
            jax.ShapeDtypeStruct((rows + PREFIX, cols), bf),
            jax.ShapeDtypeStruct((rows + PREFIX, width), bf),
            jax.ShapeDtypeStruct((rows, 1), f4),
            jax.ShapeDtypeStruct((1, 1), f4),
            jax.ShapeDtypeStruct((n_ctx,), f4),
            jax.ShapeDtypeStruct((n_ctx,), f4),
        ),
        in_specs=[sm] * 3 + [vm] + [hbm] * 2 + [vm] * 3,
        out_specs=[vm] * 5 + [sm] * 3,
        scratch_shapes=[
            pltpu.VMEM((rows, width), bf),
            pltpu.VMEM(w_qkv.shape, bf),
            pltpu.VMEM((lines, PREFIX // 4, width), bf),
            pltpu.VMEM((PREFIX // 4, width), bf),
            pltpu.VMEM((PREFIX // 4, width), bf),
            pltpu.VMEM((PREFIX, width), bf),
            pltpu.SemaphoreType.DMA((3,)),
            pltpu.SemaphoreType.DMA((lines,)),
            pltpu.SemaphoreType.DMA((lines,)),
            pltpu.SemaphoreType.DMA((lines,)),
            pltpu.SemaphoreType.DMA,
            pltpu.SemaphoreType.DMA,
            pltpu.SemaphoreType.DMA((3,)),
            pltpu.SemaphoreType.DMA((3,)),
        ],
        compiler_params=pltpu.CompilerParams(collective_id=4, has_side_effects=True, vmem_limit_bytes=50 * 2**20),
    )(lengths, placed, layer, exits[:, None], x, w_qkv, gain[None], shift[None], qv_bias)


def body(
    mesh,
    block_input,
    cotangent,
    ln1_gain,
    ln1_bias,
    w_qkv,
    qv_bias,
    w_out,
    out_bias,
    ln2_gain,
    ln2_bias,
    w_fc1,
    fc1_bias,
    w_fc2,
    fc2_bias,
    exit_layer,
    layer_index,
    lengths,
    stretch_map,
):
    n_ctx = mesh.shape["ctx"]
    row_count, width = block_input.shape
    block_rows = width // n_ctx
    turned = block_rows % 128 != 0

    def tokens_last(array):
        return array.T if turned else array

    query, key, value, h_all, active, bias, weight, theirs = first_call(
        n_ctx, lengths, stretch_map, layer_index, exit_layer, block_input, w_qkv, ln1_gain, ln1_bias, qv_bias
    )
    attended, log_total = attend(bias, query, key, value)
    middle, h2_low = branch_call(attended, w_out, block_input, active, out_bias, ln2_gain, ln2_bias)
    grad_ffn = (active * cotangent.astype(jnp.float32)).astype(jnp.bfloat16)
    hidden_pre = nn(h2_low, w_fc1) + fc1_bias
    hidden_low = jax.nn.gelu(hidden_pre).astype(jnp.bfloat16)
    d_hidden = nt(grad_ffn, w_fc2)
    d_pre_low = jax.vjp(jax.nn.gelu, hidden_pre)[1](d_hidden)[0].astype(jnp.bfloat16)
    d_fc2_bias = jnp.sum(grad_ffn.astype(jnp.float32), axis=0) / lax.axis_size("tp")
    d_fc1_bias = jnp.sum(d_pre_low.astype(jnp.float32), axis=0)
    zero = jnp.zeros((width,), jnp.float32)
    vectors = jnp.stack([zero, zero, zero, zero, zero, d_fc2_bias, d_fc1_bias, zero])
    fc2_grad, fc1_grad, out_grad, qkv_grad, input_grad, output_rows, _, _, vectors = back_call(
        n_ctx, turned, tokens_last(grad_ffn), tokens_last(h2_low), hidden_low, d_pre_low, w_fc1, w_qkv, w_fc2, w_out,
        tokens_last(h_all), attended, middle, cotangent, block_input, active, ln1_gain, ln2_gain, fc2_bias,
        bias, weight, theirs, query, key, value, log_total, vectors,
    )
    qv_grad = vectors[7, : 2 * query.shape[1]].reshape(2, -1)
    return (
        output_rows,
        input_grad,
        vectors[0],
        vectors[1],
        qkv_grad,
        qv_grad,
        out_grad,
        vectors[2],
        vectors[3],
        vectors[4],
        fc1_grad,
        vectors[6],
        fc2_grad,
        vectors[5],
    )


def solution(mesh):
    in_specs = (
        P("ctx", None),
        P("ctx", None),
        P(),
        P(),
        P(None, None, "tp"),
        P(None, "tp"),
        P("tp", None),
        P(),
        P(),
        P(),
        P(None, "tp"),
        P("tp"),
        P("tp", None),
        P(),
        P("ctx"),
        P(),
        P(),
        P(),
    )
    out_specs = (
        P("ctx", None),
        P("ctx", None),
        P(),
        P(),
        P(None, "ctx", "tp"),
        P(None, "tp"),
        P("tp", "ctx"),
        P(),
        P(),
        P(),
        P("ctx", "tp"),
        P("tp"),
        P("tp", "ctx"),
        P(),
    )
    return jax.shard_map(functools.partial(body, mesh), mesh=mesh, in_specs=in_specs, out_specs=out_specs, check_vma=False)
```

```python
import functools
import math

import jax
import jax.numpy as jnp
from jax import lax
from jax.experimental import pallas as pl
from jax.experimental.pallas import tpu as pltpu
from jax.sharding import PartitionSpec as P

HEAD = 64
PREFIX = 256
COLS = 512
MESH = pl.DeviceIdType.MESH
NEGATIVE = -1e30
EPSILON = 1e-05
AHEAD = 8
SKEW = 2
STAGES = 2
DEPTH = 2


class Ring:
    def __init__(self, lines, groups, refs, outs, later=(), prefix=None):
        self.lines, self.groups, self.outs, self.later, self.prefix = lines, groups, outs, later, prefix
        (self.xs, self.xr, self.zb, self.stage, self.turned, self.kept, self.swap, self.s_xs, self.s_xr, self.s_zs,
         self.s_zr, self.s_out, self.s_swap, self.c_x, self.c_left, self.c_right) = refs
        self.jobs = sum(group[0] for group in groups)
        marks, job = [], 0
        for group in groups:
            marks += [job + n for n in range(group[0]) if group[2]]
            job += group[0]
        self.fetched = (marks[0], marks[-1]) if marks else (self.jobs, self.jobs)
        self.steps = self.jobs * lines
        self.slots = self.xr.shape[0]
        self.lag = SKEW * (lines - 1) + 2
        ctx, tp = lax.axis_index("ctx"), lax.axis_index("tp")
        self.z, self.side = ctx // 2, lax.rem(ctx, 2)
        self.partner = (self.z * 2 + 1 - self.side, tp)
        self.left, self.right = (ctx - 2, tp), (ctx + 2, tp)

    @staticmethod
    def scratch(lines, rows):
        slots = AHEAD + SKEW * (lines - 1) + 4
        chunk = (rows, COLS)
        return [
            pltpu.VMEM((AHEAD, *chunk), jnp.bfloat16),
            pltpu.VMEM((slots, *chunk), jnp.bfloat16),
            pltpu.VMEM((DEPTH, lines + 1, *chunk), jnp.bfloat16),
            pltpu.VMEM((STAGES, *chunk), jnp.float32),
            pltpu.VMEM((STAGES, COLS, rows), jnp.float32),
            pltpu.VMEM(chunk, jnp.bfloat16),
            pltpu.VMEM((4, *chunk), jnp.bfloat16),
            pltpu.SemaphoreType.DMA((AHEAD,)),
            pltpu.SemaphoreType.DMA((slots,)),
            pltpu.SemaphoreType.DMA((slots,)),
            pltpu.SemaphoreType.DMA((DEPTH, lines + 1)),
            pltpu.SemaphoreType.DMA((STAGES,)),
            pltpu.SemaphoreType.DMA((4,)),
            pltpu.SemaphoreType.REGULAR,
            pltpu.SemaphoreType.REGULAR,
            pltpu.SemaphoreType.REGULAR,
        ]

    def sends(self, f):
        job = f // self.lines
        found = (job < self.fetched[0]) | (job > self.fetched[1]) | (lax.rem(f, self.lines) == 0)
        for pair in self.later:
            found = found & (job != pair[0]) & (job != pair[1])
        return found

    def peers(self):
        return [(None, self.partner), (self.z > 0, self.left), (self.z < self.lines - 1, self.right)]

    def x_copy(self, f):
        slot, to = lax.rem(f, AHEAD), lax.rem(f, self.slots)
        return pltpu.make_async_remote_copy(
            src_ref=self.xs.at[slot], dst_ref=self.xr.at[to], send_sem=self.s_xs.at[slot],
            recv_sem=self.s_xr.at[to], device_id=self.partner, device_id_type=MESH)

    def z_copy(self, f, to, device):
        slot, level = lax.rem(f, self.slots), lax.rem(f // self.lines, DEPTH)
        return pltpu.make_async_remote_copy(
            src_ref=self.xr.at[slot], dst_ref=self.zb.at[level, to], send_sem=self.s_zs.at[slot],
            recv_sem=self.s_zr.at[level, to], device_id=device, device_id_type=MESH)

    def out_copies(self, job, act):
        slot = lax.rem(job, STAGES)
        for there, turn, place in self.outs(job):
            @pl.when(there)
            def _():
                source = self.turned if turn else self.stage
                act(pltpu.make_async_copy(source.at[slot], place, self.s_out.at[slot]))

    def out_start(self, job):
        slot = lax.rem(job, STAGES)
        for there, turn, _ in self.outs(job):
            if turn:
                @pl.when(there)
                def _():
                    self.turned[slot] = self.stage[slot].T
        self.out_copies(job, lambda copy: copy.start())

    def out_wait(self, job):
        self.out_copies(job, lambda copy: copy.wait())

    def swap_copy(self, n):
        return pltpu.make_async_remote_copy(
            src_ref=self.swap.at[2 * n], dst_ref=self.swap.at[2 * n + 1], send_sem=self.s_swap.at[2 * n],
            recv_sem=self.s_swap.at[2 * n + 1], device_id=self.partner, device_id_type=MESH)

    def send(self, f, group, job0, fresh):
        _, part, is_prefix = group
        if not fresh:
            @pl.when(self.sends(f - AHEAD))
            def _():
                self.x_copy(f).wait_send()

            @pl.when(f >= self.slots)
            def _():
                pl.semaphore_wait(self.c_x, 1)

        @pl.when(self.sends(f))
        def _():
            owner = lax.rem(f, self.lines)
            value = part(f // self.lines - job0, None if is_prefix else owner * 2 + 1 - self.side)
            self.xs[lax.rem(f, AHEAD)] = value.astype(jnp.bfloat16)
            self.x_copy(f).start()

    def receive(self, f, group, job0):
        _, part, is_prefix = group
        job, owner, slot = f // self.lines, lax.rem(f, self.lines), lax.rem(f, self.slots)
        came = self.sends(f)

        @pl.when(came)
        def _():
            self.x_copy(f).wait_recv()
            if is_prefix:
                self.kept[...] = self.xr[slot]

        block = owner * 2 + self.side
        if is_prefix:
            mine, theirs = self.prefix[0][block], self.prefix[1][block]
            total = part(job - job0, None) * mine + self.kept[...].astype(jnp.float32) * theirs
        else:
            @pl.when(jnp.logical_not(came))
            def _():
                self.xr[slot] = jnp.zeros(self.xr.shape[1:], jnp.bfloat16)

            for pair in self.later:
                block = jnp.where(job == pair[0], owner * 2 + 1 - self.side, block)
            total = part(job - job0, block) + self.xr[slot].astype(jnp.float32)

        @pl.when(owner != self.z)
        def _():
            self.xr[slot] = total.astype(jnp.bfloat16)

        @pl.when(owner == self.z)
        def _():
            @pl.when(job >= STAGES)
            def _():
                self.out_wait(job - STAGES)
            self.stage[lax.rem(job, STAGES)] = total

    def add(self, f, index):
        job = f // self.lines
        slot, level = lax.rem(f, self.slots), lax.rem(job, DEPTH)

        @pl.when(lax.rem(f, self.lines) == self.z)
        def _():
            self.stage[lax.rem(job, STAGES)] += self.zb[level, index].astype(jnp.float32)

        @pl.when(lax.rem(f, self.lines) != self.z)
        def _():
            self.xr[slot] = (self.xr[slot].astype(jnp.float32) + self.zb[level, index].astype(jnp.float32)).astype(jnp.bfloat16)

    def flow(self, t):
        lines, z = self.lines, self.z
        f = t - SKEW * z
        owner = lax.rem(f + lines * SKEW * lines, lines)

        @pl.when((f >= 0) & (f < self.steps) & (owner >= z))
        def _():
            @pl.when(z > 0)
            def _():
                self.z_copy(f, owner, self.left).wait_recv()
                self.add(f, owner)
                pl.semaphore_signal(self.c_right, inc=1, device_id=self.left, device_id_type=MESH)

            @pl.when(owner > z)
            def _():
                @pl.when(f >= DEPTH * lines)
                def _():
                    pl.semaphore_wait(self.c_right, 1)
                self.z_copy(f, owner, self.right).start()

        g = t - SKEW * (lines - 1 - z)
        owner2 = lax.rem(g + lines * SKEW * lines, lines)

        @pl.when((g >= 0) & (g < self.steps) & (owner2 <= z))
        def _():
            @pl.when(z < lines - 1)
            def _():
                index = jnp.where(owner2 == z, lines, owner2)
                self.z_copy(g, index, self.right).wait_recv()
                self.add(g, index)
                pl.semaphore_signal(self.c_left, inc=1, device_id=self.right, device_id_type=MESH)

            @pl.when(owner2 < z)
            def _():
                @pl.when(g >= DEPTH * lines)
                def _():
                    pl.semaphore_wait(self.c_left, 1)
                self.z_copy(g, jnp.where(owner2 == z - 1, lines, owner2), self.left).start()

        h = t - SKEW * (lines - 1)

        @pl.when((h >= 0) & (h < self.steps) & (lax.rem(h + lines * SKEW * lines, lines) == z))
        def _():
            job = h // lines
            stage = lax.rem(job, STAGES)
            for n, pair in enumerate(self.later):
                @pl.when(job == pair[0])
                def _():
                    self.swap[2 * n] = self.stage[stage].astype(jnp.bfloat16)
                    self.swap_copy(n).start()

                @pl.when(job == pair[1])
                def _():
                    self.swap_copy(n).wait()
                    self.stage[stage] += self.swap[2 * n + 1].astype(jnp.float32)
            if self.prefix is not None:
                target, rows = self.prefix[2], self.stage.shape[1]

                @pl.when((job >= self.fetched[0]) & (job <= self.fetched[1]))
                def _():
                    span = pl.ds(pl.multiple_of((job - self.fetched[0]) * rows, rows), rows)
                    target[span] = self.stage[stage]
            self.out_start(job)

        d = t - self.lag

        @pl.when((d >= 0) & (d < self.steps))
        def _():
            @pl.when(lax.rem(d + lines * (SKEW * lines + 2), lines) != z)
            def _():
                self.z_copy(d, 0, self.left).wait_send()
            pl.semaphore_signal(self.c_x, inc=1, device_id=self.partner, device_id_type=MESH)

    def find(self, f):
        job = 0
        for group in self.groups:
            if f < (job + group[0]) * self.lines:
                return group, job
            job += group[0]
        return None

    def pieces(self, lo, hi):
        cuts, job = {lo, hi}, 0
        for group in self.groups:
            job += group[0]
            cuts |= {job * self.lines, job * self.lines - AHEAD}
        cuts = sorted(c for c in cuts if lo <= c <= hi)
        return zip(cuts[:-1], cuts[1:])

    def start(self):
        for lo, hi in self.pieces(0, AHEAD):
            here = self.find(lo)
            lax.fori_loop(lo, hi, lambda f, _, here=here: (self.send(f, *here, True), 0)[1], 0)

    def run(self, lo, hi):
        for a, b in self.pieces(lo, min(hi, self.steps)):
            here, ahead = self.find(a), self.find(a + AHEAD)

            def body(f, _, here=here, ahead=ahead):
                self.receive(f, *here)
                self.flow(f)
                if ahead is not None:
                    self.send(f + AHEAD, *ahead, False)
                return 0

            lax.fori_loop(a, b, body, 0)
        if hi > self.steps:
            lax.fori_loop(max(lo, self.steps), hi, lambda t, _: (self.flow(t), 0)[1], 0)

    def run_some(self, lo, count):
        here = self.find(0)

        def body(f, _):
            self.receive(f, *here)
            self.flow(f)

            @pl.when(f + AHEAD < self.steps)
            def _():
                self.send(f + AHEAD, *here, False)
            return 0

        lax.fori_loop(lo, lo + count, body, 0)

    def finish(self, lo):
        lines, z = self.lines, self.z
        self.run(lo, self.steps + self.lag)

        def drain(f, _):
            @pl.when(self.sends(f))
            def _():
                self.x_copy(f).wait_send()
            return 0

        lax.fori_loop(self.steps - AHEAD, self.steps, drain, 0)
        for job in range(self.jobs - STAGES, self.jobs):
            self.out_wait(job)
        pl.semaphore_wait(self.c_x, min(self.slots, self.steps))

        @pl.when(z < lines - 1)
        def _():
            pl.semaphore_wait(self.c_right, DEPTH * (lines - 1 - z))

        @pl.when(z > 0)
        def _():
            pl.semaphore_wait(self.c_left, DEPTH * z)


def meet(peers):
    barrier = pltpu.get_barrier_semaphore()
    count = 0
    for there, device in peers:
        if there is None:
            pl.semaphore_signal(barrier, inc=1, device_id=device, device_id_type=MESH)
            count += 1
        else:
            @pl.when(there)
            def _():
                pl.semaphore_signal(barrier, inc=1, device_id=device, device_id_type=MESH)
            count += jnp.where(there, 1, 0)
    pl.semaphore_wait(barrier, count)
class Quad:
    def __init__(self, refs, rows, height):
        (self.tmp, self.cs, self.cr, self.ys, self.yr, self.acc, self.s_c, self.r_c, self.s_y, self.r_y,
         self.s_g, self.r_g) = refs
        ctx, tp = lax.axis_index("ctx"), lax.axis_index("tp")
        self.y, self.core, self.tp = tp // 2, lax.rem(tp, 2), tp
        self.across = (ctx, self.y * 2 + 1 - self.core)
        self.over = (ctx, (1 - self.y) * 2 + self.core)
        self.head, self.rest = PREFIX // 4, (rows - PREFIX) // 4
        self.tiles = self.cs.shape[1]
        self.height = height

    @staticmethod
    def scratch(rows, width):
        tiles = width // COLS
        return [
            pltpu.VMEM((2, rows, COLS), jnp.float32),
            pltpu.VMEM((2, tiles, rows, COLS), jnp.bfloat16),
            pltpu.VMEM((2, tiles, rows, COLS), jnp.bfloat16),
            pltpu.VMEM((tiles, rows, COLS), jnp.bfloat16),
            pltpu.VMEM((tiles, rows, COLS), jnp.bfloat16),
            pltpu.VMEM((rows, width), jnp.float32),
            pltpu.SemaphoreType.DMA((2, tiles)),
            pltpu.SemaphoreType.DMA((2, tiles)),
            pltpu.SemaphoreType.DMA((tiles,)),
            pltpu.SemaphoreType.DMA((tiles,)),
            pltpu.SemaphoreType.DMA((2, 3, 2)),
            pltpu.SemaphoreType.DMA((2, 3, 2)),
        ]

    def peers(self):
        return [(None, self.across), (None, self.over)]

    def spans(self, quarter):
        return [
            pl.ds(pl.multiple_of(quarter * self.head, 16), self.head),
            pl.ds(pl.multiple_of(PREFIX + quarter * self.rest, 16), self.rest),
        ]

    def rows_of(self, ref, quarter):
        return jnp.concatenate([ref[span] for span in self.spans(quarter)], axis=0)

    def half_of(self, ref, half):
        return jnp.concatenate([self.rows_of(ref, half * 2), self.rows_of(ref, half * 2 + 1)], axis=0)

    def c_copy(self, k, n):
        return pltpu.make_async_remote_copy(
            src_ref=self.cs.at[k, n, : self.height], dst_ref=self.cr.at[k, n, : self.height], send_sem=self.s_c.at[k, n],
            recv_sem=self.r_c.at[k, n], device_id=self.across, device_id_type=MESH)

    def y_copy(self, n):
        return pltpu.make_async_remote_copy(
            src_ref=self.ys.at[n, : self.height], dst_ref=self.yr.at[n, : self.height], send_sem=self.s_y.at[n],
            recv_sem=self.r_y.at[n], device_id=self.over, device_id_type=MESH)

    def columns(self, n):
        return pl.ds(pl.multiple_of(n * COLS, COLS), COLS)

    def split(self, value, k, n):
        rows = self.height
        self.tmp[0, :rows] = value[:rows]
        self.tmp[1, :rows] = value[rows:]
        self.cs[k, n, :rows] = self.tmp[1 - self.core, :rows].astype(jnp.bfloat16)
        self.c_copy(k, n).start()
        self.acc[:rows, self.columns(n)] = self.tmp[self.core, :rows]

    def relay(self, n):
        self.c_copy(0, n).wait_recv()
        rows = self.height
        total = self.acc[:rows, self.columns(n)] + self.cr[0, n, :rows].astype(jnp.float32)
        self.ys[n, :rows] = total.astype(jnp.bfloat16)
        self.y_copy(n).start()

    def scatter_send(self, chunk):
        def far(n, _):
            self.split(chunk(1 - self.y, n), 0, n)

            @pl.when(n > 0)
            def _():
                self.relay(n - 1)
            return 0

        lax.fori_loop(0, self.tiles, far, 0)
        self.relay(self.tiles - 1)

        def near(n, _):
            self.split(chunk(self.y, n), 1, n)
            return 0

        lax.fori_loop(0, self.tiles, near, 0)

    def scatter_add(self, n):
        self.c_copy(1, n).wait_recv()
        self.y_copy(n).wait_recv()
        rows = self.height
        came = self.cr[1, n, :rows].astype(jnp.float32) + self.yr[n, :rows].astype(jnp.float32)
        self.acc[:rows, self.columns(n)] += came

    def scatter_done(self):
        for n in range(self.tiles):
            self.c_copy(0, n).wait_send()
            self.c_copy(1, n).wait_send()
            self.y_copy(n).wait_send()

    def g_copy(self, full, k, s, quarter, device, turn):
        span = self.spans(quarter)[s]
        return pltpu.make_async_remote_copy(
            src_ref=full.at[span], dst_ref=full.at[span], send_sem=self.s_g.at[turn, k, s],
            recv_sem=self.r_g.at[turn, k, s], device_id=device, device_id_type=MESH)

    def gather_send(self, full, turn=0):
        for s in range(2):
            self.g_copy(full, 0, s, self.tp, self.over, turn).start()
        for s in range(2):
            self.g_copy(full, 1, s, self.tp, self.across, turn).start()

    def gather_near(self, full, turn=0):
        for s in range(2):
            self.g_copy(full, 1, s, self.y * 2 + 1 - self.core, self.across, turn).wait_recv()

    def gather_pass(self, full, turn=0):
        other = (1 - self.y) * 2 + self.core
        for s in range(2):
            self.g_copy(full, 0, s, other, self.over, turn).wait_recv()
            self.g_copy(full, 2, s, other, self.across, turn).start()

    def gather_far(self, full, turn=0):
        for s in range(2):
            self.g_copy(full, 2, s, (1 - self.y) * 2 + 1 - self.core, self.across, turn).wait_recv()

    def gather_done(self, full, turn=0):
        other = (1 - self.y) * 2 + self.core
        for s in range(2):
            self.g_copy(full, 0, s, self.tp, self.over, turn).wait_send()
            self.g_copy(full, 1, s, self.tp, self.across, turn).wait_send()
            self.g_copy(full, 2, s, other, self.across, turn).wait_send()


def nt(left, right):
    return lax.dot_general(left, right, (((1,), (1,)), ((), ())), preferred_element_type=jnp.float32)


def normed(values_in):
    centred = values_in - jnp.mean(values_in, axis=1, keepdims=True)
    scale = lax.rsqrt(jnp.mean(centred * centred, axis=1, keepdims=True) + EPSILON)
    return centred * scale, scale


def gelu_pair(pre):
    slope = (2.0 / math.pi) ** 0.5
    square = pre * pre
    bent = jnp.tanh(slope * (pre + 0.044715 * (square * pre)))
    half = 0.5 * (1.0 + bent)
    return pre * half, half + 0.5 * pre * (1.0 - bent * bent) * (slope * (1.0 + 3 * 0.044715 * square))


def column_sum(values_in):
    return jnp.sum(values_in, axis=0, keepdims=True)


def front_kernel(*refs):
    (att, w_out, x_hbm, cot_hbm, act, w1_hbm, w2_hbm, bias, gain, shift, fc1_bias,
     mid, full, grad, hid, d_pre, vec, *scratch) = refs
    quad_refs, scratch = scratch[:12], scratch[12:]
    x, w1, w2, d_hid, some, loads = scratch
    rows, width = full.shape
    quad = Quad(quad_refs, rows, rows // 4)
    spans = quad.spans(quad.tp)

    def load(n, source, target):
        copy = pltpu.make_async_copy(source, target, loads.at[n])
        copy.start()
        return copy

    cot_copy = load(0, cot_hbm, grad)
    w2_copy = load(1, w2_hbm, w2)
    x_copies = [load(2, x_hbm.at[spans[0]], x.at[: quad.head]), load(3, x_hbm.at[spans[1]], x.at[quad.head :])]
    w1_copy = load(4, w1_hbm, w1)
    meet(quad.peers())
    quad.scatter_send(lambda half, n: jnp.dot(quad.half_of(att, half), w_out[:, quad.columns(n)], preferred_element_type=jnp.float32))
    cot_copy.wait()
    vec[...] = jnp.zeros(vec.shape, jnp.float32)
    size = 32

    def gate(i, _):
        span = pl.ds(pl.multiple_of(i * size, size), size)
        low = (act[span] * grad[span].astype(jnp.float32)).astype(jnp.bfloat16)
        grad[span] = low
        vec[5:6] += column_sum(low.astype(jnp.float32)) * 0.25
        return 0

    lax.fori_loop(0, rows // size, gate, 0)
    w2_copy.wait()
    tiles = hid.shape[1] // COLS

    def d_hidden(n, _):
        d_hid[:, quad.columns(n)] = nt(grad[...], w2[quad.columns(n), :])
        return 0

    lax.fori_loop(0, tiles, d_hidden, 0)
    for copy in x_copies:
        copy.wait()
    lax.fori_loop(0, quad.tiles, lambda n, _: (quad.scatter_add(n), 0)[1], 0)

    def norm_rows(i, _):
        first = quad.head // size
        start = jnp.where(i < first, quad.tp * quad.head + i * size, PREFIX + quad.tp * quad.rest + (i - first) * size)
        whole, own = (pl.ds(pl.multiple_of(s, size), size) for s in (start, i * size))
        middle = x[own].astype(jnp.float32) + act[whole] * (quad.acc[own] + bias[...])
        mid[own] = middle
        full[whole] = (normed(middle)[0] * gain[...] + shift[...]).astype(jnp.bfloat16)
        return 0

    lax.fori_loop(0, quad.height // size, norm_rows, 0)
    quad.gather_send(full)

    def ffn(half):
        some[...] = quad.half_of(full, half)
        places = quad.spans(half * 2) + quad.spans(half * 2 + 1)

        def tile(n, _):
            cols = quad.columns(n)
            pre = jnp.dot(some[...], w1[:, cols], preferred_element_type=jnp.float32) + fc1_bias[:, cols]
            value, slope = gelu_pair(pre)
            value = value.astype(jnp.bfloat16)
            start = 0
            for place in places:
                end = start + place.size
                hid[place, cols] = value[start:end]
                change = (d_hid[place, cols] * slope[start:end]).astype(jnp.bfloat16)
                d_pre[place, cols] = change
                vec[6:7, cols] += column_sum(change.astype(jnp.float32))
                start = end
            return 0

        lax.fori_loop(0, tiles, tile, 0)

    quad.gather_near(full)
    w1_copy.wait()
    ffn(quad.y)
    quad.gather_pass(full)
    quad.gather_far(full)
    ffn(1 - quad.y)
    quad.gather_done(full)
    quad.scatter_done()


def front_call(att, w_out, x, cot, act, w1, w2, bias, gain, shift, fc1_bias):
    rows, width = x.shape
    own, hidden = rows // 4, w1.shape[1]
    vm, hbm = (pl.BlockSpec(memory_space=s) for s in (pltpu.VMEM, pl.ANY))
    bf, f4, shape = jnp.bfloat16, jnp.float32, jax.ShapeDtypeStruct
    return pl.pallas_call(
        front_kernel,
        out_shape=(
            shape((own, width), f4),
            shape((rows, width), bf),
            shape((rows, width), bf),
            shape((rows, hidden), bf),
            shape((rows, hidden), bf),
            shape((8, width), f4),
        ),
        in_specs=[vm] * 2 + [hbm] * 2 + [vm] + [hbm] * 2 + [vm] * 4,
        out_specs=[vm] * 6,
        scratch_shapes=Quad.scratch(own, width)
        + [
            pltpu.VMEM((own, width), bf),
            pltpu.VMEM(w1.shape, bf),
            pltpu.VMEM(w2.shape, bf),
            pltpu.VMEM((rows, hidden), f4),
            pltpu.VMEM((2 * own, width), bf),
            pltpu.SemaphoreType.DMA((5,)),
        ],
        compiler_params=pltpu.CompilerParams(collective_id=1, has_side_effects=True, vmem_limit_bytes=62 * 2**20),
    )(att, w_out, x, cot, act, w1, w2, bias[None], gain[None], shift[None], fc1_bias[None])
def tn(left, right):
    return lax.dot_general(left, right, (((0,), (0,)), ((), ())), preferred_element_type=jnp.float32)


def nn(left, right):
    return jnp.dot(left, right, preferred_element_type=jnp.float32)


def lane_mask(rows, head):
    lane = lax.broadcasted_iota(jnp.int32, (rows, 2 * HEAD), 1)
    return (lane < HEAD) if head == 0 else (lane >= HEAD)


def scores_of(keys, query, bias):
    scores = nt(keys, query)
    count = scores.shape[0]
    row = lax.broadcasted_iota(jnp.int32, (PREFIX, PREFIX), 0)
    col = lax.broadcasted_iota(jnp.int32, (PREFIX, PREFIX), 1)
    parts = [scores[:PREFIX] + bias]
    if count > 2 * PREFIX:
        parts.append(scores[PREFIX : count - PREFIX])
    parts.append(jnp.where(row <= col, scores[count - PREFIX :], NEGATIVE))
    return jnp.concatenate(parts, axis=0)


def attend_back(p, bias, q_ref, k_ref, v_ref, l_ref, g_ref, d_ref, room):
    rows, width = q_ref.shape
    blocks = rows // PREFIX
    base = pl.multiple_of(p * 2 * HEAD, 2 * HEAD)
    lanes = pl.ds(base, 2 * HEAD)
    sums = jnp.zeros((1, 2 * HEAD), jnp.float32)
    for r in reversed(range(blocks)):
        count, own = (r + 2) * PREFIX, slice(r * PREFIX, (r + 1) * PREFIX)
        query, grad, keys, values = q_ref[own, lanes], g_ref[own, lanes], k_ref[:count, lanes], v_ref[:count, lanes]
        d_queries, d_keys, d_values = [], None, None
        for e in range(2):
            mask = lane_mask(PREFIX, e)
            query_e = jnp.where(mask, query, jnp.zeros_like(query))
            grad_e = jnp.where(mask, grad, jnp.zeros_like(grad))
            probs = jnp.exp(scores_of(keys, query_e, bias) - l_ref[p, e : e + 1, own])
            d_probs = nt(values, grad_e)
            inner = jnp.sum(probs * d_probs, axis=0, keepdims=True)
            d_scores = (probs * (d_probs - inner)).astype(jnp.bfloat16)
            keys_e, values_e = nn(d_scores, query_e), nn(probs.astype(jnp.bfloat16), grad_e)
            d_keys = keys_e if d_keys is None else d_keys + keys_e
            d_values = values_e if d_values is None else d_values + values_e
            d_queries.append(tn(d_scores, keys))
        d_query = jnp.where(lane_mask(PREFIX, 0), d_queries[0], d_queries[1]) * HEAD ** (-0.5)
        sums += jnp.sum(d_query, axis=0, keepdims=True)
        d_ref[(r + 1) * PREFIX : (r + 2) * PREFIX, lanes] = d_query.astype(jnp.bfloat16)
        for n in range(r + 2):
            for at, sums_of in ((n, d_keys), (blocks + 1 + n, d_values)):
                place, term = slice(at * 2 * HEAD, (at + 1) * 2 * HEAD), sums_of[n * PREFIX : (n + 1) * PREFIX]
                if r == blocks - 1:
                    room[:PREFIX, place] = term
                else:
                    room[:PREFIX, place] += term
    d_ref[:PREFIX, lanes] = jnp.zeros((PREFIX, 2 * HEAD), jnp.bfloat16)
    value_sums = jnp.zeros((1, 2 * HEAD), jnp.float32)
    for n in range(blocks + 1):
        span = slice(n * PREFIX, (n + 1) * PREFIX)
        for m, at in ((1, n), (2, blocks + 1 + n)):
            total = room[:PREFIX, at * 2 * HEAD : (at + 1) * 2 * HEAD]
            d_ref[span, pl.ds(pl.multiple_of(base + m * width, 2 * HEAD), 2 * HEAD)] = total.astype(jnp.bfloat16)
            if m == 2:
                value_sums += column_sum(total)
    return sums, value_sums


def own_block(quad, i, size):
    first = quad.head // size
    start = jnp.where(i < first, quad.tp * quad.head + i * size, PREFIX + quad.tp * quad.rest + (i - first) * size)
    return pl.ds(pl.multiple_of(start, size), size), pl.ds(pl.multiple_of(i * size, size), size)


def norm_back(grad, source, gain):
    unit, scale = normed(source)
    scaled = grad * gain
    mean = jnp.mean(scaled, axis=1, keepdims=True)
    slope = jnp.mean(scaled * unit, axis=1, keepdims=True)
    return scale * (scaled - mean - unit * slope), grad * unit


def product_part(left, right, tile, turned, rows):
    def part(j, block):
        cols = pl.ds(pl.multiple_of(tile(j) * COLS, COLS), COLS)
        span = pl.ds(pl.multiple_of(block * rows, rows), rows)
        if turned:
            return nn(left[span, :], right[:, cols])
        return tn(left[:, span], right[:, cols])

    return part


def pick(table, j):
    found = table[0]
    for n, entry in enumerate(table[1:]):
        found = jnp.where(j == n + 1, entry, found)
    return found


class Wide(Quad):
    def rows_of(self, ref, quarter):
        own = [pl.ds(pl.multiple_of(span.start + PREFIX, 16), span.size) for span in self.spans(quarter)]
        return jnp.concatenate([ref[span] for span in [self.spans(quarter)[0]] + own], axis=0)


def back_kernel(lines, turned, *refs):
    (g_hbm, h2_hbm, hid_hbm, dpre_hbm, w1_hbm, w_qkv_hbm, w2_hbm, wo_hbm, h_hbm, att_hbm, mid_hbm, cot_hbm, x_hbm,
     act, gain1, gain2, ffn_bias, bias, weight, theirs, q, k, v, lse, vec_in,
     fc2_out, fc1_out, out_grad, qkv_grad, in_hbm, act_hbm, dmid_hbm, dh_hbm, vec, *scratch) = refs
    ring_refs, scratch = scratch[:16], scratch[16:]
    quad_refs, scratch = scratch[:12], scratch[12:]
    (x0, x1, y0, y1, weights, mid, own_in, full, d_att, d_all, fresh, back, v_send, v_recv, loads, stores, s_v, r_v,
     c_over) = scratch
    rows, width = full.shape
    quad, wide = Quad(quad_refs, rows, rows // 4), Wide(quad_refs, rows, (rows + PREFIX) // 4)
    own_rows, depth = quad.height, q.shape[1]
    tiles, cols = y0.shape[1] // COLS, depth // COLS
    block_rows = ring_refs[0].shape[1]
    extra = fresh.shape[0] // block_rows
    order2 = [tiles - 1, *range(tiles - 1), tiles - 1]
    order1 = [*range(tiles - 2), tiles - 1, tiles - 2, tiles - 1]
    half = tiles + 1
    later = ((0, tiles), (half + tiles - 2, half + tiles))
    base = 2 * half + extra
    g_part = x0.at[:, :rows] if turned else x0.at[:rows]
    columns = lambda n: pl.ds(pl.multiple_of(n * COLS, COLS), COLS)

    def prefix_part(j, block):
        return fresh[pl.ds(pl.multiple_of(j * block_rows, block_rows), block_rows)]

    def outs(job):
        local = job - half
        head = jnp.maximum(job - base - cols, 0)
        place2, place1 = columns(pick(order2, job)), columns(pick(order1, local))
        is2 = (job < half) & (job != later[0][0])
        is1 = (job >= half) & (job < 2 * half) & (job != later[1][0])
        is_out = (job >= base) & (job < base + cols)
        out_span = columns(jnp.clip(job - base, 0, cols - 1))
        return [
            (is2, True, fc2_out.at[place2]),
            (is1, False, fc1_out.at[:, place1]),
            (is_out, True, out_grad.at[out_span]),
            (job >= base + cols, False, qkv_grad.at[head // cols, :, columns(lax.rem(head, cols))]),
        ]

    groups = [
        (half, product_part(g_part, y0, lambda j: pick(order2, j), turned, block_rows), False),
        (half, product_part(x1, y1, lambda j: pick(order1, j), turned, block_rows), False),
        (extra, prefix_part, True),
        (cols, product_part(x1 if turned else full, d_att, lambda j: j, turned, block_rows), False),
        (3 * cols, product_part(x0, d_all, lambda j: j, turned, block_rows), False),
    ]
    ring = Ring(lines, groups, ring_refs, outs, later, (weight, theirs, back))

    def load(n, source, target):
        return pltpu.make_async_copy(source, target, loads.at[n])

    def store(n, source, target):
        return pltpu.make_async_copy(source, target, stores.at[n])

    def begin(*copies):
        for copy in copies:
            copy.start()

    def end(*copies):
        for copy in copies:
            copy.wait()

    spans = quad.spans(quad.tp)
    first = [load(0, hid_hbm, y0), load(1, g_hbm, g_part)]
    second = [load(2, dpre_hbm, y1), load(3, w1_hbm, weights)]
    third = [
        load(4, h2_hbm, x1),
        load(5, mid_hbm, mid),
        load(6, cot_hbm.at[spans[0]], own_in.at[: quad.head]),
        load(7, cot_hbm.at[spans[1]], own_in.at[quad.head :]),
    ]
    begin(*first, *second, *third)
    ctx, tp = lax.axis_index("ctx"), lax.axis_index("tp")
    swaps, bit = [quad.across, quad.over], 1
    while bit < 2 * lines:
        swaps.append((ctx + bit - 2 * bit * lax.rem(ctx // bit, 2), tp))
        bit *= 2
    meet(ring.peers() + quad.peers() + [(None, device) for device in swaps[4:]])

    def swap(n):
        return pltpu.make_async_remote_copy(
            src_ref=v_send.at[n], dst_ref=v_recv.at[n], send_sem=s_v.at[n], recv_sem=r_v.at[n],
            device_id=swaps[n], device_id_type=MESH)

    def swap_start(n):
        v_send[n] = vec[...]
        swap(n).start()

    def swap_end(n):
        swap(n).wait()
        if n < 2:
            vec[:6] += v_recv[n, :6]
        else:
            vec[...] += v_recv[n]

    def add_all(group):
        lax.fori_loop(0, group.tiles, lambda n, _: (group.scatter_add(n), 0)[1], 0)

    end(*first)
    ring.start()
    end(*second)
    quad.scatter_send(lambda part, n: nt(quad.half_of(y1, part), weights[quad.columns(n), :]))
    wo_copy = load(3, wo_hbm, weights.at[:depth])
    wo_copy.start()
    end(*third)
    ring.run(0, 2)
    add_all(quad)
    vec[...] = vec_in[...]
    size = 32

    def middle_rows(i, _):
        whole, own = own_block(quad, i, size)
        grad = quad.acc[own]
        change, gain_terms = norm_back(grad, mid[own], gain2[...])
        d_middle = own_in[own].astype(jnp.float32) + change
        quad.acc[own] = d_middle
        low = (act[whole] * d_middle).astype(jnp.bfloat16)
        full[whole] = low
        vec[2:3] += column_sum(low.astype(jnp.float32))
        vec[3:4] += column_sum(gain_terms)
        vec[4:5] += column_sum(grad)
        return 0

    lax.fori_loop(0, own_rows // size, middle_rows, 0)
    quad.gather_send(full)
    keep = store(0, quad.acc.at[:own_rows], dmid_hbm)
    x_copies = [load(6, x_hbm.at[spans[0]], own_in.at[: quad.head]), load(7, x_hbm.at[spans[1]], own_in.at[quad.head :])]
    begin(keep, *x_copies)
    ring.run(2, 4)
    quad.gather_near(full)
    quad.gather_pass(full)
    quad.gather_far(full)
    wo_copy.wait()

    def attended_rows(i, _):
        span = pl.ds(pl.multiple_of(i * PREFIX, PREFIX), PREFIX)
        d_att[span] = nt(full[span], weights[:depth, :]).astype(jnp.bfloat16)
        return 0

    lax.fori_loop(0, rows // PREFIX, attended_rows, 0)
    heads = [load(8 + m, w_qkv_hbm.at[m], weights.at[:, m * depth : (m + 1) * depth]) for m in range(3)]
    begin(*heads)
    keep.wait()
    pairs = depth // (2 * HEAD)

    def pair(p, _):
        sums, value_sums = attend_back(p, bias[0, 0], q, k, v, lse, d_att, d_all, quad.acc)
        start = pl.multiple_of(p * 2 * HEAD, 2 * HEAD)
        vec[7:8, pl.ds(start, 2 * HEAD)] = sums
        vec[7:8, pl.ds(pl.multiple_of(start + depth, 2 * HEAD), 2 * HEAD)] = value_sums
        ring.run_some(4 + 2 * p, 2)
        return 0

    lax.fori_loop(0, pairs, pair, 0)
    now = 4 + 2 * pairs
    att_copy = load(2, att_hbm, d_att)
    att_copy.start()
    quad.gather_done(full)
    quad.scatter_done()
    end(*heads)
    wide.scatter_send(lambda part, n: nt(wide.half_of(d_all, part), weights[wide.columns(n), : 3 * depth]))
    w2_copy = load(3, w2_hbm, weights)
    w2_copy.start()
    ring.run(now, now + 4)
    add_all(wide)
    pl.semaphore_signal(c_over, inc=1, device_id=quad.over, device_id_type=MESH)
    for n in range(wide.tiles):
        fresh[n * wide.head : (n + 1) * wide.head] = wide.acc[: wide.head, n * COLS : (n + 1) * COLS]
    dh_copy = store(1, wide.acc.at[pl.ds(wide.head, own_rows)], dh_hbm)
    dh_copy.start()
    free0, free1 = half * lines, 2 * half * lines
    ring.run(now + 4, free0)
    h_copy = load(1, h_hbm, x0)
    h_copy.start()
    att_copy.wait()
    ring.run(free0, free1 - AHEAD)
    h_copy.wait()
    ring.run(free1 - AHEAD, free1)
    if turned:

        def flip(n, _):
            x1[columns(n), :] = full[:, columns(n)].T
            return 0

        lax.fori_loop(0, width // COLS, flip, 0)
    wide.scatter_done()
    end(dh_copy, w2_copy)
    pl.semaphore_wait(c_over, 1)
    quad.scatter_send(lambda part, n: nn(quad.half_of(y0, part), weights[:, quad.columns(n)]))
    ring.run(free1, free1 + lines)
    add_all(quad)

    def out_rows(i, _):
        whole, own = own_block(quad, i, size)
        y1[whole] = (mid[own] + act[whole] * (quad.acc[own] + ffn_bias[...])).astype(jnp.bfloat16)
        return 0

    lax.fori_loop(0, own_rows // size, out_rows, 0)
    quad.gather_send(y1)
    again = [load(4, dh_hbm, quad.acc.at[:own_rows]), load(5, dmid_hbm, mid)]
    begin(*again)
    ready = base * lines + SKEW * (lines - 1)
    ring.run(free1 + lines, ready)
    quad.gather_near(y1)
    quad.gather_pass(y1)
    quad.gather_far(y1)
    act_copy = store(0, y1, act_hbm)
    act_copy.start()
    end(*again, *x_copies)
    for n in range(quad.tiles):
        quad.acc[: quad.head, n * COLS : (n + 1) * COLS] += back[n * quad.head : (n + 1) * quad.head]

    def input_rows(i, _):
        whole, own = own_block(quad, i, size)
        grad = quad.acc[own]
        change, gain_terms = norm_back(grad, own_in[own].astype(jnp.float32), gain1[...])
        y0[whole] = (mid[own] + change).astype(jnp.bfloat16)
        vec[0:1] += column_sum(gain_terms)
        vec[1:2] += column_sum(grad)
        return 0

    lax.fori_loop(0, own_rows // size, input_rows, 0)
    quad.gather_send(y0, 1)
    swap_start(0)
    late = max(ready, ring.steps - lines)
    ring.run(ready, late)
    swap_end(0)
    swap_start(1)
    ring.run(late, ring.steps)
    quad.gather_near(y0, 1)
    quad.gather_pass(y0, 1)
    swap_end(1)
    swap_start(2)
    ring.run(ring.steps, ring.steps + SKEW)
    quad.gather_far(y0, 1)
    in_copy = store(1, y0, in_hbm)
    in_copy.start()
    for n in range(2, len(swaps)):
        swap_end(n)
        if n + 1 < len(swaps):
            swap_start(n + 1)
    ring.finish(ring.steps + SKEW)
    quad.gather_done(y1)
    quad.gather_done(y0, 1)
    quad.scatter_done()
    end(act_copy, in_copy)


def back_call(n_ctx, turned, g, h2, hid, dpre, w1, w_qkv, w2, w_out, h_all, att, mid, cot, x, act, gain1, gain2, ffn_bias,
              bias, weight, theirs, q, k, v, lse, vec):
    lines, rows, width = n_ctx // 2, cot.shape[0], cot.shape[1]
    block_rows, own, cols = width // n_ctx, rows // 4, q.shape[1]
    hidden = hid.shape[1]
    returned = PREFIX * width // 4 // COLS
    rounds = n_ctx.bit_length() + 1
    vm, hbm, sm = (pl.BlockSpec(memory_space=s) for s in (pltpu.VMEM, pl.ANY, pltpu.SMEM))
    bf, f4 = jnp.bfloat16, jnp.float32
    shape = jax.ShapeDtypeStruct
    return pl.pallas_call(
        functools.partial(back_kernel, lines, turned),
        out_shape=(
            shape((hidden, block_rows), f4),
            shape((block_rows, hidden), f4),
            shape((cols, block_rows), f4),
            shape((3, block_rows, cols), f4),
            shape((rows, width), bf),
            shape((rows, width), bf),
            shape((own, width), f4),
            shape((own, width), f4),
            shape(vec.shape, f4),
        ),
        in_specs=[hbm] * 13 + [vm] * 4 + [sm] * 3 + [vm] * 5,
        out_specs=[hbm] * 8 + [vm],
        scratch_shapes=Ring.scratch(lines, block_rows)
        + Quad.scratch(own + PREFIX // 4, width)
        + [
            pltpu.VMEM(h_all.shape, bf),
            pltpu.VMEM(h2.shape, bf),
            pltpu.VMEM((rows, hidden), bf),
            pltpu.VMEM((rows, hidden), bf),
            pltpu.VMEM(w1.shape, bf),
            pltpu.VMEM((own, width), f4),
            pltpu.VMEM((own, width), bf),
            pltpu.VMEM((rows, width), bf),
            pltpu.VMEM((rows, cols), bf),
            pltpu.VMEM((rows + PREFIX, 3 * cols), bf),
            pltpu.VMEM((returned, COLS), f4),
            pltpu.VMEM((returned, COLS), f4),
            pltpu.VMEM((rounds, *vec.shape), f4),
            pltpu.VMEM((rounds, *vec.shape), f4),
            pltpu.SemaphoreType.DMA((11,)),
            pltpu.SemaphoreType.DMA((2,)),
            pltpu.SemaphoreType.DMA((rounds,)),
            pltpu.SemaphoreType.DMA((rounds,)),
            pltpu.SemaphoreType.REGULAR,
        ],
        compiler_params=pltpu.CompilerParams(collective_id=2, has_side_effects=True, vmem_limit_bytes=63 * 2**20),
    )(g, h2, hid, dpre, w1, w_qkv, w2, w_out, h_all, att, mid, cot, x, act, gain1[None], gain2[None], ffn_bias[None],
      bias, weight, theirs, q, k, v, lse, vec)


def find_block(lengths, placed, block):
    mine, start, first = placed[block], 0, 0
    for s in range(lengths.shape[0]):
        first = jnp.where(start <= mine, start, first)
        start = start + lengths[s]
    owner = 0
    for e in range(placed.shape[0]):
        owner = owner + jnp.where(placed[e] == first, e, 0)
    return mine - first, jnp.minimum(owner, placed.shape[0] - 1)


def attend_own(p, q, k, v, held, peaks, totals):
    lanes = pl.ds(pl.multiple_of(p * 2 * HEAD, 2 * HEAD), 2 * HEAD)
    rows = q.shape[0]
    value_t = v[PREFIX:, lanes].T
    row = lax.broadcasted_iota(jnp.int32, (PREFIX, PREFIX), 0)
    col = lax.broadcasted_iota(jnp.int32, (PREFIX, PREFIX), 1)
    for r in range(rows // PREFIX):
        own, count = slice(r * PREFIX, (r + 1) * PREFIX), (r + 1) * PREFIX
        query, keys = q[own, lanes], k[PREFIX : PREFIX + count, lanes]
        for e in range(2):
            scores = nt(keys, jnp.where(lane_mask(PREFIX, e), query, jnp.zeros_like(query)))
            last = jnp.where(row <= col, scores[count - PREFIX :], NEGATIVE)
            scores = jnp.concatenate([scores[: count - PREFIX], last], axis=0) if r else last
            peak = jnp.max(scores, axis=0, keepdims=True)
            raised = jnp.exp(scores - peak)
            peaks[p, e : e + 1, own] = peak
            totals[p, e : e + 1, own] = jnp.sum(raised, axis=0, keepdims=True)
            part = slice(e * HEAD, (e + 1) * HEAD)
            held[p, part, own] = nn(value_t[part, :count], raised.astype(jnp.bfloat16))


def attend_prefix(p, bias, q, k, v, held, peaks, totals, out, lse):
    lanes = pl.ds(pl.multiple_of(p * 2 * HEAD, 2 * HEAD), 2 * HEAD)
    query, keys, value_t = q[:, lanes], k[:PREFIX, lanes], v[:PREFIX, lanes].T
    outs = []
    for e in range(2):
        scores = nt(keys, jnp.where(lane_mask(q.shape[0], e), query, jnp.zeros_like(query))) + bias
        before = peaks[p, e : e + 1]
        peak = jnp.maximum(before, jnp.max(scores, axis=0, keepdims=True))
        raised = jnp.exp(scores - peak)
        shrink = jnp.exp(before - peak)
        total = totals[p, e : e + 1] * shrink + jnp.sum(raised, axis=0, keepdims=True)
        lse[p, e : e + 1] = peak + jnp.log(total)
        part = slice(e * HEAD, (e + 1) * HEAD)
        summed = held[p, part] * shrink + nn(value_t[part], raised.astype(jnp.bfloat16))
        outs.append(summed * (1.0 / total))
    out[:, lanes] = jnp.concatenate(outs, axis=0).astype(jnp.bfloat16).T


def first_kernel(lines, *refs):
    (lengths, placed, layer, exits, x_hbm, w_hbm, gain, shift, qv_bias,
     q, k, v, h_all, act, att, lse, bias, weight, theirs, *scratch) = refs
    (x, w, line, x_send, x_recv, prefix, held, peaks, totals, loads, s_l, s_r, r_z, s_x, r_x, s_g, r_g) = scratch
    rows, width = x.shape
    part = prefix.shape[0] // 4
    ctx, tp = lax.axis_index("ctx"), lax.axis_index("tp")
    z, side, y, core = ctx // 2, lax.rem(ctx, 2), tp // 2, lax.rem(tp, 2)
    left, right, partner = (ctx - 2, tp), (ctx + 2, tp), (z * 2 + 1 - side, tp)
    across, over = (ctx, y * 2 + 1 - core), (ctx, (1 - y) * 2 + core)
    own = pl.ds(pl.multiple_of(tp * part, 16), part)
    copies = [
        pltpu.make_async_copy(x_hbm.at[own], line.at[z], loads.at[0]),
        pltpu.make_async_copy(x_hbm, x, loads.at[1]),
        pltpu.make_async_copy(w_hbm, w, loads.at[2]),
    ]
    for copy in copies:
        copy.start()
    meet([(None, partner), (z > 0, left), (z < lines - 1, right), (None, across), (None, over)])

    def hop(o, device, sems):
        return pltpu.make_async_remote_copy(
            src_ref=line.at[o], dst_ref=line.at[o], send_sem=sems.at[o], recv_sem=r_z.at[o],
            device_id=device, device_id_type=MESH)

    def pass_on(o, there, device, sems):
        @pl.when(there)
        def _():
            hop(o, device, sems).start()

    copies[0].wait()
    pass_on(z, z < lines - 1, right, s_r)
    pass_on(z, z > 0, left, s_l)

    def hops(d):
        @pl.when(z - d >= 0)
        def _():
            hop(z - d, left, s_l).wait_recv()
            pass_on(z - d, z < lines - 1, right, s_r)

        @pl.when(z + d < lines)
        def _():
            hop(z + d, right, s_r).wait_recv()
            pass_on(z + d, z > 0, left, s_l)

    my_part, my_owner = find_block(lengths, placed, ctx)
    partner_part, partner_owner = find_block(lengths, placed, z * 2 + 1 - side)
    bias[0, 0] = jnp.where(my_part > 0, 0.0, NEGATIVE)
    for e in range(weight.shape[0]):
        weight[e] = jnp.where((my_owner == e) & (my_part > 0), 1.0, 0.0)
        theirs[e] = jnp.where((partner_owner == e) & (partner_part > 0), 1.0, 0.0)
    row = lax.broadcasted_iota(jnp.int32, exits.shape, 0)
    first_rows = jnp.where(my_part == 0, PREFIX, 0)
    act[...] = jnp.where((exits[...] > layer[0]) | (row < first_rows), 1.0, 0.0)
    size = 64

    def norm_rows(source, start, to):
        def some(i, _):
            span = pl.ds(pl.multiple_of(start + i * size, size), size)
            values = source[span].astype(jnp.float32)
            target = pl.ds(pl.multiple_of(to + i * size, size), size)
            h_all[target] = (normed(values)[0] * gain[...] + shift[...]).astype(jnp.bfloat16)
            return 0

        lax.fori_loop(0, PREFIX // size, some, 0)

    def keys_of(span, rows_in):
        k[span] = nn(rows_in, w[1]).astype(jnp.bfloat16)
        v[span] = (nn(rows_in, w[2]) + qv_bias[1:2]).astype(jnp.bfloat16)

    for r in range(rows // PREFIX):
        norm_rows(x_wait(copies, r, x), r * PREFIX, (r + 1) * PREFIX)
        if r == 0:
            copies[2].wait()
        span = slice((r + 1) * PREFIX, (r + 2) * PREFIX)
        rows_in = h_all[span]
        low = (nn(rows_in, w[0]) + qv_bias[0:1]).astype(jnp.bfloat16)
        q[r * PREFIX : (r + 1) * PREFIX] = low * jnp.bfloat16(HEAD**-0.5)
        keys_of(span, rows_in)
        if r + 1 < lines:
            hops(r + 1)
    for d in range(rows // PREFIX + 1, lines):
        hops(d)
    x_send[...] = line[partner_owner // 2]
    trade = pltpu.make_async_remote_copy(
        src_ref=x_send, dst_ref=x_recv, send_sem=s_x, recv_sem=r_x, device_id=partner, device_id_type=MESH)
    trade.start()
    near = line[my_owner // 2]
    pairs = q.shape[1] // (2 * HEAD)

    def own_pairs(lo, hi):
        lax.fori_loop(lo, hi, lambda p, _: (attend_own(p, q, k, v, held, peaks, totals), 0)[1], 0)

    own_pairs(0, pairs // 2)
    trade.wait_recv()
    prefix[own] = jnp.where(lax.rem(my_owner, 2) == side, near, x_recv[...])

    def give(n, quarter, device):
        span = pl.ds(pl.multiple_of(quarter * part, 16), part)
        return pltpu.make_async_remote_copy(
            src_ref=prefix.at[span], dst_ref=prefix.at[span], send_sem=s_g.at[n], recv_sem=r_g.at[n],
            device_id=device, device_id_type=MESH)

    far = (1 - y) * 2 + core
    give(0, tp, over).start()
    give(1, tp, across).start()
    own_pairs(pairs // 2, pairs)
    give(0, far, over).wait_recv()
    give(2, far, across).start()
    give(1, y * 2 + 1 - core, across).wait_recv()
    give(2, (1 - y) * 2 + 1 - core, across).wait_recv()
    norm_rows(prefix, 0, 0)
    keys_of(slice(0, PREFIX), h_all[:PREFIX])
    hide = jnp.where(my_part > 0, 0.0, NEGATIVE)

    def prefix_pair(p, _):
        attend_prefix(p, hide, q, k, v, held, peaks, totals, att, lse)
        return 0

    lax.fori_loop(0, pairs, prefix_pair, 0)
    trade.wait_send()
    give(0, tp, over).wait_send()
    give(1, tp, across).wait_send()
    give(2, far, across).wait_send()
    for o in range(lines):
        @pl.when((z < lines - 1) & (z >= o))
        def _():
            hop(o, right, s_r).wait_send()

        @pl.when((z > 0) & (z <= o))
        def _():
            hop(o, left, s_l).wait_send()


def x_wait(copies, r, x):
    if r == 0:
        copies[1].wait()
    return x


def first_call(n_ctx, lengths, placed, layer, exits, x, w_qkv, gain, shift, qv_bias):
    lines, (rows, width) = n_ctx // 2, x.shape
    cols = w_qkv.shape[2]
    vm, hbm, sm = (pl.BlockSpec(memory_space=s) for s in (pltpu.VMEM, pl.ANY, pltpu.SMEM))
    bf, f4 = jnp.bfloat16, jnp.float32
    return pl.pallas_call(
        functools.partial(first_kernel, lines),
        out_shape=(
            jax.ShapeDtypeStruct((rows, cols), bf),
            jax.ShapeDtypeStruct((rows + PREFIX, cols), bf),
            jax.ShapeDtypeStruct((rows + PREFIX, cols), bf),
            jax.ShapeDtypeStruct((rows + PREFIX, width), bf),
            jax.ShapeDtypeStruct((rows, 1), f4),
            jax.ShapeDtypeStruct((rows, cols), bf),
            jax.ShapeDtypeStruct((cols // (2 * HEAD), 2, rows), f4),
            jax.ShapeDtypeStruct((1, 1), f4),
            jax.ShapeDtypeStruct((n_ctx,), f4),
            jax.ShapeDtypeStruct((n_ctx,), f4),
        ),
        in_specs=[sm] * 3 + [vm] + [hbm] * 2 + [vm] * 3,
        out_specs=[vm] * 7 + [sm] * 3,
        scratch_shapes=[
            pltpu.VMEM((rows, width), bf),
            pltpu.VMEM(w_qkv.shape, bf),
            pltpu.VMEM((lines, PREFIX // 4, width), bf),
            pltpu.VMEM((PREFIX // 4, width), bf),
            pltpu.VMEM((PREFIX // 4, width), bf),
            pltpu.VMEM((PREFIX, width), bf),
            pltpu.VMEM((cols // (2 * HEAD), 2 * HEAD, rows), f4),
            pltpu.VMEM((cols // (2 * HEAD), 2, rows), f4),
            pltpu.VMEM((cols // (2 * HEAD), 2, rows), f4),
            pltpu.SemaphoreType.DMA((3,)),
            pltpu.SemaphoreType.DMA((lines,)),
            pltpu.SemaphoreType.DMA((lines,)),
            pltpu.SemaphoreType.DMA((lines,)),
            pltpu.SemaphoreType.DMA,
            pltpu.SemaphoreType.DMA,
            pltpu.SemaphoreType.DMA((3,)),
            pltpu.SemaphoreType.DMA((3,)),
        ],
        compiler_params=pltpu.CompilerParams(collective_id=4, has_side_effects=True, vmem_limit_bytes=50 * 2**20),
    )(lengths, placed, layer, exits[:, None], x, w_qkv, gain[None], shift[None], qv_bias)


def body(
    mesh,
    block_input,
    cotangent,
    ln1_gain,
    ln1_bias,
    w_qkv,
    qv_bias,
    w_out,
    out_bias,
    ln2_gain,
    ln2_bias,
    w_fc1,
    fc1_bias,
    w_fc2,
    fc2_bias,
    exit_layer,
    layer_index,
    lengths,
    stretch_map,
):
    n_ctx = mesh.shape["ctx"]
    row_count, width = block_input.shape
    block_rows = width // n_ctx
    turned = block_rows % 128 != 0

    def tokens_last(array):
        return array.T if turned else array

    query, key, value, h_all, active, attended, log_total, bias, weight, theirs = first_call(
        n_ctx, lengths, stretch_map, layer_index, exit_layer, block_input, w_qkv, ln1_gain, ln1_bias, qv_bias
    )
    middle, h2_low, grad_ffn, hidden_low, d_pre_low, vectors = front_call(
        attended, w_out, block_input, cotangent, active, w_fc1, w_fc2, out_bias, ln2_gain, ln2_bias, fc1_bias
    )
    fc2_grad, fc1_grad, out_grad, qkv_grad, input_grad, output_rows, _, _, vectors = back_call(
        n_ctx, turned, tokens_last(grad_ffn), tokens_last(h2_low), hidden_low, d_pre_low, w_fc1, w_qkv, w_fc2, w_out,
        tokens_last(h_all), attended, middle, cotangent, block_input, active, ln1_gain, ln2_gain, fc2_bias,
        bias, weight, theirs, query, key, value, log_total, vectors,
    )
    qv_grad = vectors[7, : 2 * query.shape[1]].reshape(2, -1)
    return (
        output_rows,
        input_grad,
        vectors[0],
        vectors[1],
        qkv_grad,
        qv_grad,
        out_grad,
        vectors[2],
        vectors[3],
        vectors[4],
        fc1_grad,
        vectors[6],
        fc2_grad,
        vectors[5],
    )


def solution(mesh):
    in_specs = (
        P("ctx", None),
        P("ctx", None),
        P(),
        P(),
        P(None, None, "tp"),
        P(None, "tp"),
        P("tp", None),
        P(),
        P(),
        P(),
        P(None, "tp"),
        P("tp"),
        P("tp", None),
        P(),
        P("ctx"),
        P(),
        P(),
        P(),
    )
    out_specs = (
        P("ctx", None),
        P("ctx", None),
        P(),
        P(),
        P(None, "ctx", "tp"),
        P(None, "tp"),
        P("tp", "ctx"),
        P(),
        P(),
        P(),
        P("ctx", "tp"),
        P("tp"),
        P("tp", "ctx"),
        P(),
    )
    return jax.shard_map(functools.partial(body, mesh), mesh=mesh, in_specs=in_specs, out_specs=out_specs, check_vma=False)
```

```python
import functools
import math

import jax
import jax.numpy as jnp
from jax import lax
from jax.experimental import pallas as pl
from jax.experimental.pallas import tpu as pltpu
from jax.sharding import PartitionSpec as P

HEAD = 64
PREFIX = 256
COLS = 512
MESH = pl.DeviceIdType.MESH
NEGATIVE = -1e30
EPSILON = 1e-05
AHEAD = 8
SKEW = 2
STAGES = 2
DEPTH = 2


class Ring:
    def __init__(self, lines, groups, refs, outs, later=(), prefix=None):
        self.lines, self.groups, self.outs, self.later, self.prefix = lines, groups, outs, later, prefix
        (self.xs, self.xr, self.zb, self.stage, self.turned, self.kept, self.swap, self.s_xs, self.s_xr, self.s_zs,
         self.s_zr, self.s_out, self.s_swap, self.c_x, self.c_left, self.c_right) = refs
        self.jobs = sum(group[0] for group in groups)
        marks, job = [], 0
        for group in groups:
            marks += [job + n for n in range(group[0]) if group[2]]
            job += group[0]
        self.fetched = (marks[0], marks[-1]) if marks else (self.jobs, self.jobs)
        self.steps = self.jobs * lines
        self.slots = self.xr.shape[0]
        self.lag = SKEW * (lines - 1) + 2
        ctx, tp = lax.axis_index("ctx"), lax.axis_index("tp")
        self.z, self.side = ctx // 2, lax.rem(ctx, 2)
        self.partner = (self.z * 2 + 1 - self.side, tp)
        self.left, self.right = (ctx - 2, tp), (ctx + 2, tp)

    @staticmethod
    def scratch(lines, rows):
        slots = AHEAD + SKEW * (lines - 1) + 4
        chunk = (rows, COLS)
        return [
            pltpu.VMEM((AHEAD, *chunk), jnp.bfloat16),
            pltpu.VMEM((slots, *chunk), jnp.bfloat16),
            pltpu.VMEM((DEPTH, lines + 1, *chunk), jnp.bfloat16),
            pltpu.VMEM((STAGES, *chunk), jnp.float32),
            pltpu.VMEM((STAGES, COLS, rows), jnp.float32),
            pltpu.VMEM(chunk, jnp.bfloat16),
            pltpu.VMEM((4, *chunk), jnp.bfloat16),
            pltpu.SemaphoreType.DMA((AHEAD,)),
            pltpu.SemaphoreType.DMA((slots,)),
            pltpu.SemaphoreType.DMA((slots,)),
            pltpu.SemaphoreType.DMA((DEPTH, lines + 1)),
            pltpu.SemaphoreType.DMA((STAGES,)),
            pltpu.SemaphoreType.DMA((4,)),
            pltpu.SemaphoreType.REGULAR,
            pltpu.SemaphoreType.REGULAR,
            pltpu.SemaphoreType.REGULAR,
        ]

    def sends(self, f):
        job = f // self.lines
        found = (job < self.fetched[0]) | (job > self.fetched[1]) | (lax.rem(f, self.lines) == 0)
        for pair in self.later:
            found = found & (job != pair[0]) & (job != pair[1])
        return found

    def peers(self):
        return [(None, self.partner), (self.z > 0, self.left), (self.z < self.lines - 1, self.right)]

    def x_copy(self, f):
        slot, to = lax.rem(f, AHEAD), lax.rem(f, self.slots)
        return pltpu.make_async_remote_copy(
            src_ref=self.xs.at[slot], dst_ref=self.xr.at[to], send_sem=self.s_xs.at[slot],
            recv_sem=self.s_xr.at[to], device_id=self.partner, device_id_type=MESH)

    def z_copy(self, f, to, device):
        slot, level = lax.rem(f, self.slots), lax.rem(f // self.lines, DEPTH)
        return pltpu.make_async_remote_copy(
            src_ref=self.xr.at[slot], dst_ref=self.zb.at[level, to], send_sem=self.s_zs.at[slot],
            recv_sem=self.s_zr.at[level, to], device_id=device, device_id_type=MESH)

    def out_copies(self, job, act):
        slot = lax.rem(job, STAGES)
        for there, turn, place in self.outs(job):
            @pl.when(there)
            def _():
                source = self.turned if turn else self.stage
                act(pltpu.make_async_copy(source.at[slot], place, self.s_out.at[slot]))

    def out_start(self, job):
        slot = lax.rem(job, STAGES)
        for there, turn, _ in self.outs(job):
            if turn:
                @pl.when(there)
                def _():
                    self.turned[slot] = self.stage[slot].T
        self.out_copies(job, lambda copy: copy.start())

    def out_wait(self, job):
        self.out_copies(job, lambda copy: copy.wait())

    def swap_copy(self, n):
        return pltpu.make_async_remote_copy(
            src_ref=self.swap.at[2 * n], dst_ref=self.swap.at[2 * n + 1], send_sem=self.s_swap.at[2 * n],
            recv_sem=self.s_swap.at[2 * n + 1], device_id=self.partner, device_id_type=MESH)

    def send(self, f, group, job0, fresh):
        _, part, is_prefix = group
        if not fresh:
            @pl.when(self.sends(f - AHEAD))
            def _():
                self.x_copy(f).wait_send()

            @pl.when(f >= self.slots)
            def _():
                pl.semaphore_wait(self.c_x, 1)

        @pl.when(self.sends(f))
        def _():
            owner = lax.rem(f, self.lines)
            value = part(f // self.lines - job0, None if is_prefix else owner * 2 + 1 - self.side)
            self.xs[lax.rem(f, AHEAD)] = value.astype(jnp.bfloat16)
            self.x_copy(f).start()

    def receive(self, f, group, job0):
        _, part, is_prefix = group
        job, owner, slot = f // self.lines, lax.rem(f, self.lines), lax.rem(f, self.slots)
        came = self.sends(f)

        @pl.when(came)
        def _():
            self.x_copy(f).wait_recv()
            if is_prefix:
                self.kept[...] = self.xr[slot]

        block = owner * 2 + self.side
        if is_prefix:
            mine, theirs = self.prefix[0][block], self.prefix[1][block]
            total = part(job - job0, None) * mine + self.kept[...].astype(jnp.float32) * theirs
        else:
            @pl.when(jnp.logical_not(came))
            def _():
                self.xr[slot] = jnp.zeros(self.xr.shape[1:], jnp.bfloat16)

            for pair in self.later:
                block = jnp.where(job == pair[0], owner * 2 + 1 - self.side, block)
            total = part(job - job0, block) + self.xr[slot].astype(jnp.float32)

        @pl.when(owner != self.z)
        def _():
            self.xr[slot] = total.astype(jnp.bfloat16)

        @pl.when(owner == self.z)
        def _():
            @pl.when(job >= STAGES)
            def _():
                self.out_wait(job - STAGES)
            self.stage[lax.rem(job, STAGES)] = total

    def add(self, f, index):
        job = f // self.lines
        slot, level = lax.rem(f, self.slots), lax.rem(job, DEPTH)

        @pl.when(lax.rem(f, self.lines) == self.z)
        def _():
            self.stage[lax.rem(job, STAGES)] += self.zb[level, index].astype(jnp.float32)

        @pl.when(lax.rem(f, self.lines) != self.z)
        def _():
            self.xr[slot] = (self.xr[slot].astype(jnp.float32) + self.zb[level, index].astype(jnp.float32)).astype(jnp.bfloat16)

    def flow(self, t):
        lines, z = self.lines, self.z
        f = t - SKEW * z
        owner = lax.rem(f + lines * SKEW * lines, lines)

        @pl.when((f >= 0) & (f < self.steps) & (owner >= z))
        def _():
            @pl.when(z > 0)
            def _():
                self.z_copy(f, owner, self.left).wait_recv()
                self.add(f, owner)
                pl.semaphore_signal(self.c_right, inc=1, device_id=self.left, device_id_type=MESH)

            @pl.when(owner > z)
            def _():
                @pl.when(f >= DEPTH * lines)
                def _():
                    pl.semaphore_wait(self.c_right, 1)
                self.z_copy(f, owner, self.right).start()

        g = t - SKEW * (lines - 1 - z)
        owner2 = lax.rem(g + lines * SKEW * lines, lines)

        @pl.when((g >= 0) & (g < self.steps) & (owner2 <= z))
        def _():
            @pl.when(z < lines - 1)
            def _():
                index = jnp.where(owner2 == z, lines, owner2)
                self.z_copy(g, index, self.right).wait_recv()
                self.add(g, index)
                pl.semaphore_signal(self.c_left, inc=1, device_id=self.right, device_id_type=MESH)

            @pl.when(owner2 < z)
            def _():
                @pl.when(g >= DEPTH * lines)
                def _():
                    pl.semaphore_wait(self.c_left, 1)
                self.z_copy(g, jnp.where(owner2 == z - 1, lines, owner2), self.left).start()

        h = t - SKEW * (lines - 1)

        @pl.when((h >= 0) & (h < self.steps) & (lax.rem(h + lines * SKEW * lines, lines) == z))
        def _():
            job = h // lines
            stage = lax.rem(job, STAGES)
            for n, pair in enumerate(self.later):
                @pl.when(job == pair[0])
                def _():
                    self.swap[2 * n] = self.stage[stage].astype(jnp.bfloat16)
                    self.swap_copy(n).start()

                @pl.when(job == pair[1])
                def _():
                    self.swap_copy(n).wait()
                    self.stage[stage] += self.swap[2 * n + 1].astype(jnp.float32)
            if self.prefix is not None:
                target, rows = self.prefix[2], self.stage.shape[1]

                @pl.when((job >= self.fetched[0]) & (job <= self.fetched[1]))
                def _():
                    span = pl.ds(pl.multiple_of((job - self.fetched[0]) * rows, rows), rows)
                    target[span] = self.stage[stage]
            self.out_start(job)

        d = t - self.lag

        @pl.when((d >= 0) & (d < self.steps))
        def _():
            @pl.when(lax.rem(d + lines * (SKEW * lines + 2), lines) != z)
            def _():
                self.z_copy(d, 0, self.left).wait_send()
            pl.semaphore_signal(self.c_x, inc=1, device_id=self.partner, device_id_type=MESH)

    def find(self, f):
        job = 0
        for group in self.groups:
            if f < (job + group[0]) * self.lines:
                return group, job
            job += group[0]
        return None

    def pieces(self, lo, hi):
        cuts, job = {lo, hi}, 0
        for group in self.groups:
            job += group[0]
            cuts |= {job * self.lines, job * self.lines - AHEAD}
        cuts = sorted(c for c in cuts if lo <= c <= hi)
        return zip(cuts[:-1], cuts[1:])

    def start(self):
        for lo, hi in self.pieces(0, AHEAD):
            here = self.find(lo)
            lax.fori_loop(lo, hi, lambda f, _, here=here: (self.send(f, *here, True), 0)[1], 0)

    def run(self, lo, hi):
        for a, b in self.pieces(lo, min(hi, self.steps)):
            here, ahead = self.find(a), self.find(a + AHEAD)

            def body(f, _, here=here, ahead=ahead):
                self.receive(f, *here)
                self.flow(f)
                if ahead is not None:
                    self.send(f + AHEAD, *ahead, False)
                return 0

            lax.fori_loop(a, b, body, 0)
        if hi > self.steps:
            lax.fori_loop(max(lo, self.steps), hi, lambda t, _: (self.flow(t), 0)[1], 0)

    def run_some(self, lo, count):
        here = self.find(0)

        def body(f, _):
            self.receive(f, *here)
            self.flow(f)

            @pl.when(f + AHEAD < self.steps)
            def _():
                self.send(f + AHEAD, *here, False)
            return 0

        lax.fori_loop(lo, lo + count, body, 0)

    def finish(self, lo):
        lines, z = self.lines, self.z
        self.run(lo, self.steps + self.lag)

        def drain(f, _):
            @pl.when(self.sends(f))
            def _():
                self.x_copy(f).wait_send()
            return 0

        lax.fori_loop(self.steps - AHEAD, self.steps, drain, 0)
        for job in range(self.jobs - STAGES, self.jobs):
            self.out_wait(job)
        pl.semaphore_wait(self.c_x, min(self.slots, self.steps))

        @pl.when(z < lines - 1)
        def _():
            pl.semaphore_wait(self.c_right, DEPTH * (lines - 1 - z))

        @pl.when(z > 0)
        def _():
            pl.semaphore_wait(self.c_left, DEPTH * z)


def meet(peers):
    barrier = pltpu.get_barrier_semaphore()
    count = 0
    for there, device in peers:
        if there is None:
            pl.semaphore_signal(barrier, inc=1, device_id=device, device_id_type=MESH)
            count += 1
        else:
            @pl.when(there)
            def _():
                pl.semaphore_signal(barrier, inc=1, device_id=device, device_id_type=MESH)
            count += jnp.where(there, 1, 0)
    pl.semaphore_wait(barrier, count)
class Quad:
    def __init__(self, refs, rows, height):
        (self.tmp, self.cs, self.cr, self.ys, self.yr, self.acc, self.s_c, self.r_c, self.s_y, self.r_y,
         self.s_g, self.r_g) = refs
        ctx, tp = lax.axis_index("ctx"), lax.axis_index("tp")
        self.y, self.core, self.tp = tp // 2, lax.rem(tp, 2), tp
        self.across = (ctx, self.y * 2 + 1 - self.core)
        self.over = (ctx, (1 - self.y) * 2 + self.core)
        self.head, self.rest = PREFIX // 4, (rows - PREFIX) // 4
        self.tiles = self.cs.shape[1]
        self.height = height

    @staticmethod
    def scratch(rows, width):
        tiles = width // COLS
        return [
            pltpu.VMEM((2, rows, COLS), jnp.float32),
            pltpu.VMEM((2, tiles, rows, COLS), jnp.bfloat16),
            pltpu.VMEM((2, tiles, rows, COLS), jnp.bfloat16),
            pltpu.VMEM((tiles, rows, COLS), jnp.bfloat16),
            pltpu.VMEM((tiles, rows, COLS), jnp.bfloat16),
            pltpu.VMEM((rows, width), jnp.float32),
            pltpu.SemaphoreType.DMA((2, tiles)),
            pltpu.SemaphoreType.DMA((2, tiles)),
            pltpu.SemaphoreType.DMA((tiles,)),
            pltpu.SemaphoreType.DMA((tiles,)),
            pltpu.SemaphoreType.DMA((2, 3, 2)),
            pltpu.SemaphoreType.DMA((2, 3, 2)),
        ]

    def peers(self):
        return [(None, self.across), (None, self.over)]

    def spans(self, quarter):
        return [
            pl.ds(pl.multiple_of(quarter * self.head, 16), self.head),
            pl.ds(pl.multiple_of(PREFIX + quarter * self.rest, 16), self.rest),
        ]

    def rows_of(self, ref, quarter):
        return jnp.concatenate([ref[span] for span in self.spans(quarter)], axis=0)

    def half_of(self, ref, half):
        return jnp.concatenate([self.rows_of(ref, half * 2), self.rows_of(ref, half * 2 + 1)], axis=0)

    def c_copy(self, k, n):
        return pltpu.make_async_remote_copy(
            src_ref=self.cs.at[k, n, : self.height], dst_ref=self.cr.at[k, n, : self.height], send_sem=self.s_c.at[k, n],
            recv_sem=self.r_c.at[k, n], device_id=self.across, device_id_type=MESH)

    def y_copy(self, n):
        return pltpu.make_async_remote_copy(
            src_ref=self.ys.at[n, : self.height], dst_ref=self.yr.at[n, : self.height], send_sem=self.s_y.at[n],
            recv_sem=self.r_y.at[n], device_id=self.over, device_id_type=MESH)

    def columns(self, n):
        return pl.ds(pl.multiple_of(n * COLS, COLS), COLS)

    def split(self, value, k, n):
        rows = self.height
        self.tmp[0, :rows] = value[:rows]
        self.tmp[1, :rows] = value[rows:]
        self.cs[k, n, :rows] = self.tmp[1 - self.core, :rows].astype(jnp.bfloat16)
        self.c_copy(k, n).start()
        self.acc[:rows, self.columns(n)] = self.tmp[self.core, :rows]

    def relay(self, n):
        self.c_copy(0, n).wait_recv()
        rows = self.height
        total = self.acc[:rows, self.columns(n)] + self.cr[0, n, :rows].astype(jnp.float32)
        self.ys[n, :rows] = total.astype(jnp.bfloat16)
        self.y_copy(n).start()

    def scatter_send(self, chunk):
        def far(n, _):
            self.split(chunk(1 - self.y, n), 0, n)

            @pl.when(n > 0)
            def _():
                self.relay(n - 1)
            return 0

        lax.fori_loop(0, self.tiles, far, 0)
        self.relay(self.tiles - 1)

        def near(n, _):
            self.split(chunk(self.y, n), 1, n)
            return 0

        lax.fori_loop(0, self.tiles, near, 0)

    def scatter_add(self, n):
        self.c_copy(1, n).wait_recv()
        self.y_copy(n).wait_recv()
        rows = self.height
        came = self.cr[1, n, :rows].astype(jnp.float32) + self.yr[n, :rows].astype(jnp.float32)
        self.acc[:rows, self.columns(n)] += came

    def scatter_done(self):
        for n in range(self.tiles):
            self.c_copy(0, n).wait_send()
            self.c_copy(1, n).wait_send()
            self.y_copy(n).wait_send()

    def g_copy(self, full, k, s, quarter, device, turn):
        span = self.spans(quarter)[s]
        return pltpu.make_async_remote_copy(
            src_ref=full.at[span], dst_ref=full.at[span], send_sem=self.s_g.at[turn, k, s],
            recv_sem=self.r_g.at[turn, k, s], device_id=device, device_id_type=MESH)

    def gather_send(self, full, turn=0):
        for s in range(2):
            self.g_copy(full, 0, s, self.tp, self.over, turn).start()
        for s in range(2):
            self.g_copy(full, 1, s, self.tp, self.across, turn).start()

    def gather_near(self, full, turn=0):
        for s in range(2):
            self.g_copy(full, 1, s, self.y * 2 + 1 - self.core, self.across, turn).wait_recv()

    def gather_pass(self, full, turn=0):
        other = (1 - self.y) * 2 + self.core
        for s in range(2):
            self.g_copy(full, 0, s, other, self.over, turn).wait_recv()
            self.g_copy(full, 2, s, other, self.across, turn).start()

    def gather_far(self, full, turn=0):
        for s in range(2):
            self.g_copy(full, 2, s, (1 - self.y) * 2 + 1 - self.core, self.across, turn).wait_recv()

    def gather_done(self, full, turn=0):
        other = (1 - self.y) * 2 + self.core
        for s in range(2):
            self.g_copy(full, 0, s, self.tp, self.over, turn).wait_send()
            self.g_copy(full, 1, s, self.tp, self.across, turn).wait_send()
            self.g_copy(full, 2, s, other, self.across, turn).wait_send()


def nt(left, right):
    return lax.dot_general(left, right, (((1,), (1,)), ((), ())), preferred_element_type=jnp.float32)


def normed(values_in):
    centred = values_in - jnp.mean(values_in, axis=1, keepdims=True)
    scale = lax.rsqrt(jnp.mean(centred * centred, axis=1, keepdims=True) + EPSILON)
    return centred * scale, scale


def gelu_pair(pre):
    slope = (2.0 / math.pi) ** 0.5
    square = pre * pre
    bent = jnp.tanh(slope * (pre + 0.044715 * (square * pre)))
    half = 0.5 * (1.0 + bent)
    return pre * half, half + 0.5 * pre * (1.0 - bent * bent) * (slope * (1.0 + 3 * 0.044715 * square))


def column_sum(values_in):
    return jnp.sum(values_in, axis=0, keepdims=True)


def front_kernel(*refs):
    (att, w_out, x_hbm, cot_hbm, act, w1_hbm, w2_hbm, bias, gain, shift, fc1_bias,
     mid, full, grad, hid, d_pre, vec, *scratch) = refs
    quad_refs, scratch = scratch[:12], scratch[12:]
    x, w1, w2, d_hid, some, loads = scratch
    rows, width = full.shape
    quad = Quad(quad_refs, rows, rows // 4)
    spans = quad.spans(quad.tp)

    def load(n, source, target):
        copy = pltpu.make_async_copy(source, target, loads.at[n])
        copy.start()
        return copy

    cot_copy = load(0, cot_hbm, grad)
    w2_copy = load(1, w2_hbm, w2)
    x_copies = [load(2, x_hbm.at[spans[0]], x.at[: quad.head]), load(3, x_hbm.at[spans[1]], x.at[quad.head :])]
    w1_copy = load(4, w1_hbm, w1)
    meet(quad.peers())
    quad.scatter_send(lambda half, n: jnp.dot(quad.half_of(att, half), w_out[:, quad.columns(n)], preferred_element_type=jnp.float32))
    cot_copy.wait()
    vec[...] = jnp.zeros(vec.shape, jnp.float32)
    size = 32

    def gate(i, _):
        span = pl.ds(pl.multiple_of(i * size, size), size)
        low = (act[span] * grad[span].astype(jnp.float32)).astype(jnp.bfloat16)
        grad[span] = low
        vec[5:6] += column_sum(low.astype(jnp.float32)) * 0.25
        return 0

    lax.fori_loop(0, rows // size, gate, 0)
    w2_copy.wait()
    tiles = hid.shape[1] // COLS

    def d_hidden(n, _):
        d_hid[:, quad.columns(n)] = nt(grad[...], w2[quad.columns(n), :])
        return 0

    lax.fori_loop(0, tiles, d_hidden, 0)
    for copy in x_copies:
        copy.wait()
    lax.fori_loop(0, quad.tiles, lambda n, _: (quad.scatter_add(n), 0)[1], 0)

    def norm_rows(i, _):
        first = quad.head // size
        start = jnp.where(i < first, quad.tp * quad.head + i * size, PREFIX + quad.tp * quad.rest + (i - first) * size)
        whole, own = (pl.ds(pl.multiple_of(s, size), size) for s in (start, i * size))
        middle = x[own].astype(jnp.float32) + act[whole] * (quad.acc[own] + bias[...])
        mid[own] = middle
        full[whole] = (normed(middle)[0] * gain[...] + shift[...]).astype(jnp.bfloat16)
        return 0

    lax.fori_loop(0, quad.height // size, norm_rows, 0)
    quad.gather_send(full)

    def ffn(half):
        some[...] = quad.half_of(full, half)
        places = quad.spans(half * 2) + quad.spans(half * 2 + 1)

        def tile(n, _):
            cols = quad.columns(n)
            pre = jnp.dot(some[...], w1[:, cols], preferred_element_type=jnp.float32) + fc1_bias[:, cols]
            value, slope = gelu_pair(pre)
            value = value.astype(jnp.bfloat16)
            start = 0
            for place in places:
                end = start + place.size
                hid[place, cols] = value[start:end]
                change = (d_hid[place, cols] * slope[start:end]).astype(jnp.bfloat16)
                d_pre[place, cols] = change
                vec[6:7, cols] += column_sum(change.astype(jnp.float32))
                start = end
            return 0

        lax.fori_loop(0, tiles, tile, 0)

    quad.gather_near(full)
    w1_copy.wait()
    ffn(quad.y)
    quad.gather_pass(full)
    quad.gather_far(full)
    ffn(1 - quad.y)
    quad.gather_done(full)
    quad.scatter_done()


def front_call(att, w_out, x, cot, act, w1, w2, bias, gain, shift, fc1_bias):
    rows, width = x.shape
    own, hidden = rows // 4, w1.shape[1]
    vm, hbm = (pl.BlockSpec(memory_space=s) for s in (pltpu.VMEM, pl.ANY))
    bf, f4, shape = jnp.bfloat16, jnp.float32, jax.ShapeDtypeStruct
    return pl.pallas_call(
        front_kernel,
        out_shape=(
            shape((own, width), f4),
            shape((rows, width), bf),
            shape((rows, width), bf),
            shape((rows, hidden), bf),
            shape((rows, hidden), bf),
            shape((8, width), f4),
        ),
        in_specs=[vm] * 2 + [hbm] * 2 + [vm] + [hbm] * 2 + [vm] * 4,
        out_specs=[vm] * 6,
        scratch_shapes=Quad.scratch(own, width)
        + [
            pltpu.VMEM((own, width), bf),
            pltpu.VMEM(w1.shape, bf),
            pltpu.VMEM(w2.shape, bf),
            pltpu.VMEM((rows, hidden), f4),
            pltpu.VMEM((2 * own, width), bf),
            pltpu.SemaphoreType.DMA((5,)),
        ],
        compiler_params=pltpu.CompilerParams(collective_id=1, has_side_effects=True, vmem_limit_bytes=64 * 2**20),
    )(att, w_out, x, cot, act, w1, w2, bias[None], gain[None], shift[None], fc1_bias[None])
def tn(left, right):
    return lax.dot_general(left, right, (((0,), (0,)), ((), ())), preferred_element_type=jnp.float32)


def nn(left, right):
    return jnp.dot(left, right, preferred_element_type=jnp.float32)


def lane_mask(rows, head):
    lane = lax.broadcasted_iota(jnp.int32, (rows, 2 * HEAD), 1)
    return (lane < HEAD) if head == 0 else (lane >= HEAD)


def scores_of(keys, query, bias):
    scores = nt(keys, query)
    count = scores.shape[0]
    row = lax.broadcasted_iota(jnp.int32, (PREFIX, PREFIX), 0)
    col = lax.broadcasted_iota(jnp.int32, (PREFIX, PREFIX), 1)
    parts = [scores[:PREFIX] + bias]
    if count > 2 * PREFIX:
        parts.append(scores[PREFIX : count - PREFIX])
    parts.append(jnp.where(row <= col, scores[count - PREFIX :], NEGATIVE))
    return jnp.concatenate(parts, axis=0)


def attend_back(p, bias, q_ref, k_ref, v_ref, l_ref, g_ref, d_ref, room):
    rows, width = q_ref.shape
    blocks = rows // PREFIX
    base = pl.multiple_of(p * 2 * HEAD, 2 * HEAD)
    lanes = pl.ds(base, 2 * HEAD)
    sums = jnp.zeros((1, 2 * HEAD), jnp.float32)
    for r in reversed(range(blocks)):
        count, own = (r + 2) * PREFIX, slice(r * PREFIX, (r + 1) * PREFIX)
        query, grad, keys, values = q_ref[own, lanes], g_ref[own, lanes], k_ref[:count, lanes], v_ref[:count, lanes]
        d_queries, d_keys, d_values = [], None, None
        for e in range(2):
            mask = lane_mask(PREFIX, e)
            query_e = jnp.where(mask, query, jnp.zeros_like(query))
            grad_e = jnp.where(mask, grad, jnp.zeros_like(grad))
            probs = jnp.exp(scores_of(keys, query_e, bias) - l_ref[p, e : e + 1, own])
            d_probs = nt(values, grad_e)
            inner = jnp.sum(probs * d_probs, axis=0, keepdims=True)
            d_scores = (probs * (d_probs - inner)).astype(jnp.bfloat16)
            keys_e, values_e = nn(d_scores, query_e), nn(probs.astype(jnp.bfloat16), grad_e)
            d_keys = keys_e if d_keys is None else d_keys + keys_e
            d_values = values_e if d_values is None else d_values + values_e
            d_queries.append(tn(d_scores, keys))
        d_query = jnp.where(lane_mask(PREFIX, 0), d_queries[0], d_queries[1]) * HEAD ** (-0.5)
        sums += jnp.sum(d_query, axis=0, keepdims=True)
        d_ref[(r + 1) * PREFIX : (r + 2) * PREFIX, lanes] = d_query.astype(jnp.bfloat16)
        for n in range(r + 2):
            for at, sums_of in ((n, d_keys), (blocks + 1 + n, d_values)):
                place, term = slice(at * 2 * HEAD, (at + 1) * 2 * HEAD), sums_of[n * PREFIX : (n + 1) * PREFIX]
                if r == blocks - 1:
                    room[:PREFIX, place] = term
                else:
                    room[:PREFIX, place] += term
    d_ref[:PREFIX, lanes] = jnp.zeros((PREFIX, 2 * HEAD), jnp.bfloat16)
    value_sums = jnp.zeros((1, 2 * HEAD), jnp.float32)
    for n in range(blocks + 1):
        span = slice(n * PREFIX, (n + 1) * PREFIX)
        for m, at in ((1, n), (2, blocks + 1 + n)):
            total = room[:PREFIX, at * 2 * HEAD : (at + 1) * 2 * HEAD]
            d_ref[span, pl.ds(pl.multiple_of(base + m * width, 2 * HEAD), 2 * HEAD)] = total.astype(jnp.bfloat16)
            if m == 2:
                value_sums += column_sum(total)
    return sums, value_sums


def own_block(quad, i, size):
    first = quad.head // size
    start = jnp.where(i < first, quad.tp * quad.head + i * size, PREFIX + quad.tp * quad.rest + (i - first) * size)
    return pl.ds(pl.multiple_of(start, size), size), pl.ds(pl.multiple_of(i * size, size), size)


def norm_back(grad, source, gain):
    unit, scale = normed(source)
    scaled = grad * gain
    mean = jnp.mean(scaled, axis=1, keepdims=True)
    slope = jnp.mean(scaled * unit, axis=1, keepdims=True)
    return scale * (scaled - mean - unit * slope), grad * unit


def product_part(left, right, tile, turned, rows):
    def part(j, block):
        cols = pl.ds(pl.multiple_of(tile(j) * COLS, COLS), COLS)
        span = pl.ds(pl.multiple_of(block * rows, rows), rows)
        if turned:
            return nn(left[span, :], right[:, cols])
        return tn(left[:, span], right[:, cols])

    return part


def pick(table, j):
    found = table[0]
    for n, entry in enumerate(table[1:]):
        found = jnp.where(j == n + 1, entry, found)
    return found


class Wide(Quad):
    def rows_of(self, ref, quarter):
        own = [pl.ds(pl.multiple_of(span.start + PREFIX, 16), span.size) for span in self.spans(quarter)]
        return jnp.concatenate([ref[span] for span in [self.spans(quarter)[0]] + own], axis=0)


def back_kernel(lines, turned, *refs):
    (g_hbm, h2_hbm, hid_hbm, dpre_hbm, w1_hbm, w_qkv_hbm, w2_hbm, wo_hbm, h_hbm, att_hbm, mid_hbm, cot_hbm, x_hbm,
     act, gain1, gain2, ffn_bias, bias, weight, theirs, q, k, v, lse, vec_in,
     fc2_out, fc1_out, out_grad, qkv_grad, in_hbm, act_hbm, dmid_hbm, dh_hbm, vec, *scratch) = refs
    ring_refs, scratch = scratch[:16], scratch[16:]
    quad_refs, scratch = scratch[:12], scratch[12:]
    (x0, x1, y0, y1, weights, mid, own_in, full, d_att, d_all, fresh, back, v_send, v_recv, loads, stores, s_v, r_v,
     c_over) = scratch
    rows, width = full.shape
    quad, wide = Quad(quad_refs, rows, rows // 4), Wide(quad_refs, rows, (rows + PREFIX) // 4)
    own_rows, depth = quad.height, q.shape[1]
    tiles, cols = y0.shape[1] // COLS, depth // COLS
    block_rows = ring_refs[0].shape[1]
    extra = fresh.shape[0] // block_rows
    order2 = [tiles - 1, *range(tiles - 1), tiles - 1]
    order1 = [*range(tiles - 2), tiles - 1, tiles - 2, tiles - 1]
    half = tiles + 1
    later = ((0, tiles), (half + tiles - 2, half + tiles))
    base = 2 * half + extra
    g_part = x0.at[:, :rows] if turned else x0.at[:rows]
    columns = lambda n: pl.ds(pl.multiple_of(n * COLS, COLS), COLS)

    def prefix_part(j, block):
        return fresh[pl.ds(pl.multiple_of(j * block_rows, block_rows), block_rows)]

    def outs(job):
        local = job - half
        head = jnp.maximum(job - base - cols, 0)
        place2, place1 = columns(pick(order2, job)), columns(pick(order1, local))
        is2 = (job < half) & (job != later[0][0])
        is1 = (job >= half) & (job < 2 * half) & (job != later[1][0])
        is_out = (job >= base) & (job < base + cols)
        out_span = columns(jnp.clip(job - base, 0, cols - 1))
        return [
            (is2, True, fc2_out.at[place2]),
            (is1, False, fc1_out.at[:, place1]),
            (is_out, True, out_grad.at[out_span]),
            (job >= base + cols, False, qkv_grad.at[head // cols, :, columns(lax.rem(head, cols))]),
        ]

    groups = [
        (half, product_part(g_part, y0, lambda j: pick(order2, j), turned, block_rows), False),
        (half, product_part(x1, y1, lambda j: pick(order1, j), turned, block_rows), False),
        (extra, prefix_part, True),
        (cols, product_part(x1 if turned else full, d_att, lambda j: j, turned, block_rows), False),
        (3 * cols, product_part(x0, d_all, lambda j: j, turned, block_rows), False),
    ]
    ring = Ring(lines, groups, ring_refs, outs, later, (weight, theirs, back))

    def load(n, source, target):
        return pltpu.make_async_copy(source, target, loads.at[n])

    def store(n, source, target):
        return pltpu.make_async_copy(source, target, stores.at[n])

    def begin(*copies):
        for copy in copies:
            copy.start()

    def end(*copies):
        for copy in copies:
            copy.wait()

    spans = quad.spans(quad.tp)
    first = [load(0, hid_hbm, y0), load(1, g_hbm, g_part)]
    second = [load(2, dpre_hbm, y1), load(3, w1_hbm, weights)]
    third = [
        load(4, h2_hbm, x1),
        load(5, mid_hbm, mid),
        load(6, cot_hbm.at[spans[0]], own_in.at[: quad.head]),
        load(7, cot_hbm.at[spans[1]], own_in.at[quad.head :]),
    ]
    begin(*first, *second, *third)
    ctx, tp = lax.axis_index("ctx"), lax.axis_index("tp")
    swaps, bit = [quad.across, quad.over], 1
    while bit < 2 * lines:
        swaps.append((ctx + bit - 2 * bit * lax.rem(ctx // bit, 2), tp))
        bit *= 2
    meet(ring.peers() + quad.peers() + [(None, device) for device in swaps[4:]])

    def swap(n):
        return pltpu.make_async_remote_copy(
            src_ref=v_send.at[n], dst_ref=v_recv.at[n], send_sem=s_v.at[n], recv_sem=r_v.at[n],
            device_id=swaps[n], device_id_type=MESH)

    def swap_start(n):
        v_send[n] = vec[...]
        swap(n).start()

    def swap_end(n):
        swap(n).wait()
        if n < 2:
            vec[:6] += v_recv[n, :6]
        else:
            vec[...] += v_recv[n]

    def add_all(group):
        lax.fori_loop(0, group.tiles, lambda n, _: (group.scatter_add(n), 0)[1], 0)

    end(*first)
    ring.start()
    end(*second)
    quad.scatter_send(lambda part, n: nt(quad.half_of(y1, part), weights[quad.columns(n), :]))
    wo_copy = load(3, wo_hbm, weights.at[:depth])
    wo_copy.start()
    end(*third)
    ring.run(0, 5)
    add_all(quad)
    vec[...] = vec_in[...]
    size = 32

    def middle_rows(i, _):
        whole, own = own_block(quad, i, size)
        grad = quad.acc[own]
        change, gain_terms = norm_back(grad, mid[own], gain2[...])
        d_middle = own_in[own].astype(jnp.float32) + change
        quad.acc[own] = d_middle
        low = (act[whole] * d_middle).astype(jnp.bfloat16)
        full[whole] = low
        vec[2:3] += column_sum(low.astype(jnp.float32))
        vec[3:4] += column_sum(gain_terms)
        vec[4:5] += column_sum(grad)
        return 0

    lax.fori_loop(0, own_rows // size, middle_rows, 0)
    quad.gather_send(full)
    keep = store(0, quad.acc.at[:own_rows], dmid_hbm)
    x_copies = [load(6, x_hbm.at[spans[0]], own_in.at[: quad.head]), load(7, x_hbm.at[spans[1]], own_in.at[quad.head :])]
    begin(keep, *x_copies)
    ring.run(5, 10)
    quad.gather_near(full)
    quad.gather_pass(full)
    quad.gather_far(full)
    wo_copy.wait()

    def attended_rows(i, _):
        span = pl.ds(pl.multiple_of(i * PREFIX, PREFIX), PREFIX)
        d_att[span] = nt(full[span], weights[:depth, :]).astype(jnp.bfloat16)
        return 0

    lax.fori_loop(0, rows // PREFIX, attended_rows, 0)
    heads = [load(8 + m, w_qkv_hbm.at[m], weights.at[:, m * depth : (m + 1) * depth]) for m in range(3)]
    begin(*heads)
    keep.wait()
    pairs = depth // (2 * HEAD)

    now = 10
    for p in range(pairs):
        sums, value_sums = attend_back(p, bias[0, 0], q, k, v, lse, d_att, d_all, quad.acc)
        start = p * 2 * HEAD
        vec[7:8, start : start + 2 * HEAD] = sums
        vec[7:8, start + depth : start + depth + 2 * HEAD] = value_sums
        ring.run(now, now + 2)
        now += 2
    att_copy = load(2, att_hbm, d_att)
    att_copy.start()
    quad.gather_done(full)
    quad.scatter_done()
    end(*heads)
    wide.scatter_send(lambda part, n: nt(wide.half_of(d_all, part), weights[wide.columns(n), : 3 * depth]))
    w2_copy = load(3, w2_hbm, weights)
    w2_copy.start()
    free0, free1 = half * lines, 2 * half * lines
    ring.run(now, free0)
    h_copy = load(1, h_hbm, x0)
    h_copy.start()
    ring.run(free0, free0 + 2)
    add_all(wide)
    pl.semaphore_signal(c_over, inc=1, device_id=quad.over, device_id_type=MESH)
    for n in range(wide.tiles):
        fresh[n * wide.head : (n + 1) * wide.head] = wide.acc[: wide.head, n * COLS : (n + 1) * COLS]
    dh_copy = store(1, wide.acc.at[pl.ds(wide.head, own_rows)], dh_hbm)
    dh_copy.start()
    att_copy.wait()
    ring.run(free0 + 2, free1 - AHEAD)
    h_copy.wait()
    ring.run(free1 - AHEAD, free1)
    if turned:

        def flip(n, _):
            x1[columns(n), :] = full[:, columns(n)].T
            return 0

        lax.fori_loop(0, width // COLS, flip, 0)
    wide.scatter_done()
    end(dh_copy, w2_copy)
    pl.semaphore_wait(c_over, 1)
    quad.scatter_send(lambda part, n: nn(quad.half_of(y0, part), weights[:, quad.columns(n)]))
    ring.run(free1, free1 + lines)
    add_all(quad)

    def out_rows(i, _):
        whole, own = own_block(quad, i, size)
        y1[whole] = (mid[own] + act[whole] * (quad.acc[own] + ffn_bias[...])).astype(jnp.bfloat16)
        return 0

    lax.fori_loop(0, own_rows // size, out_rows, 0)
    quad.gather_send(y1)
    again = [load(4, dh_hbm, quad.acc.at[:own_rows]), load(5, dmid_hbm, mid)]
    begin(*again)
    ready = base * lines + SKEW * (lines - 1)
    ring.run(free1 + lines, ready)
    quad.gather_near(y1)
    quad.gather_pass(y1)
    quad.gather_far(y1)
    act_copy = store(0, y1, act_hbm)
    act_copy.start()
    end(*again, *x_copies)
    for n in range(quad.tiles):
        quad.acc[: quad.head, n * COLS : (n + 1) * COLS] += back[n * quad.head : (n + 1) * quad.head]

    def input_rows(i, _):
        whole, own = own_block(quad, i, size)
        grad = quad.acc[own]
        change, gain_terms = norm_back(grad, own_in[own].astype(jnp.float32), gain1[...])
        y0[whole] = (mid[own] + change).astype(jnp.bfloat16)
        vec[0:1] += column_sum(gain_terms)
        vec[1:2] += column_sum(grad)
        return 0

    lax.fori_loop(0, own_rows // size, input_rows, 0)
    quad.gather_send(y0, 1)
    swap_start(0)
    late = min(max(ready, ring.steps - AHEAD), ring.steps - 4)
    ring.run(ready, late)
    swap_end(0)
    swap_start(1)
    ring.run(late, late + 2)
    swap_end(1)
    swap_start(2)
    ring.run(late + 2, ring.steps)
    quad.gather_near(y0, 1)
    quad.gather_pass(y0, 1)
    swap_end(2)
    swap_start(3)
    ring.run(ring.steps, ring.steps + SKEW)
    quad.gather_far(y0, 1)
    in_copy = store(1, y0, in_hbm)
    in_copy.start()
    swap_end(3)
    for n in range(4, len(swaps)):
        swap_start(n)
        if n + 1 == len(swaps):
            ring.run(ring.steps + SKEW, ring.steps + 2 * SKEW)
        swap_end(n)
    ring.finish(ring.steps + 2 * SKEW)
    quad.gather_done(y1)
    quad.gather_done(y0, 1)
    quad.scatter_done()
    end(act_copy, in_copy)


def back_call(n_ctx, turned, g, h2, hid, dpre, w1, w_qkv, w2, w_out, h_all, att, mid, cot, x, act, gain1, gain2, ffn_bias,
              bias, weight, theirs, q, k, v, lse, vec):
    lines, rows, width = n_ctx // 2, cot.shape[0], cot.shape[1]
    block_rows, own, cols = width // n_ctx, rows // 4, q.shape[1]
    hidden = hid.shape[1]
    returned = PREFIX * width // 4 // COLS
    rounds = n_ctx.bit_length() + 1
    vm, hbm, sm = (pl.BlockSpec(memory_space=s) for s in (pltpu.VMEM, pl.ANY, pltpu.SMEM))
    bf, f4 = jnp.bfloat16, jnp.float32
    shape = jax.ShapeDtypeStruct
    return pl.pallas_call(
        functools.partial(back_kernel, lines, turned),
        out_shape=(
            shape((hidden, block_rows), f4),
            shape((block_rows, hidden), f4),
            shape((cols, block_rows), f4),
            shape((3, block_rows, cols), f4),
            shape((rows, width), bf),
            shape((rows, width), bf),
            shape((own, width), f4),
            shape((own, width), f4),
            shape(vec.shape, f4),
        ),
        in_specs=[hbm] * 13 + [vm] * 4 + [sm] * 3 + [vm] * 5,
        out_specs=[hbm] * 8 + [vm],
        scratch_shapes=Ring.scratch(lines, block_rows)
        + Quad.scratch(own + PREFIX // 4, width)
        + [
            pltpu.VMEM(h_all.shape, bf),
            pltpu.VMEM(h2.shape, bf),
            pltpu.VMEM((rows, hidden), bf),
            pltpu.VMEM((rows, hidden), bf),
            pltpu.VMEM(w1.shape, bf),
            pltpu.VMEM((own, width), f4),
            pltpu.VMEM((own, width), bf),
            pltpu.VMEM((rows, width), bf),
            pltpu.VMEM((rows, cols), bf),
            pltpu.VMEM((rows + PREFIX, 3 * cols), bf),
            pltpu.VMEM((returned, COLS), f4),
            pltpu.VMEM((returned, COLS), f4),
            pltpu.VMEM((rounds, *vec.shape), f4),
            pltpu.VMEM((rounds, *vec.shape), f4),
            pltpu.SemaphoreType.DMA((11,)),
            pltpu.SemaphoreType.DMA((2,)),
            pltpu.SemaphoreType.DMA((rounds,)),
            pltpu.SemaphoreType.DMA((rounds,)),
            pltpu.SemaphoreType.REGULAR,
        ],
        compiler_params=pltpu.CompilerParams(collective_id=2, has_side_effects=True, vmem_limit_bytes=64 * 2**20),
    )(g, h2, hid, dpre, w1, w_qkv, w2, w_out, h_all, att, mid, cot, x, act, gain1[None], gain2[None], ffn_bias[None],
      bias, weight, theirs, q, k, v, lse, vec)


def find_block(lengths, placed, block):
    mine, start, first = placed[block], 0, 0
    for s in range(lengths.shape[0]):
        first = jnp.where(start <= mine, start, first)
        start = start + lengths[s]
    owner = 0
    for e in range(placed.shape[0]):
        owner = owner + jnp.where(placed[e] == first, e, 0)
    return mine - first, jnp.minimum(owner, placed.shape[0] - 1)


def attend_own(p, q, k, v, held, peaks, totals):
    lanes = pl.ds(pl.multiple_of(p * 2 * HEAD, 2 * HEAD), 2 * HEAD)
    rows = q.shape[0]
    value_t = v[PREFIX:, lanes].T
    row = lax.broadcasted_iota(jnp.int32, (PREFIX, PREFIX), 0)
    col = lax.broadcasted_iota(jnp.int32, (PREFIX, PREFIX), 1)
    for r in range(rows // PREFIX):
        own, count = slice(r * PREFIX, (r + 1) * PREFIX), (r + 1) * PREFIX
        query, keys = q[own, lanes], k[PREFIX : PREFIX + count, lanes]
        for e in range(2):
            scores = nt(keys, jnp.where(lane_mask(PREFIX, e), query, jnp.zeros_like(query)))
            last = jnp.where(row <= col, scores[count - PREFIX :], NEGATIVE)
            scores = jnp.concatenate([scores[: count - PREFIX], last], axis=0) if r else last
            peak = jnp.max(scores, axis=0, keepdims=True)
            raised = jnp.exp(scores - peak)
            peaks[p, e : e + 1, own] = peak
            totals[p, e : e + 1, own] = jnp.sum(raised, axis=0, keepdims=True)
            part = slice(e * HEAD, (e + 1) * HEAD)
            held[p, part, own] = nn(value_t[part, :count], raised.astype(jnp.bfloat16))


def attend_prefix(p, bias, q, k, v, held, peaks, totals, out, lse):
    lanes = pl.ds(pl.multiple_of(p * 2 * HEAD, 2 * HEAD), 2 * HEAD)
    query, keys, value_t = q[:, lanes], k[:PREFIX, lanes], v[:PREFIX, lanes].T
    outs = []
    for e in range(2):
        scores = nt(keys, jnp.where(lane_mask(q.shape[0], e), query, jnp.zeros_like(query))) + bias
        before = peaks[p, e : e + 1]
        peak = jnp.maximum(before, jnp.max(scores, axis=0, keepdims=True))
        raised = jnp.exp(scores - peak)
        shrink = jnp.exp(before - peak)
        total = totals[p, e : e + 1] * shrink + jnp.sum(raised, axis=0, keepdims=True)
        lse[p, e : e + 1] = peak + jnp.log(total)
        part = slice(e * HEAD, (e + 1) * HEAD)
        summed = held[p, part] * shrink + nn(value_t[part], raised.astype(jnp.bfloat16))
        outs.append(summed * (1.0 / total))
    out[:, lanes] = jnp.concatenate(outs, axis=0).astype(jnp.bfloat16).T


def first_kernel(lines, *refs):
    (lengths, placed, layer, exits, x_hbm, w_hbm, gain, shift, qv_bias,
     q, k, v, h_all, act, att, lse, bias, weight, theirs, *scratch) = refs
    (x, w, line, x_send, x_recv, prefix, held, peaks, totals, loads, s_l, s_r, r_z, s_x, r_x, s_g, r_g) = scratch
    rows, width = x.shape
    part = prefix.shape[0] // 4
    ctx, tp = lax.axis_index("ctx"), lax.axis_index("tp")
    z, side, y, core = ctx // 2, lax.rem(ctx, 2), tp // 2, lax.rem(tp, 2)
    left, right, partner = (ctx - 2, tp), (ctx + 2, tp), (z * 2 + 1 - side, tp)
    across, over = (ctx, y * 2 + 1 - core), (ctx, (1 - y) * 2 + core)
    own = pl.ds(pl.multiple_of(tp * part, 16), part)
    copies = [
        pltpu.make_async_copy(x_hbm.at[own], line.at[z], loads.at[0]),
        pltpu.make_async_copy(x_hbm, x, loads.at[1]),
        pltpu.make_async_copy(w_hbm, w, loads.at[2]),
    ]
    for copy in copies:
        copy.start()
    meet([(None, partner), (z > 0, left), (z < lines - 1, right), (None, across), (None, over)])

    def hop(o, device, sems):
        return pltpu.make_async_remote_copy(
            src_ref=line.at[o], dst_ref=line.at[o], send_sem=sems.at[o], recv_sem=r_z.at[o],
            device_id=device, device_id_type=MESH)

    def pass_on(o, there, device, sems):
        @pl.when(there)
        def _():
            hop(o, device, sems).start()

    copies[0].wait()
    pass_on(z, z < lines - 1, right, s_r)
    pass_on(z, z > 0, left, s_l)

    def hops(d):
        @pl.when(z - d >= 0)
        def _():
            hop(z - d, left, s_l).wait_recv()
            pass_on(z - d, z < lines - 1, right, s_r)

        @pl.when(z + d < lines)
        def _():
            hop(z + d, right, s_r).wait_recv()
            pass_on(z + d, z > 0, left, s_l)

    my_part, my_owner = find_block(lengths, placed, ctx)
    partner_part, partner_owner = find_block(lengths, placed, z * 2 + 1 - side)
    bias[0, 0] = jnp.where(my_part > 0, 0.0, NEGATIVE)
    for e in range(weight.shape[0]):
        weight[e] = jnp.where((my_owner == e) & (my_part > 0), 1.0, 0.0)
        theirs[e] = jnp.where((partner_owner == e) & (partner_part > 0), 1.0, 0.0)
    row = lax.broadcasted_iota(jnp.int32, exits.shape, 0)
    first_rows = jnp.where(my_part == 0, PREFIX, 0)
    act[...] = jnp.where((exits[...] > layer[0]) | (row < first_rows), 1.0, 0.0)
    size = 64

    def norm_rows(source, start, to):
        def some(i, _):
            span = pl.ds(pl.multiple_of(start + i * size, size), size)
            values = source[span].astype(jnp.float32)
            target = pl.ds(pl.multiple_of(to + i * size, size), size)
            h_all[target] = (normed(values)[0] * gain[...] + shift[...]).astype(jnp.bfloat16)
            return 0

        lax.fori_loop(0, PREFIX // size, some, 0)

    def keys_of(span, rows_in):
        k[span] = nn(rows_in, w[1]).astype(jnp.bfloat16)
        v[span] = (nn(rows_in, w[2]) + qv_bias[1:2]).astype(jnp.bfloat16)

    for r in range(rows // PREFIX):
        norm_rows(x_wait(copies, r, x), r * PREFIX, (r + 1) * PREFIX)
        if r == 0:
            copies[2].wait()
        span = slice((r + 1) * PREFIX, (r + 2) * PREFIX)
        rows_in = h_all[span]
        low = (nn(rows_in, w[0]) + qv_bias[0:1]).astype(jnp.bfloat16)
        q[r * PREFIX : (r + 1) * PREFIX] = low * jnp.bfloat16(HEAD**-0.5)
        keys_of(span, rows_in)
        if r + 1 < lines:
            hops(r + 1)
    for d in range(rows // PREFIX + 1, lines):
        hops(d)
    x_send[...] = line[partner_owner // 2]
    trade = pltpu.make_async_remote_copy(
        src_ref=x_send, dst_ref=x_recv, send_sem=s_x, recv_sem=r_x, device_id=partner, device_id_type=MESH)
    trade.start()
    near = line[my_owner // 2]
    pairs = q.shape[1] // (2 * HEAD)

    def own_pairs(lo, hi):
        lax.fori_loop(lo, hi, lambda p, _: (attend_own(p, q, k, v, held, peaks, totals), 0)[1], 0)

    own_pairs(0, pairs // 2)
    trade.wait_recv()
    prefix[own] = jnp.where(lax.rem(my_owner, 2) == side, near, x_recv[...])

    def give(n, quarter, device):
        span = pl.ds(pl.multiple_of(quarter * part, 16), part)
        return pltpu.make_async_remote_copy(
            src_ref=prefix.at[span], dst_ref=prefix.at[span], send_sem=s_g.at[n], recv_sem=r_g.at[n],
            device_id=device, device_id_type=MESH)

    far = (1 - y) * 2 + core
    give(0, tp, over).start()
    give(1, tp, across).start()
    own_pairs(pairs // 2, pairs)
    give(0, far, over).wait_recv()
    give(2, far, across).start()
    give(1, y * 2 + 1 - core, across).wait_recv()
    give(2, (1 - y) * 2 + 1 - core, across).wait_recv()
    norm_rows(prefix, 0, 0)
    keys_of(slice(0, PREFIX), h_all[:PREFIX])
    hide = jnp.where(my_part > 0, 0.0, NEGATIVE)

    def prefix_pair(p, _):
        attend_prefix(p, hide, q, k, v, held, peaks, totals, att, lse)
        return 0

    lax.fori_loop(0, pairs, prefix_pair, 0)
    trade.wait_send()
    give(0, tp, over).wait_send()
    give(1, tp, across).wait_send()
    give(2, far, across).wait_send()
    for o in range(lines):
        @pl.when((z < lines - 1) & (z >= o))
        def _():
            hop(o, right, s_r).wait_send()

        @pl.when((z > 0) & (z <= o))
        def _():
            hop(o, left, s_l).wait_send()


def x_wait(copies, r, x):
    if r == 0:
        copies[1].wait()
    return x


def first_call(n_ctx, lengths, placed, layer, exits, x, w_qkv, gain, shift, qv_bias):
    lines, (rows, width) = n_ctx // 2, x.shape
    cols = w_qkv.shape[2]
    vm, hbm, sm = (pl.BlockSpec(memory_space=s) for s in (pltpu.VMEM, pl.ANY, pltpu.SMEM))
    bf, f4 = jnp.bfloat16, jnp.float32
    return pl.pallas_call(
        functools.partial(first_kernel, lines),
        out_shape=(
            jax.ShapeDtypeStruct((rows, cols), bf),
            jax.ShapeDtypeStruct((rows + PREFIX, cols), bf),
            jax.ShapeDtypeStruct((rows + PREFIX, cols), bf),
            jax.ShapeDtypeStruct((rows + PREFIX, width), bf),
            jax.ShapeDtypeStruct((rows, 1), f4),
            jax.ShapeDtypeStruct((rows, cols), bf),
            jax.ShapeDtypeStruct((cols // (2 * HEAD), 2, rows), f4),
            jax.ShapeDtypeStruct((1, 1), f4),
            jax.ShapeDtypeStruct((n_ctx,), f4),
            jax.ShapeDtypeStruct((n_ctx,), f4),
        ),
        in_specs=[sm] * 3 + [vm] + [hbm] * 2 + [vm] * 3,
        out_specs=[vm] * 7 + [sm] * 3,
        scratch_shapes=[
            pltpu.VMEM((rows, width), bf),
            pltpu.VMEM(w_qkv.shape, bf),
            pltpu.VMEM((lines, PREFIX // 4, width), bf),
            pltpu.VMEM((PREFIX // 4, width), bf),
            pltpu.VMEM((PREFIX // 4, width), bf),
            pltpu.VMEM((PREFIX, width), bf),
            pltpu.VMEM((cols // (2 * HEAD), 2 * HEAD, rows), f4),
            pltpu.VMEM((cols // (2 * HEAD), 2, rows), f4),
            pltpu.VMEM((cols // (2 * HEAD), 2, rows), f4),
            pltpu.SemaphoreType.DMA((3,)),
            pltpu.SemaphoreType.DMA((lines,)),
            pltpu.SemaphoreType.DMA((lines,)),
            pltpu.SemaphoreType.DMA((lines,)),
            pltpu.SemaphoreType.DMA,
            pltpu.SemaphoreType.DMA,
            pltpu.SemaphoreType.DMA((3,)),
            pltpu.SemaphoreType.DMA((3,)),
        ],
        compiler_params=pltpu.CompilerParams(collective_id=4, has_side_effects=True, vmem_limit_bytes=64 * 2**20),
    )(lengths, placed, layer, exits[:, None], x, w_qkv, gain[None], shift[None], qv_bias)


def body(
    mesh,
    block_input,
    cotangent,
    ln1_gain,
    ln1_bias,
    w_qkv,
    qv_bias,
    w_out,
    out_bias,
    ln2_gain,
    ln2_bias,
    w_fc1,
    fc1_bias,
    w_fc2,
    fc2_bias,
    exit_layer,
    layer_index,
    lengths,
    stretch_map,
):
    n_ctx = mesh.shape["ctx"]
    row_count, width = block_input.shape
    block_rows = width // n_ctx
    turned = block_rows % 128 != 0

    def tokens_last(array):
        return array.T if turned else array

    query, key, value, h_all, active, attended, log_total, bias, weight, theirs = first_call(
        n_ctx, lengths, stretch_map, layer_index, exit_layer, block_input, w_qkv, ln1_gain, ln1_bias, qv_bias
    )
    middle, h2_low, grad_ffn, hidden_low, d_pre_low, vectors = front_call(
        attended, w_out, block_input, cotangent, active, w_fc1, w_fc2, out_bias, ln2_gain, ln2_bias, fc1_bias
    )
    fc2_grad, fc1_grad, out_grad, qkv_grad, input_grad, output_rows, _, _, vectors = back_call(
        n_ctx, turned, tokens_last(grad_ffn), tokens_last(h2_low), hidden_low, d_pre_low, w_fc1, w_qkv, w_fc2, w_out,
        tokens_last(h_all), attended, middle, cotangent, block_input, active, ln1_gain, ln2_gain, fc2_bias,
        bias, weight, theirs, query, key, value, log_total, vectors,
    )
    qv_grad = vectors[7, : 2 * query.shape[1]].reshape(2, -1)
    return (
        output_rows,
        input_grad,
        vectors[0],
        vectors[1],
        qkv_grad,
        qv_grad,
        out_grad,
        vectors[2],
        vectors[3],
        vectors[4],
        fc1_grad,
        vectors[6],
        fc2_grad,
        vectors[5],
    )


def solution(mesh):
    in_specs = (
        P("ctx", None),
        P("ctx", None),
        P(),
        P(),
        P(None, None, "tp"),
        P(None, "tp"),
        P("tp", None),
        P(),
        P(),
        P(),
        P(None, "tp"),
        P("tp"),
        P("tp", None),
        P(),
        P("ctx"),
        P(),
        P(),
        P(),
    )
    out_specs = (
        P("ctx", None),
        P("ctx", None),
        P(),
        P(),
        P(None, "ctx", "tp"),
        P(None, "tp"),
        P("tp", "ctx"),
        P(),
        P(),
        P(),
        P("ctx", "tp"),
        P("tp"),
        P("tp", "ctx"),
        P(),
    )
    return jax.shard_map(functools.partial(body, mesh), mesh=mesh, in_specs=in_specs, out_specs=out_specs, check_vma=False)
```

```python
import functools
import math

import jax
import jax.numpy as jnp
from jax import lax
from jax.experimental import pallas as pl
from jax.experimental.pallas import tpu as pltpu
from jax.sharding import PartitionSpec as P

HEAD = 64
PREFIX = 256
COLS = 512
MESH = pl.DeviceIdType.MESH
NEGATIVE = -1e30
EPSILON = 1e-05
AHEAD = 8
SKEW = 2
STAGES = 2
DEPTH = 2


class Ring:
    def __init__(self, lines, groups, refs, outs, later=(), prefix=None):
        self.lines, self.groups, self.outs, self.later, self.prefix = lines, groups, outs, later, prefix
        (self.xs, self.xr, self.zb, self.stage, self.turned, self.kept, self.swap, self.s_xs, self.s_xr, self.s_zs,
         self.s_zr, self.s_out, self.s_swap, self.c_x, self.c_left, self.c_right) = refs
        self.jobs = sum(group[0] for group in groups)
        marks, alone, job = [], [], 0
        for group in groups:
            marks += [job + n for n in range(group[0]) if group[2] == "p"]
            alone += [job + n for n in range(group[0]) if group[2] == "t"]
            job += group[0]
        self.alone = (alone[0], alone[-1]) if alone else None
        self.fetched = (marks[0], marks[-1]) if marks else (self.jobs, self.jobs)
        self.steps = self.jobs * lines
        self.slots = self.xr.shape[0]
        self.lag = SKEW * (lines - 1) + 2
        ctx, tp = lax.axis_index("ctx"), lax.axis_index("tp")
        self.z, self.side = ctx // 2, lax.rem(ctx, 2)
        self.partner = (self.z * 2 + 1 - self.side, tp)
        self.left, self.right = (ctx - 2, tp), (ctx + 2, tp)

    @staticmethod
    def scratch(lines, rows):
        slots = AHEAD + SKEW * (lines - 1) + 4
        chunk = (rows, COLS)
        return [
            pltpu.VMEM((AHEAD, *chunk), jnp.bfloat16),
            pltpu.VMEM((slots, *chunk), jnp.bfloat16),
            pltpu.VMEM((DEPTH, lines + 1, *chunk), jnp.bfloat16),
            pltpu.VMEM((STAGES, *chunk), jnp.float32),
            pltpu.VMEM((STAGES, COLS, rows), jnp.float32),
            pltpu.VMEM(chunk, jnp.bfloat16),
            pltpu.VMEM((4, *chunk), jnp.bfloat16),
            pltpu.SemaphoreType.DMA((AHEAD,)),
            pltpu.SemaphoreType.DMA((slots,)),
            pltpu.SemaphoreType.DMA((slots,)),
            pltpu.SemaphoreType.DMA((DEPTH, lines + 1)),
            pltpu.SemaphoreType.DMA((STAGES,)),
            pltpu.SemaphoreType.DMA((4,)),
            pltpu.SemaphoreType.REGULAR,
            pltpu.SemaphoreType.REGULAR,
            pltpu.SemaphoreType.REGULAR,
        ]

    def sends(self, f):
        job = f // self.lines
        found = (job < self.fetched[0]) | (job > self.fetched[1]) | (lax.rem(f, self.lines) == 0)
        for pair in self.later:
            found = found & (job != pair[0]) & (job != pair[1])
        if self.alone:
            found = found & ((job < self.alone[0]) | (job > self.alone[1]))
        return found

    def peers(self):
        return [(None, self.partner), (self.z > 0, self.left), (self.z < self.lines - 1, self.right)]

    def x_copy(self, f):
        slot, to = lax.rem(f, AHEAD), lax.rem(f, self.slots)
        return pltpu.make_async_remote_copy(
            src_ref=self.xs.at[slot], dst_ref=self.xr.at[to], send_sem=self.s_xs.at[slot],
            recv_sem=self.s_xr.at[to], device_id=self.partner, device_id_type=MESH)

    def z_copy(self, f, to, device):
        slot, level = lax.rem(f, self.slots), lax.rem(f // self.lines, DEPTH)
        return pltpu.make_async_remote_copy(
            src_ref=self.xr.at[slot], dst_ref=self.zb.at[level, to], send_sem=self.s_zs.at[slot],
            recv_sem=self.s_zr.at[level, to], device_id=device, device_id_type=MESH)

    def out_copies(self, job, act):
        slot = lax.rem(job, STAGES)
        for there, turn, place in self.outs(job):
            @pl.when(there)
            def _():
                source = self.turned if turn else self.stage
                act(pltpu.make_async_copy(source.at[slot], place, self.s_out.at[slot]))

    def out_start(self, job):
        slot = lax.rem(job, STAGES)
        for there, turn, _ in self.outs(job):
            if turn:
                @pl.when(there)
                def _():
                    self.turned[slot] = self.stage[slot].T
        self.out_copies(job, lambda copy: copy.start())

    def out_wait(self, job):
        self.out_copies(job, lambda copy: copy.wait())

    def swap_copy(self, n):
        return pltpu.make_async_remote_copy(
            src_ref=self.swap.at[2 * n], dst_ref=self.swap.at[2 * n + 1], send_sem=self.s_swap.at[2 * n],
            recv_sem=self.s_swap.at[2 * n + 1], device_id=self.partner, device_id_type=MESH)

    def send(self, f, group, job0, fresh):
        _, part, kind = group
        is_prefix = kind == "p"
        if not fresh:
            @pl.when(self.sends(f - AHEAD))
            def _():
                self.x_copy(f).wait_send()

            @pl.when(f >= self.slots)
            def _():
                pl.semaphore_wait(self.c_x, 1)

        if kind == "t":
            return

        @pl.when(self.sends(f))
        def _():
            owner = lax.rem(f, self.lines)
            value = part(f // self.lines - job0, None if is_prefix else owner * 2 + 1 - self.side)
            self.xs[lax.rem(f, AHEAD)] = value.astype(jnp.bfloat16)
            self.x_copy(f).start()

    def receive(self, f, group, job0):
        _, part, kind = group
        is_prefix = kind == "p"
        job, owner, slot = f // self.lines, lax.rem(f, self.lines), lax.rem(f, self.slots)
        came = self.sends(f)

        if kind != "t":
            @pl.when(came)
            def _():
                self.x_copy(f).wait_recv()
                if is_prefix:
                    self.kept[...] = self.xr[slot]

        block = owner * 2 + self.side
        if is_prefix:
            mine, theirs = self.prefix[0][block], self.prefix[1][block]
            total = part(job - job0, None) * mine + self.kept[...].astype(jnp.float32) * theirs
        elif kind == "t":
            total = part(job - job0, block)
        else:
            @pl.when(jnp.logical_not(came))
            def _():
                self.xr[slot] = jnp.zeros(self.xr.shape[1:], jnp.bfloat16)

            for pair in self.later:
                block = jnp.where(job == pair[0], owner * 2 + 1 - self.side, block)
            total = part(job - job0, block) + self.xr[slot].astype(jnp.float32)

        @pl.when(owner != self.z)
        def _():
            self.xr[slot] = total.astype(jnp.bfloat16)

        @pl.when(owner == self.z)
        def _():
            @pl.when(job >= STAGES)
            def _():
                self.out_wait(job - STAGES)
            self.stage[lax.rem(job, STAGES)] = total

    def add(self, f, index):
        job = f // self.lines
        slot, level = lax.rem(f, self.slots), lax.rem(job, DEPTH)

        @pl.when(lax.rem(f, self.lines) == self.z)
        def _():
            self.stage[lax.rem(job, STAGES)] += self.zb[level, index].astype(jnp.float32)

        @pl.when(lax.rem(f, self.lines) != self.z)
        def _():
            self.xr[slot] = (self.xr[slot].astype(jnp.float32) + self.zb[level, index].astype(jnp.float32)).astype(jnp.bfloat16)

    def flow(self, t):
        lines, z = self.lines, self.z
        f = t - SKEW * z
        owner = lax.rem(f + lines * SKEW * lines, lines)

        @pl.when((f >= 0) & (f < self.steps) & (owner >= z))
        def _():
            @pl.when(z > 0)
            def _():
                self.z_copy(f, owner, self.left).wait_recv()
                self.add(f, owner)
                pl.semaphore_signal(self.c_right, inc=1, device_id=self.left, device_id_type=MESH)

            @pl.when(owner > z)
            def _():
                @pl.when(f >= DEPTH * lines)
                def _():
                    pl.semaphore_wait(self.c_right, 1)
                self.z_copy(f, owner, self.right).start()

        g = t - SKEW * (lines - 1 - z)
        owner2 = lax.rem(g + lines * SKEW * lines, lines)

        @pl.when((g >= 0) & (g < self.steps) & (owner2 <= z))
        def _():
            @pl.when(z < lines - 1)
            def _():
                index = jnp.where(owner2 == z, lines, owner2)
                self.z_copy(g, index, self.right).wait_recv()
                self.add(g, index)
                pl.semaphore_signal(self.c_left, inc=1, device_id=self.right, device_id_type=MESH)

            @pl.when(owner2 < z)
            def _():
                @pl.when(g >= DEPTH * lines)
                def _():
                    pl.semaphore_wait(self.c_left, 1)
                self.z_copy(g, jnp.where(owner2 == z - 1, lines, owner2), self.left).start()

        h = t - SKEW * (lines - 1)

        @pl.when((h >= 0) & (h < self.steps) & (lax.rem(h + lines * SKEW * lines, lines) == z))
        def _():
            job = h // lines
            stage = lax.rem(job, STAGES)
            for n, pair in enumerate(self.later):
                @pl.when(job == pair[0])
                def _():
                    self.swap[2 * n] = self.stage[stage].astype(jnp.bfloat16)
                    self.swap_copy(n).start()

                @pl.when(job == pair[1])
                def _():
                    self.swap_copy(n).wait()
                    self.stage[stage] += self.swap[2 * n + 1].astype(jnp.float32)
            if self.prefix is not None:
                target, rows = self.prefix[2], self.stage.shape[1]

                @pl.when((job >= self.fetched[0]) & (job <= self.fetched[1]))
                def _():
                    span = pl.ds(pl.multiple_of((job - self.fetched[0]) * rows, rows), rows)
                    target[span] = self.stage[stage]
            self.out_start(job)

        d = t - self.lag

        @pl.when((d >= 0) & (d < self.steps))
        def _():
            @pl.when(lax.rem(d + lines * (SKEW * lines + 2), lines) != z)
            def _():
                self.z_copy(d, 0, self.left).wait_send()
            pl.semaphore_signal(self.c_x, inc=1, device_id=self.partner, device_id_type=MESH)

    def find(self, f):
        job = 0
        for group in self.groups:
            if f < (job + group[0]) * self.lines:
                return group, job
            job += group[0]
        return None

    def pieces(self, lo, hi):
        cuts, job = {lo, hi}, 0
        for group in self.groups:
            job += group[0]
            cuts |= {job * self.lines, job * self.lines - AHEAD}
        cuts = sorted(c for c in cuts if lo <= c <= hi)
        return zip(cuts[:-1], cuts[1:])

    def start(self):
        for lo, hi in self.pieces(0, AHEAD):
            here = self.find(lo)
            lax.fori_loop(lo, hi, lambda f, _, here=here: (self.send(f, *here, True), 0)[1], 0)

    def run(self, lo, hi):
        for a, b in self.pieces(lo, min(hi, self.steps)):
            here, ahead = self.find(a), self.find(a + AHEAD)

            def body(f, _, here=here, ahead=ahead):
                self.receive(f, *here)
                self.flow(f)
                if ahead is not None:
                    self.send(f + AHEAD, *ahead, False)
                return 0

            lax.fori_loop(a, b, body, 0)
        if hi > self.steps:
            lax.fori_loop(max(lo, self.steps), hi, lambda t, _: (self.flow(t), 0)[1], 0)

    def run_some(self, lo, count):
        here = self.find(0)

        def body(f, _):
            self.receive(f, *here)
            self.flow(f)

            @pl.when(f + AHEAD < self.steps)
            def _():
                self.send(f + AHEAD, *here, False)
            return 0

        lax.fori_loop(lo, lo + count, body, 0)

    def finish(self, lo):
        lines, z = self.lines, self.z
        self.run(lo, self.steps + self.lag)

        def drain(f, _):
            @pl.when(self.sends(f))
            def _():
                self.x_copy(f).wait_send()
            return 0

        lax.fori_loop(self.steps - AHEAD, self.steps, drain, 0)
        for job in range(self.jobs - STAGES, self.jobs):
            self.out_wait(job)
        pl.semaphore_wait(self.c_x, min(self.slots, self.steps))

        @pl.when(z < lines - 1)
        def _():
            pl.semaphore_wait(self.c_right, DEPTH * (lines - 1 - z))

        @pl.when(z > 0)
        def _():
            pl.semaphore_wait(self.c_left, DEPTH * z)


def meet(peers):
    barrier = pltpu.get_barrier_semaphore()
    count = 0
    for there, device in peers:
        if there is None:
            pl.semaphore_signal(barrier, inc=1, device_id=device, device_id_type=MESH)
            count += 1
        else:
            @pl.when(there)
            def _():
                pl.semaphore_signal(barrier, inc=1, device_id=device, device_id_type=MESH)
            count += jnp.where(there, 1, 0)
    pl.semaphore_wait(barrier, count)
class Quad:
    def __init__(self, refs, rows, height):
        (self.tmp, self.cs, self.cr, self.ys, self.yr, self.acc, self.s_c, self.r_c, self.s_y, self.r_y,
         self.s_g, self.r_g) = refs
        ctx, tp = lax.axis_index("ctx"), lax.axis_index("tp")
        self.y, self.core, self.tp = tp // 2, lax.rem(tp, 2), tp
        self.across = (ctx, self.y * 2 + 1 - self.core)
        self.over = (ctx, (1 - self.y) * 2 + self.core)
        self.head, self.rest = PREFIX // 4, (rows - PREFIX) // 4
        self.tiles = self.cs.shape[1]
        self.height = height

    @staticmethod
    def scratch(rows, width):
        tiles = width // COLS
        return [
            pltpu.VMEM((2, rows, COLS), jnp.float32),
            pltpu.VMEM((2, tiles, rows, COLS), jnp.bfloat16),
            pltpu.VMEM((2, tiles, rows, COLS), jnp.bfloat16),
            pltpu.VMEM((tiles, rows, COLS), jnp.bfloat16),
            pltpu.VMEM((tiles, rows, COLS), jnp.bfloat16),
            pltpu.VMEM((rows, width), jnp.float32),
            pltpu.SemaphoreType.DMA((2, tiles)),
            pltpu.SemaphoreType.DMA((2, tiles)),
            pltpu.SemaphoreType.DMA((tiles,)),
            pltpu.SemaphoreType.DMA((tiles,)),
            pltpu.SemaphoreType.DMA((2, 3, 2)),
            pltpu.SemaphoreType.DMA((2, 3, 2)),
        ]

    def peers(self):
        return [(None, self.across), (None, self.over)]

    def spans(self, quarter):
        return [
            pl.ds(pl.multiple_of(quarter * self.head, 16), self.head),
            pl.ds(pl.multiple_of(PREFIX + quarter * self.rest, 16), self.rest),
        ]

    def rows_of(self, ref, quarter):
        return jnp.concatenate([ref[span] for span in self.spans(quarter)], axis=0)

    def half_of(self, ref, half):
        return jnp.concatenate([self.rows_of(ref, half * 2), self.rows_of(ref, half * 2 + 1)], axis=0)

    def c_copy(self, k, n):
        return pltpu.make_async_remote_copy(
            src_ref=self.cs.at[k, n, : self.height], dst_ref=self.cr.at[k, n, : self.height], send_sem=self.s_c.at[k, n],
            recv_sem=self.r_c.at[k, n], device_id=self.across, device_id_type=MESH)

    def y_copy(self, n):
        return pltpu.make_async_remote_copy(
            src_ref=self.ys.at[n, : self.height], dst_ref=self.yr.at[n, : self.height], send_sem=self.s_y.at[n],
            recv_sem=self.r_y.at[n], device_id=self.over, device_id_type=MESH)

    def columns(self, n):
        return pl.ds(pl.multiple_of(n * COLS, COLS), COLS)

    def split(self, value, k, n):
        rows = self.height
        self.tmp[0, :rows] = value[:rows]
        self.tmp[1, :rows] = value[rows:]
        self.cs[k, n, :rows] = self.tmp[1 - self.core, :rows].astype(jnp.bfloat16)
        self.c_copy(k, n).start()
        self.acc[:rows, self.columns(n)] = self.tmp[self.core, :rows]

    def relay(self, n):
        self.c_copy(0, n).wait_recv()
        rows = self.height
        total = self.acc[:rows, self.columns(n)] + self.cr[0, n, :rows].astype(jnp.float32)
        self.ys[n, :rows] = total.astype(jnp.bfloat16)
        self.y_copy(n).start()

    def scatter_send(self, chunk):
        def far(n, _):
            self.split(chunk(1 - self.y, n), 0, n)

            @pl.when(n > 0)
            def _():
                self.relay(n - 1)
            return 0

        lax.fori_loop(0, self.tiles, far, 0)
        self.relay(self.tiles - 1)

        def near(n, _):
            self.split(chunk(self.y, n), 1, n)
            return 0

        lax.fori_loop(0, self.tiles, near, 0)

    def scatter_add(self, n):
        self.c_copy(1, n).wait_recv()
        self.y_copy(n).wait_recv()
        rows = self.height
        came = self.cr[1, n, :rows].astype(jnp.float32) + self.yr[n, :rows].astype(jnp.float32)
        self.acc[:rows, self.columns(n)] += came

    def scatter_done(self):
        for n in range(self.tiles):
            self.c_copy(0, n).wait_send()
            self.c_copy(1, n).wait_send()
            self.y_copy(n).wait_send()

    def g_copy(self, full, k, s, quarter, device, turn):
        span = self.spans(quarter)[s]
        return pltpu.make_async_remote_copy(
            src_ref=full.at[span], dst_ref=full.at[span], send_sem=self.s_g.at[turn, k, s],
            recv_sem=self.r_g.at[turn, k, s], device_id=device, device_id_type=MESH)

    def gather_send(self, full, turn=0):
        for s in range(2):
            self.g_copy(full, 0, s, self.tp, self.over, turn).start()
        for s in range(2):
            self.g_copy(full, 1, s, self.tp, self.across, turn).start()

    def gather_near(self, full, turn=0):
        for s in range(2):
            self.g_copy(full, 1, s, self.y * 2 + 1 - self.core, self.across, turn).wait_recv()

    def gather_pass(self, full, turn=0):
        other = (1 - self.y) * 2 + self.core
        for s in range(2):
            self.g_copy(full, 0, s, other, self.over, turn).wait_recv()
            self.g_copy(full, 2, s, other, self.across, turn).start()

    def gather_far(self, full, turn=0):
        for s in range(2):
            self.g_copy(full, 2, s, (1 - self.y) * 2 + 1 - self.core, self.across, turn).wait_recv()

    def gather_done(self, full, turn=0):
        other = (1 - self.y) * 2 + self.core
        for s in range(2):
            self.g_copy(full, 0, s, self.tp, self.over, turn).wait_send()
            self.g_copy(full, 1, s, self.tp, self.across, turn).wait_send()
            self.g_copy(full, 2, s, other, self.across, turn).wait_send()


def nt(left, right):
    return lax.dot_general(left, right, (((1,), (1,)), ((), ())), preferred_element_type=jnp.float32)


def normed(values_in):
    centred = values_in - jnp.mean(values_in, axis=1, keepdims=True)
    scale = lax.rsqrt(jnp.mean(centred * centred, axis=1, keepdims=True) + EPSILON)
    return centred * scale, scale


def gelu_pair(pre):
    slope = (2.0 / math.pi) ** 0.5
    square = pre * pre
    bent = jnp.tanh(slope * (pre + 0.044715 * (square * pre)))
    half = 0.5 * (1.0 + bent)
    return pre * half, half + 0.5 * pre * (1.0 - bent * bent) * (slope * (1.0 + 3 * 0.044715 * square))


def column_sum(values_in):
    return jnp.sum(values_in, axis=0, keepdims=True)


def front_kernel(early, *refs):
    (att, w_out, x_hbm, cot_hbm, act, w1_hbm, w2_hbm, bias, gain, shift, fc1_bias,
     mid, full, grad, hid, d_pre, vec, theirs, *scratch) = refs
    quad_refs, scratch = scratch[:12], scratch[12:]
    x, w1, w2, d_hid, some, loads, s_x, r_x = scratch
    rows, width = full.shape
    quad = Quad(quad_refs, rows, rows // 4)
    spans = quad.spans(quad.tp)

    def load(n, source, target):
        copy = pltpu.make_async_copy(source, target, loads.at[n])
        copy.start()
        return copy

    cot_copy = load(0, cot_hbm, grad)
    w2_copy = load(1, w2_hbm, w2)
    x_copies = [load(2, x_hbm.at[spans[0]], x.at[: quad.head]), load(3, x_hbm.at[spans[1]], x.at[quad.head :])]
    w1_copy = load(4, w1_hbm, w1)
    ctx, tp = lax.axis_index("ctx"), lax.axis_index("tp")
    side = lax.rem(ctx, 2)
    partner = (ctx + 1 - 2 * side, tp)
    meet(quad.peers() + ([(None, partner)] if early else []))

    def half_copy(o):
        step = width // (2 * early)
        source = grad.at[:, pl.ds(pl.multiple_of((o * 2 + 1 - side) * step, step), step)]
        return pltpu.make_async_remote_copy(
            src_ref=source, dst_ref=theirs.at[:, o * step : (o + 1) * step], send_sem=s_x.at[o], recv_sem=r_x.at[o],
            device_id=partner, device_id_type=MESH)

    quad.scatter_send(lambda half, n: jnp.dot(quad.half_of(att, half), w_out[:, quad.columns(n)], preferred_element_type=jnp.float32))
    cot_copy.wait()
    vec[...] = jnp.zeros(vec.shape, jnp.float32)
    size = 32

    def gate(i, _):
        span = pl.ds(pl.multiple_of(i * size, size), size)
        low = (act[span] * grad[span].astype(jnp.float32)).astype(jnp.bfloat16)
        grad[span] = low
        vec[5:6] += column_sum(low.astype(jnp.float32)) * 0.25
        return 0

    lax.fori_loop(0, rows // size, gate, 0)
    for o in range(early):
        half_copy(o).start()
    w2_copy.wait()
    tiles = hid.shape[1] // COLS

    def d_hidden(n, _):
        d_hid[:, quad.columns(n)] = nt(grad[...], w2[quad.columns(n), :])
        return 0

    lax.fori_loop(0, tiles, d_hidden, 0)
    for copy in x_copies:
        copy.wait()
    lax.fori_loop(0, quad.tiles, lambda n, _: (quad.scatter_add(n), 0)[1], 0)

    def norm_rows(i, _):
        first = quad.head // size
        start = jnp.where(i < first, quad.tp * quad.head + i * size, PREFIX + quad.tp * quad.rest + (i - first) * size)
        whole, own = (pl.ds(pl.multiple_of(s, size), size) for s in (start, i * size))
        middle = x[own].astype(jnp.float32) + act[whole] * (quad.acc[own] + bias[...])
        mid[own] = middle
        full[whole] = (normed(middle)[0] * gain[...] + shift[...]).astype(jnp.bfloat16)
        return 0

    lax.fori_loop(0, quad.height // size, norm_rows, 0)
    quad.gather_send(full)

    def ffn(half):
        some[...] = quad.half_of(full, half)
        places = quad.spans(half * 2) + quad.spans(half * 2 + 1)

        def tile(n, _):
            cols = quad.columns(n)
            pre = jnp.dot(some[...], w1[:, cols], preferred_element_type=jnp.float32) + fc1_bias[:, cols]
            value, slope = gelu_pair(pre)
            value = value.astype(jnp.bfloat16)
            start = 0
            for place in places:
                end = start + place.size
                hid[place, cols] = value[start:end]
                change = (d_hid[place, cols] * slope[start:end]).astype(jnp.bfloat16)
                d_pre[place, cols] = change
                vec[6:7, cols] += column_sum(change.astype(jnp.float32))
                start = end
            return 0

        lax.fori_loop(0, tiles, tile, 0)

    quad.gather_near(full)
    w1_copy.wait()
    ffn(quad.y)
    quad.gather_pass(full)
    quad.gather_far(full)
    ffn(1 - quad.y)
    quad.gather_done(full)
    quad.scatter_done()
    for o in range(early):
        half_copy(o).wait()


def front_call(early, att, w_out, x, cot, act, w1, w2, bias, gain, shift, fc1_bias):
    rows, width = x.shape
    own, hidden = rows // 4, w1.shape[1]
    vm, hbm = (pl.BlockSpec(memory_space=s) for s in (pltpu.VMEM, pl.ANY))
    bf, f4, shape = jnp.bfloat16, jnp.float32, jax.ShapeDtypeStruct
    return pl.pallas_call(
        functools.partial(front_kernel, early),
        out_shape=(
            shape((own, width), f4),
            shape((rows, width), bf),
            shape((rows, width), bf),
            shape((rows, hidden), bf),
            shape((rows, hidden), bf),
            shape((8, width), f4),
            shape((rows, width // 2), bf),
        ),
        in_specs=[vm] * 2 + [hbm] * 2 + [vm] + [hbm] * 2 + [vm] * 4,
        out_specs=[vm] * 6 + [hbm],
        scratch_shapes=Quad.scratch(own, width)
        + [
            pltpu.VMEM((own, width), bf),
            pltpu.VMEM(w1.shape, bf),
            pltpu.VMEM(w2.shape, bf),
            pltpu.VMEM((rows, hidden), f4),
            pltpu.VMEM((2 * own, width), bf),
            pltpu.SemaphoreType.DMA((5,)),
            pltpu.SemaphoreType.DMA((max(early, 1),)),
            pltpu.SemaphoreType.DMA((max(early, 1),)),
        ],
        compiler_params=pltpu.CompilerParams(collective_id=1, has_side_effects=True, vmem_limit_bytes=64 * 2**20),
    )(att, w_out, x, cot, act, w1, w2, bias[None], gain[None], shift[None], fc1_bias[None])
def tn(left, right):
    return lax.dot_general(left, right, (((0,), (0,)), ((), ())), preferred_element_type=jnp.float32)


def nn(left, right):
    return jnp.dot(left, right, preferred_element_type=jnp.float32)


def lane_mask(rows, head):
    lane = lax.broadcasted_iota(jnp.int32, (rows, 2 * HEAD), 1)
    return (lane < HEAD) if head == 0 else (lane >= HEAD)


def scores_of(keys, query, bias):
    scores = nt(keys, query)
    count = scores.shape[0]
    row = lax.broadcasted_iota(jnp.int32, (PREFIX, PREFIX), 0)
    col = lax.broadcasted_iota(jnp.int32, (PREFIX, PREFIX), 1)
    parts = [scores[:PREFIX] + bias]
    if count > 2 * PREFIX:
        parts.append(scores[PREFIX : count - PREFIX])
    parts.append(jnp.where(row <= col, scores[count - PREFIX :], NEGATIVE))
    return jnp.concatenate(parts, axis=0)


def attend_back(p, bias, q_ref, k_ref, v_ref, l_ref, g_ref, d_ref, room):
    rows, width = q_ref.shape
    blocks = rows // PREFIX
    base = pl.multiple_of(p * 2 * HEAD, 2 * HEAD)
    lanes = pl.ds(base, 2 * HEAD)
    sums = jnp.zeros((1, 2 * HEAD), jnp.float32)
    for r in reversed(range(blocks)):
        count, own = (r + 2) * PREFIX, slice(r * PREFIX, (r + 1) * PREFIX)
        query, grad, keys, values = q_ref[own, lanes], g_ref[own, lanes], k_ref[:count, lanes], v_ref[:count, lanes]
        d_queries, d_keys, d_values = [], None, None
        for e in range(2):
            mask = lane_mask(PREFIX, e)
            query_e = jnp.where(mask, query, jnp.zeros_like(query))
            grad_e = jnp.where(mask, grad, jnp.zeros_like(grad))
            probs = jnp.exp(scores_of(keys, query_e, bias) - l_ref[p, e : e + 1, own])
            d_probs = nt(values, grad_e)
            inner = jnp.sum(probs * d_probs, axis=0, keepdims=True)
            d_scores = (probs * (d_probs - inner)).astype(jnp.bfloat16)
            keys_e, values_e = nn(d_scores, query_e), nn(probs.astype(jnp.bfloat16), grad_e)
            d_keys = keys_e if d_keys is None else d_keys + keys_e
            d_values = values_e if d_values is None else d_values + values_e
            d_queries.append(tn(d_scores, keys))
        d_query = jnp.where(lane_mask(PREFIX, 0), d_queries[0], d_queries[1]) * HEAD ** (-0.5)
        sums += jnp.sum(d_query, axis=0, keepdims=True)
        d_ref[(r + 1) * PREFIX : (r + 2) * PREFIX, lanes] = d_query.astype(jnp.bfloat16)
        for n in range(r + 2):
            for at, sums_of in ((n, d_keys), (blocks + 1 + n, d_values)):
                place, term = slice(at * 2 * HEAD, (at + 1) * 2 * HEAD), sums_of[n * PREFIX : (n + 1) * PREFIX]
                if r == blocks - 1:
                    room[:PREFIX, place] = term
                else:
                    room[:PREFIX, place] += term
    d_ref[:PREFIX, lanes] = jnp.zeros((PREFIX, 2 * HEAD), jnp.bfloat16)
    value_sums = jnp.zeros((1, 2 * HEAD), jnp.float32)
    for n in range(blocks + 1):
        span = slice(n * PREFIX, (n + 1) * PREFIX)
        for m, at in ((1, n), (2, blocks + 1 + n)):
            total = room[:PREFIX, at * 2 * HEAD : (at + 1) * 2 * HEAD]
            d_ref[span, pl.ds(pl.multiple_of(base + m * width, 2 * HEAD), 2 * HEAD)] = total.astype(jnp.bfloat16)
            if m == 2:
                value_sums += column_sum(total)
    return sums, value_sums


def own_block(quad, i, size):
    first = quad.head // size
    start = jnp.where(i < first, quad.tp * quad.head + i * size, PREFIX + quad.tp * quad.rest + (i - first) * size)
    return pl.ds(pl.multiple_of(start, size), size), pl.ds(pl.multiple_of(i * size, size), size)


def norm_back(grad, source, gain):
    unit, scale = normed(source)
    scaled = grad * gain
    mean = jnp.mean(scaled, axis=1, keepdims=True)
    slope = jnp.mean(scaled * unit, axis=1, keepdims=True)
    return scale * (scaled - mean - unit * slope), grad * unit


def product_part(left, right, tile, turned, rows):
    def part(j, block):
        cols = pl.ds(pl.multiple_of(tile(j) * COLS, COLS), COLS)
        span = pl.ds(pl.multiple_of(block * rows, rows), rows)
        if turned:
            return nn(left[span, :], right[:, cols])
        return tn(left[:, span], right[:, cols])

    return part


def pick(table, j):
    found = table[0]
    for n, entry in enumerate(table[1:]):
        found = jnp.where(j == n + 1, entry, found)
    return found


class Wide(Quad):
    def rows_of(self, ref, quarter):
        own = [pl.ds(pl.multiple_of(span.start + PREFIX, 16), span.size) for span in self.spans(quarter)]
        return jnp.concatenate([ref[span] for span in [self.spans(quarter)[0]] + own], axis=0)


def back_kernel(lines, turned, *refs):
    (g_hbm, h2_hbm, hid_hbm, dpre_hbm, w1_hbm, w_qkv_hbm, w2_hbm, wo_hbm, h_hbm, att_hbm, mid_hbm, cot_hbm, x_hbm, gp_hbm,
     act, gain1, gain2, ffn_bias, bias, weight, theirs, q, k, v, lse, vec_in,
     fc2_out, fc1_out, out_grad, qkv_grad, in_hbm, act_hbm, dmid_hbm, dh_hbm, land_hbm, vec, *scratch) = refs
    ring_refs, scratch = scratch[:16], scratch[16:]
    quad_refs, scratch = scratch[:12], scratch[12:]
    (x0, x1, y0, y1, weights, mid, own_in, full, d_att, d_all, fresh, back, v_send, v_recv, g_theirs, tile_in,
     loads, stores, s_v, r_v, s_t, r_t, c_over) = scratch
    rows, width = full.shape
    quad, wide = Quad(quad_refs, rows, rows // 4), Wide(quad_refs, rows, (rows + PREFIX) // 4)
    own_rows, depth = quad.height, q.shape[1]
    tiles, cols = y0.shape[1] // COLS, depth // COLS
    block_rows = ring_refs[0].shape[1]
    extra = fresh.shape[0] // block_rows
    order1 = [*range(tiles - 2), tiles - 1, tiles - 2]
    later = ((0, 2 * tiles - 1),)
    base = 2 * tiles + 1 + extra
    g_part = x0.at[:, :rows] if turned else x0.at[:rows]
    columns = lambda n: pl.ds(pl.multiple_of(n * COLS, COLS), COLS)

    def tile_copy(n):
        return pltpu.make_async_remote_copy(
            src_ref=y0.at[:, n * COLS : (n + 1) * COLS], dst_ref=land_hbm.at[n], send_sem=s_t.at[n], recv_sem=r_t.at[n],
            device_id=ring.partner, device_id_type=MESH)

    def tile_part(j, block):
        @pl.when(block < 2)
        def _():
            for n in range(tiles):
                @pl.when(j == n)
                def _():
                    tile_copy(n).wait_recv()
            fetch = pltpu.make_async_copy(land_hbm.at[j], tile_in, loads.at[11])
            fetch.start()
            fetch.wait()

        span = pl.ds(pl.multiple_of(block * block_rows, block_rows), block_rows)
        side_span = pl.ds(pl.multiple_of(block // 2 * block_rows, block_rows), block_rows)
        return tn(g_part[:, span], y0[:, columns(j)]) + tn(g_theirs[:, side_span], tile_in[...])

    def prefix_part(j, block):
        return fresh[pl.ds(pl.multiple_of(j * block_rows, block_rows), block_rows)]

    def outs(job):
        local = job - tiles - 1
        head = jnp.maximum(job - base - cols, 0)
        place2, place1 = columns(jnp.clip(job - 1, 0, tiles - 1)), columns(pick(order1, local))
        is2 = (job > 0) & (job <= tiles)
        is1 = (job > tiles) & (job <= 2 * tiles)
        is_out = (job >= base) & (job < base + cols)
        out_span = columns(jnp.clip(job - base, 0, cols - 1))
        return [
            (is2, True, fc2_out.at[place2]),
            (is1, False, fc1_out.at[:, place1]),
            (is_out, True, out_grad.at[out_span]),
            (job >= base + cols, False, qkv_grad.at[head // cols, :, columns(lax.rem(head, cols))]),
        ]

    fc2_part = product_part(g_part, y0, lambda j: j, turned, block_rows) if turned else tile_part
    groups = [
        (1, product_part(x1, y1, lambda j: tiles - 1, turned, block_rows), "x"),
        (tiles, fc2_part, "x" if turned else "t"),
        (tiles, product_part(x1, y1, lambda j: pick(order1, j), turned, block_rows), "x"),
        (extra, prefix_part, "p"),
        (cols, product_part(x1 if turned else full, d_att, lambda j: j, turned, block_rows), "x"),
        (3 * cols, product_part(x0, d_all, lambda j: j, turned, block_rows), "x"),
    ]
    ring = Ring(lines, groups, ring_refs, outs, later, (weight, theirs, back))

    def load(n, source, target):
        return pltpu.make_async_copy(source, target, loads.at[n])

    def store(n, source, target):
        return pltpu.make_async_copy(source, target, stores.at[n])

    def begin(*copies):
        for copy in copies:
            copy.start()

    def end(*copies):
        for copy in copies:
            copy.wait()

    spans = quad.spans(quad.tp)
    first = [load(2, dpre_hbm, y1), load(4, h2_hbm, x1), load(0, hid_hbm, y0), load(1, g_hbm, g_part)]
    second = [load(3, w1_hbm, weights)]
    if not turned:
        second.append(load(12, gp_hbm, g_theirs))
    third = [
        load(5, mid_hbm, mid),
        load(6, cot_hbm.at[spans[0]], own_in.at[: quad.head]),
        load(7, cot_hbm.at[spans[1]], own_in.at[quad.head :]),
    ]
    begin(*first, *second, *third)
    ctx, tp = lax.axis_index("ctx"), lax.axis_index("tp")
    swaps, bit = [quad.across, quad.over], 1
    while bit < 2 * lines:
        swaps.append((ctx + bit - 2 * bit * lax.rem(ctx // bit, 2), tp))
        bit *= 2
    meet(ring.peers() + quad.peers() + [(None, device) for device in swaps[4:]])

    def swap(n):
        return pltpu.make_async_remote_copy(
            src_ref=v_send.at[n], dst_ref=v_recv.at[n], send_sem=s_v.at[n], recv_sem=r_v.at[n],
            device_id=swaps[n], device_id_type=MESH)

    def swap_start(n):
        v_send[n] = vec[...]
        swap(n).start()

    def swap_end(n):
        swap(n).wait()
        if n < 2:
            vec[:6] += v_recv[n, :6]
        else:
            vec[...] += v_recv[n]

    def add_all(group):
        lax.fori_loop(0, group.tiles, lambda n, _: (group.scatter_add(n), 0)[1], 0)

    end(*first)
    if not turned:
        for n in range(tiles):
            tile_copy(n).start()
    ring.start()
    end(*second)
    quad.scatter_send(lambda part, n: nt(quad.half_of(y1, part), weights[quad.columns(n), :]))
    wo_copy = load(3, wo_hbm, weights.at[:depth])
    wo_copy.start()
    end(*third)
    ring.run(0, 5)
    add_all(quad)
    vec[...] = vec_in[...]
    size = 32

    def middle_rows(i, _):
        whole, own = own_block(quad, i, size)
        grad = quad.acc[own]
        change, gain_terms = norm_back(grad, mid[own], gain2[...])
        d_middle = own_in[own].astype(jnp.float32) + change
        quad.acc[own] = d_middle
        low = (act[whole] * d_middle).astype(jnp.bfloat16)
        full[whole] = low
        vec[2:3] += column_sum(low.astype(jnp.float32))
        vec[3:4] += column_sum(gain_terms)
        vec[4:5] += column_sum(grad)
        return 0

    lax.fori_loop(0, own_rows // size, middle_rows, 0)
    quad.gather_send(full)
    keep = store(0, quad.acc.at[:own_rows], dmid_hbm)
    x_copies = [load(6, x_hbm.at[spans[0]], own_in.at[: quad.head]), load(7, x_hbm.at[spans[1]], own_in.at[quad.head :])]
    begin(keep, *x_copies)
    ring.run(5, 10)
    quad.gather_near(full)
    quad.gather_pass(full)
    quad.gather_far(full)
    wo_copy.wait()

    def attended_rows(i, _):
        span = pl.ds(pl.multiple_of(i * PREFIX, PREFIX), PREFIX)
        d_att[span] = nt(full[span], weights[:depth, :]).astype(jnp.bfloat16)
        return 0

    lax.fori_loop(0, rows // PREFIX, attended_rows, 0)
    heads = [load(8 + m, w_qkv_hbm.at[m], weights.at[:, m * depth : (m + 1) * depth]) for m in range(3)]
    begin(*heads)
    keep.wait()
    pairs = depth // (2 * HEAD)

    now = 10
    for p in range(pairs):
        sums, value_sums = attend_back(p, bias[0, 0], q, k, v, lse, d_att, d_all, quad.acc)
        start = p * 2 * HEAD
        vec[7:8, start : start + 2 * HEAD] = sums
        vec[7:8, start + depth : start + depth + 2 * HEAD] = value_sums
        ring.run(now, now + 2)
        now += 2
    att_copy = load(2, att_hbm, d_att)
    att_copy.start()
    quad.gather_done(full)
    quad.scatter_done()
    end(*heads)
    wide.scatter_send(lambda part, n: nt(wide.half_of(d_all, part), weights[wide.columns(n), : 3 * depth]))
    w2_copy = load(3, w2_hbm, weights)
    w2_copy.start()
    free0, free1 = (tiles + 1) * lines, (2 * tiles + 1) * lines
    ring.run(now, free0)
    h_copy = load(1, h_hbm, x0)
    h_copy.start()
    ring.run(free0, free0 + 2)
    add_all(wide)
    pl.semaphore_signal(c_over, inc=1, device_id=quad.over, device_id_type=MESH)
    for n in range(wide.tiles):
        fresh[n * wide.head : (n + 1) * wide.head] = wide.acc[: wide.head, n * COLS : (n + 1) * COLS]
    dh_copy = store(1, wide.acc.at[pl.ds(wide.head, own_rows)], dh_hbm)
    dh_copy.start()
    att_copy.wait()
    ring.run(free0 + 2, free1 - AHEAD)
    h_copy.wait()
    ring.run(free1 - AHEAD, free1)
    if turned:

        def flip(n, _):
            x1[columns(n), :] = full[:, columns(n)].T
            return 0

        lax.fori_loop(0, width // COLS, flip, 0)
    wide.scatter_done()
    end(dh_copy, w2_copy)
    pl.semaphore_wait(c_over, 1)
    if not turned:
        for n in range(tiles):
            tile_copy(n).wait_send()
    quad.scatter_send(lambda part, n: nn(quad.half_of(y0, part), weights[:, quad.columns(n)]))
    ring.run(free1, free1 + lines)
    add_all(quad)

    def out_rows(i, _):
        whole, own = own_block(quad, i, size)
        y1[whole] = (mid[own] + act[whole] * (quad.acc[own] + ffn_bias[...])).astype(jnp.bfloat16)
        return 0

    lax.fori_loop(0, own_rows // size, out_rows, 0)
    quad.gather_send(y1)
    again = [load(4, dh_hbm, quad.acc.at[:own_rows]), load(5, dmid_hbm, mid)]
    begin(*again)
    ready = base * lines + SKEW * (lines - 1)
    ring.run(free1 + lines, ready)
    quad.gather_near(y1)
    quad.gather_pass(y1)
    quad.gather_far(y1)
    act_copy = store(0, y1, act_hbm)
    act_copy.start()
    end(*again, *x_copies)
    for n in range(quad.tiles):
        quad.acc[: quad.head, n * COLS : (n + 1) * COLS] += back[n * quad.head : (n + 1) * quad.head]

    def input_rows(i, _):
        whole, own = own_block(quad, i, size)
        grad = quad.acc[own]
        change, gain_terms = norm_back(grad, own_in[own].astype(jnp.float32), gain1[...])
        y0[whole] = (mid[own] + change).astype(jnp.bfloat16)
        vec[0:1] += column_sum(gain_terms)
        vec[1:2] += column_sum(grad)
        return 0

    lax.fori_loop(0, own_rows // size, input_rows, 0)
    quad.gather_send(y0, 1)
    swap_start(0)
    late = min(max(ready, ring.steps - AHEAD), ring.steps - 4)
    ring.run(ready, late)
    swap_end(0)
    swap_start(1)
    ring.run(late, late + 2)
    swap_end(1)
    swap_start(2)
    ring.run(late + 2, ring.steps)
    quad.gather_near(y0, 1)
    quad.gather_pass(y0, 1)
    swap_end(2)
    swap_start(3)
    ring.run(ring.steps, ring.steps + SKEW)
    quad.gather_far(y0, 1)
    in_copy = store(1, y0, in_hbm)
    in_copy.start()
    swap_end(3)
    for n in range(4, len(swaps)):
        swap_start(n)
        if n + 1 == len(swaps):
            ring.run(ring.steps + SKEW, ring.steps + 2 * SKEW)
        swap_end(n)
    ring.finish(ring.steps + 2 * SKEW)
    quad.gather_done(y1)
    quad.gather_done(y0, 1)
    quad.scatter_done()
    end(act_copy, in_copy)


def back_call(n_ctx, turned, g, h2, hid, dpre, w1, w_qkv, w2, w_out, h_all, att, mid, cot, x, g_theirs, act, gain1, gain2, ffn_bias,
              bias, weight, theirs, q, k, v, lse, vec):
    lines, rows, width = n_ctx // 2, cot.shape[0], cot.shape[1]
    block_rows, own, cols = width // n_ctx, rows // 4, q.shape[1]
    hidden = hid.shape[1]
    returned = PREFIX * width // 4 // COLS
    rounds = n_ctx.bit_length() + 1
    vm, hbm, sm = (pl.BlockSpec(memory_space=s) for s in (pltpu.VMEM, pl.ANY, pltpu.SMEM))
    bf, f4 = jnp.bfloat16, jnp.float32
    shape = jax.ShapeDtypeStruct
    return pl.pallas_call(
        functools.partial(back_kernel, lines, turned),
        out_shape=(
            shape((hidden, block_rows), f4),
            shape((block_rows, hidden), f4),
            shape((cols, block_rows), f4),
            shape((3, block_rows, cols), f4),
            shape((rows, width), bf),
            shape((rows, width), bf),
            shape((own, width), f4),
            shape((own, width), f4),
            shape((hidden // COLS, rows, COLS), bf),
            shape(vec.shape, f4),
        ),
        in_specs=[hbm] * 14 + [vm] * 4 + [sm] * 3 + [vm] * 5,
        out_specs=[hbm] * 9 + [vm],
        scratch_shapes=Ring.scratch(lines, block_rows)
        + Quad.scratch(own + PREFIX // 4, width)
        + [
            pltpu.VMEM(h_all.shape, bf),
            pltpu.VMEM(h2.shape, bf),
            pltpu.VMEM((rows, hidden), bf),
            pltpu.VMEM((rows, hidden), bf),
            pltpu.VMEM(w1.shape, bf),
            pltpu.VMEM((own, width), f4),
            pltpu.VMEM((own, width), bf),
            pltpu.VMEM((rows, width), bf),
            pltpu.VMEM((rows, cols), bf),
            pltpu.VMEM((rows + PREFIX, 3 * cols), bf),
            pltpu.VMEM((returned, COLS), f4),
            pltpu.VMEM((returned, COLS), f4),
            pltpu.VMEM((rounds, *vec.shape), f4),
            pltpu.VMEM((rounds, *vec.shape), f4),
            pltpu.VMEM((16, 128) if turned else g_theirs.shape, bf),
            pltpu.VMEM((16, 128) if turned else (rows, COLS), bf),
            pltpu.SemaphoreType.DMA((13,)),
            pltpu.SemaphoreType.DMA((2,)),
            pltpu.SemaphoreType.DMA((rounds,)),
            pltpu.SemaphoreType.DMA((rounds,)),
            pltpu.SemaphoreType.DMA((hidden // COLS,)),
            pltpu.SemaphoreType.DMA((hidden // COLS,)),
            pltpu.SemaphoreType.REGULAR,
        ],
        compiler_params=pltpu.CompilerParams(collective_id=2, has_side_effects=True, vmem_limit_bytes=64 * 2**20),
    )(g, h2, hid, dpre, w1, w_qkv, w2, w_out, h_all, att, mid, cot, x, g_theirs, act, gain1[None], gain2[None], ffn_bias[None],
      bias, weight, theirs, q, k, v, lse, vec)


def find_block(lengths, placed, block):
    mine, start, first = placed[block], 0, 0
    for s in range(lengths.shape[0]):
        first = jnp.where(start <= mine, start, first)
        start = start + lengths[s]
    owner = 0
    for e in range(placed.shape[0]):
        owner = owner + jnp.where(placed[e] == first, e, 0)
    return mine - first, jnp.minimum(owner, placed.shape[0] - 1)


def attend_own(p, q, k, v, held, peaks, totals):
    lanes = pl.ds(pl.multiple_of(p * 2 * HEAD, 2 * HEAD), 2 * HEAD)
    rows = q.shape[0]
    value_t = v[PREFIX:, lanes].T
    row = lax.broadcasted_iota(jnp.int32, (PREFIX, PREFIX), 0)
    col = lax.broadcasted_iota(jnp.int32, (PREFIX, PREFIX), 1)
    for r in range(rows // PREFIX):
        own, count = slice(r * PREFIX, (r + 1) * PREFIX), (r + 1) * PREFIX
        query, keys = q[own, lanes], k[PREFIX : PREFIX + count, lanes]
        for e in range(2):
            scores = nt(keys, jnp.where(lane_mask(PREFIX, e), query, jnp.zeros_like(query)))
            last = jnp.where(row <= col, scores[count - PREFIX :], NEGATIVE)
            scores = jnp.concatenate([scores[: count - PREFIX], last], axis=0) if r else last
            peak = jnp.max(scores, axis=0, keepdims=True)
            raised = jnp.exp(scores - peak)
            peaks[p, e : e + 1, own] = peak
            totals[p, e : e + 1, own] = jnp.sum(raised, axis=0, keepdims=True)
            part = slice(e * HEAD, (e + 1) * HEAD)
            held[p, part, own] = nn(value_t[part, :count], raised.astype(jnp.bfloat16))


def attend_prefix(p, bias, q, k, v, held, peaks, totals, out, lse):
    lanes = pl.ds(pl.multiple_of(p * 2 * HEAD, 2 * HEAD), 2 * HEAD)
    query, keys, value_t = q[:, lanes], k[:PREFIX, lanes], v[:PREFIX, lanes].T
    outs = []
    for e in range(2):
        scores = nt(keys, jnp.where(lane_mask(q.shape[0], e), query, jnp.zeros_like(query))) + bias
        before = peaks[p, e : e + 1]
        peak = jnp.maximum(before, jnp.max(scores, axis=0, keepdims=True))
        raised = jnp.exp(scores - peak)
        shrink = jnp.exp(before - peak)
        total = totals[p, e : e + 1] * shrink + jnp.sum(raised, axis=0, keepdims=True)
        lse[p, e : e + 1] = peak + jnp.log(total)
        part = slice(e * HEAD, (e + 1) * HEAD)
        summed = held[p, part] * shrink + nn(value_t[part], raised.astype(jnp.bfloat16))
        outs.append(summed * (1.0 / total))
    out[:, lanes] = jnp.concatenate(outs, axis=0).astype(jnp.bfloat16).T


def first_kernel(lines, *refs):
    (lengths, placed, layer, exits, x_hbm, w_hbm, gain, shift, qv_bias,
     q, k, v, h_all, act, att, lse, bias, weight, theirs, *scratch) = refs
    (x, w, line, x_send, x_recv, prefix, held, peaks, totals, loads, s_l, s_r, r_z, s_x, r_x, s_g, r_g) = scratch
    rows, width = x.shape
    part = prefix.shape[0] // 4
    ctx, tp = lax.axis_index("ctx"), lax.axis_index("tp")
    z, side, y, core = ctx // 2, lax.rem(ctx, 2), tp // 2, lax.rem(tp, 2)
    left, right, partner = (ctx - 2, tp), (ctx + 2, tp), (z * 2 + 1 - side, tp)
    across, over = (ctx, y * 2 + 1 - core), (ctx, (1 - y) * 2 + core)
    own = pl.ds(pl.multiple_of(tp * part, 16), part)
    copies = [
        pltpu.make_async_copy(x_hbm.at[own], line.at[z], loads.at[0]),
        pltpu.make_async_copy(x_hbm, x, loads.at[1]),
        pltpu.make_async_copy(w_hbm, w, loads.at[2]),
    ]
    for copy in copies:
        copy.start()
    meet([(None, partner), (z > 0, left), (z < lines - 1, right), (None, across), (None, over)])

    def hop(o, device, sems):
        return pltpu.make_async_remote_copy(
            src_ref=line.at[o], dst_ref=line.at[o], send_sem=sems.at[o], recv_sem=r_z.at[o],
            device_id=device, device_id_type=MESH)

    def pass_on(o, there, device, sems):
        @pl.when(there)
        def _():
            hop(o, device, sems).start()

    copies[0].wait()
    pass_on(z, z < lines - 1, right, s_r)
    pass_on(z, z > 0, left, s_l)

    def hops(d):
        @pl.when(z - d >= 0)
        def _():
            hop(z - d, left, s_l).wait_recv()
            pass_on(z - d, z < lines - 1, right, s_r)

        @pl.when(z + d < lines)
        def _():
            hop(z + d, right, s_r).wait_recv()
            pass_on(z + d, z > 0, left, s_l)

    my_part, my_owner = find_block(lengths, placed, ctx)
    partner_part, partner_owner = find_block(lengths, placed, z * 2 + 1 - side)
    bias[0, 0] = jnp.where(my_part > 0, 0.0, NEGATIVE)
    for e in range(weight.shape[0]):
        weight[e] = jnp.where((my_owner == e) & (my_part > 0), 1.0, 0.0)
        theirs[e] = jnp.where((partner_owner == e) & (partner_part > 0), 1.0, 0.0)
    row = lax.broadcasted_iota(jnp.int32, exits.shape, 0)
    first_rows = jnp.where(my_part == 0, PREFIX, 0)
    act[...] = jnp.where((exits[...] > layer[0]) | (row < first_rows), 1.0, 0.0)
    size = 64

    def norm_rows(source, start, to):
        def some(i, _):
            span = pl.ds(pl.multiple_of(start + i * size, size), size)
            values = source[span].astype(jnp.float32)
            target = pl.ds(pl.multiple_of(to + i * size, size), size)
            h_all[target] = (normed(values)[0] * gain[...] + shift[...]).astype(jnp.bfloat16)
            return 0

        lax.fori_loop(0, PREFIX // size, some, 0)

    def keys_of(span, rows_in):
        k[span] = nn(rows_in, w[1]).astype(jnp.bfloat16)
        v[span] = (nn(rows_in, w[2]) + qv_bias[1:2]).astype(jnp.bfloat16)

    for r in range(rows // PREFIX):
        norm_rows(x_wait(copies, r, x), r * PREFIX, (r + 1) * PREFIX)
        if r == 0:
            copies[2].wait()
        span = slice((r + 1) * PREFIX, (r + 2) * PREFIX)
        rows_in = h_all[span]
        low = (nn(rows_in, w[0]) + qv_bias[0:1]).astype(jnp.bfloat16)
        q[r * PREFIX : (r + 1) * PREFIX] = low * jnp.bfloat16(HEAD**-0.5)
        keys_of(span, rows_in)
        if r + 1 < lines:
            hops(r + 1)
    for d in range(rows // PREFIX + 1, lines):
        hops(d)
    x_send[...] = line[partner_owner // 2]
    trade = pltpu.make_async_remote_copy(
        src_ref=x_send, dst_ref=x_recv, send_sem=s_x, recv_sem=r_x, device_id=partner, device_id_type=MESH)
    trade.start()
    near = line[my_owner // 2]
    pairs = q.shape[1] // (2 * HEAD)

    def own_pairs(lo, hi):
        lax.fori_loop(lo, hi, lambda p, _: (attend_own(p, q, k, v, held, peaks, totals), 0)[1], 0)

    own_pairs(0, pairs // 2)
    trade.wait_recv()
    prefix[own] = jnp.where(lax.rem(my_owner, 2) == side, near, x_recv[...])

    def give(n, quarter, device):
        span = pl.ds(pl.multiple_of(quarter * part, 16), part)
        return pltpu.make_async_remote_copy(
            src_ref=prefix.at[span], dst_ref=prefix.at[span], send_sem=s_g.at[n], recv_sem=r_g.at[n],
            device_id=device, device_id_type=MESH)

    far = (1 - y) * 2 + core
    give(0, tp, over).start()
    give(1, tp, across).start()
    own_pairs(pairs // 2, pairs)
    give(0, far, over).wait_recv()
    give(2, far, across).start()
    give(1, y * 2 + 1 - core, across).wait_recv()
    give(2, (1 - y) * 2 + 1 - core, across).wait_recv()
    norm_rows(prefix, 0, 0)
    keys_of(slice(0, PREFIX), h_all[:PREFIX])
    hide = jnp.where(my_part > 0, 0.0, NEGATIVE)

    def prefix_pair(p, _):
        attend_prefix(p, hide, q, k, v, held, peaks, totals, att, lse)
        return 0

    lax.fori_loop(0, pairs, prefix_pair, 0)
    trade.wait_send()
    give(0, tp, over).wait_send()
    give(1, tp, across).wait_send()
    give(2, far, across).wait_send()
    for o in range(lines):
        @pl.when((z < lines - 1) & (z >= o))
        def _():
            hop(o, right, s_r).wait_send()

        @pl.when((z > 0) & (z <= o))
        def _():
            hop(o, left, s_l).wait_send()


def x_wait(copies, r, x):
    if r == 0:
        copies[1].wait()
    return x


def first_call(n_ctx, lengths, placed, layer, exits, x, w_qkv, gain, shift, qv_bias):
    lines, (rows, width) = n_ctx // 2, x.shape
    cols = w_qkv.shape[2]
    vm, hbm, sm = (pl.BlockSpec(memory_space=s) for s in (pltpu.VMEM, pl.ANY, pltpu.SMEM))
    bf, f4 = jnp.bfloat16, jnp.float32
    return pl.pallas_call(
        functools.partial(first_kernel, lines),
        out_shape=(
            jax.ShapeDtypeStruct((rows, cols), bf),
            jax.ShapeDtypeStruct((rows + PREFIX, cols), bf),
            jax.ShapeDtypeStruct((rows + PREFIX, cols), bf),
            jax.ShapeDtypeStruct((rows + PREFIX, width), bf),
            jax.ShapeDtypeStruct((rows, 1), f4),
            jax.ShapeDtypeStruct((rows, cols), bf),
            jax.ShapeDtypeStruct((cols // (2 * HEAD), 2, rows), f4),
            jax.ShapeDtypeStruct((1, 1), f4),
            jax.ShapeDtypeStruct((n_ctx,), f4),
            jax.ShapeDtypeStruct((n_ctx,), f4),
        ),
        in_specs=[sm] * 3 + [vm] + [hbm] * 2 + [vm] * 3,
        out_specs=[vm] * 7 + [sm] * 3,
        scratch_shapes=[
            pltpu.VMEM((rows, width), bf),
            pltpu.VMEM(w_qkv.shape, bf),
            pltpu.VMEM((lines, PREFIX // 4, width), bf),
            pltpu.VMEM((PREFIX // 4, width), bf),
            pltpu.VMEM((PREFIX // 4, width), bf),
            pltpu.VMEM((PREFIX, width), bf),
            pltpu.VMEM((cols // (2 * HEAD), 2 * HEAD, rows), f4),
            pltpu.VMEM((cols // (2 * HEAD), 2, rows), f4),
            pltpu.VMEM((cols // (2 * HEAD), 2, rows), f4),
            pltpu.SemaphoreType.DMA((3,)),
            pltpu.SemaphoreType.DMA((lines,)),
            pltpu.SemaphoreType.DMA((lines,)),
            pltpu.SemaphoreType.DMA((lines,)),
            pltpu.SemaphoreType.DMA,
            pltpu.SemaphoreType.DMA,
            pltpu.SemaphoreType.DMA((3,)),
            pltpu.SemaphoreType.DMA((3,)),
        ],
        compiler_params=pltpu.CompilerParams(collective_id=4, has_side_effects=True, vmem_limit_bytes=64 * 2**20),
    )(lengths, placed, layer, exits[:, None], x, w_qkv, gain[None], shift[None], qv_bias)


def body(
    mesh,
    block_input,
    cotangent,
    ln1_gain,
    ln1_bias,
    w_qkv,
    qv_bias,
    w_out,
    out_bias,
    ln2_gain,
    ln2_bias,
    w_fc1,
    fc1_bias,
    w_fc2,
    fc2_bias,
    exit_layer,
    layer_index,
    lengths,
    stretch_map,
):
    n_ctx = mesh.shape["ctx"]
    row_count, width = block_input.shape
    block_rows = width // n_ctx
    turned = block_rows % 128 != 0

    def tokens_last(array):
        return array.T if turned else array

    query, key, value, h_all, active, attended, log_total, bias, weight, theirs = first_call(
        n_ctx, lengths, stretch_map, layer_index, exit_layer, block_input, w_qkv, ln1_gain, ln1_bias, qv_bias
    )
    middle, h2_low, grad_ffn, hidden_low, d_pre_low, vectors, grad_theirs = front_call(
        0 if turned else n_ctx // 2, attended, w_out, block_input, cotangent, active, w_fc1, w_fc2, out_bias, ln2_gain, ln2_bias, fc1_bias
    )
    fc2_grad, fc1_grad, out_grad, qkv_grad, input_grad, output_rows, _, _, _, vectors = back_call(
        n_ctx, turned, tokens_last(grad_ffn), tokens_last(h2_low), hidden_low, d_pre_low, w_fc1, w_qkv, w_fc2, w_out,
        tokens_last(h_all), attended, middle, cotangent, block_input, grad_theirs, active, ln1_gain, ln2_gain, fc2_bias,
        bias, weight, theirs, query, key, value, log_total, vectors,
    )
    qv_grad = vectors[7, : 2 * query.shape[1]].reshape(2, -1)
    return (
        output_rows,
        input_grad,
        vectors[0],
        vectors[1],
        qkv_grad,
        qv_grad,
        out_grad,
        vectors[2],
        vectors[3],
        vectors[4],
        fc1_grad,
        vectors[6],
        fc2_grad,
        vectors[5],
    )


def solution(mesh):
    in_specs = (
        P("ctx", None),
        P("ctx", None),
        P(),
        P(),
        P(None, None, "tp"),
        P(None, "tp"),
        P("tp", None),
        P(),
        P(),
        P(),
        P(None, "tp"),
        P("tp"),
        P("tp", None),
        P(),
        P("ctx"),
        P(),
        P(),
        P(),
    )
    out_specs = (
        P("ctx", None),
        P("ctx", None),
        P(),
        P(),
        P(None, "ctx", "tp"),
        P(None, "tp"),
        P("tp", "ctx"),
        P(),
        P(),
        P(),
        P("ctx", "tp"),
        P("tp"),
        P("tp", "ctx"),
        P(),
    )
    return jax.shard_map(functools.partial(body, mesh), mesh=mesh, in_specs=in_specs, out_specs=out_specs, check_vma=False)
```

```python
import functools
import math

import jax
import jax.numpy as jnp
from jax import lax
from jax.experimental import pallas as pl
from jax.experimental.pallas import tpu as pltpu
from jax.sharding import PartitionSpec as P

HEAD = 64
PREFIX = 256
COLS = 512
MESH = pl.DeviceIdType.MESH
NEGATIVE = -1e30
EPSILON = 1e-05
AHEAD = 8
SKEW = 2
STAGES = 2
DEPTH = 2


class Ring:
    def __init__(self, lines, groups, refs, outs, later=(), prefix=None):
        self.lines, self.groups, self.outs, self.later, self.prefix = lines, groups, outs, later, prefix
        (self.xs, self.xr, self.zb, self.stage, self.turned, self.kept, self.swap, self.s_xs, self.s_xr, self.s_zs,
         self.s_zr, self.s_out, self.s_swap, self.c_x, self.c_left, self.c_right) = refs
        self.jobs = sum(group[0] for group in groups)
        marks, alone, job = [], [], 0
        for group in groups:
            marks += [job + n for n in range(group[0]) if group[2] == "p"]
            alone += [job + n for n in range(group[0]) if group[2] == "t"]
            job += group[0]
        self.alone = (alone[0], alone[-1]) if alone else None
        self.fetched = (marks[0], marks[-1]) if marks else (self.jobs, self.jobs)
        self.steps = self.jobs * lines
        self.slots = self.xr.shape[0]
        self.lag = SKEW * (lines - 1) + 2
        ctx, tp = lax.axis_index("ctx"), lax.axis_index("tp")
        self.z, self.side = ctx // 2, lax.rem(ctx, 2)
        self.partner = (self.z * 2 + 1 - self.side, tp)
        self.left, self.right = (ctx - 2, tp), (ctx + 2, tp)

    @staticmethod
    def scratch(lines, rows):
        slots = AHEAD + SKEW * (lines - 1) + 4
        chunk = (rows, COLS)
        return [
            pltpu.VMEM((AHEAD, *chunk), jnp.bfloat16),
            pltpu.VMEM((slots, *chunk), jnp.bfloat16),
            pltpu.VMEM((DEPTH, lines + 1, *chunk), jnp.bfloat16),
            pltpu.VMEM((STAGES, *chunk), jnp.float32),
            pltpu.VMEM((STAGES, COLS, rows), jnp.float32),
            pltpu.VMEM(chunk, jnp.bfloat16),
            pltpu.VMEM((4, *chunk), jnp.bfloat16),
            pltpu.SemaphoreType.DMA((AHEAD,)),
            pltpu.SemaphoreType.DMA((slots,)),
            pltpu.SemaphoreType.DMA((slots,)),
            pltpu.SemaphoreType.DMA((DEPTH, lines + 1)),
            pltpu.SemaphoreType.DMA((STAGES,)),
            pltpu.SemaphoreType.DMA((4,)),
            pltpu.SemaphoreType.REGULAR,
            pltpu.SemaphoreType.REGULAR,
            pltpu.SemaphoreType.REGULAR,
        ]

    def sends(self, f):
        job = f // self.lines
        found = (job < self.fetched[0]) | (job > self.fetched[1]) | (lax.rem(f, self.lines) == 0)
        for pair in self.later:
            found = found & (job != pair[0]) & (job != pair[1])
        if self.alone:
            found = found & ((job < self.alone[0]) | (job > self.alone[1]))
        return found

    def owner(self, f):
        turn = lax.rem(f + 2 * SKEW * self.lines * self.lines, self.lines)
        return jnp.where(lax.rem(turn, 2) == 0, turn // 2, self.lines - 1 - turn // 2)

    def peers(self):
        return [(None, self.partner), (self.z > 0, self.left), (self.z < self.lines - 1, self.right)]

    def x_copy(self, f):
        slot, to = lax.rem(f, AHEAD), lax.rem(f, self.slots)
        return pltpu.make_async_remote_copy(
            src_ref=self.xs.at[slot], dst_ref=self.xr.at[to], send_sem=self.s_xs.at[slot],
            recv_sem=self.s_xr.at[to], device_id=self.partner, device_id_type=MESH)

    def z_copy(self, f, to, device):
        slot, level = lax.rem(f, self.slots), lax.rem(f // self.lines, DEPTH)
        return pltpu.make_async_remote_copy(
            src_ref=self.xr.at[slot], dst_ref=self.zb.at[level, to], send_sem=self.s_zs.at[slot],
            recv_sem=self.s_zr.at[level, to], device_id=device, device_id_type=MESH)

    def out_copies(self, job, act):
        slot = lax.rem(job, STAGES)
        for there, turn, place in self.outs(job):
            @pl.when(there)
            def _():
                source = self.turned if turn else self.stage
                act(pltpu.make_async_copy(source.at[slot], place, self.s_out.at[slot]))

    def out_start(self, job):
        slot = lax.rem(job, STAGES)
        for there, turn, _ in self.outs(job):
            if turn:
                @pl.when(there)
                def _():
                    self.turned[slot] = self.stage[slot].T
        self.out_copies(job, lambda copy: copy.start())

    def out_wait(self, job):
        self.out_copies(job, lambda copy: copy.wait())

    def swap_copy(self, n):
        return pltpu.make_async_remote_copy(
            src_ref=self.swap.at[2 * n], dst_ref=self.swap.at[2 * n + 1], send_sem=self.s_swap.at[2 * n],
            recv_sem=self.s_swap.at[2 * n + 1], device_id=self.partner, device_id_type=MESH)

    def send(self, f, group, job0, fresh):
        _, part, kind = group
        is_prefix = kind == "p"
        if not fresh:
            @pl.when(self.sends(f - AHEAD))
            def _():
                self.x_copy(f).wait_send()

            @pl.when(f >= self.slots)
            def _():
                pl.semaphore_wait(self.c_x, 1)

        if kind == "t":
            return

        @pl.when(self.sends(f))
        def _():
            owner = self.owner(f)
            value = part(f // self.lines - job0, None if is_prefix else owner * 2 + 1 - self.side)
            self.xs[lax.rem(f, AHEAD)] = value.astype(jnp.bfloat16)
            self.x_copy(f).start()

    def receive(self, f, group, job0):
        _, part, kind = group
        is_prefix = kind == "p"
        job, owner, slot = f // self.lines, self.owner(f), lax.rem(f, self.slots)
        came = self.sends(f)

        if kind != "t":
            @pl.when(came)
            def _():
                self.x_copy(f).wait_recv()
                if is_prefix:
                    self.kept[...] = self.xr[slot]

        block = owner * 2 + self.side
        if is_prefix:
            mine, theirs = self.prefix[0][block], self.prefix[1][block]
            total = part(job - job0, None) * mine + self.kept[...].astype(jnp.float32) * theirs
        elif kind == "t":
            total = part(job - job0, block)
        else:
            @pl.when(jnp.logical_not(came))
            def _():
                self.xr[slot] = jnp.zeros(self.xr.shape[1:], jnp.bfloat16)

            for pair in self.later:
                block = jnp.where(job == pair[0], owner * 2 + 1 - self.side, block)
            total = part(job - job0, block) + self.xr[slot].astype(jnp.float32)

        @pl.when(owner != self.z)
        def _():
            self.xr[slot] = total.astype(jnp.bfloat16)

        @pl.when(owner == self.z)
        def _():
            @pl.when(job >= STAGES)
            def _():
                self.out_wait(job - STAGES)
            self.stage[lax.rem(job, STAGES)] = total

    def add(self, f, index):
        job = f // self.lines
        slot, level = lax.rem(f, self.slots), lax.rem(job, DEPTH)

        @pl.when(self.owner(f) == self.z)
        def _():
            self.stage[lax.rem(job, STAGES)] += self.zb[level, index].astype(jnp.float32)

        @pl.when(self.owner(f) != self.z)
        def _():
            self.xr[slot] = (self.xr[slot].astype(jnp.float32) + self.zb[level, index].astype(jnp.float32)).astype(jnp.bfloat16)

    def flow(self, t):
        lines, z = self.lines, self.z
        f = t - SKEW * z
        owner = self.owner(f)

        @pl.when((f >= 0) & (f < self.steps) & (owner >= z))
        def _():
            @pl.when(z > 0)
            def _():
                self.z_copy(f, owner, self.left).wait_recv()
                self.add(f, owner)
                pl.semaphore_signal(self.c_right, inc=1, device_id=self.left, device_id_type=MESH)

            @pl.when(owner > z)
            def _():
                @pl.when(f >= DEPTH * lines)
                def _():
                    pl.semaphore_wait(self.c_right, 1)
                self.z_copy(f, owner, self.right).start()

        g = t - SKEW * (lines - 1 - z)
        owner2 = self.owner(g)

        @pl.when((g >= 0) & (g < self.steps) & (owner2 <= z))
        def _():
            @pl.when(z < lines - 1)
            def _():
                index = jnp.where(owner2 == z, lines, owner2)
                self.z_copy(g, index, self.right).wait_recv()
                self.add(g, index)
                pl.semaphore_signal(self.c_left, inc=1, device_id=self.right, device_id_type=MESH)

            @pl.when(owner2 < z)
            def _():
                @pl.when(g >= DEPTH * lines)
                def _():
                    pl.semaphore_wait(self.c_left, 1)
                self.z_copy(g, jnp.where(owner2 == z - 1, lines, owner2), self.left).start()

        h = t - SKEW * (lines - 1)

        @pl.when((h >= 0) & (h < self.steps) & (self.owner(h) == z))
        def _():
            job = h // lines
            stage = lax.rem(job, STAGES)
            for n, pair in enumerate(self.later):
                @pl.when(job == pair[0])
                def _():
                    self.swap[2 * n] = self.stage[stage].astype(jnp.bfloat16)
                    self.swap_copy(n).start()

                @pl.when(job == pair[1])
                def _():
                    self.swap_copy(n).wait()
                    self.stage[stage] += self.swap[2 * n + 1].astype(jnp.float32)
            if self.prefix is not None:
                target, rows = self.prefix[2], self.stage.shape[1]

                @pl.when((job >= self.fetched[0]) & (job <= self.fetched[1]))
                def _():
                    span = pl.ds(pl.multiple_of((job - self.fetched[0]) * rows, rows), rows)
                    target[span] = self.stage[stage]
            self.out_start(job)

        d = t - self.lag

        @pl.when((d >= 0) & (d < self.steps))
        def _():
            @pl.when(self.owner(d) != z)
            def _():
                self.z_copy(d, 0, self.left).wait_send()
            pl.semaphore_signal(self.c_x, inc=1, device_id=self.partner, device_id_type=MESH)

    def find(self, f):
        job = 0
        for group in self.groups:
            if f < (job + group[0]) * self.lines:
                return group, job
            job += group[0]
        return None

    def pieces(self, lo, hi):
        cuts, job = {lo, hi}, 0
        for group in self.groups:
            job += group[0]
            cuts |= {job * self.lines, job * self.lines - AHEAD}
        cuts = sorted(c for c in cuts if lo <= c <= hi)
        return zip(cuts[:-1], cuts[1:])

    def start(self):
        for lo, hi in self.pieces(0, AHEAD):
            here = self.find(lo)
            lax.fori_loop(lo, hi, lambda f, _, here=here: (self.send(f, *here, True), 0)[1], 0)

    def run(self, lo, hi):
        for a, b in self.pieces(lo, min(hi, self.steps)):
            here, ahead = self.find(a), self.find(a + AHEAD)

            def body(f, _, here=here, ahead=ahead):
                self.receive(f, *here)
                self.flow(f)
                if ahead is not None:
                    self.send(f + AHEAD, *ahead, False)
                return 0

            lax.fori_loop(a, b, body, 0)
        if hi > self.steps:
            lax.fori_loop(max(lo, self.steps), hi, lambda t, _: (self.flow(t), 0)[1], 0)

    def run_some(self, lo, count):
        here = self.find(0)

        def body(f, _):
            self.receive(f, *here)
            self.flow(f)

            @pl.when(f + AHEAD < self.steps)
            def _():
                self.send(f + AHEAD, *here, False)
            return 0

        lax.fori_loop(lo, lo + count, body, 0)

    def finish(self, lo):
        lines, z = self.lines, self.z
        self.run(lo, self.steps + self.lag)

        def drain(f, _):
            @pl.when(self.sends(f))
            def _():
                self.x_copy(f).wait_send()
            return 0

        lax.fori_loop(self.steps - AHEAD, self.steps, drain, 0)
        for job in range(self.jobs - STAGES, self.jobs):
            self.out_wait(job)
        pl.semaphore_wait(self.c_x, min(self.slots, self.steps))

        @pl.when(z < lines - 1)
        def _():
            pl.semaphore_wait(self.c_right, DEPTH * (lines - 1 - z))

        @pl.when(z > 0)
        def _():
            pl.semaphore_wait(self.c_left, DEPTH * z)


def meet(peers):
    barrier = pltpu.get_barrier_semaphore()
    count = 0
    for there, device in peers:
        if there is None:
            pl.semaphore_signal(barrier, inc=1, device_id=device, device_id_type=MESH)
            count += 1
        else:
            @pl.when(there)
            def _():
                pl.semaphore_signal(barrier, inc=1, device_id=device, device_id_type=MESH)
            count += jnp.where(there, 1, 0)
    pl.semaphore_wait(barrier, count)
class Quad:
    def __init__(self, refs, rows, height):
        (self.tmp, self.cs, self.cr, self.ys, self.yr, self.acc, self.s_c, self.r_c, self.s_y, self.r_y,
         self.s_g, self.r_g) = refs
        ctx, tp = lax.axis_index("ctx"), lax.axis_index("tp")
        self.y, self.core, self.tp = tp // 2, lax.rem(tp, 2), tp
        self.across = (ctx, self.y * 2 + 1 - self.core)
        self.over = (ctx, (1 - self.y) * 2 + self.core)
        self.head, self.rest = PREFIX // 4, (rows - PREFIX) // 4
        self.tiles = self.cs.shape[1]
        self.height = height

    @staticmethod
    def scratch(rows, width):
        tiles = width // COLS
        return [
            pltpu.VMEM((2, rows, COLS), jnp.float32),
            pltpu.VMEM((2, tiles, rows, COLS), jnp.bfloat16),
            pltpu.VMEM((2, tiles, rows, COLS), jnp.bfloat16),
            pltpu.VMEM((tiles, rows, COLS), jnp.bfloat16),
            pltpu.VMEM((tiles, rows, COLS), jnp.bfloat16),
            pltpu.VMEM((rows, width), jnp.float32),
            pltpu.SemaphoreType.DMA((2, tiles)),
            pltpu.SemaphoreType.DMA((2, tiles)),
            pltpu.SemaphoreType.DMA((tiles,)),
            pltpu.SemaphoreType.DMA((tiles,)),
            pltpu.SemaphoreType.DMA((2, 3, 2)),
            pltpu.SemaphoreType.DMA((2, 3, 2)),
        ]

    def peers(self):
        return [(None, self.across), (None, self.over)]

    def spans(self, quarter):
        return [
            pl.ds(pl.multiple_of(quarter * self.head, 16), self.head),
            pl.ds(pl.multiple_of(PREFIX + quarter * self.rest, 16), self.rest),
        ]

    def rows_of(self, ref, quarter):
        return jnp.concatenate([ref[span] for span in self.spans(quarter)], axis=0)

    def half_of(self, ref, half):
        return jnp.concatenate([self.rows_of(ref, half * 2), self.rows_of(ref, half * 2 + 1)], axis=0)

    def c_copy(self, k, n):
        return pltpu.make_async_remote_copy(
            src_ref=self.cs.at[k, n, : self.height], dst_ref=self.cr.at[k, n, : self.height], send_sem=self.s_c.at[k, n],
            recv_sem=self.r_c.at[k, n], device_id=self.across, device_id_type=MESH)

    def y_copy(self, n):
        return pltpu.make_async_remote_copy(
            src_ref=self.ys.at[n, : self.height], dst_ref=self.yr.at[n, : self.height], send_sem=self.s_y.at[n],
            recv_sem=self.r_y.at[n], device_id=self.over, device_id_type=MESH)

    def columns(self, n):
        return pl.ds(pl.multiple_of(n * COLS, COLS), COLS)

    def split(self, value, k, n):
        rows = self.height
        self.tmp[0, :rows] = value[:rows]
        self.tmp[1, :rows] = value[rows:]
        self.cs[k, n, :rows] = self.tmp[1 - self.core, :rows].astype(jnp.bfloat16)
        self.c_copy(k, n).start()
        self.acc[:rows, self.columns(n)] = self.tmp[self.core, :rows]

    def relay(self, n):
        self.c_copy(0, n).wait_recv()
        rows = self.height
        total = self.acc[:rows, self.columns(n)] + self.cr[0, n, :rows].astype(jnp.float32)
        self.ys[n, :rows] = total.astype(jnp.bfloat16)
        self.y_copy(n).start()

    def scatter_send(self, chunk):
        def far(n, _):
            self.split(chunk(1 - self.y, n), 0, n)

            @pl.when(n > 0)
            def _():
                self.relay(n - 1)
            return 0

        lax.fori_loop(0, self.tiles, far, 0)
        self.relay(self.tiles - 1)

        def near(n, _):
            self.split(chunk(self.y, n), 1, n)
            return 0

        lax.fori_loop(0, self.tiles, near, 0)

    def scatter_add(self, n):
        self.c_copy(1, n).wait_recv()
        self.y_copy(n).wait_recv()
        rows = self.height
        came = self.cr[1, n, :rows].astype(jnp.float32) + self.yr[n, :rows].astype(jnp.float32)
        self.acc[:rows, self.columns(n)] += came

    def scatter_done(self):
        for n in range(self.tiles):
            self.c_copy(0, n).wait_send()
            self.c_copy(1, n).wait_send()
            self.y_copy(n).wait_send()

    def g_copy(self, full, k, s, quarter, device, turn):
        span = self.spans(quarter)[s]
        return pltpu.make_async_remote_copy(
            src_ref=full.at[span], dst_ref=full.at[span], send_sem=self.s_g.at[turn, k, s],
            recv_sem=self.r_g.at[turn, k, s], device_id=device, device_id_type=MESH)

    def gather_send(self, full, turn=0):
        for s in range(2):
            self.g_copy(full, 0, s, self.tp, self.over, turn).start()
        for s in range(2):
            self.g_copy(full, 1, s, self.tp, self.across, turn).start()

    def gather_near(self, full, turn=0):
        for s in range(2):
            self.g_copy(full, 1, s, self.y * 2 + 1 - self.core, self.across, turn).wait_recv()

    def gather_pass(self, full, turn=0):
        other = (1 - self.y) * 2 + self.core
        for s in range(2):
            self.g_copy(full, 0, s, other, self.over, turn).wait_recv()
            self.g_copy(full, 2, s, other, self.across, turn).start()

    def gather_far(self, full, turn=0):
        for s in range(2):
            self.g_copy(full, 2, s, (1 - self.y) * 2 + 1 - self.core, self.across, turn).wait_recv()

    def gather_done(self, full, turn=0):
        other = (1 - self.y) * 2 + self.core
        for s in range(2):
            self.g_copy(full, 0, s, self.tp, self.over, turn).wait_send()
            self.g_copy(full, 1, s, self.tp, self.across, turn).wait_send()
            self.g_copy(full, 2, s, other, self.across, turn).wait_send()


def nt(left, right):
    return lax.dot_general(left, right, (((1,), (1,)), ((), ())), preferred_element_type=jnp.float32)


def normed(values_in):
    centred = values_in - jnp.mean(values_in, axis=1, keepdims=True)
    scale = lax.rsqrt(jnp.mean(centred * centred, axis=1, keepdims=True) + EPSILON)
    return centred * scale, scale


def gelu_pair(pre):
    slope = (2.0 / math.pi) ** 0.5
    square = pre * pre
    bent = jnp.tanh(slope * (pre + 0.044715 * (square * pre)))
    half = 0.5 * (1.0 + bent)
    return pre * half, half + 0.5 * pre * (1.0 - bent * bent) * (slope * (1.0 + 3 * 0.044715 * square))


def column_sum(values_in):
    return jnp.sum(values_in, axis=0, keepdims=True)


def front_kernel(early, *refs):
    (att, w_out, x_hbm, cot_hbm, act, w1_hbm, w2_hbm, bias, gain, shift, fc1_bias,
     mid, full, grad, hid, d_pre, vec, theirs, *scratch) = refs
    quad_refs, scratch = scratch[:12], scratch[12:]
    x, w1, w2, d_hid, some, loads, s_x, r_x = scratch
    rows, width = full.shape
    quad = Quad(quad_refs, rows, rows // 4)
    spans = quad.spans(quad.tp)

    def load(n, source, target):
        copy = pltpu.make_async_copy(source, target, loads.at[n])
        copy.start()
        return copy

    cot_copy = load(0, cot_hbm, grad)
    w2_copy = load(1, w2_hbm, w2)
    x_copies = [load(2, x_hbm.at[spans[0]], x.at[: quad.head]), load(3, x_hbm.at[spans[1]], x.at[quad.head :])]
    w1_copy = load(4, w1_hbm, w1)
    ctx, tp = lax.axis_index("ctx"), lax.axis_index("tp")
    side = lax.rem(ctx, 2)
    partner = (ctx + 1 - 2 * side, tp)
    meet(quad.peers() + ([(None, partner)] if early else []))

    def half_copy(o):
        step = width // (2 * early)
        source = grad.at[:, pl.ds(pl.multiple_of((o * 2 + 1 - side) * step, step), step)]
        return pltpu.make_async_remote_copy(
            src_ref=source, dst_ref=theirs.at[:, o * step : (o + 1) * step], send_sem=s_x.at[o], recv_sem=r_x.at[o],
            device_id=partner, device_id_type=MESH)

    quad.scatter_send(lambda half, n: jnp.dot(quad.half_of(att, half), w_out[:, quad.columns(n)], preferred_element_type=jnp.float32))
    cot_copy.wait()
    vec[...] = jnp.zeros(vec.shape, jnp.float32)
    size = 32

    def gate(i, _):
        span = pl.ds(pl.multiple_of(i * size, size), size)
        low = (act[span] * grad[span].astype(jnp.float32)).astype(jnp.bfloat16)
        grad[span] = low
        vec[5:6] += column_sum(low.astype(jnp.float32)) * 0.25
        return 0

    lax.fori_loop(0, rows // size, gate, 0)
    for o in range(early):
        half_copy(o).start()
    w2_copy.wait()
    tiles = hid.shape[1] // COLS

    def d_hidden(n, _):
        d_hid[:, quad.columns(n)] = nt(grad[...], w2[quad.columns(n), :])
        return 0

    lax.fori_loop(0, tiles, d_hidden, 0)
    for copy in x_copies:
        copy.wait()
    lax.fori_loop(0, quad.tiles, lambda n, _: (quad.scatter_add(n), 0)[1], 0)

    def norm_rows(i, _):
        first = quad.head // size
        start = jnp.where(i < first, quad.tp * quad.head + i * size, PREFIX + quad.tp * quad.rest + (i - first) * size)
        whole, own = (pl.ds(pl.multiple_of(s, size), size) for s in (start, i * size))
        middle = x[own].astype(jnp.float32) + act[whole] * (quad.acc[own] + bias[...])
        mid[own] = middle
        full[whole] = (normed(middle)[0] * gain[...] + shift[...]).astype(jnp.bfloat16)
        return 0

    lax.fori_loop(0, quad.height // size, norm_rows, 0)
    quad.gather_send(full)

    def ffn(half):
        some[...] = quad.half_of(full, half)
        places = quad.spans(half * 2) + quad.spans(half * 2 + 1)

        def tile(n, _):
            cols = quad.columns(n)
            pre = jnp.dot(some[...], w1[:, cols], preferred_element_type=jnp.float32) + fc1_bias[:, cols]
            value, slope = gelu_pair(pre)
            value = value.astype(jnp.bfloat16)
            start = 0
            for place in places:
                end = start + place.size
                hid[place, cols] = value[start:end]
                change = (d_hid[place, cols] * slope[start:end]).astype(jnp.bfloat16)
                d_pre[place, cols] = change
                vec[6:7, cols] += column_sum(change.astype(jnp.float32))
                start = end
            return 0

        lax.fori_loop(0, tiles, tile, 0)

    quad.gather_near(full)
    w1_copy.wait()
    ffn(quad.y)
    quad.gather_pass(full)
    quad.gather_far(full)
    ffn(1 - quad.y)
    quad.gather_done(full)
    quad.scatter_done()
    for o in range(early):
        half_copy(o).wait()


def front_call(early, att, w_out, x, cot, act, w1, w2, bias, gain, shift, fc1_bias):
    rows, width = x.shape
    own, hidden = rows // 4, w1.shape[1]
    vm, hbm = (pl.BlockSpec(memory_space=s) for s in (pltpu.VMEM, pl.ANY))
    bf, f4, shape = jnp.bfloat16, jnp.float32, jax.ShapeDtypeStruct
    return pl.pallas_call(
        functools.partial(front_kernel, early),
        out_shape=(
            shape((own, width), f4),
            shape((rows, width), bf),
            shape((rows, width), bf),
            shape((rows, hidden), bf),
            shape((rows, hidden), bf),
            shape((8, width), f4),
            shape((rows, width // 2), bf),
        ),
        in_specs=[vm] * 2 + [hbm] * 2 + [vm] + [hbm] * 2 + [vm] * 4,
        out_specs=[vm] * 6 + [hbm],
        scratch_shapes=Quad.scratch(own, width)
        + [
            pltpu.VMEM((own, width), bf),
            pltpu.VMEM(w1.shape, bf),
            pltpu.VMEM(w2.shape, bf),
            pltpu.VMEM((rows, hidden), f4),
            pltpu.VMEM((2 * own, width), bf),
            pltpu.SemaphoreType.DMA((5,)),
            pltpu.SemaphoreType.DMA((max(early, 1),)),
            pltpu.SemaphoreType.DMA((max(early, 1),)),
        ],
        compiler_params=pltpu.CompilerParams(collective_id=1, has_side_effects=True, vmem_limit_bytes=64 * 2**20),
    )(att, w_out, x, cot, act, w1, w2, bias[None], gain[None], shift[None], fc1_bias[None])
def tn(left, right):
    return lax.dot_general(left, right, (((0,), (0,)), ((), ())), preferred_element_type=jnp.float32)


def nn(left, right):
    return jnp.dot(left, right, preferred_element_type=jnp.float32)


def lane_mask(rows, head):
    lane = lax.broadcasted_iota(jnp.int32, (rows, 2 * HEAD), 1)
    return (lane < HEAD) if head == 0 else (lane >= HEAD)


def scores_of(keys, query, bias):
    scores = nt(keys, query)
    count = scores.shape[0]
    row = lax.broadcasted_iota(jnp.int32, (PREFIX, PREFIX), 0)
    col = lax.broadcasted_iota(jnp.int32, (PREFIX, PREFIX), 1)
    parts = [scores[:PREFIX] + bias]
    if count > 2 * PREFIX:
        parts.append(scores[PREFIX : count - PREFIX])
    parts.append(jnp.where(row <= col, scores[count - PREFIX :], NEGATIVE))
    return jnp.concatenate(parts, axis=0)


def attend_back(p, bias, q_ref, k_ref, v_ref, l_ref, g_ref, d_ref, room):
    rows, width = q_ref.shape
    blocks = rows // PREFIX
    base = pl.multiple_of(p * 2 * HEAD, 2 * HEAD)
    lanes = pl.ds(base, 2 * HEAD)
    sums = jnp.zeros((1, 2 * HEAD), jnp.float32)
    for r in reversed(range(blocks)):
        count, own = (r + 2) * PREFIX, slice(r * PREFIX, (r + 1) * PREFIX)
        query, grad, keys, values = q_ref[own, lanes], g_ref[own, lanes], k_ref[:count, lanes], v_ref[:count, lanes]
        d_queries, d_keys, d_values = [], None, None
        for e in range(2):
            mask = lane_mask(PREFIX, e)
            query_e = jnp.where(mask, query, jnp.zeros_like(query))
            grad_e = jnp.where(mask, grad, jnp.zeros_like(grad))
            probs = jnp.exp(scores_of(keys, query_e, bias) - l_ref[p, e : e + 1, own])
            d_probs = nt(values, grad_e)
            inner = jnp.sum(probs * d_probs, axis=0, keepdims=True)
            d_scores = (probs * (d_probs - inner)).astype(jnp.bfloat16)
            keys_e, values_e = nn(d_scores, query_e), nn(probs.astype(jnp.bfloat16), grad_e)
            d_keys = keys_e if d_keys is None else d_keys + keys_e
            d_values = values_e if d_values is None else d_values + values_e
            d_queries.append(tn(d_scores, keys))
        d_query = jnp.where(lane_mask(PREFIX, 0), d_queries[0], d_queries[1]) * HEAD ** (-0.5)
        sums += jnp.sum(d_query, axis=0, keepdims=True)
        d_ref[(r + 1) * PREFIX : (r + 2) * PREFIX, lanes] = d_query.astype(jnp.bfloat16)
        for n in range(r + 2):
            for at, sums_of in ((n, d_keys), (blocks + 1 + n, d_values)):
                place, term = slice(at * 2 * HEAD, (at + 1) * 2 * HEAD), sums_of[n * PREFIX : (n + 1) * PREFIX]
                if r == blocks - 1:
                    room[:PREFIX, place] = term
                else:
                    room[:PREFIX, place] += term
    d_ref[:PREFIX, lanes] = jnp.zeros((PREFIX, 2 * HEAD), jnp.bfloat16)
    value_sums = jnp.zeros((1, 2 * HEAD), jnp.float32)
    for n in range(blocks + 1):
        span = slice(n * PREFIX, (n + 1) * PREFIX)
        for m, at in ((1, n), (2, blocks + 1 + n)):
            total = room[:PREFIX, at * 2 * HEAD : (at + 1) * 2 * HEAD]
            d_ref[span, pl.ds(pl.multiple_of(base + m * width, 2 * HEAD), 2 * HEAD)] = total.astype(jnp.bfloat16)
            if m == 2:
                value_sums += column_sum(total)
    return sums, value_sums


def own_block(quad, i, size):
    first = quad.head // size
    start = jnp.where(i < first, quad.tp * quad.head + i * size, PREFIX + quad.tp * quad.rest + (i - first) * size)
    return pl.ds(pl.multiple_of(start, size), size), pl.ds(pl.multiple_of(i * size, size), size)


def norm_back(grad, source, gain):
    unit, scale = normed(source)
    scaled = grad * gain
    mean = jnp.mean(scaled, axis=1, keepdims=True)
    slope = jnp.mean(scaled * unit, axis=1, keepdims=True)
    return scale * (scaled - mean - unit * slope), grad * unit


def product_part(left, right, tile, turned, rows):
    def part(j, block):
        cols = pl.ds(pl.multiple_of(tile(j) * COLS, COLS), COLS)
        span = pl.ds(pl.multiple_of(block * rows, rows), rows)
        if turned:
            return nn(left[span, :], right[:, cols])
        return tn(left[:, span], right[:, cols])

    return part


def pick(table, j):
    found = table[0]
    for n, entry in enumerate(table[1:]):
        found = jnp.where(j == n + 1, entry, found)
    return found


class Wide(Quad):
    def rows_of(self, ref, quarter):
        own = [pl.ds(pl.multiple_of(span.start + PREFIX, 16), span.size) for span in self.spans(quarter)]
        return jnp.concatenate([ref[span] for span in [self.spans(quarter)[0]] + own], axis=0)


def back_kernel(lines, turned, *refs):
    (g_hbm, h2_hbm, hid_hbm, dpre_hbm, w1_hbm, w_qkv_hbm, w2_hbm, wo_hbm, h_hbm, att_hbm, mid_hbm, cot_hbm, x_hbm, gp_hbm,
     act, gain1, gain2, ffn_bias, bias, weight, theirs, q, k, v, lse, vec_in,
     fc2_out, fc1_out, out_grad, qkv_grad, in_hbm, act_hbm, dmid_hbm, dh_hbm, land_hbm, vec, *scratch) = refs
    ring_refs, scratch = scratch[:16], scratch[16:]
    quad_refs, scratch = scratch[:12], scratch[12:]
    (x0, x1, y0, y1, weights, mid, own_in, full, d_att, d_all, fresh, back, v_send, v_recv, g_theirs, tile_in,
     loads, stores, s_v, r_v, s_t, r_t, c_over) = scratch
    rows, width = full.shape
    quad, wide = Quad(quad_refs, rows, rows // 4), Wide(quad_refs, rows, (rows + PREFIX) // 4)
    own_rows, depth = quad.height, q.shape[1]
    tiles, cols = y0.shape[1] // COLS, depth // COLS
    block_rows = ring_refs[0].shape[1]
    extra = fresh.shape[0] // block_rows
    order1 = [*range(tiles - 2), tiles - 1, tiles - 2]
    later = ((0, 2 * tiles - 1),)
    base = 2 * tiles + 1 + extra
    g_part = x0.at[:, :rows] if turned else x0.at[:rows]
    columns = lambda n: pl.ds(pl.multiple_of(n * COLS, COLS), COLS)

    def tile_copy(n):
        return pltpu.make_async_remote_copy(
            src_ref=y0.at[:, n * COLS : (n + 1) * COLS], dst_ref=land_hbm.at[n], send_sem=s_t.at[n], recv_sem=r_t.at[n],
            device_id=ring.partner, device_id_type=MESH)

    def tile_part(j, block):
        @pl.when(block < 2)
        def _():
            for n in range(tiles):
                @pl.when(j == n)
                def _():
                    tile_copy(n).wait_recv()
            fetch = pltpu.make_async_copy(land_hbm.at[j], tile_in, loads.at[11])
            fetch.start()
            fetch.wait()

        span = pl.ds(pl.multiple_of(block * block_rows, block_rows), block_rows)
        side_span = pl.ds(pl.multiple_of(block // 2 * block_rows, block_rows), block_rows)
        return tn(g_part[:, span], y0[:, columns(j)]) + tn(g_theirs[:, side_span], tile_in[...])

    def prefix_part(j, block):
        return fresh[pl.ds(pl.multiple_of(j * block_rows, block_rows), block_rows)]

    def outs(job):
        local = job - tiles - 1
        head = jnp.maximum(job - base - cols, 0)
        place2, place1 = columns(jnp.clip(job - 1, 0, tiles - 1)), columns(pick(order1, local))
        is2 = (job > 0) & (job <= tiles)
        is1 = (job > tiles) & (job <= 2 * tiles)
        is_out = (job >= base) & (job < base + cols)
        out_span = columns(jnp.clip(job - base, 0, cols - 1))
        return [
            (is2, True, fc2_out.at[place2]),
            (is1, False, fc1_out.at[:, place1]),
            (is_out, True, out_grad.at[out_span]),
            (job >= base + cols, False, qkv_grad.at[head // cols, :, columns(lax.rem(head, cols))]),
        ]

    fc2_part = product_part(g_part, y0, lambda j: j, turned, block_rows) if turned else tile_part
    groups = [
        (1, product_part(x1, y1, lambda j: tiles - 1, turned, block_rows), "x"),
        (tiles, fc2_part, "x" if turned else "t"),
        (tiles, product_part(x1, y1, lambda j: pick(order1, j), turned, block_rows), "x"),
        (extra, prefix_part, "p"),
        (cols, product_part(x1 if turned else full, d_att, lambda j: j, turned, block_rows), "x"),
        (3 * cols, product_part(x0, d_all, lambda j: j, turned, block_rows), "x"),
    ]
    ring = Ring(lines, groups, ring_refs, outs, later, (weight, theirs, back))

    def load(n, source, target):
        return pltpu.make_async_copy(source, target, loads.at[n])

    def store(n, source, target):
        return pltpu.make_async_copy(source, target, stores.at[n])

    def begin(*copies):
        for copy in copies:
            copy.start()

    def end(*copies):
        for copy in copies:
            copy.wait()

    spans = quad.spans(quad.tp)
    first = [load(2, dpre_hbm, y1), load(4, h2_hbm, x1), load(0, hid_hbm, y0), load(1, g_hbm, g_part)]
    second = [load(3, w1_hbm, weights)]
    if not turned:
        second.append(load(12, gp_hbm, g_theirs))
    third = [
        load(5, mid_hbm, mid),
        load(6, cot_hbm.at[spans[0]], own_in.at[: quad.head]),
        load(7, cot_hbm.at[spans[1]], own_in.at[quad.head :]),
    ]
    begin(*first, *second, *third)
    ctx, tp = lax.axis_index("ctx"), lax.axis_index("tp")
    swaps, bit = [quad.across, quad.over], 1
    while bit < 2 * lines:
        swaps.append((ctx + bit - 2 * bit * lax.rem(ctx // bit, 2), tp))
        bit *= 2
    meet(ring.peers() + quad.peers() + [(None, device) for device in swaps[4:]])

    def swap(n):
        return pltpu.make_async_remote_copy(
            src_ref=v_send.at[n], dst_ref=v_recv.at[n], send_sem=s_v.at[n], recv_sem=r_v.at[n],
            device_id=swaps[n], device_id_type=MESH)

    def swap_start(n):
        v_send[n] = vec[...]
        swap(n).start()

    def swap_end(n):
        swap(n).wait()
        if n < 2:
            vec[:6] += v_recv[n, :6]
        else:
            vec[...] += v_recv[n]

    def add_all(group):
        lax.fori_loop(0, group.tiles, lambda n, _: (group.scatter_add(n), 0)[1], 0)

    end(*first)
    if not turned:
        for n in range(tiles):
            tile_copy(n).start()
    ring.start()
    end(*second)
    quad.scatter_send(lambda part, n: nt(quad.half_of(y1, part), weights[quad.columns(n), :]))
    wo_copy = load(3, wo_hbm, weights.at[:depth])
    wo_copy.start()
    end(*third)
    ring.run(0, 5)
    add_all(quad)
    vec[...] = vec_in[...]
    size = 32

    def middle_rows(i, _):
        whole, own = own_block(quad, i, size)
        grad = quad.acc[own]
        change, gain_terms = norm_back(grad, mid[own], gain2[...])
        d_middle = own_in[own].astype(jnp.float32) + change
        quad.acc[own] = d_middle
        low = (act[whole] * d_middle).astype(jnp.bfloat16)
        full[whole] = low
        vec[2:3] += column_sum(low.astype(jnp.float32))
        vec[3:4] += column_sum(gain_terms)
        vec[4:5] += column_sum(grad)
        return 0

    lax.fori_loop(0, own_rows // size, middle_rows, 0)
    quad.gather_send(full)
    keep = store(0, quad.acc.at[:own_rows], dmid_hbm)
    x_copies = [load(6, x_hbm.at[spans[0]], own_in.at[: quad.head]), load(7, x_hbm.at[spans[1]], own_in.at[quad.head :])]
    begin(keep, *x_copies)
    ring.run(5, 10)
    quad.gather_near(full)
    quad.gather_pass(full)
    quad.gather_far(full)
    wo_copy.wait()

    def attended_rows(i, _):
        span = pl.ds(pl.multiple_of(i * PREFIX, PREFIX), PREFIX)
        d_att[span] = nt(full[span], weights[:depth, :]).astype(jnp.bfloat16)
        return 0

    lax.fori_loop(0, rows // PREFIX, attended_rows, 0)
    heads = [load(8 + m, w_qkv_hbm.at[m], weights.at[:, m * depth : (m + 1) * depth]) for m in range(3)]
    begin(*heads)
    keep.wait()
    pairs = depth // (2 * HEAD)

    now = 10
    for p in range(pairs):
        sums, value_sums = attend_back(p, bias[0, 0], q, k, v, lse, d_att, d_all, quad.acc)
        start = p * 2 * HEAD
        vec[7:8, start : start + 2 * HEAD] = sums
        vec[7:8, start + depth : start + depth + 2 * HEAD] = value_sums
        ring.run(now, now + 2)
        now += 2
    att_copy = load(2, att_hbm, d_att)
    att_copy.start()
    quad.gather_done(full)
    quad.scatter_done()
    end(*heads)
    wide.scatter_send(lambda part, n: nt(wide.half_of(d_all, part), weights[wide.columns(n), : 3 * depth]))
    w2_copy = load(3, w2_hbm, weights)
    w2_copy.start()
    free0, free1 = (tiles + 1) * lines, (2 * tiles + 1) * lines
    ring.run(now, free0)
    h_copy = load(1, h_hbm, x0)
    h_copy.start()
    ring.run(free0, free0 + 2)
    add_all(wide)
    pl.semaphore_signal(c_over, inc=1, device_id=quad.over, device_id_type=MESH)
    for n in range(wide.tiles):
        fresh[n * wide.head : (n + 1) * wide.head] = wide.acc[: wide.head, n * COLS : (n + 1) * COLS]
    dh_copy = store(1, wide.acc.at[pl.ds(wide.head, own_rows)], dh_hbm)
    dh_copy.start()
    att_copy.wait()
    ring.run(free0 + 2, free1 - AHEAD)
    h_copy.wait()
    ring.run(free1 - AHEAD, free1)
    if turned:

        def flip(n, _):
            x1[columns(n), :] = full[:, columns(n)].T
            return 0

        lax.fori_loop(0, width // COLS, flip, 0)
    wide.scatter_done()
    end(dh_copy, w2_copy)
    pl.semaphore_wait(c_over, 1)
    if not turned:
        for n in range(tiles):
            tile_copy(n).wait_send()
    quad.scatter_send(lambda part, n: nn(quad.half_of(y0, part), weights[:, quad.columns(n)]))
    ring.run(free1, free1 + lines)
    add_all(quad)

    def out_rows(i, _):
        whole, own = own_block(quad, i, size)
        y1[whole] = (mid[own] + act[whole] * (quad.acc[own] + ffn_bias[...])).astype(jnp.bfloat16)
        return 0

    lax.fori_loop(0, own_rows // size, out_rows, 0)
    quad.gather_send(y1)
    again = [load(4, dh_hbm, quad.acc.at[:own_rows]), load(5, dmid_hbm, mid)]
    begin(*again)
    ready = base * lines + SKEW * (lines - 1)
    ring.run(free1 + lines, ready)
    quad.gather_near(y1)
    quad.gather_pass(y1)
    quad.gather_far(y1)
    act_copy = store(0, y1, act_hbm)
    act_copy.start()
    end(*again, *x_copies)
    for n in range(quad.tiles):
        quad.acc[: quad.head, n * COLS : (n + 1) * COLS] += back[n * quad.head : (n + 1) * quad.head]

    def input_rows(i, _):
        whole, own = own_block(quad, i, size)
        grad = quad.acc[own]
        change, gain_terms = norm_back(grad, own_in[own].astype(jnp.float32), gain1[...])
        y0[whole] = (mid[own] + change).astype(jnp.bfloat16)
        vec[0:1] += column_sum(gain_terms)
        vec[1:2] += column_sum(grad)
        return 0

    lax.fori_loop(0, own_rows // size, input_rows, 0)
    quad.gather_send(y0, 1)
    swap_start(0)
    late = min(max(ready, ring.steps - AHEAD), ring.steps - 4)
    ring.run(ready, late)
    swap_end(0)
    swap_start(1)
    ring.run(late, late + 2)
    swap_end(1)
    swap_start(2)
    ring.run(late + 2, ring.steps)
    quad.gather_near(y0, 1)
    quad.gather_pass(y0, 1)
    swap_end(2)
    swap_start(3)
    ring.run(ring.steps, ring.steps + SKEW)
    quad.gather_far(y0, 1)
    in_copy = store(1, y0, in_hbm)
    in_copy.start()
    swap_end(3)
    for n in range(4, len(swaps)):
        swap_start(n)
        if n + 1 == len(swaps):
            ring.run(ring.steps + SKEW, ring.steps + 2 * SKEW)
        swap_end(n)
    ring.finish(ring.steps + 2 * SKEW)
    quad.gather_done(y1)
    quad.gather_done(y0, 1)
    quad.scatter_done()
    end(act_copy, in_copy)


def back_call(n_ctx, turned, g, h2, hid, dpre, w1, w_qkv, w2, w_out, h_all, att, mid, cot, x, g_theirs, act, gain1, gain2, ffn_bias,
              bias, weight, theirs, q, k, v, lse, vec):
    lines, rows, width = n_ctx // 2, cot.shape[0], cot.shape[1]
    block_rows, own, cols = width // n_ctx, rows // 4, q.shape[1]
    hidden = hid.shape[1]
    returned = PREFIX * width // 4 // COLS
    rounds = n_ctx.bit_length() + 1
    vm, hbm, sm = (pl.BlockSpec(memory_space=s) for s in (pltpu.VMEM, pl.ANY, pltpu.SMEM))
    bf, f4 = jnp.bfloat16, jnp.float32
    shape = jax.ShapeDtypeStruct
    return pl.pallas_call(
        functools.partial(back_kernel, lines, turned),
        out_shape=(
            shape((hidden, block_rows), f4),
            shape((block_rows, hidden), f4),
            shape((cols, block_rows), f4),
            shape((3, block_rows, cols), f4),
            shape((rows, width), bf),
            shape((rows, width), bf),
            shape((own, width), f4),
            shape((own, width), f4),
            shape((hidden // COLS, rows, COLS), bf),
            shape(vec.shape, f4),
        ),
        in_specs=[hbm] * 14 + [vm] * 4 + [sm] * 3 + [vm] * 5,
        out_specs=[hbm] * 9 + [vm],
        scratch_shapes=Ring.scratch(lines, block_rows)
        + Quad.scratch(own + PREFIX // 4, width)
        + [
            pltpu.VMEM(h_all.shape, bf),
            pltpu.VMEM(h2.shape, bf),
            pltpu.VMEM((rows, hidden), bf),
            pltpu.VMEM((rows, hidden), bf),
            pltpu.VMEM(w1.shape, bf),
            pltpu.VMEM((own, width), f4),
            pltpu.VMEM((own, width), bf),
            pltpu.VMEM((rows, width), bf),
            pltpu.VMEM((rows, cols), bf),
            pltpu.VMEM((rows + PREFIX, 3 * cols), bf),
            pltpu.VMEM((returned, COLS), f4),
            pltpu.VMEM((returned, COLS), f4),
            pltpu.VMEM((rounds, *vec.shape), f4),
            pltpu.VMEM((rounds, *vec.shape), f4),
            pltpu.VMEM((16, 128) if turned else g_theirs.shape, bf),
            pltpu.VMEM((16, 128) if turned else (rows, COLS), bf),
            pltpu.SemaphoreType.DMA((13,)),
            pltpu.SemaphoreType.DMA((2,)),
            pltpu.SemaphoreType.DMA((rounds,)),
            pltpu.SemaphoreType.DMA((rounds,)),
            pltpu.SemaphoreType.DMA((hidden // COLS,)),
            pltpu.SemaphoreType.DMA((hidden // COLS,)),
            pltpu.SemaphoreType.REGULAR,
        ],
        compiler_params=pltpu.CompilerParams(collective_id=2, has_side_effects=True, vmem_limit_bytes=64 * 2**20),
    )(g, h2, hid, dpre, w1, w_qkv, w2, w_out, h_all, att, mid, cot, x, g_theirs, act, gain1[None], gain2[None], ffn_bias[None],
      bias, weight, theirs, q, k, v, lse, vec)


def find_block(lengths, placed, block):
    mine, start, first = placed[block], 0, 0
    for s in range(lengths.shape[0]):
        first = jnp.where(start <= mine, start, first)
        start = start + lengths[s]
    owner = 0
    for e in range(placed.shape[0]):
        owner = owner + jnp.where(placed[e] == first, e, 0)
    return mine - first, jnp.minimum(owner, placed.shape[0] - 1)


def attend_own(p, q, k, v, held, peaks, totals):
    lanes = pl.ds(pl.multiple_of(p * 2 * HEAD, 2 * HEAD), 2 * HEAD)
    rows = q.shape[0]
    value_t = v[PREFIX:, lanes].T
    row = lax.broadcasted_iota(jnp.int32, (PREFIX, PREFIX), 0)
    col = lax.broadcasted_iota(jnp.int32, (PREFIX, PREFIX), 1)
    for r in range(rows // PREFIX):
        own, count = slice(r * PREFIX, (r + 1) * PREFIX), (r + 1) * PREFIX
        query, keys = q[own, lanes], k[PREFIX : PREFIX + count, lanes]
        for e in range(2):
            scores = nt(keys, jnp.where(lane_mask(PREFIX, e), query, jnp.zeros_like(query)))
            last = jnp.where(row <= col, scores[count - PREFIX :], NEGATIVE)
            scores = jnp.concatenate([scores[: count - PREFIX], last], axis=0) if r else last
            peak = jnp.max(scores, axis=0, keepdims=True)
            raised = jnp.exp(scores - peak)
            peaks[p, e : e + 1, own] = peak
            totals[p, e : e + 1, own] = jnp.sum(raised, axis=0, keepdims=True)
            part = slice(e * HEAD, (e + 1) * HEAD)
            held[p, part, own] = nn(value_t[part, :count], raised.astype(jnp.bfloat16))


def attend_prefix(p, bias, q, k, v, held, peaks, totals, out, lse):
    lanes = pl.ds(pl.multiple_of(p * 2 * HEAD, 2 * HEAD), 2 * HEAD)
    query, keys, value_t = q[:, lanes], k[:PREFIX, lanes], v[:PREFIX, lanes].T
    outs = []
    for e in range(2):
        scores = nt(keys, jnp.where(lane_mask(q.shape[0], e), query, jnp.zeros_like(query))) + bias
        before = peaks[p, e : e + 1]
        peak = jnp.maximum(before, jnp.max(scores, axis=0, keepdims=True))
        raised = jnp.exp(scores - peak)
        shrink = jnp.exp(before - peak)
        total = totals[p, e : e + 1] * shrink + jnp.sum(raised, axis=0, keepdims=True)
        lse[p, e : e + 1] = peak + jnp.log(total)
        part = slice(e * HEAD, (e + 1) * HEAD)
        summed = held[p, part] * shrink + nn(value_t[part], raised.astype(jnp.bfloat16))
        outs.append(summed * (1.0 / total))
    out[:, lanes] = jnp.concatenate(outs, axis=0).astype(jnp.bfloat16).T


def first_kernel(lines, *refs):
    (lengths, placed, layer, exits, x_hbm, w_hbm, gain, shift, qv_bias,
     q, k, v, h_all, act, att, lse, bias, weight, theirs, *scratch) = refs
    (x, w, line, x_send, x_recv, prefix, held, peaks, totals, loads, s_l, s_r, r_z, s_x, r_x, s_g, r_g) = scratch
    rows, width = x.shape
    part = prefix.shape[0] // 4
    ctx, tp = lax.axis_index("ctx"), lax.axis_index("tp")
    z, side, y, core = ctx // 2, lax.rem(ctx, 2), tp // 2, lax.rem(tp, 2)
    left, right, partner = (ctx - 2, tp), (ctx + 2, tp), (z * 2 + 1 - side, tp)
    across, over = (ctx, y * 2 + 1 - core), (ctx, (1 - y) * 2 + core)
    own = pl.ds(pl.multiple_of(tp * part, 16), part)
    copies = [
        pltpu.make_async_copy(x_hbm.at[own], line.at[z], loads.at[0]),
        pltpu.make_async_copy(x_hbm, x, loads.at[1]),
        pltpu.make_async_copy(w_hbm, w, loads.at[2]),
    ]
    for copy in copies:
        copy.start()
    meet([(None, partner), (z > 0, left), (z < lines - 1, right), (None, across), (None, over)])

    def hop(o, device, sems):
        return pltpu.make_async_remote_copy(
            src_ref=line.at[o], dst_ref=line.at[o], send_sem=sems.at[o], recv_sem=r_z.at[o],
            device_id=device, device_id_type=MESH)

    def pass_on(o, there, device, sems):
        @pl.when(there)
        def _():
            hop(o, device, sems).start()

    copies[0].wait()
    pass_on(z, z < lines - 1, right, s_r)
    pass_on(z, z > 0, left, s_l)

    def hops(d):
        @pl.when(z - d >= 0)
        def _():
            hop(z - d, left, s_l).wait_recv()
            pass_on(z - d, z < lines - 1, right, s_r)

        @pl.when(z + d < lines)
        def _():
            hop(z + d, right, s_r).wait_recv()
            pass_on(z + d, z > 0, left, s_l)

    my_part, my_owner = find_block(lengths, placed, ctx)
    partner_part, partner_owner = find_block(lengths, placed, z * 2 + 1 - side)
    bias[0, 0] = jnp.where(my_part > 0, 0.0, NEGATIVE)
    for e in range(weight.shape[0]):
        weight[e] = jnp.where((my_owner == e) & (my_part > 0), 1.0, 0.0)
        theirs[e] = jnp.where((partner_owner == e) & (partner_part > 0), 1.0, 0.0)
    row = lax.broadcasted_iota(jnp.int32, exits.shape, 0)
    first_rows = jnp.where(my_part == 0, PREFIX, 0)
    act[...] = jnp.where((exits[...] > layer[0]) | (row < first_rows), 1.0, 0.0)
    size = 64

    def norm_rows(source, start, to):
        def some(i, _):
            span = pl.ds(pl.multiple_of(start + i * size, size), size)
            values = source[span].astype(jnp.float32)
            target = pl.ds(pl.multiple_of(to + i * size, size), size)
            h_all[target] = (normed(values)[0] * gain[...] + shift[...]).astype(jnp.bfloat16)
            return 0

        lax.fori_loop(0, PREFIX // size, some, 0)

    def keys_of(span, rows_in):
        k[span] = nn(rows_in, w[1]).astype(jnp.bfloat16)
        v[span] = (nn(rows_in, w[2]) + qv_bias[1:2]).astype(jnp.bfloat16)

    for r in range(rows // PREFIX):
        norm_rows(x_wait(copies, r, x), r * PREFIX, (r + 1) * PREFIX)
        if r == 0:
            copies[2].wait()
        span = slice((r + 1) * PREFIX, (r + 2) * PREFIX)
        rows_in = h_all[span]
        low = (nn(rows_in, w[0]) + qv_bias[0:1]).astype(jnp.bfloat16)
        q[r * PREFIX : (r + 1) * PREFIX] = low * jnp.bfloat16(HEAD**-0.5)
        keys_of(span, rows_in)
        if r + 1 < lines:
            hops(r + 1)
    for d in range(rows // PREFIX + 1, lines):
        hops(d)
    x_send[...] = line[partner_owner // 2]
    trade = pltpu.make_async_remote_copy(
        src_ref=x_send, dst_ref=x_recv, send_sem=s_x, recv_sem=r_x, device_id=partner, device_id_type=MESH)
    trade.start()
    near = line[my_owner // 2]
    pairs = q.shape[1] // (2 * HEAD)

    def own_pairs(lo, hi):
        lax.fori_loop(lo, hi, lambda p, _: (attend_own(p, q, k, v, held, peaks, totals), 0)[1], 0)

    own_pairs(0, pairs // 2)
    trade.wait_recv()
    prefix[own] = jnp.where(lax.rem(my_owner, 2) == side, near, x_recv[...])

    def give(n, quarter, device):
        span = pl.ds(pl.multiple_of(quarter * part, 16), part)
        return pltpu.make_async_remote_copy(
            src_ref=prefix.at[span], dst_ref=prefix.at[span], send_sem=s_g.at[n], recv_sem=r_g.at[n],
            device_id=device, device_id_type=MESH)

    far = (1 - y) * 2 + core
    give(0, tp, over).start()
    give(1, tp, across).start()
    own_pairs(pairs // 2, pairs)
    give(0, far, over).wait_recv()
    give(2, far, across).start()
    give(1, y * 2 + 1 - core, across).wait_recv()
    give(2, (1 - y) * 2 + 1 - core, across).wait_recv()
    norm_rows(prefix, 0, 0)
    keys_of(slice(0, PREFIX), h_all[:PREFIX])
    hide = jnp.where(my_part > 0, 0.0, NEGATIVE)

    def prefix_pair(p, _):
        attend_prefix(p, hide, q, k, v, held, peaks, totals, att, lse)
        return 0

    lax.fori_loop(0, pairs, prefix_pair, 0)
    trade.wait_send()
    give(0, tp, over).wait_send()
    give(1, tp, across).wait_send()
    give(2, far, across).wait_send()
    for o in range(lines):
        @pl.when((z < lines - 1) & (z >= o))
        def _():
            hop(o, right, s_r).wait_send()

        @pl.when((z > 0) & (z <= o))
        def _():
            hop(o, left, s_l).wait_send()


def x_wait(copies, r, x):
    if r == 0:
        copies[1].wait()
    return x


def first_call(n_ctx, lengths, placed, layer, exits, x, w_qkv, gain, shift, qv_bias):
    lines, (rows, width) = n_ctx // 2, x.shape
    cols = w_qkv.shape[2]
    vm, hbm, sm = (pl.BlockSpec(memory_space=s) for s in (pltpu.VMEM, pl.ANY, pltpu.SMEM))
    bf, f4 = jnp.bfloat16, jnp.float32
    return pl.pallas_call(
        functools.partial(first_kernel, lines),
        out_shape=(
            jax.ShapeDtypeStruct((rows, cols), bf),
            jax.ShapeDtypeStruct((rows + PREFIX, cols), bf),
            jax.ShapeDtypeStruct((rows + PREFIX, cols), bf),
            jax.ShapeDtypeStruct((rows + PREFIX, width), bf),
            jax.ShapeDtypeStruct((rows, 1), f4),
            jax.ShapeDtypeStruct((rows, cols), bf),
            jax.ShapeDtypeStruct((cols // (2 * HEAD), 2, rows), f4),
            jax.ShapeDtypeStruct((1, 1), f4),
            jax.ShapeDtypeStruct((n_ctx,), f4),
            jax.ShapeDtypeStruct((n_ctx,), f4),
        ),
        in_specs=[sm] * 3 + [vm] + [hbm] * 2 + [vm] * 3,
        out_specs=[vm] * 7 + [sm] * 3,
        scratch_shapes=[
            pltpu.VMEM((rows, width), bf),
            pltpu.VMEM(w_qkv.shape, bf),
            pltpu.VMEM((lines, PREFIX // 4, width), bf),
            pltpu.VMEM((PREFIX // 4, width), bf),
            pltpu.VMEM((PREFIX // 4, width), bf),
            pltpu.VMEM((PREFIX, width), bf),
            pltpu.VMEM((cols // (2 * HEAD), 2 * HEAD, rows), f4),
            pltpu.VMEM((cols // (2 * HEAD), 2, rows), f4),
            pltpu.VMEM((cols // (2 * HEAD), 2, rows), f4),
            pltpu.SemaphoreType.DMA((3,)),
            pltpu.SemaphoreType.DMA((lines,)),
            pltpu.SemaphoreType.DMA((lines,)),
            pltpu.SemaphoreType.DMA((lines,)),
            pltpu.SemaphoreType.DMA,
            pltpu.SemaphoreType.DMA,
            pltpu.SemaphoreType.DMA((3,)),
            pltpu.SemaphoreType.DMA((3,)),
        ],
        compiler_params=pltpu.CompilerParams(collective_id=4, has_side_effects=True, vmem_limit_bytes=64 * 2**20),
    )(lengths, placed, layer, exits[:, None], x, w_qkv, gain[None], shift[None], qv_bias)


def body(
    mesh,
    block_input,
    cotangent,
    ln1_gain,
    ln1_bias,
    w_qkv,
    qv_bias,
    w_out,
    out_bias,
    ln2_gain,
    ln2_bias,
    w_fc1,
    fc1_bias,
    w_fc2,
    fc2_bias,
    exit_layer,
    layer_index,
    lengths,
    stretch_map,
):
    n_ctx = mesh.shape["ctx"]
    row_count, width = block_input.shape
    block_rows = width // n_ctx
    turned = block_rows % 128 != 0

    def tokens_last(array):
        return array.T if turned else array

    query, key, value, h_all, active, attended, log_total, bias, weight, theirs = first_call(
        n_ctx, lengths, stretch_map, layer_index, exit_layer, block_input, w_qkv, ln1_gain, ln1_bias, qv_bias
    )
    middle, h2_low, grad_ffn, hidden_low, d_pre_low, vectors, grad_theirs = front_call(
        0 if turned else n_ctx // 2, attended, w_out, block_input, cotangent, active, w_fc1, w_fc2, out_bias, ln2_gain, ln2_bias, fc1_bias
    )
    fc2_grad, fc1_grad, out_grad, qkv_grad, input_grad, output_rows, _, _, _, vectors = back_call(
        n_ctx, turned, tokens_last(grad_ffn), tokens_last(h2_low), hidden_low, d_pre_low, w_fc1, w_qkv, w_fc2, w_out,
        tokens_last(h_all), attended, middle, cotangent, block_input, grad_theirs, active, ln1_gain, ln2_gain, fc2_bias,
        bias, weight, theirs, query, key, value, log_total, vectors,
    )
    qv_grad = vectors[7, : 2 * query.shape[1]].reshape(2, -1)
    return (
        output_rows,
        input_grad,
        vectors[0],
        vectors[1],
        qkv_grad,
        qv_grad,
        out_grad,
        vectors[2],
        vectors[3],
        vectors[4],
        fc1_grad,
        vectors[6],
        fc2_grad,
        vectors[5],
    )


def solution(mesh):
    in_specs = (
        P("ctx", None),
        P("ctx", None),
        P(),
        P(),
        P(None, None, "tp"),
        P(None, "tp"),
        P("tp", None),
        P(),
        P(),
        P(),
        P(None, "tp"),
        P("tp"),
        P("tp", None),
        P(),
        P("ctx"),
        P(),
        P(),
        P(),
    )
    out_specs = (
        P("ctx", None),
        P("ctx", None),
        P(),
        P(),
        P(None, "ctx", "tp"),
        P(None, "tp"),
        P("tp", "ctx"),
        P(),
        P(),
        P(),
        P("ctx", "tp"),
        P("tp"),
        P("tp", "ctx"),
        P(),
    )
    return jax.shard_map(functools.partial(body, mesh), mesh=mesh, in_specs=in_specs, out_specs=out_specs, check_vma=False)
```

```python
import functools
import math

import jax
import jax.numpy as jnp
from jax import lax
from jax.experimental import pallas as pl
from jax.experimental.pallas import tpu as pltpu
from jax.sharding import PartitionSpec as P

HEAD = 64
PREFIX = 256
COLS = 512
MESH = pl.DeviceIdType.MESH
NEGATIVE = -1e30
EPSILON = 1e-05
AHEAD = 8
SKEW = 2
STAGES = 2
DEPTH = 2


class Ring:
    def __init__(self, lines, groups, refs, outs, later=(), prefix=None):
        self.lines, self.groups, self.outs, self.later, self.prefix = lines, groups, outs, later, prefix
        (self.xs, self.xr, self.zb, self.stage, self.turned, self.kept, self.swap, self.s_xs, self.s_xr, self.s_zs,
         self.s_zr, self.s_out, self.s_swap, self.c_x, self.c_left, self.c_right) = refs
        self.jobs = sum(group[0] for group in groups)
        marks, alone, job = [], [], 0
        for group in groups:
            marks += [job + n for n in range(group[0]) if group[2] == "p"]
            alone += [job + n for n in range(group[0]) if group[2] == "t"]
            job += group[0]
        self.alone = (alone[0], alone[-1]) if alone else None
        self.fetched = (marks[0], marks[-1]) if marks else (self.jobs, self.jobs)
        self.steps = self.jobs * lines
        self.slots = self.xr.shape[0]
        self.lag = SKEW * (lines - 1) + 2
        ctx, tp = lax.axis_index("ctx"), lax.axis_index("tp")
        self.z, self.side = ctx // 2, lax.rem(ctx, 2)
        self.partner = (self.z * 2 + 1 - self.side, tp)
        self.left, self.right = (ctx - 2, tp), (ctx + 2, tp)

    @staticmethod
    def scratch(lines, rows):
        slots = AHEAD + SKEW * (lines - 1) + 4
        chunk = (rows, COLS)
        return [
            pltpu.VMEM((AHEAD, *chunk), jnp.bfloat16),
            pltpu.VMEM((slots, *chunk), jnp.bfloat16),
            pltpu.VMEM((DEPTH, lines + 1, *chunk), jnp.bfloat16),
            pltpu.VMEM((STAGES, *chunk), jnp.float32),
            pltpu.VMEM((STAGES, COLS, rows), jnp.float32),
            pltpu.VMEM(chunk, jnp.bfloat16),
            pltpu.VMEM((4, *chunk), jnp.bfloat16),
            pltpu.SemaphoreType.DMA((AHEAD,)),
            pltpu.SemaphoreType.DMA((slots,)),
            pltpu.SemaphoreType.DMA((slots,)),
            pltpu.SemaphoreType.DMA((DEPTH, lines + 1)),
            pltpu.SemaphoreType.DMA((STAGES,)),
            pltpu.SemaphoreType.DMA((4,)),
            pltpu.SemaphoreType.REGULAR,
            pltpu.SemaphoreType.REGULAR,
            pltpu.SemaphoreType.REGULAR,
        ]

    def sends(self, f):
        job = f // self.lines
        found = (job < self.fetched[0]) | (job > self.fetched[1]) | (lax.rem(f, self.lines) == 0)
        for pair in self.later:
            found = found & (job != pair[0]) & (job != pair[1])
        if self.alone:
            found = found & ((job < self.alone[0]) | (job > self.alone[1]))
        return found

    def owner(self, f):
        turn = lax.rem(f + 2 * SKEW * self.lines * self.lines, self.lines)
        return jnp.where(lax.rem(turn, 2) == 0, turn // 2, self.lines - 1 - turn // 2)

    def peers(self):
        return [(None, self.partner), (self.z > 0, self.left), (self.z < self.lines - 1, self.right)]

    def x_copy(self, f):
        slot, to = lax.rem(f, AHEAD), lax.rem(f, self.slots)
        return pltpu.make_async_remote_copy(
            src_ref=self.xs.at[slot], dst_ref=self.xr.at[to], send_sem=self.s_xs.at[slot],
            recv_sem=self.s_xr.at[to], device_id=self.partner, device_id_type=MESH)

    def z_copy(self, f, to, device):
        slot, level = lax.rem(f, self.slots), lax.rem(f // self.lines, DEPTH)
        return pltpu.make_async_remote_copy(
            src_ref=self.xr.at[slot], dst_ref=self.zb.at[level, to], send_sem=self.s_zs.at[slot],
            recv_sem=self.s_zr.at[level, to], device_id=device, device_id_type=MESH)

    def out_copies(self, job, act):
        slot = lax.rem(job, STAGES)
        for there, turn, place in self.outs(job):
            @pl.when(there)
            def _():
                source = self.turned if turn else self.stage
                act(pltpu.make_async_copy(source.at[slot], place, self.s_out.at[slot]))

    def out_start(self, job):
        slot = lax.rem(job, STAGES)
        for there, turn, _ in self.outs(job):
            if turn:
                @pl.when(there)
                def _():
                    self.turned[slot] = self.stage[slot].T
        self.out_copies(job, lambda copy: copy.start())

    def out_wait(self, job):
        self.out_copies(job, lambda copy: copy.wait())

    def swap_copy(self, n):
        return pltpu.make_async_remote_copy(
            src_ref=self.swap.at[2 * n], dst_ref=self.swap.at[2 * n + 1], send_sem=self.s_swap.at[2 * n],
            recv_sem=self.s_swap.at[2 * n + 1], device_id=self.partner, device_id_type=MESH)

    def send(self, f, group, job0, fresh):
        _, part, kind = group
        is_prefix = kind == "p"
        if not fresh:
            @pl.when(self.sends(f - AHEAD))
            def _():
                self.x_copy(f).wait_send()

            @pl.when(f >= self.slots)
            def _():
                pl.semaphore_wait(self.c_x, 1)

        if kind == "t":
            return

        @pl.when(self.sends(f))
        def _():
            owner = self.owner(f)
            value = part(f // self.lines - job0, None if is_prefix else owner * 2 + 1 - self.side)
            self.xs[lax.rem(f, AHEAD)] = value.astype(jnp.bfloat16)
            self.x_copy(f).start()

    def receive(self, f, group, job0):
        _, part, kind = group
        is_prefix = kind == "p"
        job, owner, slot = f // self.lines, self.owner(f), lax.rem(f, self.slots)
        came = self.sends(f)

        if kind != "t":
            @pl.when(came)
            def _():
                self.x_copy(f).wait_recv()
                if is_prefix:
                    self.kept[...] = self.xr[slot]

        block = owner * 2 + self.side
        if is_prefix:
            mine, theirs = self.prefix[0][block], self.prefix[1][block]
            total = part(job - job0, None) * mine + self.kept[...].astype(jnp.float32) * theirs
        elif kind == "t":
            total = part(job - job0, block)
        else:
            @pl.when(jnp.logical_not(came))
            def _():
                self.xr[slot] = jnp.zeros(self.xr.shape[1:], jnp.bfloat16)

            for pair in self.later:
                block = jnp.where(job == pair[0], owner * 2 + 1 - self.side, block)
            total = part(job - job0, block) + self.xr[slot].astype(jnp.float32)

        @pl.when(owner != self.z)
        def _():
            self.xr[slot] = total.astype(jnp.bfloat16)

        @pl.when(owner == self.z)
        def _():
            @pl.when(job >= STAGES)
            def _():
                self.out_wait(job - STAGES)
            self.stage[lax.rem(job, STAGES)] = total

    def add(self, f, index):
        job = f // self.lines
        slot, level = lax.rem(f, self.slots), lax.rem(job, DEPTH)

        @pl.when(self.owner(f) == self.z)
        def _():
            self.stage[lax.rem(job, STAGES)] += self.zb[level, index].astype(jnp.float32)

        @pl.when(self.owner(f) != self.z)
        def _():
            self.xr[slot] = (self.xr[slot].astype(jnp.float32) + self.zb[level, index].astype(jnp.float32)).astype(jnp.bfloat16)

    def flow(self, t):
        lines, z = self.lines, self.z
        f = t - SKEW * z
        owner = self.owner(f)

        @pl.when((f >= 0) & (f < self.steps) & (owner >= z))
        def _():
            @pl.when(z > 0)
            def _():
                self.z_copy(f, owner, self.left).wait_recv()
                self.add(f, owner)
                pl.semaphore_signal(self.c_right, inc=1, device_id=self.left, device_id_type=MESH)

            @pl.when(owner > z)
            def _():
                @pl.when(f >= DEPTH * lines)
                def _():
                    pl.semaphore_wait(self.c_right, 1)
                self.z_copy(f, owner, self.right).start()

        g = t - SKEW * (lines - 1 - z)
        owner2 = self.owner(g)

        @pl.when((g >= 0) & (g < self.steps) & (owner2 <= z))
        def _():
            @pl.when(z < lines - 1)
            def _():
                index = jnp.where(owner2 == z, lines, owner2)
                self.z_copy(g, index, self.right).wait_recv()
                self.add(g, index)
                pl.semaphore_signal(self.c_left, inc=1, device_id=self.right, device_id_type=MESH)

            @pl.when(owner2 < z)
            def _():
                @pl.when(g >= DEPTH * lines)
                def _():
                    pl.semaphore_wait(self.c_left, 1)
                self.z_copy(g, jnp.where(owner2 == z - 1, lines, owner2), self.left).start()

        h = t - SKEW * (lines - 1)

        @pl.when((h >= 0) & (h < self.steps) & (self.owner(h) == z))
        def _():
            job = h // lines
            stage = lax.rem(job, STAGES)
            for n, pair in enumerate(self.later):
                @pl.when(job == pair[0])
                def _():
                    self.swap[2 * n] = self.stage[stage].astype(jnp.bfloat16)
                    self.swap_copy(n).start()

                @pl.when(job == pair[1])
                def _():
                    self.swap_copy(n).wait()
                    self.stage[stage] += self.swap[2 * n + 1].astype(jnp.float32)
            if self.prefix is not None:
                target, rows = self.prefix[2], self.stage.shape[1]

                @pl.when((job >= self.fetched[0]) & (job <= self.fetched[1]))
                def _():
                    span = pl.ds(pl.multiple_of((job - self.fetched[0]) * rows, rows), rows)
                    target[span] = self.stage[stage]
            self.out_start(job)

        d = t - self.lag

        @pl.when((d >= 0) & (d < self.steps))
        def _():
            @pl.when(self.owner(d) != z)
            def _():
                self.z_copy(d, 0, self.left).wait_send()
            pl.semaphore_signal(self.c_x, inc=1, device_id=self.partner, device_id_type=MESH)

    def find(self, f):
        job = 0
        for group in self.groups:
            if f < (job + group[0]) * self.lines:
                return group, job
            job += group[0]
        return None

    def pieces(self, lo, hi):
        cuts, job = {lo, hi}, 0
        for group in self.groups:
            job += group[0]
            cuts |= {job * self.lines, job * self.lines - AHEAD}
        cuts = sorted(c for c in cuts if lo <= c <= hi)
        return zip(cuts[:-1], cuts[1:])

    def start(self):
        for lo, hi in self.pieces(0, AHEAD):
            here = self.find(lo)
            lax.fori_loop(lo, hi, lambda f, _, here=here: (self.send(f, *here, True), 0)[1], 0)

    def run(self, lo, hi):
        for a, b in self.pieces(lo, min(hi, self.steps)):
            here, ahead = self.find(a), self.find(a + AHEAD)

            def body(f, _, here=here, ahead=ahead):
                self.receive(f, *here)
                self.flow(f)
                if ahead is not None:
                    self.send(f + AHEAD, *ahead, False)
                return 0

            lax.fori_loop(a, b, body, 0)
        if hi > self.steps:
            lax.fori_loop(max(lo, self.steps), hi, lambda t, _: (self.flow(t), 0)[1], 0)

    def run_some(self, lo, count):
        here = self.find(0)

        def body(f, _):
            self.receive(f, *here)
            self.flow(f)

            @pl.when(f + AHEAD < self.steps)
            def _():
                self.send(f + AHEAD, *here, False)
            return 0

        lax.fori_loop(lo, lo + count, body, 0)

    def finish(self, lo):
        lines, z = self.lines, self.z
        self.run(lo, self.steps + self.lag)

        def drain(f, _):
            @pl.when(self.sends(f))
            def _():
                self.x_copy(f).wait_send()
            return 0

        lax.fori_loop(self.steps - AHEAD, self.steps, drain, 0)
        for job in range(self.jobs - STAGES, self.jobs):
            self.out_wait(job)
        pl.semaphore_wait(self.c_x, min(self.slots, self.steps))

        @pl.when(z < lines - 1)
        def _():
            pl.semaphore_wait(self.c_right, DEPTH * (lines - 1 - z))

        @pl.when(z > 0)
        def _():
            pl.semaphore_wait(self.c_left, DEPTH * z)


def meet(peers):
    barrier = pltpu.get_barrier_semaphore()
    count = 0
    for there, device in peers:
        if there is None:
            pl.semaphore_signal(barrier, inc=1, device_id=device, device_id_type=MESH)
            count += 1
        else:
            @pl.when(there)
            def _():
                pl.semaphore_signal(barrier, inc=1, device_id=device, device_id_type=MESH)
            count += jnp.where(there, 1, 0)
    pl.semaphore_wait(barrier, count)
class Quad:
    def __init__(self, refs, rows, height):
        (self.tmp, self.cs, self.cr, self.ys, self.yr, self.acc, self.s_c, self.r_c, self.s_y, self.r_y,
         self.s_g, self.r_g) = refs
        ctx, tp = lax.axis_index("ctx"), lax.axis_index("tp")
        self.y, self.core, self.tp = tp // 2, lax.rem(tp, 2), tp
        self.across = (ctx, self.y * 2 + 1 - self.core)
        self.over = (ctx, (1 - self.y) * 2 + self.core)
        self.head, self.rest = PREFIX // 4, (rows - PREFIX) // 4
        self.tiles = self.cs.shape[1]
        self.height = height

    @staticmethod
    def scratch(rows, width):
        tiles = width // COLS
        return [
            pltpu.VMEM((2, rows, COLS), jnp.float32),
            pltpu.VMEM((2, tiles, rows, COLS), jnp.bfloat16),
            pltpu.VMEM((2, tiles, rows, COLS), jnp.bfloat16),
            pltpu.VMEM((tiles, rows, COLS), jnp.bfloat16),
            pltpu.VMEM((tiles, rows, COLS), jnp.bfloat16),
            pltpu.VMEM((rows, width), jnp.float32),
            pltpu.SemaphoreType.DMA((2, tiles)),
            pltpu.SemaphoreType.DMA((2, tiles)),
            pltpu.SemaphoreType.DMA((tiles,)),
            pltpu.SemaphoreType.DMA((tiles,)),
            pltpu.SemaphoreType.DMA((2, 3, 2)),
            pltpu.SemaphoreType.DMA((2, 3, 2)),
        ]

    def peers(self):
        return [(None, self.across), (None, self.over)]

    def spans(self, quarter):
        return [
            pl.ds(pl.multiple_of(quarter * self.head, 16), self.head),
            pl.ds(pl.multiple_of(PREFIX + quarter * self.rest, 16), self.rest),
        ]

    def rows_of(self, ref, quarter):
        return jnp.concatenate([ref[span] for span in self.spans(quarter)], axis=0)

    def half_of(self, ref, half):
        return jnp.concatenate([self.rows_of(ref, half * 2), self.rows_of(ref, half * 2 + 1)], axis=0)

    def c_copy(self, k, n):
        return pltpu.make_async_remote_copy(
            src_ref=self.cs.at[k, n, : self.height], dst_ref=self.cr.at[k, n, : self.height], send_sem=self.s_c.at[k, n],
            recv_sem=self.r_c.at[k, n], device_id=self.across, device_id_type=MESH)

    def y_copy(self, n):
        return pltpu.make_async_remote_copy(
            src_ref=self.ys.at[n, : self.height], dst_ref=self.yr.at[n, : self.height], send_sem=self.s_y.at[n],
            recv_sem=self.r_y.at[n], device_id=self.over, device_id_type=MESH)

    def columns(self, n):
        return pl.ds(pl.multiple_of(n * COLS, COLS), COLS)

    def split(self, value, k, n):
        rows = self.height
        self.tmp[0, :rows] = value[:rows]
        self.tmp[1, :rows] = value[rows:]
        self.cs[k, n, :rows] = self.tmp[1 - self.core, :rows].astype(jnp.bfloat16)
        self.c_copy(k, n).start()
        self.acc[:rows, self.columns(n)] = self.tmp[self.core, :rows]

    def relay(self, n):
        self.c_copy(0, n).wait_recv()
        rows = self.height
        total = self.acc[:rows, self.columns(n)] + self.cr[0, n, :rows].astype(jnp.float32)
        self.ys[n, :rows] = total.astype(jnp.bfloat16)
        self.y_copy(n).start()

    def scatter_send(self, chunk):
        def far(n, _):
            self.split(chunk(1 - self.y, n), 0, n)

            @pl.when(n > 0)
            def _():
                self.relay(n - 1)
            return 0

        lax.fori_loop(0, self.tiles, far, 0)
        self.relay(self.tiles - 1)

        def near(n, _):
            self.split(chunk(self.y, n), 1, n)
            return 0

        lax.fori_loop(0, self.tiles, near, 0)

    def scatter_add(self, n):
        self.c_copy(1, n).wait_recv()
        self.y_copy(n).wait_recv()
        rows = self.height
        came = self.cr[1, n, :rows].astype(jnp.float32) + self.yr[n, :rows].astype(jnp.float32)
        self.acc[:rows, self.columns(n)] += came

    def scatter_done(self):
        for n in range(self.tiles):
            self.c_copy(0, n).wait_send()
            self.c_copy(1, n).wait_send()
            self.y_copy(n).wait_send()

    def g_copy(self, full, k, s, quarter, device, turn):
        span = self.spans(quarter)[s]
        return pltpu.make_async_remote_copy(
            src_ref=full.at[span], dst_ref=full.at[span], send_sem=self.s_g.at[turn, k, s],
            recv_sem=self.r_g.at[turn, k, s], device_id=device, device_id_type=MESH)

    def gather_send(self, full, turn=0):
        for s in range(2):
            self.g_copy(full, 0, s, self.tp, self.over, turn).start()
        for s in range(2):
            self.g_copy(full, 1, s, self.tp, self.across, turn).start()

    def gather_near(self, full, turn=0):
        for s in range(2):
            self.g_copy(full, 1, s, self.y * 2 + 1 - self.core, self.across, turn).wait_recv()

    def gather_pass(self, full, turn=0):
        other = (1 - self.y) * 2 + self.core
        for s in range(2):
            self.g_copy(full, 0, s, other, self.over, turn).wait_recv()
            self.g_copy(full, 2, s, other, self.across, turn).start()

    def gather_far(self, full, turn=0):
        for s in range(2):
            self.g_copy(full, 2, s, (1 - self.y) * 2 + 1 - self.core, self.across, turn).wait_recv()

    def gather_done(self, full, turn=0):
        other = (1 - self.y) * 2 + self.core
        for s in range(2):
            self.g_copy(full, 0, s, self.tp, self.over, turn).wait_send()
            self.g_copy(full, 1, s, self.tp, self.across, turn).wait_send()
            self.g_copy(full, 2, s, other, self.across, turn).wait_send()


def nt(left, right):
    return lax.dot_general(left, right, (((1,), (1,)), ((), ())), preferred_element_type=jnp.float32)


def normed(values_in):
    centred = values_in - jnp.mean(values_in, axis=1, keepdims=True)
    scale = lax.rsqrt(jnp.mean(centred * centred, axis=1, keepdims=True) + EPSILON)
    return centred * scale, scale


def gelu_pair(pre):
    slope = (2.0 / math.pi) ** 0.5
    square = pre * pre
    bent = jnp.tanh(slope * (pre + 0.044715 * (square * pre)))
    half = 0.5 * (1.0 + bent)
    return pre * half, half + 0.5 * pre * (1.0 - bent * bent) * (slope * (1.0 + 3 * 0.044715 * square))


def column_sum(values_in):
    return jnp.sum(values_in, axis=0, keepdims=True)


def front_kernel(early, *refs):
    (att, w_out, x_hbm, cot_hbm, act, w1_hbm, w2_hbm, bias, gain, shift, fc1_bias,
     mid, full, grad, hid, d_pre, vec, theirs, *scratch) = refs
    quad_refs, scratch = scratch[:12], scratch[12:]
    x, w1, w2, d_hid, some, loads, s_x, r_x = scratch
    rows, width = full.shape
    quad = Quad(quad_refs, rows, rows // 4)
    spans = quad.spans(quad.tp)

    def load(n, source, target):
        copy = pltpu.make_async_copy(source, target, loads.at[n])
        copy.start()
        return copy

    cot_copy = load(0, cot_hbm, grad)
    w2_copy = load(1, w2_hbm, w2)
    x_copies = [load(2, x_hbm.at[spans[0]], x.at[: quad.head]), load(3, x_hbm.at[spans[1]], x.at[quad.head :])]
    w1_copy = load(4, w1_hbm, w1)
    ctx, tp = lax.axis_index("ctx"), lax.axis_index("tp")
    side = lax.rem(ctx, 2)
    partner = (ctx + 1 - 2 * side, tp)
    meet(quad.peers() + ([(None, partner)] if early else []))

    def half_copy(o):
        step = width // (2 * early)
        source = grad.at[:, pl.ds(pl.multiple_of((o * 2 + 1 - side) * step, step), step)]
        return pltpu.make_async_remote_copy(
            src_ref=source, dst_ref=theirs.at[:, o * step : (o + 1) * step], send_sem=s_x.at[o], recv_sem=r_x.at[o],
            device_id=partner, device_id_type=MESH)

    quad.scatter_send(lambda half, n: jnp.dot(quad.half_of(att, half), w_out[:, quad.columns(n)], preferred_element_type=jnp.float32))
    cot_copy.wait()
    vec[...] = jnp.zeros(vec.shape, jnp.float32)
    size = 32

    def gate(i, _):
        span = pl.ds(pl.multiple_of(i * size, size), size)
        low = (act[span] * grad[span].astype(jnp.float32)).astype(jnp.bfloat16)
        grad[span] = low
        vec[5:6] += column_sum(low.astype(jnp.float32)) * 0.25
        return 0

    lax.fori_loop(0, rows // size, gate, 0)
    for o in range(early):
        half_copy(o).start()
    w2_copy.wait()
    tiles = hid.shape[1] // COLS

    def d_hidden(n, _):
        d_hid[:, quad.columns(n)] = nt(grad[...], w2[quad.columns(n), :])
        return 0

    lax.fori_loop(0, tiles, d_hidden, 0)
    for copy in x_copies:
        copy.wait()
    lax.fori_loop(0, quad.tiles, lambda n, _: (quad.scatter_add(n), 0)[1], 0)

    def norm_rows(i, _):
        first = quad.head // size
        start = jnp.where(i < first, quad.tp * quad.head + i * size, PREFIX + quad.tp * quad.rest + (i - first) * size)
        whole, own = (pl.ds(pl.multiple_of(s, size), size) for s in (start, i * size))
        middle = x[own].astype(jnp.float32) + act[whole] * (quad.acc[own] + bias[...])
        mid[own] = middle
        full[whole] = (normed(middle)[0] * gain[...] + shift[...]).astype(jnp.bfloat16)
        return 0

    lax.fori_loop(0, quad.height // size, norm_rows, 0)
    quad.gather_send(full)

    def ffn(half):
        some[...] = quad.half_of(full, half)
        places = quad.spans(half * 2) + quad.spans(half * 2 + 1)

        def tile(n, _):
            cols = quad.columns(n)
            pre = jnp.dot(some[...], w1[:, cols], preferred_element_type=jnp.float32) + fc1_bias[:, cols]
            value, slope = gelu_pair(pre)
            value = value.astype(jnp.bfloat16)
            start = 0
            for place in places:
                end = start + place.size
                hid[place, cols] = value[start:end]
                change = (d_hid[place, cols] * slope[start:end]).astype(jnp.bfloat16)
                d_pre[place, cols] = change
                vec[6:7, cols] += column_sum(change.astype(jnp.float32))
                start = end
            return 0

        lax.fori_loop(0, tiles, tile, 0)

    quad.gather_near(full)
    w1_copy.wait()
    ffn(quad.y)
    quad.gather_pass(full)
    quad.gather_far(full)
    ffn(1 - quad.y)
    quad.gather_done(full)
    quad.scatter_done()
    for o in range(early):
        half_copy(o).wait()


def front_call(early, att, w_out, x, cot, act, w1, w2, bias, gain, shift, fc1_bias):
    rows, width = x.shape
    own, hidden = rows // 4, w1.shape[1]
    vm, hbm = (pl.BlockSpec(memory_space=s) for s in (pltpu.VMEM, pl.ANY))
    bf, f4, shape = jnp.bfloat16, jnp.float32, jax.ShapeDtypeStruct
    return pl.pallas_call(
        functools.partial(front_kernel, early),
        out_shape=(
            shape((own, width), f4),
            shape((rows, width), bf),
            shape((rows, width), bf),
            shape((rows, hidden), bf),
            shape((rows, hidden), bf),
            shape((8, width), f4),
            shape((rows, width // 2), bf),
        ),
        in_specs=[vm] * 2 + [hbm] * 2 + [vm] + [hbm] * 2 + [vm] * 4,
        out_specs=[vm] * 6 + [hbm],
        scratch_shapes=Quad.scratch(own, width)
        + [
            pltpu.VMEM((own, width), bf),
            pltpu.VMEM(w1.shape, bf),
            pltpu.VMEM(w2.shape, bf),
            pltpu.VMEM((rows, hidden), f4),
            pltpu.VMEM((2 * own, width), bf),
            pltpu.SemaphoreType.DMA((5,)),
            pltpu.SemaphoreType.DMA((max(early, 1),)),
            pltpu.SemaphoreType.DMA((max(early, 1),)),
        ],
        compiler_params=pltpu.CompilerParams(collective_id=1, has_side_effects=True, vmem_limit_bytes=64 * 2**20),
    )(att, w_out, x, cot, act, w1, w2, bias[None], gain[None], shift[None], fc1_bias[None])
def tn(left, right):
    return lax.dot_general(left, right, (((0,), (0,)), ((), ())), preferred_element_type=jnp.float32)


def nn(left, right):
    return jnp.dot(left, right, preferred_element_type=jnp.float32)


def lane_mask(rows, head):
    lane = lax.broadcasted_iota(jnp.int32, (rows, 2 * HEAD), 1)
    return (lane < HEAD) if head == 0 else (lane >= HEAD)


def scores_of(keys, query, bias):
    scores = nt(keys, query)
    count = scores.shape[0]
    row = lax.broadcasted_iota(jnp.int32, (PREFIX, PREFIX), 0)
    col = lax.broadcasted_iota(jnp.int32, (PREFIX, PREFIX), 1)
    parts = [scores[:PREFIX] + bias]
    if count > 2 * PREFIX:
        parts.append(scores[PREFIX : count - PREFIX])
    parts.append(jnp.where(row <= col, scores[count - PREFIX :], NEGATIVE))
    return jnp.concatenate(parts, axis=0)


def attend_back(p, bias, q_ref, k_ref, v_ref, l_ref, g_ref, d_ref, room):
    rows, width = q_ref.shape
    blocks = rows // PREFIX
    base = pl.multiple_of(p * 2 * HEAD, 2 * HEAD)
    lanes = pl.ds(base, 2 * HEAD)
    sums = jnp.zeros((1, 2 * HEAD), jnp.float32)
    for r in reversed(range(blocks)):
        count, own = (r + 2) * PREFIX, slice(r * PREFIX, (r + 1) * PREFIX)
        query, grad, keys, values = q_ref[own, lanes], g_ref[own, lanes], k_ref[:count, lanes], v_ref[:count, lanes]
        d_queries, d_keys, d_values = [], None, None
        for e in range(2):
            mask = lane_mask(PREFIX, e)
            query_e = jnp.where(mask, query, jnp.zeros_like(query))
            grad_e = jnp.where(mask, grad, jnp.zeros_like(grad))
            probs = jnp.exp(scores_of(keys, query_e, bias) - l_ref[p, e : e + 1, own])
            d_probs = nt(values, grad_e)
            inner = jnp.sum(probs * d_probs, axis=0, keepdims=True)
            d_scores = (probs * (d_probs - inner)).astype(jnp.bfloat16)
            keys_e, values_e = nn(d_scores, query_e), nn(probs.astype(jnp.bfloat16), grad_e)
            d_keys = keys_e if d_keys is None else d_keys + keys_e
            d_values = values_e if d_values is None else d_values + values_e
            d_queries.append(tn(d_scores, keys))
        d_query = jnp.where(lane_mask(PREFIX, 0), d_queries[0], d_queries[1]) * HEAD ** (-0.5)
        sums += jnp.sum(d_query, axis=0, keepdims=True)
        d_ref[(r + 1) * PREFIX : (r + 2) * PREFIX, lanes] = d_query.astype(jnp.bfloat16)
        for n in range(r + 2):
            for at, sums_of in ((n, d_keys), (blocks + 1 + n, d_values)):
                place, term = slice(at * 2 * HEAD, (at + 1) * 2 * HEAD), sums_of[n * PREFIX : (n + 1) * PREFIX]
                if r == blocks - 1:
                    room[:PREFIX, place] = term
                else:
                    room[:PREFIX, place] += term
    d_ref[:PREFIX, lanes] = jnp.zeros((PREFIX, 2 * HEAD), jnp.bfloat16)
    value_sums = jnp.zeros((1, 2 * HEAD), jnp.float32)
    for n in range(blocks + 1):
        span = slice(n * PREFIX, (n + 1) * PREFIX)
        for m, at in ((1, n), (2, blocks + 1 + n)):
            total = room[:PREFIX, at * 2 * HEAD : (at + 1) * 2 * HEAD]
            d_ref[span, pl.ds(pl.multiple_of(base + m * width, 2 * HEAD), 2 * HEAD)] = total.astype(jnp.bfloat16)
            if m == 2:
                value_sums += column_sum(total)
    return sums, value_sums


def own_block(quad, i, size):
    first = quad.head // size
    start = jnp.where(i < first, quad.tp * quad.head + i * size, PREFIX + quad.tp * quad.rest + (i - first) * size)
    return pl.ds(pl.multiple_of(start, size), size), pl.ds(pl.multiple_of(i * size, size), size)


def norm_back(grad, source, gain):
    unit, scale = normed(source)
    scaled = grad * gain
    mean = jnp.mean(scaled, axis=1, keepdims=True)
    slope = jnp.mean(scaled * unit, axis=1, keepdims=True)
    return scale * (scaled - mean - unit * slope), grad * unit


def product_part(left, right, tile, turned, rows):
    def part(j, block):
        cols = pl.ds(pl.multiple_of(tile(j) * COLS, COLS), COLS)
        span = pl.ds(pl.multiple_of(block * rows, rows), rows)
        if turned:
            return nn(left[span, :], right[:, cols])
        return tn(left[:, span], right[:, cols])

    return part


def pick(table, j):
    found = table[0]
    for n, entry in enumerate(table[1:]):
        found = jnp.where(j == n + 1, entry, found)
    return found


class Wide(Quad):
    def rows_of(self, ref, quarter):
        own = [pl.ds(pl.multiple_of(span.start + PREFIX, 16), span.size) for span in self.spans(quarter)]
        return jnp.concatenate([ref[span] for span in [self.spans(quarter)[0]] + own], axis=0)


def back_kernel(lines, turned, *refs):
    (g_hbm, h2_hbm, hid_hbm, dpre_hbm, w1_hbm, w_qkv_hbm, w2_hbm, wo_hbm, h_hbm, att_hbm, mid_hbm, cot_hbm, x_hbm, gp_hbm,
     act, gain1, gain2, ffn_bias, bias, weight, theirs, q, k, v, lse, vec_in,
     fc2_out, fc1_out, out_grad, qkv_grad, in_hbm, act_hbm, dmid_hbm, dh_hbm, land_hbm, vec, *scratch) = refs
    ring_refs, scratch = scratch[:16], scratch[16:]
    quad_refs, scratch = scratch[:12], scratch[12:]
    (x0, x1, y0, y1, weights, mid, own_in, full, d_att, d_all, fresh, back, v_send, v_recv, g_theirs, tile_in,
     loads, stores, s_v, r_v, s_t, r_t, c_over) = scratch
    rows, width = full.shape
    quad, wide = Quad(quad_refs, rows, rows // 4), Wide(quad_refs, rows, (rows + PREFIX) // 4)
    own_rows, depth = quad.height, q.shape[1]
    tiles, cols = y0.shape[1] // COLS, depth // COLS
    block_rows = ring_refs[0].shape[1]
    extra = fresh.shape[0] // block_rows
    order1 = [*range(tiles - 2), tiles - 1, tiles - 2]
    later = ((0, 2 * tiles - 1),)
    base = 2 * tiles + 1 + extra
    g_part = x0.at[:, :rows] if turned else x0.at[:rows]
    columns = lambda n: pl.ds(pl.multiple_of(n * COLS, COLS), COLS)

    def tile_copy(n):
        return pltpu.make_async_remote_copy(
            src_ref=y0.at[:, n * COLS : (n + 1) * COLS], dst_ref=land_hbm.at[n], send_sem=s_t.at[n], recv_sem=r_t.at[n],
            device_id=ring.partner, device_id_type=MESH)

    def tile_part(j, block):
        @pl.when(block < 2)
        def _():
            for n in range(tiles):
                @pl.when(j == n)
                def _():
                    tile_copy(n).wait_recv()
            fetch = pltpu.make_async_copy(land_hbm.at[j], tile_in, loads.at[11])
            fetch.start()
            fetch.wait()

        span = pl.ds(pl.multiple_of(block * block_rows, block_rows), block_rows)
        side_span = pl.ds(pl.multiple_of(block // 2 * block_rows, block_rows), block_rows)
        return tn(g_part[:, span], y0[:, columns(j)]) + tn(g_theirs[:, side_span], tile_in[...])

    def prefix_part(j, block):
        return fresh[pl.ds(pl.multiple_of(j * block_rows, block_rows), block_rows)]

    def outs(job):
        local = job - tiles - 1
        head = jnp.maximum(job - base - cols, 0)
        place2, place1 = columns(jnp.clip(job - 1, 0, tiles - 1)), columns(pick(order1, local))
        is2 = (job > 0) & (job <= tiles)
        is1 = (job > tiles) & (job <= 2 * tiles)
        is_out = (job >= base) & (job < base + cols)
        out_span = columns(jnp.clip(job - base, 0, cols - 1))
        return [
            (is2, True, fc2_out.at[place2]),
            (is1, False, fc1_out.at[:, place1]),
            (is_out, True, out_grad.at[out_span]),
            (job >= base + cols, False, qkv_grad.at[head // cols, :, columns(lax.rem(head, cols))]),
        ]

    fc2_part = product_part(g_part, y0, lambda j: j, turned, block_rows) if turned else tile_part
    groups = [
        (1, product_part(x1, y1, lambda j: tiles - 1, turned, block_rows), "x"),
        (tiles, fc2_part, "x" if turned else "t"),
        (tiles, product_part(x1, y1, lambda j: pick(order1, j), turned, block_rows), "x"),
        (extra, prefix_part, "p"),
        (cols, product_part(x1 if turned else full, d_att, lambda j: j, turned, block_rows), "x"),
        (3 * cols, product_part(x0, d_all, lambda j: j, turned, block_rows), "x"),
    ]
    ring = Ring(lines, groups, ring_refs, outs, later, (weight, theirs, back))

    def load(n, source, target):
        return pltpu.make_async_copy(source, target, loads.at[n])

    def store(n, source, target):
        return pltpu.make_async_copy(source, target, stores.at[n])

    def begin(*copies):
        for copy in copies:
            copy.start()

    def end(*copies):
        for copy in copies:
            copy.wait()

    spans = quad.spans(quad.tp)
    first = [load(0, hid_hbm, y0), load(2, dpre_hbm, y1), load(4, h2_hbm, x1)]
    second = [load(3, w1_hbm, weights), load(1, g_hbm, g_part)]
    if not turned:
        second.append(load(12, gp_hbm, g_theirs))
    third = [
        load(5, mid_hbm, mid),
        load(6, cot_hbm.at[spans[0]], own_in.at[: quad.head]),
        load(7, cot_hbm.at[spans[1]], own_in.at[quad.head :]),
    ]
    begin(*first, *second, *third)
    ctx, tp = lax.axis_index("ctx"), lax.axis_index("tp")
    swaps, bit = [quad.across, quad.over], 1
    while bit < 2 * lines:
        swaps.append((ctx + bit - 2 * bit * lax.rem(ctx // bit, 2), tp))
        bit *= 2
    meet(ring.peers() + quad.peers() + [(None, device) for device in swaps[4:]])

    def swap(n):
        return pltpu.make_async_remote_copy(
            src_ref=v_send.at[n], dst_ref=v_recv.at[n], send_sem=s_v.at[n], recv_sem=r_v.at[n],
            device_id=swaps[n], device_id_type=MESH)

    def swap_start(n):
        v_send[n] = vec[...]
        swap(n).start()

    def swap_end(n):
        swap(n).wait()
        if n < 2:
            vec[:6] += v_recv[n, :6]
        else:
            vec[...] += v_recv[n]

    def add_all(group):
        lax.fori_loop(0, group.tiles, lambda n, _: (group.scatter_add(n), 0)[1], 0)

    end(first[0])
    if not turned:
        for n in range(tiles):
            tile_copy(n).start()
    end(*first[1:])
    ring.start()
    ring.run(0, 2)
    end(*second)
    quad.scatter_send(lambda part, n: nt(quad.half_of(y1, part), weights[quad.columns(n), :]))
    wo_copy = load(3, wo_hbm, weights.at[:depth])
    wo_copy.start()
    end(*third)
    ring.run(2, 5)
    add_all(quad)
    vec[...] = vec_in[...]
    size = 32

    def middle_rows(i, _):
        whole, own = own_block(quad, i, size)
        grad = quad.acc[own]
        change, gain_terms = norm_back(grad, mid[own], gain2[...])
        d_middle = own_in[own].astype(jnp.float32) + change
        quad.acc[own] = d_middle
        low = (act[whole] * d_middle).astype(jnp.bfloat16)
        full[whole] = low
        vec[2:3] += column_sum(low.astype(jnp.float32))
        vec[3:4] += column_sum(gain_terms)
        vec[4:5] += column_sum(grad)
        return 0

    lax.fori_loop(0, own_rows // size, middle_rows, 0)
    quad.gather_send(full)
    keep = store(0, quad.acc.at[:own_rows], dmid_hbm)
    x_copies = [load(6, x_hbm.at[spans[0]], own_in.at[: quad.head]), load(7, x_hbm.at[spans[1]], own_in.at[quad.head :])]
    begin(keep, *x_copies)
    ring.run(5, 10)
    quad.gather_near(full)
    quad.gather_pass(full)
    quad.gather_far(full)
    wo_copy.wait()

    def attended_rows(i, _):
        span = pl.ds(pl.multiple_of(i * PREFIX, PREFIX), PREFIX)
        d_att[span] = nt(full[span], weights[:depth, :]).astype(jnp.bfloat16)
        return 0

    lax.fori_loop(0, rows // PREFIX, attended_rows, 0)
    heads = [load(8 + m, w_qkv_hbm.at[m], weights.at[:, m * depth : (m + 1) * depth]) for m in range(3)]
    begin(*heads)
    keep.wait()
    pairs = depth // (2 * HEAD)

    now = 10
    for p in range(pairs):
        sums, value_sums = attend_back(p, bias[0, 0], q, k, v, lse, d_att, d_all, quad.acc)
        start = p * 2 * HEAD
        vec[7:8, start : start + 2 * HEAD] = sums
        vec[7:8, start + depth : start + depth + 2 * HEAD] = value_sums
        ring.run(now, now + 2)
        now += 2
    att_copy = load(2, att_hbm, d_att)
    att_copy.start()
    quad.gather_done(full)
    quad.scatter_done()
    end(*heads)
    wide.scatter_send(lambda part, n: nt(wide.half_of(d_all, part), weights[wide.columns(n), : 3 * depth]))
    w2_copy = load(3, w2_hbm, weights)
    w2_copy.start()
    free0, free1 = (tiles + 1) * lines, (2 * tiles + 1) * lines
    ring.run(now, free0)
    h_copy = load(1, h_hbm, x0)
    h_copy.start()
    ring.run(free0, free0 + 2)
    add_all(wide)
    pl.semaphore_signal(c_over, inc=1, device_id=quad.over, device_id_type=MESH)
    for n in range(wide.tiles):
        fresh[n * wide.head : (n + 1) * wide.head] = wide.acc[: wide.head, n * COLS : (n + 1) * COLS]
    dh_copy = store(1, wide.acc.at[pl.ds(wide.head, own_rows)], dh_hbm)
    dh_copy.start()
    att_copy.wait()
    ring.run(free0 + 2, free1 - AHEAD)
    h_copy.wait()
    ring.run(free1 - AHEAD, free1)
    if turned:

        def flip(n, _):
            x1[columns(n), :] = full[:, columns(n)].T
            return 0

        lax.fori_loop(0, width // COLS, flip, 0)
    wide.scatter_done()
    end(dh_copy, w2_copy)
    pl.semaphore_wait(c_over, 1)
    if not turned:
        for n in range(tiles):
            tile_copy(n).wait_send()
    quad.scatter_send(lambda part, n: nn(quad.half_of(y0, part), weights[:, quad.columns(n)]))
    ring.run(free1, free1 + lines)
    add_all(quad)

    def out_rows(i, _):
        whole, own = own_block(quad, i, size)
        y1[whole] = (mid[own] + act[whole] * (quad.acc[own] + ffn_bias[...])).astype(jnp.bfloat16)
        return 0

    lax.fori_loop(0, own_rows // size, out_rows, 0)
    quad.gather_send(y1)
    again = [load(4, dh_hbm, quad.acc.at[:own_rows]), load(5, dmid_hbm, mid)]
    begin(*again)
    ready = base * lines + SKEW * (lines - 1)
    ring.run(free1 + lines, ready)
    quad.gather_near(y1)
    quad.gather_pass(y1)
    quad.gather_far(y1)
    act_copy = store(0, y1, act_hbm)
    act_copy.start()
    end(*again, *x_copies)
    for n in range(quad.tiles):
        quad.acc[: quad.head, n * COLS : (n + 1) * COLS] += back[n * quad.head : (n + 1) * quad.head]

    def input_rows(i, _):
        whole, own = own_block(quad, i, size)
        grad = quad.acc[own]
        change, gain_terms = norm_back(grad, own_in[own].astype(jnp.float32), gain1[...])
        y0[whole] = (mid[own] + change).astype(jnp.bfloat16)
        vec[0:1] += column_sum(gain_terms)
        vec[1:2] += column_sum(grad)
        return 0

    lax.fori_loop(0, own_rows // size, input_rows, 0)
    quad.gather_send(y0, 1)
    swap_start(0)
    late = min(max(ready, ring.steps - AHEAD), ring.steps - 4)
    ring.run(ready, late)
    swap_end(0)
    swap_start(1)
    ring.run(late, late + 2)
    swap_end(1)
    swap_start(2)
    ring.run(late + 2, ring.steps)
    quad.gather_near(y0, 1)
    quad.gather_pass(y0, 1)
    swap_end(2)
    swap_start(3)
    ring.run(ring.steps, ring.steps + SKEW)
    quad.gather_far(y0, 1)
    in_copy = store(1, y0, in_hbm)
    in_copy.start()
    swap_end(3)
    for n in range(4, len(swaps)):
        swap_start(n)
        if n + 1 == len(swaps):
            ring.run(ring.steps + SKEW, ring.steps + 2 * SKEW)
        swap_end(n)
    ring.finish(ring.steps + 2 * SKEW)
    quad.gather_done(y1)
    quad.gather_done(y0, 1)
    quad.scatter_done()
    end(act_copy, in_copy)


def back_call(n_ctx, turned, g, h2, hid, dpre, w1, w_qkv, w2, w_out, h_all, att, mid, cot, x, g_theirs, act, gain1, gain2, ffn_bias,
              bias, weight, theirs, q, k, v, lse, vec):
    lines, rows, width = n_ctx // 2, cot.shape[0], cot.shape[1]
    block_rows, own, cols = width // n_ctx, rows // 4, q.shape[1]
    hidden = hid.shape[1]
    returned = PREFIX * width // 4 // COLS
    rounds = n_ctx.bit_length() + 1
    vm, hbm, sm = (pl.BlockSpec(memory_space=s) for s in (pltpu.VMEM, pl.ANY, pltpu.SMEM))
    bf, f4 = jnp.bfloat16, jnp.float32
    shape = jax.ShapeDtypeStruct
    return pl.pallas_call(
        functools.partial(back_kernel, lines, turned),
        out_shape=(
            shape((hidden, block_rows), f4),
            shape((block_rows, hidden), f4),
            shape((cols, block_rows), f4),
            shape((3, block_rows, cols), f4),
            shape((rows, width), bf),
            shape((rows, width), bf),
            shape((own, width), f4),
            shape((own, width), f4),
            shape((hidden // COLS, rows, COLS), bf),
            shape(vec.shape, f4),
        ),
        in_specs=[hbm] * 14 + [vm] * 4 + [sm] * 3 + [vm] * 5,
        out_specs=[hbm] * 9 + [vm],
        scratch_shapes=Ring.scratch(lines, block_rows)
        + Quad.scratch(own + PREFIX // 4, width)
        + [
            pltpu.VMEM(h_all.shape, bf),
            pltpu.VMEM(h2.shape, bf),
            pltpu.VMEM((rows, hidden), bf),
            pltpu.VMEM((rows, hidden), bf),
            pltpu.VMEM(w1.shape, bf),
            pltpu.VMEM((own, width), f4),
            pltpu.VMEM((own, width), bf),
            pltpu.VMEM((rows, width), bf),
            pltpu.VMEM((rows, cols), bf),
            pltpu.VMEM((rows + PREFIX, 3 * cols), bf),
            pltpu.VMEM((returned, COLS), f4),
            pltpu.VMEM((returned, COLS), f4),
            pltpu.VMEM((rounds, *vec.shape), f4),
            pltpu.VMEM((rounds, *vec.shape), f4),
            pltpu.VMEM((16, 128) if turned else g_theirs.shape, bf),
            pltpu.VMEM((16, 128) if turned else (rows, COLS), bf),
            pltpu.SemaphoreType.DMA((13,)),
            pltpu.SemaphoreType.DMA((2,)),
            pltpu.SemaphoreType.DMA((rounds,)),
            pltpu.SemaphoreType.DMA((rounds,)),
            pltpu.SemaphoreType.DMA((hidden // COLS,)),
            pltpu.SemaphoreType.DMA((hidden // COLS,)),
            pltpu.SemaphoreType.REGULAR,
        ],
        compiler_params=pltpu.CompilerParams(collective_id=2, has_side_effects=True, vmem_limit_bytes=64 * 2**20),
    )(g, h2, hid, dpre, w1, w_qkv, w2, w_out, h_all, att, mid, cot, x, g_theirs, act, gain1[None], gain2[None], ffn_bias[None],
      bias, weight, theirs, q, k, v, lse, vec)


def find_block(lengths, placed, block):
    mine, start, first = placed[block], 0, 0
    for s in range(lengths.shape[0]):
        first = jnp.where(start <= mine, start, first)
        start = start + lengths[s]
    owner = 0
    for e in range(placed.shape[0]):
        owner = owner + jnp.where(placed[e] == first, e, 0)
    return mine - first, jnp.minimum(owner, placed.shape[0] - 1)


def attend_own(p, q, k, v, held, peaks, totals):
    lanes = pl.ds(pl.multiple_of(p * 2 * HEAD, 2 * HEAD), 2 * HEAD)
    rows = q.shape[0]
    value_t = v[PREFIX:, lanes].T
    row = lax.broadcasted_iota(jnp.int32, (PREFIX, PREFIX), 0)
    col = lax.broadcasted_iota(jnp.int32, (PREFIX, PREFIX), 1)
    for r in range(rows // PREFIX):
        own, count = slice(r * PREFIX, (r + 1) * PREFIX), (r + 1) * PREFIX
        query, keys = q[own, lanes], k[PREFIX : PREFIX + count, lanes]
        for e in range(2):
            scores = nt(keys, jnp.where(lane_mask(PREFIX, e), query, jnp.zeros_like(query)))
            last = jnp.where(row <= col, scores[count - PREFIX :], NEGATIVE)
            scores = jnp.concatenate([scores[: count - PREFIX], last], axis=0) if r else last
            peak = jnp.max(scores, axis=0, keepdims=True)
            raised = jnp.exp(scores - peak)
            peaks[p, e : e + 1, own] = peak
            totals[p, e : e + 1, own] = jnp.sum(raised, axis=0, keepdims=True)
            part = slice(e * HEAD, (e + 1) * HEAD)
            held[p, part, own] = nn(value_t[part, :count], raised.astype(jnp.bfloat16))


def attend_prefix(p, bias, q, k, v, held, peaks, totals, out, lse):
    lanes = pl.ds(pl.multiple_of(p * 2 * HEAD, 2 * HEAD), 2 * HEAD)
    query, keys, value_t = q[:, lanes], k[:PREFIX, lanes], v[:PREFIX, lanes].T
    outs = []
    for e in range(2):
        scores = nt(keys, jnp.where(lane_mask(q.shape[0], e), query, jnp.zeros_like(query))) + bias
        before = peaks[p, e : e + 1]
        peak = jnp.maximum(before, jnp.max(scores, axis=0, keepdims=True))
        raised = jnp.exp(scores - peak)
        shrink = jnp.exp(before - peak)
        total = totals[p, e : e + 1] * shrink + jnp.sum(raised, axis=0, keepdims=True)
        lse[p, e : e + 1] = peak + jnp.log(total)
        part = slice(e * HEAD, (e + 1) * HEAD)
        summed = held[p, part] * shrink + nn(value_t[part], raised.astype(jnp.bfloat16))
        outs.append(summed * (1.0 / total))
    out[:, lanes] = jnp.concatenate(outs, axis=0).astype(jnp.bfloat16).T


def first_kernel(lines, *refs):
    (lengths, placed, layer, exits, x_hbm, w_hbm, gain, shift, qv_bias,
     q, k, v, h_all, act, att, lse, bias, weight, theirs, *scratch) = refs
    (x, w, line, x_send, x_recv, prefix, held, peaks, totals, loads, s_l, s_r, r_z, s_x, r_x, s_g, r_g) = scratch
    rows, width = x.shape
    part = prefix.shape[0] // 4
    ctx, tp = lax.axis_index("ctx"), lax.axis_index("tp")
    z, side, y, core = ctx // 2, lax.rem(ctx, 2), tp // 2, lax.rem(tp, 2)
    left, right, partner = (ctx - 2, tp), (ctx + 2, tp), (z * 2 + 1 - side, tp)
    across, over = (ctx, y * 2 + 1 - core), (ctx, (1 - y) * 2 + core)
    own = pl.ds(pl.multiple_of(tp * part, 16), part)
    copies = [
        pltpu.make_async_copy(x_hbm.at[own], line.at[z], loads.at[0]),
        pltpu.make_async_copy(x_hbm, x, loads.at[1]),
        pltpu.make_async_copy(w_hbm, w, loads.at[2]),
    ]
    for copy in copies:
        copy.start()
    meet([(None, partner), (z > 0, left), (z < lines - 1, right), (None, across), (None, over)])

    def hop(o, device, sems):
        return pltpu.make_async_remote_copy(
            src_ref=line.at[o], dst_ref=line.at[o], send_sem=sems.at[o], recv_sem=r_z.at[o],
            device_id=device, device_id_type=MESH)

    def pass_on(o, there, device, sems):
        @pl.when(there)
        def _():
            hop(o, device, sems).start()

    copies[0].wait()
    pass_on(z, z < lines - 1, right, s_r)
    pass_on(z, z > 0, left, s_l)

    def hops(d):
        @pl.when(z - d >= 0)
        def _():
            hop(z - d, left, s_l).wait_recv()
            pass_on(z - d, z < lines - 1, right, s_r)

        @pl.when(z + d < lines)
        def _():
            hop(z + d, right, s_r).wait_recv()
            pass_on(z + d, z > 0, left, s_l)

    my_part, my_owner = find_block(lengths, placed, ctx)
    partner_part, partner_owner = find_block(lengths, placed, z * 2 + 1 - side)
    bias[0, 0] = jnp.where(my_part > 0, 0.0, NEGATIVE)
    for e in range(weight.shape[0]):
        weight[e] = jnp.where((my_owner == e) & (my_part > 0), 1.0, 0.0)
        theirs[e] = jnp.where((partner_owner == e) & (partner_part > 0), 1.0, 0.0)
    row = lax.broadcasted_iota(jnp.int32, exits.shape, 0)
    first_rows = jnp.where(my_part == 0, PREFIX, 0)
    act[...] = jnp.where((exits[...] > layer[0]) | (row < first_rows), 1.0, 0.0)
    size = 64

    def norm_rows(source, start, to):
        def some(i, _):
            span = pl.ds(pl.multiple_of(start + i * size, size), size)
            values = source[span].astype(jnp.float32)
            target = pl.ds(pl.multiple_of(to + i * size, size), size)
            h_all[target] = (normed(values)[0] * gain[...] + shift[...]).astype(jnp.bfloat16)
            return 0

        lax.fori_loop(0, PREFIX // size, some, 0)

    def keys_of(span, rows_in):
        k[span] = nn(rows_in, w[1]).astype(jnp.bfloat16)
        v[span] = (nn(rows_in, w[2]) + qv_bias[1:2]).astype(jnp.bfloat16)

    for r in range(rows // PREFIX):
        norm_rows(x_wait(copies, r, x), r * PREFIX, (r + 1) * PREFIX)
        if r == 0:
            copies[2].wait()
        span = slice((r + 1) * PREFIX, (r + 2) * PREFIX)
        rows_in = h_all[span]
        low = (nn(rows_in, w[0]) + qv_bias[0:1]).astype(jnp.bfloat16)
        q[r * PREFIX : (r + 1) * PREFIX] = low * jnp.bfloat16(HEAD**-0.5)
        keys_of(span, rows_in)
        if r + 1 < lines:
            hops(r + 1)
    for d in range(rows // PREFIX + 1, lines):
        hops(d)
    x_send[...] = line[partner_owner // 2]
    trade = pltpu.make_async_remote_copy(
        src_ref=x_send, dst_ref=x_recv, send_sem=s_x, recv_sem=r_x, device_id=partner, device_id_type=MESH)
    trade.start()
    near = line[my_owner // 2]
    pairs = q.shape[1] // (2 * HEAD)

    def own_pairs(lo, hi):
        lax.fori_loop(lo, hi, lambda p, _: (attend_own(p, q, k, v, held, peaks, totals), 0)[1], 0)

    own_pairs(0, pairs // 2)
    trade.wait_recv()
    prefix[own] = jnp.where(lax.rem(my_owner, 2) == side, near, x_recv[...])

    def give(n, quarter, device):
        span = pl.ds(pl.multiple_of(quarter * part, 16), part)
        return pltpu.make_async_remote_copy(
            src_ref=prefix.at[span], dst_ref=prefix.at[span], send_sem=s_g.at[n], recv_sem=r_g.at[n],
            device_id=device, device_id_type=MESH)

    far = (1 - y) * 2 + core
    give(0, tp, over).start()
    give(1, tp, across).start()
    own_pairs(pairs // 2, pairs)
    give(0, far, over).wait_recv()
    give(2, far, across).start()
    give(1, y * 2 + 1 - core, across).wait_recv()
    give(2, (1 - y) * 2 + 1 - core, across).wait_recv()
    norm_rows(prefix, 0, 0)
    keys_of(slice(0, PREFIX), h_all[:PREFIX])
    hide = jnp.where(my_part > 0, 0.0, NEGATIVE)

    def prefix_pair(p, _):
        attend_prefix(p, hide, q, k, v, held, peaks, totals, att, lse)
        return 0

    lax.fori_loop(0, pairs, prefix_pair, 0)
    trade.wait_send()
    give(0, tp, over).wait_send()
    give(1, tp, across).wait_send()
    give(2, far, across).wait_send()
    for o in range(lines):
        @pl.when((z < lines - 1) & (z >= o))
        def _():
            hop(o, right, s_r).wait_send()

        @pl.when((z > 0) & (z <= o))
        def _():
            hop(o, left, s_l).wait_send()


def x_wait(copies, r, x):
    if r == 0:
        copies[1].wait()
    return x


def first_call(n_ctx, lengths, placed, layer, exits, x, w_qkv, gain, shift, qv_bias):
    lines, (rows, width) = n_ctx // 2, x.shape
    cols = w_qkv.shape[2]
    vm, hbm, sm = (pl.BlockSpec(memory_space=s) for s in (pltpu.VMEM, pl.ANY, pltpu.SMEM))
    bf, f4 = jnp.bfloat16, jnp.float32
    return pl.pallas_call(
        functools.partial(first_kernel, lines),
        out_shape=(
            jax.ShapeDtypeStruct((rows, cols), bf),
            jax.ShapeDtypeStruct((rows + PREFIX, cols), bf),
            jax.ShapeDtypeStruct((rows + PREFIX, cols), bf),
            jax.ShapeDtypeStruct((rows + PREFIX, width), bf),
            jax.ShapeDtypeStruct((rows, 1), f4),
            jax.ShapeDtypeStruct((rows, cols), bf),
            jax.ShapeDtypeStruct((cols // (2 * HEAD), 2, rows), f4),
            jax.ShapeDtypeStruct((1, 1), f4),
            jax.ShapeDtypeStruct((n_ctx,), f4),
            jax.ShapeDtypeStruct((n_ctx,), f4),
        ),
        in_specs=[sm] * 3 + [vm] + [hbm] * 2 + [vm] * 3,
        out_specs=[vm] * 7 + [sm] * 3,
        scratch_shapes=[
            pltpu.VMEM((rows, width), bf),
            pltpu.VMEM(w_qkv.shape, bf),
            pltpu.VMEM((lines, PREFIX // 4, width), bf),
            pltpu.VMEM((PREFIX // 4, width), bf),
            pltpu.VMEM((PREFIX // 4, width), bf),
            pltpu.VMEM((PREFIX, width), bf),
            pltpu.VMEM((cols // (2 * HEAD), 2 * HEAD, rows), f4),
            pltpu.VMEM((cols // (2 * HEAD), 2, rows), f4),
            pltpu.VMEM((cols // (2 * HEAD), 2, rows), f4),
            pltpu.SemaphoreType.DMA((3,)),
            pltpu.SemaphoreType.DMA((lines,)),
            pltpu.SemaphoreType.DMA((lines,)),
            pltpu.SemaphoreType.DMA((lines,)),
            pltpu.SemaphoreType.DMA,
            pltpu.SemaphoreType.DMA,
            pltpu.SemaphoreType.DMA((3,)),
            pltpu.SemaphoreType.DMA((3,)),
        ],
        compiler_params=pltpu.CompilerParams(collective_id=4, has_side_effects=True, vmem_limit_bytes=64 * 2**20),
    )(lengths, placed, layer, exits[:, None], x, w_qkv, gain[None], shift[None], qv_bias)


def body(
    mesh,
    block_input,
    cotangent,
    ln1_gain,
    ln1_bias,
    w_qkv,
    qv_bias,
    w_out,
    out_bias,
    ln2_gain,
    ln2_bias,
    w_fc1,
    fc1_bias,
    w_fc2,
    fc2_bias,
    exit_layer,
    layer_index,
    lengths,
    stretch_map,
):
    n_ctx = mesh.shape["ctx"]
    row_count, width = block_input.shape
    block_rows = width // n_ctx
    turned = block_rows % 128 != 0

    def tokens_last(array):
        return array.T if turned else array

    query, key, value, h_all, active, attended, log_total, bias, weight, theirs = first_call(
        n_ctx, lengths, stretch_map, layer_index, exit_layer, block_input, w_qkv, ln1_gain, ln1_bias, qv_bias
    )
    middle, h2_low, grad_ffn, hidden_low, d_pre_low, vectors, grad_theirs = front_call(
        0 if turned else n_ctx // 2, attended, w_out, block_input, cotangent, active, w_fc1, w_fc2, out_bias, ln2_gain, ln2_bias, fc1_bias
    )
    fc2_grad, fc1_grad, out_grad, qkv_grad, input_grad, output_rows, _, _, _, vectors = back_call(
        n_ctx, turned, tokens_last(grad_ffn), tokens_last(h2_low), hidden_low, d_pre_low, w_fc1, w_qkv, w_fc2, w_out,
        tokens_last(h_all), attended, middle, cotangent, block_input, grad_theirs, active, ln1_gain, ln2_gain, fc2_bias,
        bias, weight, theirs, query, key, value, log_total, vectors,
    )
    qv_grad = vectors[7, : 2 * query.shape[1]].reshape(2, -1)
    return (
        output_rows,
        input_grad,
        vectors[0],
        vectors[1],
        qkv_grad,
        qv_grad,
        out_grad,
        vectors[2],
        vectors[3],
        vectors[4],
        fc1_grad,
        vectors[6],
        fc2_grad,
        vectors[5],
    )


def solution(mesh):
    in_specs = (
        P("ctx", None),
        P("ctx", None),
        P(),
        P(),
        P(None, None, "tp"),
        P(None, "tp"),
        P("tp", None),
        P(),
        P(),
        P(),
        P(None, "tp"),
        P("tp"),
        P("tp", None),
        P(),
        P("ctx"),
        P(),
        P(),
        P(),
    )
    out_specs = (
        P("ctx", None),
        P("ctx", None),
        P(),
        P(),
        P(None, "ctx", "tp"),
        P(None, "tp"),
        P("tp", "ctx"),
        P(),
        P(),
        P(),
        P("ctx", "tp"),
        P("tp"),
        P("tp", "ctx"),
        P(),
    )
    return jax.shard_map(functools.partial(body, mesh), mesh=mesh, in_specs=in_specs, out_specs=out_specs, check_vma=False)
```
